32 devices in a mesh: doc: 16 (over z, x, core), pair: 2 (over y).
Axes of the slice: x: 2, y: 2, z: 4, core: 2. Of those that a mesh axis runs over, the one named last changes fastest.
Arguments:
- hidden_in: bfloat16 [16384, 768], P(('doc', 'pair')), may hold values from -6 to 6
- cotangent: bfloat16 [16384, 768], P(('doc', 'pair')), may hold values from -6 to 6
- span_lengths: int32 [128], P(('doc', 'pair')), may hold values from 32 to 128, as said below
- partner_span: int32 [16, 4], P('doc'), may hold values from 0 to 3, each once within a row
- query_weight: bfloat16 [768, 768], P(('doc', 'pair')), may hold values from -0.21875 to 0.21875
- query_bias: bfloat16 [768], P(('doc', 'pair')), may hold values from -3 to 3
- key_weight: bfloat16 [768, 768], P(('doc', 'pair')), may hold values from -0.21875 to 0.21875
- value_weight: bfloat16 [768, 768], P(('doc', 'pair')), may hold values from -0.21875 to 0.21875
- value_bias: bfloat16 [768], P(('doc', 'pair')), may hold values from -3 to 3
- output_weight: bfloat16 [768, 768], P(('doc', 'pair')), may hold values from -0.625 to 0.625
- output_bias: bfloat16 [768], P(('doc', 'pair')), may hold values from -3 to 3
- first_gain: bfloat16 [768], P(('doc', 'pair')), may hold values from 0.5 to 1.5
- first_shift: bfloat16 [768], P(('doc', 'pair')), may hold values from -2 to 2
- inner_weight: bfloat16 [768, 3072], P(('doc', 'pair')), may hold values from -0.21875 to 0.21875
- inner_bias: bfloat16 [3072], P(('doc', 'pair')), may hold values from -3 to 3
- outer_weight: bfloat16 [3072, 768], P(('doc', 'pair')), may hold values from -0.109375 to 0.109375
- outer_bias: bfloat16 [768], P(('doc', 'pair')), may hold values from -3 to 3
- second_gain: bfloat16 [768], P(('doc', 'pair')), may hold values from 0.5 to 1.5
- second_shift: bfloat16 [768], P(('doc', 'pair')), may hold values from -3 to 3
Outputs:
- layer_out: bfloat16 [16384, 768], P(('doc', 'pair'))
- input_gradient: bfloat16 [16384, 768], P(('doc', 'pair'))
- span_loss: float32 [128], P(('doc', 'pair'))
- query_weight_gradient: float32 [768, 768], P(('doc', 'pair'))
- query_bias_gradient: float32 [768], P(('doc', 'pair'))
- key_weight_gradient: float32 [768, 768], P(('doc', 'pair'))
- value_weight_gradient: float32 [768, 768], P(('doc', 'pair'))
- value_bias_gradient: float32 [768], P(('doc', 'pair'))
- output_weight_gradient: float32 [768, 768], P(('doc', 'pair'))
- output_bias_gradient: float32 [768], P(('doc', 'pair'))
- first_gain_gradient: float32 [768], P(('doc', 'pair'))
- first_shift_gradient: float32 [768], P(('doc', 'pair'))
- inner_weight_gradient: float32 [768, 3072], P(('doc', 'pair'))
- inner_bias_gradient: float32 [3072], P(('doc', 'pair'))
- outer_weight_gradient: float32 [3072, 768], P(('doc', 'pair'))
- outer_bias_gradient: float32 [768], P(('doc', 'pair'))
- second_gain_gradient: float32 [768], P(('doc', 'pair'))
- second_shift_gradient: float32 [768], P(('doc', 'pair'))
The draws below stay inside these ranges and needn't reach their ends.
Inputs may be any that keep to these rules, and one draw needn't show every extreme that they name: A span's live tokens fill the first span_lengths of its 128 slots; the rest is padding. `partner_span`: each row is a permutation of the 4 spans of a document's second partner.
All inputs are finite; a program needn't handle non-finite values.
Results may differ from the reference program's by a relative error of at most 0.014.
Values may be sent and summed in bfloat16 or wider, within the bound.
No kernel may reach another device: no remote copies, remote signals or barrier semaphores. Data moves between devices by JAX's collectives and lax.ppermute only.
A program may use at most 192 MiB of HBM per device.

```python
import math
import jax
import jax.numpy as jnp
from jax import lax

D = 768
HEAD_DIM = 64
FF = 3072
SPAN = 128
SPANS_ROW = 4
SPANS_DEV = 4
TOKENS = 16384
SPANS = 128
N_DOC = 16


def draw_span_lengths(key, part):
    key = jax.random.fold_in(key, 11)
    first_key, second_key = jax.random.split(key)
    lengths = jax.random.randint(first_key, (SPANS,), SPAN // 4, SPAN + 1)
    chosen = jax.random.randint(second_key, (), 0, SPANS)
    return jnp.where(jnp.arange(SPANS) == chosen, SPAN, lengths).astype(jnp.int32)


def strengthened(entries, stream_key, source, target, parts, factor):
    owner, partner = [(jnp.arange(entries.shape[axis_at]) // (entries.shape[axis_at] // parts)).reshape([-1 if axis == axis_at else 1 for axis in range(entries.ndim)]) for axis_at in (source, target)]
    chosen = jax.random.permutation(stream_key, parts)[partner]
    strong = (owner == chosen) | (owner == (partner + parts // 2) % parts)
    return jnp.where(strong, factor * entries, entries)


def levels(stream_key, shape, pieces, smallest, high):
    loudness = 1.0
    for axis_at, blocks in pieces:
        steps = jax.random.uniform(jax.random.fold_in(jax.random.fold_in(stream_key, 6), axis_at), (blocks,), jnp.float32, smallest / len(pieces), high / len(pieces))
        loudness = loudness * jnp.repeat(jnp.exp(steps), shape[axis_at] // blocks).reshape((-1,) + (1,) * (len(shape) - 1 - axis_at))
    return loudness


def gaussian(rng, shape, deviation, most, pieces=(), dtype=jnp.bfloat16):
    entries = deviation * jax.random.normal(rng, shape, jnp.float32)
    if pieces:
        entries = entries * levels(rng, shape, pieces, -0.22, 0.18)
    return jnp.clip(entries, -most, most).astype(dtype)


def heavy_noise(own_key, extent, spread, most, pieces, heavy, kind=jnp.bfloat16):
    values = spread * jax.random.normal(own_key, extent, jnp.float32)
    if pieces:
        values = values * levels(own_key, extent, pieces, -0.22, 0.18)
    return jnp.clip(strengthened(values, jax.random.fold_in(own_key, 3), *heavy), -most, most).astype(kind)


def setup_inputs(seed: int = 0) -> dict:
    streams_of = jax.random.split(jax.random.key(seed), 20)
    hidden_in = gaussian(streams_of[0], (TOKENS, D), 1.0, 6.0, ((0, 32),))
    cotangent = heavy_noise(streams_of[1], (TOKENS, D), 1.0, 6.0, ((0, 32),), (0, 1, 32, 2.75))
    span_lengths = draw_span_lengths(jax.random.fold_in(streams_of[19], 71), 0)
    partner_span = jax.vmap(lambda own: jax.random.permutation(own, SPANS_DEV))(jax.random.split(streams_of[3], N_DOC)).reshape((N_DOC, SPANS_DEV)).astype(jnp.int32)
    query_weight = gaussian(streams_of[4], (D, D), D ** -0.5, 0.21875, ((0, 32),))
    query_bias = gaussian(streams_of[5], (D,), 0.5, 3.0, ((0, 32),))
    key_weight = gaussian(streams_of[6], (D, D), D ** -0.5, 0.21875, ((0, 32),))
    value_weight = gaussian(streams_of[7], (D, D), D ** -0.5, 0.21875, ((0, 32),))
    value_bias = gaussian(streams_of[8], (D,), 0.5, 3.0, ((0, 32),))
    output_weight = gaussian(streams_of[9], (D, D), (D // 8) ** -0.5, 0.625, ((0, 32),))
    output_bias = gaussian(streams_of[10], (D,), 0.5, 3.0, ((0, 32),))
    first_gain = jnp.clip(1.0 + 0.1 * jax.random.normal(streams_of[11], (D,), jnp.float32), 0.5, 1.5).astype(jnp.bfloat16)
    first_shift = gaussian(streams_of[12], (D,), 0.3, 2.0, ((0, 32),))
    inner_weight = gaussian(streams_of[13], (D, FF), D ** -0.5, 0.21875, ((0, 32),))
    inner_bias = gaussian(streams_of[14], (FF,), 0.5, 3.0, ((0, 32),))
    outer_weight = gaussian(streams_of[15], (FF, D), FF ** -0.5, 0.109375, ((0, 32),))
    outer_bias = gaussian(streams_of[16], (D,), 0.5, 3.0, ((0, 32),))
    second_gain = jnp.clip(1.0 + 0.1 * jax.random.normal(streams_of[17], (D,), jnp.float32), 0.5, 1.5).astype(jnp.bfloat16)
    second_shift = gaussian(streams_of[18], (D,), 0.5, 3.0, ((0, 32),))
    return {"hidden_in": hidden_in, "cotangent": cotangent, "span_lengths": span_lengths, "partner_span": partner_span, "query_weight": query_weight, "query_bias": query_bias, "key_weight": key_weight, "value_weight": value_weight, "value_bias": value_bias, "output_weight": output_weight, "output_bias": output_bias, "first_gain": first_gain, "first_shift": first_shift, "inner_weight": inner_weight, "inner_bias": inner_bias, "outer_weight": outer_weight, "outer_bias": outer_bias, "second_gain": second_gain, "second_shift": second_shift}


@jax.custom_vjp
def low(v):
    return lax.optimization_barrier(v.astype(jnp.bfloat16)).astype(jnp.float32)

@jax.custom_vjp
def low_back(v):
    return v

def low_keep(v):
    return (low(v), None)

def low_pass(kept, grad):
    return (grad,)

def back_keep(v):
    return (v, None)

def back_low(kept, grad):
    return (low(grad),)
low.defvjp(low_keep, low_pass)
low_back.defvjp(back_keep, back_low)
epsilon = 1e-06
masked_out = -1000000000.0
highest = lax.Precision.HIGHEST

def product(left, right):
    return jnp.dot(left, right, precision=highest)

def normalize(hidden, gain, shift):
    average = lax.optimization_barrier(jnp.mean(hidden, axis=-1, keepdims=True))
    centred = hidden - average
    factor = lax.rsqrt(lax.optimization_barrier(jnp.mean(centred * centred, axis=-1, keepdims=True)) + epsilon)
    return centred * factor * gain + shift

def encode_rows(row_block, live_keys, params):
    query_mat, query_add, key_mat, value_mat, value_add, output_mat, output_add, gain_one, shift_one, inner_mat, inner_add, outer_mat, outer_add, gain_two, shift_two = params
    row_count = row_block.shape[0]
    head_count = D // HEAD_DIM
    length = SPAN * SPANS_ROW
    tokens = row_block.reshape(row_count * length, D)
    queries = low(low_back(product(tokens, query_mat) + query_add))
    key_rows = low(low_back(product(tokens, key_mat)))
    value_rows = low(low_back(product(tokens, value_mat) + value_add))
    shaped = (row_count, length, head_count, HEAD_DIM)
    scores = jnp.einsum('rqhd,rkhd->rhqk', queries.reshape(shaped), key_rows.reshape(shaped), precision=highest)
    scores = low_back(scores * HEAD_DIM ** (-0.5))
    segment = jnp.arange(length) // SPAN
    allowed = (segment[:, None] == segment[None, :])[None, None] & live_keys[:, None, None, :]
    scores = jnp.where(allowed, scores, masked_out)
    highest_score = lax.optimization_barrier(jnp.max(scores, axis=-1, keepdims=True))
    exponent = jnp.exp(scores - highest_score)
    attention = exponent / lax.optimization_barrier(jnp.sum(exponent, axis=-1, keepdims=True))
    context = jnp.einsum('rhqk,rkhd->rqhd', low(attention), value_rows.reshape(shaped), precision=highest)
    context = low(low_back(context.reshape(row_count * length, D)))
    residual = tokens + low_back(product(context, output_mat)) + output_add
    first_out = normalize(residual, gain_one, shift_one)
    preact = low_back(product(low(first_out), inner_mat)) + inner_add
    active = low(jax.nn.gelu(preact, approximate=False))
    second = first_out + low_back(product(active, outer_mat)) + outer_add
    return normalize(second, gain_two, shift_two).reshape(row_count, length, D)

def contrast(own_rows, other_rows, target):
    logits = jnp.einsum('nsd,ntd->nst', own_rows, other_rows, precision=highest) / math.sqrt(D)
    highest_logit = lax.optimization_barrier(jnp.max(logits, axis=-1, keepdims=True))
    logsum = highest_logit[..., 0] + jnp.log(lax.optimization_barrier(jnp.sum(jnp.exp(logits - highest_logit), axis=-1)))
    return logsum - lax.optimization_barrier(jnp.sum(target * logits, axis=-1))

def reference(hidden_in, cotangent, span_lengths, partner_span, query_weight, query_bias, key_weight, value_weight, value_bias, output_weight, output_bias, first_gain, first_shift, inner_weight, inner_bias, outer_weight, outer_bias, second_gain, second_shift):
    params = tuple((weight.astype(jnp.float32) for weight in (query_weight, query_bias, key_weight, value_weight, value_bias, output_weight, output_bias, first_gain, first_shift, inner_weight, inner_bias, outer_weight, outer_bias, second_gain, second_shift)))
    length = SPAN * SPANS_ROW
    total_rows = hidden_in.shape[0] // length
    group_rows = math.gcd(total_rows, max(1, 4096 // length))
    live_keys = jnp.arange(SPAN)[None, None, :] < span_lengths.reshape(total_rows, SPANS_ROW, 1)
    live_keys = live_keys.reshape(total_rows // group_rows, group_rows, length)
    blocks = hidden_in.astype(jnp.float32).reshape(total_rows // group_rows, group_rows, length, D)
    matches = (partner_span[:, :, None] == jnp.arange(SPANS_DEV)[None, None, :]).astype(jnp.float32)
    encode_block = jax.checkpoint(encode_rows)

    def whole(inputs, weights):

        def encode_one(element):
            return encode_block(element[0], element[1], weights)
        encoded = lax.map(encode_one, (inputs, live_keys)).reshape(-1, D)
        cls_rows = low(encoded.reshape(-1, SPANS_ROW, SPAN, D)[:, :, 0, :]).reshape(-1, 2, SPANS_DEV, D)
        loss_first = contrast(cls_rows[:, 0], low_back(cls_rows[:, 1]), matches)
        loss_second = contrast(cls_rows[:, 1], low_back(cls_rows[:, 0]), jnp.swapaxes(matches, 1, 2))
        return (encoded, jnp.stack([loss_first, loss_second], axis=1).reshape(-1))
    (encoded, span_loss), pullback = jax.vjp(whole, blocks, params)
    cotangents = (cotangent.astype(jnp.float32), jnp.full(span_loss.shape, math.sqrt(D), jnp.float32))
    input_part, weight_parts = pullback(cotangents)
    return (encoded.astype(jnp.bfloat16), input_part.reshape(-1, D).astype(jnp.bfloat16), span_loss, weight_parts[0], weight_parts[1], weight_parts[2], weight_parts[3], weight_parts[4], weight_parts[5], weight_parts[6], weight_parts[7], weight_parts[8], weight_parts[9], weight_parts[10], weight_parts[11], weight_parts[12], weight_parts[13], weight_parts[14])
```

```python
from functools import partial
import math

import jax
import jax.numpy as jnp
from jax import lax
from jax.sharding import PartitionSpec as P

D = 768
HEAD_DIM = 64
SPAN = 128
SPANS_ROW = 4


epsilon = 1e-06
masked_out = -1000000000.0
highest = lax.Precision.HIGHEST


def across(block, mask):
    count = lax.axis_size("doc")
    return lax.ppermute(block, "doc", [(at, at ^ mask) for at in range(count)])


def mate(block):
    return lax.ppermute(block, "pair", [(0, 1), (1, 0)])


def far_groups():
    bits = lax.axis_size("doc").bit_length() - 1
    far = [1 << at for at in range(2, bits)]
    return [far[at : at + 2] for at in range(0, len(far), 2)]


def is_upper(mask):
    return (lax.axis_index("doc") & mask) != 0


def joined(own, other, upper):
    return jnp.where(upper, jnp.stack([other, own]), jnp.stack([own, other]))


def gather_rows(block):
    rows, columns = block.shape
    total = block[None]
    for masks in far_groups():
        low = masks[0]
        near = joined(total, across(total, low), is_upper(low))
        if len(masks) == 2:
            high = masks[1]
            straight, crossed = across(total, high), across(total, high | low)
            far = joined(straight, crossed, is_upper(low))
            near = joined(near, far, is_upper(high)).reshape((4,) + total.shape)
        total = near.reshape((-1, rows, columns))
    half = columns // 2
    left, right = total[..., :half], total[..., half:]
    on_pair = lax.axis_index("pair") == 1
    left_x, right_y = across(left, 2), mate(right)
    left, right = joined(left, left_x, is_upper(2)), joined(right, right_y, on_pair)
    left_y, right_x = mate(left), across(right, 2)
    left, right = joined(left, left_y, on_pair), joined(right, right_x, is_upper(2))
    left = joined(left, across(left, 1), is_upper(1))
    right = joined(right, across(right, 1), is_upper(1))
    left = jnp.transpose(left, (3, 2, 0, 1, 4, 5))
    right = jnp.transpose(right, (3, 1, 0, 2, 4, 5))
    return jnp.concatenate([left, right], axis=-1).reshape(-1, rows, columns)


def halves(blocks, axis, upper):
    lower = lax.index_in_dim(blocks, 0, axis, keepdims=False)
    higher = lax.index_in_dim(blocks, 1, axis, keepdims=False)
    return (jnp.where(upper, higher, lower), jnp.where(upper, lower, higher))


def plus(kept, received):
    return kept.astype(jnp.float32) + received.astype(jnp.float32)


def scatter_rows(blocks):
    rows, columns = blocks.shape[1:]
    on_pair = lax.axis_index("pair") == 1
    blocks = blocks.astype(jnp.bfloat16).reshape(-1, 2, 2, 2, rows, columns)
    kept, sent = halves(blocks, 2, is_upper(1))
    total = plus(kept, across(sent, 1)).astype(jnp.bfloat16)
    half = columns // 2
    left, right = total[..., :half], total[..., half:]
    left_kept, left_sent = halves(left, 2, on_pair)
    right_kept, right_sent = halves(right, 1, is_upper(2))
    left = plus(left_kept, mate(left_sent)).astype(jnp.bfloat16)
    right = plus(right_kept, across(right_sent, 2)).astype(jnp.bfloat16)
    left_kept, left_sent = halves(left, 1, is_upper(2))
    right_kept, right_sent = halves(right, 1, on_pair)
    left = plus(left_kept, across(left_sent, 2))
    right = plus(right_kept, mate(right_sent))
    total = jnp.concatenate([left, right], axis=-1)
    for masks in far_groups()[::-1]:
        total = total.astype(jnp.bfloat16).reshape(2 ** len(masks), -1, rows, columns)
        place = (lax.axis_index("doc") // masks[0]) % 2 ** len(masks)
        summed = lax.dynamic_index_in_dim(total, place, 0, keepdims=False).astype(jnp.float32)
        for step in range(1, 2 ** len(masks)):
            sent = lax.dynamic_index_in_dim(total, place ^ step, 0, keepdims=False)
            summed = plus(summed, across(sent, masks[0] * step))
        total = summed
    return total.reshape(rows, columns)


VECTORS = (1, 4, 6, 7, 8, 10, 12, 13, 14)


def pack_vectors(pieces):
    flat = jnp.concatenate(pieces, axis=-1)
    width = -(-flat.shape[-1] // D) * D
    flat = jnp.pad(flat, [(0, 0)] * (flat.ndim - 1) + [(0, width - flat.shape[-1])])
    return flat.reshape(flat.shape[:-1] + (-1, D))


def fold(matrix):
    return jnp.concatenate([matrix[:, at : at + D] for at in range(0, matrix.shape[1], D)])


def collect(shards):
    rows = shards[0].shape[0]
    devices = lax.axis_size("doc") * lax.axis_size("pair")
    small = pack_vectors([shards[at] for at in VECTORS])
    first = gather_rows(jnp.concatenate([shards[0], shards[2], shards[3], small]))
    second = gather_rows(jnp.concatenate([shards[5], fold(shards[9])]))
    outer = lax.all_gather(shards[11], ("doc", "pair"), axis=0, tiled=True)
    whole = {
        0: first[:, :rows].reshape(-1, D),
        2: first[:, rows : 2 * rows].reshape(-1, D),
        3: first[:, 2 * rows : 3 * rows].reshape(-1, D),
        5: second[:, :rows].reshape(-1, D),
        9: jnp.concatenate(
            [
                second[:, at : at + rows].reshape(-1, D)
                for at in range(rows, second.shape[1], rows)
            ],
            axis=1,
        ),
        11: outer,
    }
    vectors, start = first[:, 3 * rows :].reshape(devices, -1), 0
    for at in VECTORS:
        size = shards[at].shape[0]
        whole[at] = vectors[:, start : start + size].reshape(-1).astype(jnp.float32)
        start += size
    return tuple(whole[at] for at in range(15))


def spread(gradients):
    devices = lax.axis_size("doc") * lax.axis_size("pair")
    by_device = [
        piece.reshape((devices, -1) + piece.shape[1:]) for piece in gradients
    ]
    rows = by_device[0].shape[1]
    outer = scatter_rows(by_device[11])
    inner = by_device[9]
    parts = [inner[..., at : at + D] for at in range(0, inner.shape[-1], D)]
    second = scatter_rows(jnp.concatenate([by_device[5]] + parts, axis=1))
    small = pack_vectors([by_device[at] for at in VECTORS])
    first = scatter_rows(
        jnp.concatenate([by_device[0], by_device[2], by_device[3], small], axis=1)
    )
    own = {
        0: first[:rows],
        2: first[rows : 2 * rows],
        3: first[2 * rows : 3 * rows],
        5: second[:rows],
        9: jnp.concatenate(
            [second[at : at + rows] for at in range(rows, second.shape[0], rows)], axis=1
        ),
        11: outer,
    }
    vectors, start = first[3 * rows :].reshape(-1), 0
    for at in VECTORS:
        size = by_device[at].shape[1]
        own[at] = vectors[start : start + size]
        start += size
    return tuple(own[at] for at in range(15))


def normalize(hidden, gain, shift):
    average = jnp.mean(hidden, axis=-1, keepdims=True)
    centred = hidden - average
    factor = lax.rsqrt(jnp.mean(centred * centred, axis=-1, keepdims=True) + epsilon)
    normed = centred * factor
    return (normed * gain + shift, normed, factor)


def normalize_back(upstream, normed, factor, gain):
    scaled = upstream * gain
    hidden_grad = factor * (
        scaled
        - jnp.mean(scaled, axis=-1, keepdims=True)
        - normed * jnp.mean(scaled * normed, axis=-1, keepdims=True)
    )
    return (hidden_grad, jnp.sum(upstream * normed, axis=0), jnp.sum(upstream, axis=0))


def head_scores(query_row, key_row, live_row):
    product = jnp.einsum("sqhd,skhd->shqk", query_row, key_row, preferred_element_type=jnp.float32)
    return jnp.where(live_row[:, None, None, :], product * HEAD_DIM ** (-0.5), masked_out)


def encode(hidden_in, allowed, gathered):
    (
        query_mat,
        query_add,
        key_mat,
        value_mat,
        value_add,
        output_mat,
        output_add,
        gain_one,
        shift_one,
        inner_mat,
        inner_add,
        outer_mat,
        outer_add,
        gain_two,
        shift_two,
    ) = gathered
    row_count = allowed.shape[0]
    shaped = (row_count, SPANS_ROW, SPAN, D // HEAD_DIM, HEAD_DIM)
    queries = (
        jnp.dot(hidden_in, query_mat, preferred_element_type=jnp.float32) + query_add
    ).astype(jnp.bfloat16)
    key_rows = jnp.dot(hidden_in, key_mat, preferred_element_type=jnp.float32).astype(jnp.bfloat16)
    value_rows = (
        jnp.dot(hidden_in, value_mat, preferred_element_type=jnp.float32) + value_add
    ).astype(jnp.bfloat16)

    def attend(element):
        query_row, key_row, value_row, live_row = element
        scores = head_scores(query_row, key_row, live_row)
        highest_score = jnp.max(scores, axis=-1, keepdims=True)
        exponent = jnp.exp(scores - highest_score)
        totals = jnp.sum(exponent, axis=-1, keepdims=True)
        attention = (exponent / totals).astype(jnp.bfloat16)
        context_row = jnp.einsum(
            "shqk,skhd->sqhd", attention, value_row, preferred_element_type=jnp.float32
        )
        return (context_row.astype(jnp.bfloat16), (highest_score + jnp.log(totals))[..., 0])

    context, logsum = lax.map(
        attend,
        (queries.reshape(shaped), key_rows.reshape(shaped), value_rows.reshape(shaped), allowed),
    )
    context = context.reshape(-1, D)
    residual = (
        hidden_in.astype(jnp.float32)
        + jnp.dot(context, output_mat, preferred_element_type=jnp.float32)
        + output_add
    )
    first_out, first_normed, first_factor = normalize(residual, gain_one, shift_one)
    first16 = first_out.astype(jnp.bfloat16)
    preact = jnp.dot(first16, inner_mat, preferred_element_type=jnp.float32) + inner_add
    active = jax.nn.gelu(preact, approximate=False).astype(jnp.bfloat16)
    second = first_out + jnp.dot(active, outer_mat, preferred_element_type=jnp.float32) + outer_add
    encoded, second_normed, second_factor = normalize(second, gain_two, shift_two)
    stored = (
        queries,
        key_rows,
        value_rows,
        logsum,
        context,
        first_normed,
        first_factor,
        first16,
        preact,
        active,
        second_normed,
        second_factor,
    )
    return (encoded, stored)


def backward(hidden_in, allowed, gathered, stored, out_gradient):
    (
        query_mat,
        query_add,
        key_mat,
        value_mat,
        value_add,
        output_mat,
        output_add,
        gain_one,
        shift_one,
        inner_mat,
        inner_add,
        outer_mat,
        outer_add,
        gain_two,
        shift_two,
    ) = gathered
    (
        queries,
        key_rows,
        value_rows,
        logsum,
        context,
        first_normed,
        first_factor,
        first16,
        preact,
        active,
        second_normed,
        second_factor,
    ) = stored
    row_count = allowed.shape[0]
    shaped = (row_count, SPANS_ROW, SPAN, D // HEAD_DIM, HEAD_DIM)
    second_grad, gain_two_grad, shift_two_grad = normalize_back(
        out_gradient, second_normed, second_factor, gain_two
    )
    outer_add_grad = jnp.sum(second_grad, axis=0)
    second16 = second_grad.astype(jnp.bfloat16)
    outer_mat_grad = jnp.dot(active.T, second16, preferred_element_type=jnp.float32)
    active_grad = jnp.dot(second16, outer_mat.T, preferred_element_type=jnp.float32)
    unused, gelu_back = jax.vjp(partial(jax.nn.gelu, approximate=False), preact)
    preact_grad = gelu_back(active_grad)[0]
    inner_add_grad = jnp.sum(preact_grad, axis=0)
    preact16 = preact_grad.astype(jnp.bfloat16)
    inner_mat_grad = jnp.dot(first16.T, preact16, preferred_element_type=jnp.float32)
    first_grad = second_grad + jnp.dot(preact16, inner_mat.T, preferred_element_type=jnp.float32)
    residual_grad, gain_one_grad, shift_one_grad = normalize_back(
        first_grad, first_normed, first_factor, gain_one
    )
    output_add_grad = jnp.sum(residual_grad, axis=0)
    residual16 = residual_grad.astype(jnp.bfloat16)
    output_mat_grad = jnp.dot(context.T, residual16, preferred_element_type=jnp.float32)
    context_grad = jnp.dot(residual16, output_mat.T, preferred_element_type=jnp.float32).astype(
        jnp.bfloat16
    )

    def attend_back(element):
        query_row, key_row, value_row, live_row, logsum_row, context_row = element
        scores = head_scores(query_row, key_row, live_row)
        attention = jnp.exp(scores - logsum_row[..., None])
        attention16 = attention.astype(jnp.bfloat16)
        value_grad = jnp.einsum(
            "shqk,sqhd->skhd", attention16, context_row, preferred_element_type=jnp.float32
        )
        attention_grad = jnp.einsum(
            "sqhd,skhd->shqk", context_row, value_row, preferred_element_type=jnp.float32
        )
        weighted = jnp.sum(attention * attention_grad, axis=-1, keepdims=True)
        scores_grad = (attention * (attention_grad - weighted)).astype(jnp.bfloat16)
        query_grad = jnp.einsum(
            "shqk,skhd->sqhd", scores_grad, key_row, preferred_element_type=jnp.float32
        ) * HEAD_DIM ** (-0.5)
        key_grad = jnp.einsum(
            "shqk,sqhd->skhd", scores_grad, query_row, preferred_element_type=jnp.float32
        ) * HEAD_DIM ** (-0.5)
        return (
            query_grad.astype(jnp.bfloat16),
            key_grad.astype(jnp.bfloat16),
            value_grad.astype(jnp.bfloat16),
        )

    query_grad, key_grad, value_grad = lax.map(
        attend_back,
        (
            queries.reshape(shaped),
            key_rows.reshape(shaped),
            value_rows.reshape(shaped),
            allowed,
            logsum,
            context_grad.reshape(shaped),
        ),
    )
    query_grad = query_grad.reshape(-1, D)
    key_grad = key_grad.reshape(-1, D)
    value_grad = value_grad.reshape(-1, D)
    query_add_grad = jnp.sum(query_grad.astype(jnp.float32), axis=0)
    value_add_grad = jnp.sum(value_grad.astype(jnp.float32), axis=0)
    query_mat_grad = jnp.dot(hidden_in.T, query_grad, preferred_element_type=jnp.float32)
    key_mat_grad = jnp.dot(hidden_in.T, key_grad, preferred_element_type=jnp.float32)
    value_mat_grad = jnp.dot(hidden_in.T, value_grad, preferred_element_type=jnp.float32)
    input_grad = (
        residual_grad
        + jnp.dot(query_grad, query_mat.T, preferred_element_type=jnp.float32)
        + jnp.dot(key_grad, key_mat.T, preferred_element_type=jnp.float32)
        + jnp.dot(value_grad, value_mat.T, preferred_element_type=jnp.float32)
    )
    gradients = (
        query_mat_grad,
        query_add_grad,
        key_mat_grad,
        value_mat_grad,
        value_add_grad,
        output_mat_grad,
        output_add_grad,
        gain_one_grad,
        shift_one_grad,
        inner_mat_grad,
        inner_add_grad,
        outer_mat_grad,
        outer_add_grad,
        gain_two_grad,
        shift_two_grad,
    )
    return (input_grad, gradients)


def per_device(
    hidden_in,
    cotangent,
    span_lengths,
    partner_span,
    query_weight,
    query_bias,
    key_weight,
    value_weight,
    value_bias,
    output_weight,
    output_bias,
    first_gain,
    first_shift,
    inner_weight,
    inner_bias,
    outer_weight,
    outer_bias,
    second_gain,
    second_shift,
):
    shards = (
        query_weight,
        query_bias,
        key_weight,
        value_weight,
        value_bias,
        output_weight,
        output_bias,
        first_gain,
        first_shift,
        inner_weight,
        inner_bias,
        outer_weight,
        outer_bias,
        second_gain,
        second_shift,
    )
    length = SPAN * SPANS_ROW
    row_count = hidden_in.shape[0] // length
    allowed = jnp.arange(SPAN)[None, None, :] < span_lengths.reshape(row_count, SPANS_ROW, 1)
    gathered = collect(shards)
    encoded, stored = encode(hidden_in, allowed, gathered)
    cls_rows = (
        encoded.reshape(row_count, SPANS_ROW, SPAN, D)[:, :, 0, :]
        .reshape(-1, D)
        .astype(jnp.bfloat16)
    )
    other_rows = mate(cls_rows)
    logits = jnp.dot(cls_rows, other_rows.T, preferred_element_type=jnp.float32) / math.sqrt(D)
    span_count = cls_rows.shape[0]
    matches = (partner_span.reshape(span_count, 1) == jnp.arange(span_count)[None, :]).astype(
        jnp.float32
    )
    target = jnp.where(lax.axis_index("pair") == 0, matches, matches.T)
    highest_logit = jnp.max(logits, axis=-1, keepdims=True)
    exponent = jnp.exp(logits - highest_logit)
    totals = jnp.sum(exponent, axis=-1, keepdims=True)
    span_loss = highest_logit[:, 0] + jnp.log(totals[:, 0]) - jnp.sum(target * logits, axis=-1)
    softened = exponent / totals - target
    own_grad = jnp.dot(softened, other_rows.astype(jnp.float32), precision=highest)
    other_logits = logits.T
    other_highest = jnp.max(other_logits, axis=-1, keepdims=True)
    other_exponent = jnp.exp(other_logits - other_highest)
    other_softened = (
        other_exponent / jnp.sum(other_exponent, axis=-1, keepdims=True) - target.T
    )
    back_grad = jnp.dot(
        other_softened.T, other_rows.astype(jnp.float32), precision=highest
    ).astype(jnp.bfloat16)
    cls_gradient = (own_grad + back_grad.astype(jnp.float32)).reshape(row_count, SPANS_ROW, 1, D)
    placed = jnp.concatenate(
        [cls_gradient, jnp.zeros((row_count, SPANS_ROW, SPAN - 1, D), jnp.float32)], axis=2
    )
    out_gradient = cotangent.astype(jnp.float32) + placed.reshape(-1, D)
    input_grad, gradients = backward(hidden_in, allowed, gathered, stored, out_gradient)
    reduced = spread(gradients)
    return (encoded.astype(jnp.bfloat16), input_grad.astype(jnp.bfloat16), span_loss) + tuple(
        reduced
    )


def solution(mesh):
    return jax.shard_map(
        per_device,
        mesh=mesh,
        in_specs=(
            P(("doc", "pair"), None),
            P(("doc", "pair"), None),
            P(("doc", "pair")),
            P("doc", None),
            P(("doc", "pair"), None),
            P(("doc", "pair")),
            P(("doc", "pair"), None),
            P(("doc", "pair"), None),
            P(("doc", "pair")),
            P(("doc", "pair"), None),
            P(("doc", "pair")),
            P(("doc", "pair")),
            P(("doc", "pair")),
            P(("doc", "pair"), None),
            P(("doc", "pair")),
            P(("doc", "pair"), None),
            P(("doc", "pair")),
            P(("doc", "pair")),
            P(("doc", "pair")),
        ),
        out_specs=(
            P(("doc", "pair"), None),
            P(("doc", "pair"), None),
            P(("doc", "pair")),
            P(("doc", "pair"), None),
            P(("doc", "pair")),
            P(("doc", "pair"), None),
            P(("doc", "pair"), None),
            P(("doc", "pair")),
            P(("doc", "pair"), None),
            P(("doc", "pair")),
            P(("doc", "pair")),
            P(("doc", "pair")),
            P(("doc", "pair"), None),
            P(("doc", "pair")),
            P(("doc", "pair"), None),
            P(("doc", "pair")),
            P(("doc", "pair")),
            P(("doc", "pair")),
        ),
        check_vma=False,
    )
```

```python
from functools import partial
import math

import jax
import jax.numpy as jnp
from jax import lax
from jax.experimental import pallas as pl
from jax.experimental.pallas import tpu as pltpu
from jax.sharding import PartitionSpec as P

D = 768
HEAD_DIM = 64
SPAN = 128
SPANS_ROW = 4


epsilon = 1e-06
masked_out = -1000000000.0
highest = lax.Precision.HIGHEST


def across(block, mask):
    count = lax.axis_size("doc")
    return lax.ppermute(block, "doc", [(at, at ^ mask) for at in range(count)])


def mate(block):
    return lax.ppermute(block, "pair", [(0, 1), (1, 0)])


def far_groups():
    bits = lax.axis_size("doc").bit_length() - 1
    far = [1 << at for at in range(2, bits)]
    return [far[at : at + 2] for at in range(0, len(far), 2)]


def is_upper(mask):
    return (lax.axis_index("doc") & mask) != 0


def joined(own, other, upper):
    return jnp.where(upper, jnp.stack([other, own]), jnp.stack([own, other]))


def gather_rows(block):
    rows, columns = block.shape
    total = block[None]
    for masks in far_groups():
        low = masks[0]
        near = joined(total, across(total, low), is_upper(low))
        if len(masks) == 2:
            high = masks[1]
            straight, crossed = across(total, high), across(total, high | low)
            far = joined(straight, crossed, is_upper(low))
            near = joined(near, far, is_upper(high)).reshape((4,) + total.shape)
        total = near.reshape((-1, rows, columns))
    half = columns // 2
    left, right = total[..., :half], total[..., half:]
    on_pair = lax.axis_index("pair") == 1
    left_x, right_y = across(left, 2), mate(right)
    left, right = joined(left, left_x, is_upper(2)), joined(right, right_y, on_pair)
    left_y, right_x = mate(left), across(right, 2)
    left, right = joined(left, left_y, on_pair), joined(right, right_x, is_upper(2))
    left = joined(left, across(left, 1), is_upper(1))
    right = joined(right, across(right, 1), is_upper(1))
    left = jnp.transpose(left, (3, 2, 0, 1, 4, 5))
    right = jnp.transpose(right, (3, 1, 0, 2, 4, 5))
    return jnp.concatenate([left, right], axis=-1).reshape(-1, rows, columns)


def halves(blocks, axis, upper):
    lower = lax.index_in_dim(blocks, 0, axis, keepdims=False)
    higher = lax.index_in_dim(blocks, 1, axis, keepdims=False)
    return (jnp.where(upper, higher, lower), jnp.where(upper, lower, higher))


def plus(kept, received):
    return kept.astype(jnp.float32) + received.astype(jnp.float32)


def scatter_rows(blocks):
    rows, columns = blocks.shape[1:]
    on_pair = lax.axis_index("pair") == 1
    blocks = blocks.astype(jnp.bfloat16).reshape(-1, 2, 2, 2, rows, columns)
    kept, sent = halves(blocks, 2, is_upper(1))
    total = plus(kept, across(sent, 1)).astype(jnp.bfloat16)
    half = columns // 2
    left, right = total[..., :half], total[..., half:]
    left_kept, left_sent = halves(left, 2, on_pair)
    right_kept, right_sent = halves(right, 1, is_upper(2))
    left = plus(left_kept, mate(left_sent)).astype(jnp.bfloat16)
    right = plus(right_kept, across(right_sent, 2)).astype(jnp.bfloat16)
    left_kept, left_sent = halves(left, 1, is_upper(2))
    right_kept, right_sent = halves(right, 1, on_pair)
    left = plus(left_kept, across(left_sent, 2))
    right = plus(right_kept, mate(right_sent))
    total = jnp.concatenate([left, right], axis=-1)
    for masks in far_groups()[::-1]:
        total = total.astype(jnp.bfloat16).reshape(2 ** len(masks), -1, rows, columns)
        place = (lax.axis_index("doc") // masks[0]) % 2 ** len(masks)
        summed = lax.dynamic_index_in_dim(total, place, 0, keepdims=False).astype(jnp.float32)
        for step in range(1, 2 ** len(masks)):
            sent = lax.dynamic_index_in_dim(total, place ^ step, 0, keepdims=False)
            summed = plus(summed, across(sent, masks[0] * step))
        total = summed
    return total.reshape(rows, columns)


VECTORS = (1, 4, 6, 7, 8, 10, 12, 13, 14)


def pack_vectors(pieces):
    flat = jnp.concatenate(pieces, axis=-1)
    width = -(-flat.shape[-1] // D) * D
    flat = jnp.pad(flat, [(0, 0)] * (flat.ndim - 1) + [(0, width - flat.shape[-1])])
    return flat.reshape(flat.shape[:-1] + (-1, D))


def fold(matrix):
    return jnp.concatenate([matrix[:, at : at + D] for at in range(0, matrix.shape[1], D)])


def collect(shards):
    rows = shards[0].shape[0]
    devices = lax.axis_size("doc") * lax.axis_size("pair")
    small = pack_vectors([shards[at] for at in VECTORS])
    first = gather_rows(jnp.concatenate([shards[0], shards[2], shards[3], small]))
    second = gather_rows(jnp.concatenate([shards[5], fold(shards[9])]))
    outer = lax.all_gather(shards[11], ("doc", "pair"), axis=0, tiled=True)
    whole = {
        0: first[:, :rows].reshape(-1, D),
        2: first[:, rows : 2 * rows].reshape(-1, D),
        3: first[:, 2 * rows : 3 * rows].reshape(-1, D),
        5: second[:, :rows].reshape(-1, D),
        9: jnp.concatenate(
            [
                second[:, at : at + rows].reshape(-1, D)
                for at in range(rows, second.shape[1], rows)
            ],
            axis=1,
        ),
        11: outer,
    }
    vectors, start = first[:, 3 * rows :].reshape(devices, -1), 0
    for at in VECTORS:
        size = shards[at].shape[0]
        whole[at] = vectors[:, start : start + size].reshape(-1).astype(jnp.float32)
        start += size
    return tuple(whole[at] for at in range(15))


def spread(gradients):
    devices = lax.axis_size("doc") * lax.axis_size("pair")
    by_device = [
        piece.reshape((devices, -1) + piece.shape[1:]) for piece in gradients
    ]
    rows = by_device[0].shape[1]
    outer = scatter_rows(by_device[11])
    inner = by_device[9]
    parts = [inner[..., at : at + D] for at in range(0, inner.shape[-1], D)]
    second = scatter_rows(jnp.concatenate([by_device[5]] + parts, axis=1))
    small = pack_vectors([by_device[at] for at in VECTORS])
    first = scatter_rows(
        jnp.concatenate([by_device[0], by_device[2], by_device[3], small], axis=1)
    )
    own = {
        0: first[:rows],
        2: first[rows : 2 * rows],
        3: first[2 * rows : 3 * rows],
        5: second[:rows],
        9: jnp.concatenate(
            [second[at : at + rows] for at in range(rows, second.shape[0], rows)], axis=1
        ),
        11: outer,
    }
    vectors, start = first[3 * rows :].reshape(-1), 0
    for at in VECTORS:
        size = by_device[at].shape[1]
        own[at] = vectors[start : start + size]
        start += size
    return tuple(own[at] for at in range(15))


def normalize(hidden, gain, shift):
    average = jnp.mean(hidden, axis=-1, keepdims=True)
    centred = hidden - average
    factor = lax.rsqrt(jnp.mean(centred * centred, axis=-1, keepdims=True) + epsilon)
    normed = centred * factor
    return (normed * gain + shift, normed, factor)


def normalize_back(upstream, normed, factor, gain):
    scaled = upstream * gain
    hidden_grad = factor * (
        scaled
        - jnp.mean(scaled, axis=-1, keepdims=True)
        - normed * jnp.mean(scaled * normed, axis=-1, keepdims=True)
    )
    return (hidden_grad, jnp.sum(upstream * normed, axis=0), jnp.sum(upstream, axis=0))


def head_scores(query_row, key_row, live_row):
    product = jnp.einsum("sqhd,skhd->shqk", query_row, key_row, preferred_element_type=jnp.float32)
    return jnp.where(live_row[:, None, None, :], product * HEAD_DIM ** (-0.5), masked_out)


def encode(hidden_in, allowed, gathered):
    (
        query_mat,
        query_add,
        key_mat,
        value_mat,
        value_add,
        output_mat,
        output_add,
        gain_one,
        shift_one,
        inner_mat,
        inner_add,
        outer_mat,
        outer_add,
        gain_two,
        shift_two,
    ) = gathered
    row_count = allowed.shape[0]
    shaped = (row_count, SPANS_ROW, SPAN, D // HEAD_DIM, HEAD_DIM)
    queries = (
        jnp.dot(hidden_in, query_mat, preferred_element_type=jnp.float32) + query_add
    ).astype(jnp.bfloat16)
    key_rows = jnp.dot(hidden_in, key_mat, preferred_element_type=jnp.float32).astype(jnp.bfloat16)
    value_rows = (
        jnp.dot(hidden_in, value_mat, preferred_element_type=jnp.float32) + value_add
    ).astype(jnp.bfloat16)

    def attend(element):
        query_row, key_row, value_row, live_row = element
        scores = head_scores(query_row, key_row, live_row)
        highest_score = jnp.max(scores, axis=-1, keepdims=True)
        exponent = jnp.exp(scores - highest_score)
        totals = jnp.sum(exponent, axis=-1, keepdims=True)
        attention = (exponent / totals).astype(jnp.bfloat16)
        context_row = jnp.einsum(
            "shqk,skhd->sqhd", attention, value_row, preferred_element_type=jnp.float32
        )
        return (context_row.astype(jnp.bfloat16), (highest_score + jnp.log(totals))[..., 0])

    context, logsum = lax.map(
        attend,
        (queries.reshape(shaped), key_rows.reshape(shaped), value_rows.reshape(shaped), allowed),
    )
    context = context.reshape(-1, D)
    residual = (
        hidden_in.astype(jnp.float32)
        + jnp.dot(context, output_mat, preferred_element_type=jnp.float32)
        + output_add
    )
    first_out, first_normed, first_factor = normalize(residual, gain_one, shift_one)
    first16 = first_out.astype(jnp.bfloat16)
    preact = jnp.dot(first16, inner_mat, preferred_element_type=jnp.float32) + inner_add
    active = jax.nn.gelu(preact, approximate=False).astype(jnp.bfloat16)
    second = first_out + jnp.dot(active, outer_mat, preferred_element_type=jnp.float32) + outer_add
    encoded, second_normed, second_factor = normalize(second, gain_two, shift_two)
    stored = (
        queries,
        key_rows,
        value_rows,
        logsum,
        context,
        first_normed,
        first_factor,
        first16,
        preact,
        active,
        second_normed,
        second_factor,
    )
    return (encoded, stored)


def backward(hidden_in, allowed, gathered, stored, out_gradient):
    (
        query_mat,
        query_add,
        key_mat,
        value_mat,
        value_add,
        output_mat,
        output_add,
        gain_one,
        shift_one,
        inner_mat,
        inner_add,
        outer_mat,
        outer_add,
        gain_two,
        shift_two,
    ) = gathered
    (
        queries,
        key_rows,
        value_rows,
        logsum,
        context,
        first_normed,
        first_factor,
        first16,
        preact,
        active,
        second_normed,
        second_factor,
    ) = stored
    row_count = allowed.shape[0]
    shaped = (row_count, SPANS_ROW, SPAN, D // HEAD_DIM, HEAD_DIM)
    second_grad, gain_two_grad, shift_two_grad = normalize_back(
        out_gradient, second_normed, second_factor, gain_two
    )
    outer_add_grad = jnp.sum(second_grad, axis=0)
    second16 = second_grad.astype(jnp.bfloat16)
    outer_mat_grad = jnp.dot(active.T, second16, preferred_element_type=jnp.float32)
    active_grad = jnp.dot(second16, outer_mat.T, preferred_element_type=jnp.float32)
    unused, gelu_back = jax.vjp(partial(jax.nn.gelu, approximate=False), preact)
    preact_grad = gelu_back(active_grad)[0]
    inner_add_grad = jnp.sum(preact_grad, axis=0)
    preact16 = preact_grad.astype(jnp.bfloat16)
    inner_mat_grad = jnp.dot(first16.T, preact16, preferred_element_type=jnp.float32)
    first_grad = second_grad + jnp.dot(preact16, inner_mat.T, preferred_element_type=jnp.float32)
    residual_grad, gain_one_grad, shift_one_grad = normalize_back(
        first_grad, first_normed, first_factor, gain_one
    )
    output_add_grad = jnp.sum(residual_grad, axis=0)
    residual16 = residual_grad.astype(jnp.bfloat16)
    output_mat_grad = jnp.dot(context.T, residual16, preferred_element_type=jnp.float32)
    context_grad = jnp.dot(residual16, output_mat.T, preferred_element_type=jnp.float32).astype(
        jnp.bfloat16
    )

    def attend_back(element):
        query_row, key_row, value_row, live_row, logsum_row, context_row = element
        scores = head_scores(query_row, key_row, live_row)
        attention = jnp.exp(scores - logsum_row[..., None])
        attention16 = attention.astype(jnp.bfloat16)
        value_grad = jnp.einsum(
            "shqk,sqhd->skhd", attention16, context_row, preferred_element_type=jnp.float32
        )
        attention_grad = jnp.einsum(
            "sqhd,skhd->shqk", context_row, value_row, preferred_element_type=jnp.float32
        )
        weighted = jnp.sum(attention * attention_grad, axis=-1, keepdims=True)
        scores_grad = (attention * (attention_grad - weighted)).astype(jnp.bfloat16)
        query_grad = jnp.einsum(
            "shqk,skhd->sqhd", scores_grad, key_row, preferred_element_type=jnp.float32
        ) * HEAD_DIM ** (-0.5)
        key_grad = jnp.einsum(
            "shqk,sqhd->skhd", scores_grad, query_row, preferred_element_type=jnp.float32
        ) * HEAD_DIM ** (-0.5)
        return (
            query_grad.astype(jnp.bfloat16),
            key_grad.astype(jnp.bfloat16),
            value_grad.astype(jnp.bfloat16),
        )

    query_grad, key_grad, value_grad = lax.map(
        attend_back,
        (
            queries.reshape(shaped),
            key_rows.reshape(shaped),
            value_rows.reshape(shaped),
            allowed,
            logsum,
            context_grad.reshape(shaped),
        ),
    )
    query_grad = query_grad.reshape(-1, D)
    key_grad = key_grad.reshape(-1, D)
    value_grad = value_grad.reshape(-1, D)
    query_add_grad = jnp.sum(query_grad.astype(jnp.float32), axis=0)
    value_add_grad = jnp.sum(value_grad.astype(jnp.float32), axis=0)
    query_mat_grad = jnp.dot(hidden_in.T, query_grad, preferred_element_type=jnp.float32)
    key_mat_grad = jnp.dot(hidden_in.T, key_grad, preferred_element_type=jnp.float32)
    value_mat_grad = jnp.dot(hidden_in.T, value_grad, preferred_element_type=jnp.float32)
    input_grad = (
        residual_grad
        + jnp.dot(query_grad, query_mat.T, preferred_element_type=jnp.float32)
        + jnp.dot(key_grad, key_mat.T, preferred_element_type=jnp.float32)
        + jnp.dot(value_grad, value_mat.T, preferred_element_type=jnp.float32)
    )
    gradients = (
        query_mat_grad,
        query_add_grad,
        key_mat_grad,
        value_mat_grad,
        value_add_grad,
        output_mat_grad,
        output_add_grad,
        gain_one_grad,
        shift_one_grad,
        inner_mat_grad,
        inner_add_grad,
        outer_mat_grad,
        outer_add_grad,
        gain_two_grad,
        shift_two_grad,
    )
    return (input_grad, gradients)


def per_device(
    hidden_in,
    cotangent,
    span_lengths,
    partner_span,
    query_weight,
    query_bias,
    key_weight,
    value_weight,
    value_bias,
    output_weight,
    output_bias,
    first_gain,
    first_shift,
    inner_weight,
    inner_bias,
    outer_weight,
    outer_bias,
    second_gain,
    second_shift,
):
    shards = (
        query_weight,
        query_bias,
        key_weight,
        value_weight,
        value_bias,
        output_weight,
        output_bias,
        first_gain,
        first_shift,
        inner_weight,
        inner_bias,
        outer_weight,
        outer_bias,
        second_gain,
        second_shift,
    )
    length = SPAN * SPANS_ROW
    row_count = hidden_in.shape[0] // length
    allowed = jnp.arange(SPAN)[None, None, :] < span_lengths.reshape(row_count, SPANS_ROW, 1)
    gathered = collect(shards)
    encoded, stored = encode(hidden_in, allowed, gathered)
    cls_rows = (
        encoded.reshape(row_count, SPANS_ROW, SPAN, D)[:, :, 0, :]
        .reshape(-1, D)
        .astype(jnp.bfloat16)
    )
    other_rows = mate(cls_rows)
    logits = jnp.dot(cls_rows, other_rows.T, preferred_element_type=jnp.float32) / math.sqrt(D)
    span_count = cls_rows.shape[0]
    matches = (partner_span.reshape(span_count, 1) == jnp.arange(span_count)[None, :]).astype(
        jnp.float32
    )
    target = jnp.where(lax.axis_index("pair") == 0, matches, matches.T)
    highest_logit = jnp.max(logits, axis=-1, keepdims=True)
    exponent = jnp.exp(logits - highest_logit)
    totals = jnp.sum(exponent, axis=-1, keepdims=True)
    span_loss = highest_logit[:, 0] + jnp.log(totals[:, 0]) - jnp.sum(target * logits, axis=-1)
    softened = exponent / totals - target
    own_grad = jnp.dot(softened, other_rows.astype(jnp.float32), precision=highest)
    other_logits = logits.T
    other_highest = jnp.max(other_logits, axis=-1, keepdims=True)
    other_exponent = jnp.exp(other_logits - other_highest)
    other_softened = (
        other_exponent / jnp.sum(other_exponent, axis=-1, keepdims=True) - target.T
    )
    back_grad = jnp.dot(
        other_softened.T, other_rows.astype(jnp.float32), precision=highest
    ).astype(jnp.bfloat16)
    cls_gradient = (own_grad + back_grad.astype(jnp.float32)).reshape(row_count, SPANS_ROW, 1, D)
    placed = jnp.concatenate(
        [cls_gradient, jnp.zeros((row_count, SPANS_ROW, SPAN - 1, D), jnp.float32)], axis=2
    )
    out_gradient = cotangent.astype(jnp.float32) + placed.reshape(-1, D)
    input_grad, gradients = backward(hidden_in, allowed, gathered, stored, out_gradient)
    reduced = spread(gradients)
    return (encoded.astype(jnp.bfloat16), input_grad.astype(jnp.bfloat16), span_loss) + tuple(
        reduced
    )


ROW = 24
PLACES = 8


def coordinates():
    doc = lax.axis_index("doc")
    return (doc & 1, (doc >> 1) & 1, doc >> 2, lax.axis_index("pair"))


def permutations():
    core, x_at, z_at, y_at = coordinates()
    row = jnp.arange(D, dtype=jnp.int32)
    block, inside = row // ROW, row % ROW
    y_off, x_off = (block & 1) ^ y_at, ((block >> 2) & 1) ^ x_at
    block_core, z_off = (block >> 1) & 1, (block >> 3) ^ z_at
    arrived = ((((block_core ^ core) * 2 + y_off) * 2 + x_off) * 4 + z_off) * ROW + inside
    leaving = ((y_off * 2 + x_off) * 4 + z_off) * 2 * ROW + block_core * ROW + inside
    restore = (arrived[:, None] == row[None, :]).astype(jnp.bfloat16)
    arrange = (leaving[None, :] == row[:, None]).astype(jnp.bfloat16)
    return (restore, arrange)


def after(value, *others):
    return lax.optimization_barrier((value,) + others)[0]


def z_exchange(block):
    return [across(block, mask) for mask in (4, 8, 12)]


def tied(values, *others):
    return lax.optimization_barrier(tuple(values) + others)[: len(values)]


def near_exchange(block):
    return across(block[0], 2), mate(block[1])


def stack_near(block, received):
    return stack_pair(block[0], received[0], block[1], received[1])


def far_exchange(block):
    return mate(block[0]), across(block[1], 2)


def core_exchange(block):
    return across(block[0], 1), across(block[1], 1)


def pieces_of(near, far, core, far_core):
    return [near[0], far[0], near[1], far[1], core[0], far_core[0], core[1], far_core[1]]


VMEM = pl.BlockSpec(memory_space=pltpu.VMEM)
SMEM = pl.BlockSpec(memory_space=pltpu.SMEM)


def full(shape):
    return pl.BlockSpec(shape, lambda *at: (0,) * len(shape))


class Fetched:
    def __init__(self, source, held, semaphore):
        self.copy, self.held, self.waiting = pltpu.make_async_copy(source, held, semaphore), held, True
        self.shape = held.shape
        self.copy.start()

    def ready(self):
        if self.waiting:
            self.copy.wait()
            self.waiting = False
        return self.held

    def __getitem__(self, at):
        return self.ready()[at]


class Stored:
    def __init__(self, target, held, semaphores):
        self.target, self.held, self.semaphores, self.copies = target, held, semaphores, []
        self.shape = held.shape

    def __getitem__(self, at):
        return self.held[at]

    def __setitem__(self, at, value):
        self.held[at] = value

    def done(self, at=None):
        semaphore = self.semaphores.at[len(self.copies)]
        held, target = (self.held, self.target) if at is None else (self.held.at[at], self.target.at[at])
        self.copies.append(pltpu.make_async_copy(held, target, semaphore))
        self.copies[-1].start()


PARTS = 8


def run(kernel, name, operands, results, flops, scratch=(), mib=12):
    in_hbm = pl.BlockSpec(memory_space=pltpu.HBM)
    spaces = {"S": SMEM, "V": VMEM, "H": in_hbm, "A": in_hbm}
    in_places = [place for _, place in operands]
    out_places = [place for _, _, place in results]
    staged = [pltpu.VMEM(array.shape, array.dtype) for array, place in operands if place == "H"]
    made = [pltpu.VMEM(shape, dtype) for shape, dtype, place in results if place == "H"]
    semaphores = [pltpu.SemaphoreType.DMA((max(1, len(staged)),))]
    semaphores += [pltpu.SemaphoreType.DMA((max(1, len(made)), PARTS))]

    def body(*refs):
        ins, refs = refs[: len(operands)], refs[len(operands) :]
        outs, refs = refs[: len(results)], refs[len(results) :]
        held_in, refs = refs[: len(staged)], refs[len(staged) :]
        held_out, refs = refs[: len(made)], refs[len(made) :]
        fetching, storing, own = refs[0], refs[1], refs[2:]
        arguments, at = [], 0
        for ref, place in zip(ins, in_places):
            if place == "H":
                ref, at = Fetched(ref, held_in[at], fetching.at[at]), at + 1
            arguments.append(ref)
        inputs, at = list(arguments), 0
        for ref, place in zip(outs, out_places):
            if place == "H":
                ref, at = Stored(ref, held_out[at], storing.at[at]), at + 1
            arguments.append(ref)
        kernel(*arguments, *own)
        for ref in inputs:
            if isinstance(ref, Fetched):
                ref.ready()
        made_here = [ref for ref in arguments if isinstance(ref, Stored)]
        for ref in made_here:
            if not ref.copies:
                ref.done()
        for ref in made_here:
            for copy in ref.copies:
                copy.wait()

    size = lambda shape, dtype: math.prod(shape) * jnp.dtype(dtype).itemsize
    inside = sum(size(array.shape, array.dtype) for array, place in operands if place == "H")
    inside += sum(size(shape, dtype) for shape, dtype, place in results if place == "H")
    mib = mib + inside // 2**20
    return pl.pallas_call(
        body,
        in_specs=[spaces[place] for place in in_places],
        out_specs=[spaces[place] for place in out_places],
        out_shape=[jax.ShapeDtypeStruct(shape, dtype) for shape, dtype, _ in results],
        scratch_shapes=staged + made + semaphores + list(scratch),
        compiler_params=params(mib),
        cost_estimate=cost(1, 1),
        name=name,
    )(*[array for array, _ in operands])


def placed_at(place, *arrays):
    return [(array, place) for array in arrays]


bf16, f32 = jnp.bfloat16, jnp.float32


def params(mib=16):
    return pltpu.CompilerParams(vmem_limit_bytes=mib << 20)


def cost(flops, moved):
    return pl.CostEstimate(flops=int(flops), bytes_accessed=int(moved), transcendentals=0)


def dot(left, right):
    return jnp.dot(left, right, preferred_element_type=jnp.float32)


def dot_nt(left, right):
    return lax.dot_general(
        left, right, (((1,), (1,)), ((), ())), preferred_element_type=jnp.float32
    )


def dot_tn(left, right):
    return lax.dot_general(
        left, right, (((0,), (0,)), ((), ())), preferred_element_type=jnp.float32
    )


def pack_kernel(*refs):
    query, key, value, output, inner, inner_bias = refs[:6]
    vectors, (first, second, turned) = refs[6:-3], refs[-3:]
    turned[...] = jnp.zeros_like(turned)
    for at, vector in enumerate(vectors):
        turned[at : at + 1, :ROW] = vector[...].astype(jnp.float32)
    bias = inner_bias[...].astype(jnp.float32)
    for at in range(4):
        turned[8 + at : 9 + at, :ROW] = bias[:, at * ROW : (at + 1) * ROW]
    small = jnp.transpose(turned[...])[:ROW].astype(jnp.bfloat16)
    first[:, :D] = query[...]
    first[:, D : D + 512] = key[:, :512]
    first[:, D + 512 : D + 640] = small
    first[:, D + 640 : D + 768] = jnp.zeros_like(small)
    first[:, D + 768 : D + 1024] = key[:, 512:]
    first[:, D + 1024 :] = value[...]
    second[:, :D] = output[...]
    second[:, D:] = inner[...]


def pack(query, key, value, output, inner, inner_bias, vectors):
    rows = [vector.reshape(1, -1) for vector in (inner_bias, *vectors)]
    return run(
        pack_kernel,
        "pack",
        placed_at("H", query, key, value, output, inner, *rows),
        [((ROW, 2 * FIRST_HALF), bf16, "V"), ((ROW, D + inner.shape[1]), bf16, "V")],
        1e6,
        [pltpu.VMEM((128, 128), f32)],
        mib=58,
    )


def stack_z_kernel(split, first, second, third, fourth, left, right):
    blocks = [ref[...].astype(jnp.float32) for ref in (first, second, third, fourth)]
    whole = jnp.concatenate(blocks).astype(jnp.bfloat16)
    left[...] = whole[:, :split]
    right[...] = whole[:, split:]


def stack_z(block, received, split):
    rows, columns = block.shape
    return pl.pallas_call(
        partial(stack_z_kernel, split),
        in_specs=[VMEM] * 4,
        out_specs=[VMEM] * 2,
        out_shape=[
            jax.ShapeDtypeStruct((4 * rows, split), jnp.bfloat16),
            jax.ShapeDtypeStruct((4 * rows, columns - split), jnp.bfloat16),
        ],
        compiler_params=params(),
        cost_estimate=cost(1, 1),
        name="stack_z",
    )(block, *received)


def stack_pair_kernel(left, left_in, right, right_in, left_out, right_out):
    for own, received, out in ((left, left_in, left_out), (right, right_in, right_out)):
        rows = own.shape[0]
        out[:rows, :] = own[...]
        out[rows:, :] = received[...]


def stack_pair(left, left_in, right, right_in):
    double = lambda block: jax.ShapeDtypeStruct((2 * block.shape[0], block.shape[1]), block.dtype)
    return pl.pallas_call(
        stack_pair_kernel,
        in_specs=[VMEM] * 4,
        out_specs=[VMEM] * 2,
        out_shape=[double(left), double(right)],
        compiler_params=params(),
        cost_estimate=cost(1, 1),
        name="stack_pair",
    )(left, left_in, right, right_in)


def left_tile(refs, columns):
    return jnp.concatenate([ref[:, columns] for ref in refs])


def right_tile(refs, columns):
    near, far, other_near, other_far = refs
    rows = near.shape[0] // 2
    order = [(near, 0), (far, 0), (near, 1), (far, 1)]
    order += [(other_near, 0), (other_far, 0), (other_near, 1), (other_far, 1)]
    return jnp.concatenate([ref[at * rows : (at + 1) * rows, columns] for ref, at in order])


def in_order(pieces):
    left, left_far, right, right_far, c_left, c_left_far, c_right, c_right_far = pieces
    return (left, left_far, c_left, c_left_far, right, right_far, c_right, c_right_far)


FIRST_HALF = 1280
SECOND_HALF = 1792
def head_pair(pair, low):
    nothing = jnp.zeros_like(pair)
    return jnp.concatenate([jnp.where(low, pair, nothing), jnp.where(low, nothing, pair)])


def key_columns(left_rows, right_rows, rows, at):
    if at < 512:
        return left_rows[rows, D + at : D + at + 128]
    return right_rows[rows, at - 256 : at - 128]


def front_kernel(
    lengths,
    hidden,
    restore,
    arrange,
    l0,
    l1,
    l2,
    l3,
    r0,
    r1,
    r2,
    r3,
    left_rows,
    right_rows,
    vectors,
    attention_out,
    context_arrived,
    hidden_t,
    context_t,
    context,
):
    tokens = hidden.shape[0]
    hidden_t[...] = dot_nt(arrange[...], hidden[...]).astype(jnp.bfloat16)
    moved = dot(hidden[...], restore[...]).astype(jnp.bfloat16)
    small = dot(restore[...], right_tile((r0, r1, r2, r3), slice(0, 128)))
    turned = jnp.transpose(small)[:16]
    vectors[...] = turned
    for at in range(0, FIRST_HALF, 256):
        columns = slice(at, at + 256)
        rows = dot(moved, left_tile((l0, l1, l2, l3), columns))
        if at < D:
            rows += turned[0:1, columns]
        left_rows[:, columns] = rows.astype(jnp.bfloat16)
        if at == 0:
            right_rows[:, columns] = jnp.zeros((tokens, 256), jnp.bfloat16)
            continue
        rows = dot(moved, right_tile((r0, r1, r2, r3), columns))
        if at >= 512:
            rows += turned[1:2, at - 512 : at - 256]
        right_rows[:, columns] = rows.astype(jnp.bfloat16)
    low = lax.broadcasted_iota(jnp.int32, (SPAN, 128), 1) < HEAD_DIM

    def attend(span, carry):
        rows = pl.ds(pl.multiple_of(span * SPAN, SPAN), SPAN)
        live = lax.broadcasted_iota(jnp.int32, (SPAN, SPAN), 1) < lengths[span]
        for at in range(0, D, 128):
            query = left_rows[rows, at : at + 128]
            keys = head_pair(key_columns(left_rows, right_rows, rows, at), low)
            values = head_pair(right_rows[rows, 512 + at : 640 + at], low)
            scores = dot_nt(query, keys) * HEAD_DIM ** (-0.5)
            parts = []
            for head in range(2):
                part = jnp.where(live, scores[:, head * SPAN : (head + 1) * SPAN], masked_out)
                exponent = jnp.exp(part - jnp.max(part, axis=-1, keepdims=True))
                parts.append(
                    (exponent * (1.0 / jnp.sum(exponent, axis=-1, keepdims=True))).astype(jnp.bfloat16)
                )
            attention = jnp.concatenate(parts, axis=1)
            attention_out[rows, 2 * at : 2 * at + 256] = attention
            context[rows, at : at + 128] = dot(attention, values).astype(jnp.bfloat16)
        return carry

    lax.fori_loop(0, tokens // SPAN, attend, 0)
    context_arrived[...] = dot(context[...], restore[...]).astype(jnp.bfloat16)
    context_t[...] = dot_nt(arrange[...], context[...]).astype(jnp.bfloat16)


def front(lengths, hidden, restore, arrange, pieces):
    tokens = hidden.shape[0]
    return run(
        front_kernel,
        "front",
        [(lengths, "S")] + placed_at("H", hidden, restore, arrange, *in_order(pieces)),
        [
            ((tokens, FIRST_HALF), bf16, "H"),
            ((tokens, FIRST_HALF), bf16, "H"),
            ((16, D), f32, "V"),
            ((tokens, 2 * D), bf16, "H"),
            ((tokens, D), bf16, "H"),
            ((D, tokens), bf16, "H"),
            ((D, tokens), bf16, "H"),
        ],
        9e9,
        [pltpu.VMEM((tokens, D), bf16)],
    )


def gelu_parts(preact):
    scaled = jnp.abs(preact) * (0.5**0.5)
    near = 1.0 / (1.0 + 0.3275911 * scaled)
    poly = near * (
        0.254829592
        + near * (-0.284496736 + near * (1.421413741 + near * (-1.453152027 + near * 1.061405429)))
    )
    bell = jnp.exp(-0.5 * preact * preact)
    tail = 0.5 * poly * bell
    below = jnp.where(preact < 0.0, tail, 1.0 - tail)
    return (preact * below, below + preact * bell * (0.5 / math.pi) ** 0.5)


FF_TILE = 512


def second_tiles(left, right):
    for at in range(D, SECOND_HALF, FF_TILE):
        yield at - D, left_tile(left, slice(at, at + FF_TILE))
    for at in range(0, right[0].shape[1], FF_TILE):
        yield SECOND_HALF - D + at, right_tile(right, slice(at, at + FF_TILE))


def vector_places():
    for device in range(D // ROW):
        for part in range(4):
            yield (8 + part, device * ROW), (device * 4 + part) * ROW


def middle_kernel(
    hidden,
    context_arrived,
    restore,
    arrange,
    vectors,
    l0,
    l1,
    l2,
    l3,
    r0,
    r1,
    r2,
    r3,
    active,
    active_t,
    slope,
    normed_out,
    factor_out,
    first_t,
    inner_bias,
):
    for at, column in vector_places():
        inner_bias[:, column : column + ROW] = vectors[at[0] : at[0] + 1, at[1] : at[1] + ROW]
    left, right = (l0, l1, l2, l3), (r0, r1, r2, r3)
    residual = hidden[...].astype(jnp.float32) + vectors[2:3, :]
    residual += dot(context_arrived[...], left_tile(left, slice(0, D)))
    first_out, normed, factor = normalize(residual, vectors[3:4, :], vectors[4:5, :])
    normed_out[...] = normed
    factor_out[...] = factor
    first16 = first_out.astype(jnp.bfloat16)
    first_t[...] = dot_nt(arrange[...], first16).astype(jnp.bfloat16)
    normed_out.done()
    first_t.done()
    moved = dot(first16, restore[...]).astype(jnp.bfloat16)
    for at, tile in second_tiles(left, right):
        columns = slice(at, at + FF_TILE)
        value, derivative = gelu_parts(dot(moved, tile) + inner_bias[:, columns])
        value16 = value.astype(jnp.bfloat16)
        active[:, columns] = value16
        active_t[columns, :] = jnp.transpose(value16)
        slope[:, columns] = derivative.astype(jnp.bfloat16)
        active.done((slice(None), columns))
        active_t.done((columns, slice(None)))
        slope.done((slice(None), columns))


def middle(hidden, context_arrived, restore, arrange, vectors, ff, pieces):
    tokens = hidden.shape[0]
    return run(
        middle_kernel,
        "middle",
        placed_at("H", hidden, context_arrived, restore, arrange)
        + placed_at("V", vectors)
        + placed_at("H", *in_order(pieces)),
        [
            ((tokens, ff), bf16, "H"),
            ((ff, tokens), bf16, "H"),
            ((tokens, ff), bf16, "H"),
            ((tokens, D), f32, "H"),
            ((tokens, 1), f32, "V"),
            ((D, tokens), bf16, "H"),
        ],
        8e9,
        [pltpu.VMEM((1, ff), f32)],
    )


def natural_rows(place, pieces, target, semaphore):
    rows = 4 * ROW
    for at, piece in enumerate(pieces):
        half = piece.shape[1]
        is_right, core_off, far_off = at // 4, at // 2 % 2, at % 2
        for near_off in range(2):
            for z_off in range(4):
                x_off, y_off = (far_off, near_off) if is_right else (near_off, far_off)
                block = ((z_off ^ place[3]) * 2 + (x_off ^ place[2])) * 2 + (core_off ^ place[0])
                block = block * 2 + (y_off ^ place[1])
                to = pl.ds(pl.multiple_of(block * rows, rows), rows)
                pltpu.make_async_copy(
                    piece.at[pl.ds((near_off * 4 + z_off) * rows, rows), :],
                    target.at[to, pl.ds(is_right * half, half)],
                    semaphore,
                ).start()
    pltpu.make_async_copy(target, target, semaphore).wait()


def last_kernel(
    place,
    active,
    first_normed,
    vectors,
    l0,
    l1,
    l2,
    l3,
    r0,
    r1,
    r2,
    r3,
    layer_out,
    normed_out,
    factor_out,
    cls_rows,
    outer_mat,
    semaphore,
):
    natural_rows(place, (l0, l1, l2, l3, r0, r1, r2, r3), outer_mat, semaphore)
    total = first_normed[...] * vectors[3:4, :] + vectors[4:5, :] + vectors[5:6, :]
    total += dot(active[...], outer_mat[...])
    encoded, normed, factor = normalize(total, vectors[6:7, :], vectors[7:8, :])
    layer_out[...] = encoded.astype(jnp.bfloat16)
    normed_out[...] = normed
    factor_out[...] = factor
    for span in range(encoded.shape[0] // SPAN):
        cls_rows[span : span + 1, :] = encoded[span * SPAN : span * SPAN + 1].astype(jnp.bfloat16)


def last(place, active, first_normed, vectors, pieces):
    tokens, ff = active.shape
    return run(
        last_kernel,
        "last",
        [(place, "S")]
        + placed_at("H", active, first_normed)
        + [(vectors, "V")]
        + placed_at("A", *in_order(pieces)),
        [
            ((tokens, D), bf16, "H"),
            ((tokens, D), f32, "V"),
            ((tokens, 1), f32, "V"),
            ((tokens // SPAN, D), bf16, "V"),
            ((ff, D), bf16, "V"),
        ],
        2.5e9,
        [pltpu.SemaphoreType.DMA],
    )


def pick(place, first, second):
    return jnp.where(place == 0, first, second)


def turn_kernel(
    place,
    partner_span,
    cotangent,
    normed,
    factor,
    vectors,
    own_rows,
    other_rows,
    second_grad,
    kept,
    sent,
    sums,
    loss,
):
    spans = own_rows.shape[0]
    own, other = own_rows[...].astype(jnp.float32), other_rows[...].astype(jnp.float32)
    logits = dot_nt(own_rows[...], other_rows[...]) / math.sqrt(D)
    row = lax.broadcasted_iota(jnp.int32, (spans, spans), 0)
    column = lax.broadcasted_iota(jnp.int32, (spans, spans), 1)
    first_place = place[1] == 0
    target = jnp.zeros((spans, spans), jnp.float32)
    for span in range(spans):
        match = partner_span[0, span]
        hit_row = jnp.where(first_place, span, match)
        hit_column = jnp.where(first_place, match, span)
        target += ((row == hit_row) & (column == hit_column)).astype(jnp.float32)
    highest_logit = jnp.max(logits, axis=1, keepdims=True)
    exponent = jnp.exp(logits - highest_logit)
    totals = jnp.sum(exponent, axis=1, keepdims=True)
    losses = highest_logit + jnp.log(totals) - jnp.sum(target * logits, axis=1, keepdims=True)
    loss[...] = jnp.sum(jnp.where(row == column, losses, 0.0), axis=0, keepdims=True)
    soft = exponent / totals - target
    exponent = jnp.exp(logits - jnp.max(logits, axis=0, keepdims=True))
    back = exponent / jnp.sum(exponent, axis=0, keepdims=True) - target
    own_term, back_term = jnp.zeros_like(own), jnp.zeros_like(own)
    for span in range(spans):
        own_term += soft[:, span : span + 1] * other[span : span + 1]
        back_term += back[:, span : span + 1] * other[span : span + 1]
    cls_gradient = own_term + back_term.astype(jnp.bfloat16).astype(jnp.float32)
    start = lax.broadcasted_iota(jnp.int32, (SPAN, 1), 0) == 0
    gain = vectors[6:7, :]
    gain_sum = jnp.zeros((1, D), jnp.float32)
    shift_sum, bias_sum = gain_sum, gain_sum
    for span in range(spans):
        rows = slice(span * SPAN, (span + 1) * SPAN)
        upstream = cotangent[rows, :].astype(jnp.float32)
        upstream += jnp.where(start, cls_gradient[span : span + 1], 0.0)
        grad, gain_part, shift_part = normalize_back(upstream, normed[rows, :], factor[rows, :], gain)
        second_grad[rows, :] = grad
        gain_sum += gain_part[None]
        shift_sum += shift_part[None]
        bias_sum += jnp.sum(grad, axis=0, keepdims=True)
        grad16 = grad.astype(jnp.bfloat16)
        kept[rows, :] = pick(place[0], grad16[:, : D // 2], grad16[:, D // 2 :])
        sent[rows, :] = pick(place[0], grad16[:, D // 2 :], grad16[:, : D // 2])
    sums[0:1, :] = bias_sum
    sums[1:2, :] = gain_sum
    sums[2:3, :] = shift_sum


def turn(place, partner_span, cotangent, normed, factor, vectors, own_rows, other_rows):
    tokens = cotangent.shape[0]
    return run(
        turn_kernel,
        "turn",
        placed_at("S", place, partner_span)
        + [(cotangent, "H")]
        + placed_at("V", normed, factor, vectors, own_rows, other_rows),
        [
            ((tokens, D), f32, "H"),
            ((tokens, D // 2), bf16, "V"),
            ((tokens, D // 2), bf16, "V"),
            ((3, D), f32, "V"),
            ((1, own_rows.shape[0]), f32, "V"),
        ],
        1e8,
    )


def both_halves(place, kept, sent):
    return jnp.concatenate([pick(place, kept, sent), pick(place, sent, kept)], axis=1)


def slope_kernel(place, second_kept, second_sent, outer_mat, slope, kept, sent, sums):
    second16 = both_halves(place[0], second_kept[...], second_sent[...])
    half = kept.shape[1]
    for at in range(0, 2 * half, D):
        columns, inside = slice(at, at + D), slice(at % half, at % half + D)
        grad = dot_nt(second16, outer_mat[columns, :]) * slope[:, columns].astype(jnp.float32)
        sums[:, columns] = jnp.sum(grad, axis=0, keepdims=True)
        grad16 = grad.astype(jnp.bfloat16)
        mine = place[0] == at // half

        @pl.when(mine)
        def keep():
            kept[:, inside] = grad16

        @pl.when(jnp.logical_not(mine))
        def send():
            sent[:, inside] = grad16


def slope_back(place, second_kept, second_sent, outer_mat, slope):
    tokens, ff = slope.shape
    half = ((tokens, ff // 2), bf16, "V")
    return run(
        slope_kernel,
        "slope_back",
        [(place, "S")] + placed_at("V", second_kept, second_sent, outer_mat) + [(slope, "H")],
        [half, half, ((1, ff), f32, "V")],
        2.5e9,
    )


def outer_kernel(place, active_t, other_active_t, kept, received, left_kept, left_sent, right_kept, right_sent):
    rows = 2 * ROW
    active_t, other_active_t = active_t.ready(), other_active_t.ready()

    def chip_rows(chip, carry):
        x_off, z_off = (chip & 1) ^ place[2], (chip >> 1) ^ place[3]
        tile = pl.ds(pl.multiple_of(chip * 8 * rows, 8 * rows), 8 * rows)
        grad = dot(active_t[tile, :], kept[...]) + dot(other_active_t[tile, :], received[...])
        grad = grad.astype(jnp.bfloat16)
        for core in range(2):
            for y_at in range(2):
                start = (core * 2 + y_at) * 2 * rows
                left, right = grad[start : start + rows], grad[start + rows : start + 2 * rows]
                y_off = place[1] ^ y_at
                left_at = (x_off * 4 + z_off) * 2 + core
                right_at = (y_off * 4 + z_off) * 2 + core

                @pl.when(y_off == 0)
                def left_here():
                    left_kept[left_at] = left

                @pl.when(y_off == 1)
                def left_there():
                    left_sent[left_at] = left

                @pl.when(x_off == 0)
                def right_here():
                    right_kept[right_at] = right

                @pl.when(x_off == 1)
                def right_there():
                    right_sent[right_at] = right

        return carry

    lax.fori_loop(0, PLACES, chip_rows, 0)


def outer_gradient(place, active_t, other_active_t, kept, received):
    piece = ((2 * PLACES, 2 * ROW, kept.shape[1]), bf16, "V")
    return run(
        outer_kernel,
        "outer_gradient",
        [(place, "S")] + placed_at("H", active_t, other_active_t) + placed_at("V", kept, received),
        [piece] * 4,
        2.5e9,
    )


def whole_precision(left, right):
    high = left.astype(jnp.bfloat16)
    rest = (left - high.astype(jnp.float32)).astype(jnp.bfloat16)
    return dot_nt(high, right) + dot_nt(rest, right)


def first_kernel(
    place,
    preact_kept,
    preact_sent,
    second_grad,
    normed,
    factor,
    vectors,
    restore,
    l0,
    l1,
    l2,
    l3,
    r0,
    r1,
    r2,
    r3,
    residual_grad,
    kept,
    sent,
    context_grad,
    sums,
):
    left, right = (l0, l1, l2, l3), (r0, r1, r2, r3)
    total = jnp.zeros(second_grad.shape, jnp.float32)
    half = preact_kept.shape[1]
    for at, tile in second_tiles(left, right):
        columns = slice(at % half, at % half + FF_TILE)
        kept_part, sent_part = preact_kept[:, columns], preact_sent[:, columns]
        if at >= half:
            kept_part, sent_part = sent_part, kept_part
        total += dot_nt(pick(place[0], kept_part, sent_part), tile)
    first_grad = second_grad[...] + whole_precision(total, restore[...])
    grad, gain_sum, shift_sum = normalize_back(first_grad, normed[...], factor[...], vectors[3:4, :])
    residual_grad[...] = grad
    sums[0:1, :] = jnp.sum(grad, axis=0, keepdims=True)
    sums[1:2, :] = gain_sum[None]
    sums[2:3, :] = shift_sum[None]
    grad16 = grad.astype(jnp.bfloat16)
    kept[...] = pick(place[0], grad16[:, : D // 2], grad16[:, D // 2 :])
    sent[...] = pick(place[0], grad16[:, D // 2 :], grad16[:, : D // 2])
    moved = dot_nt(grad16, left_tile(left, slice(0, D))).astype(jnp.bfloat16)
    context_grad[...] = dot_nt(moved, restore[...]).astype(jnp.bfloat16)


def first_back(place, preact_kept, preact_sent, second_grad, normed, factor, vectors, restore, pieces):
    tokens = second_grad.shape[0]
    half = ((tokens, D // 2), bf16, "V")
    return run(
        first_kernel,
        "first_back",
        [(place, "S")]
        + placed_at("V", preact_kept, preact_sent)
        + placed_at("H", second_grad, normed)
        + placed_at("V", factor, vectors)
        + placed_at("H", restore, *in_order(pieces)),
        [((tokens, D), f32, "H"), half, half, ((tokens, D), bf16, "V"), ((3, D), f32, "V")],
        4.9e9,
    )


def part_rows(grad, left_kept, left_sent, right_kept, right_sent, is_left):
    quarter = D // 4
    if is_left:
        left_kept[...] = grad[: 2 * quarter]
        left_sent[...] = grad[2 * quarter :]
    else:
        right_kept[:quarter, :] = grad[:quarter]
        right_sent[:quarter, :] = grad[quarter : 2 * quarter]
        right_kept[quarter:, :] = grad[2 * quarter : 3 * quarter]
        right_sent[quarter:, :] = grad[3 * quarter :]


def inner_kernel(first_t, other_first_t, kept, received, left_kept, left_sent, right_kept, right_sent):
    for is_left in (True, False):
        columns = slice(0, D) if is_left else slice(D, 2 * D)
        grad = dot(first_t[...], kept[:, columns]) + dot(other_first_t[...], received[:, columns])
        part_rows(grad.astype(jnp.bfloat16), left_kept, left_sent, right_kept, right_sent, is_left)


def inner_gradient(first_t, other_first_t, kept, received):
    piece = ((D // 2, kept.shape[1] // 2), bf16, "V")
    return run(
        inner_kernel,
        "inner_gradient",
        placed_at("H", first_t, other_first_t) + placed_at("V", kept, received),
        [piece] * 4,
        2.5e9,
    )


def attend_kernel(
    place,
    context_grad,
    left_rows,
    right_rows,
    attention_in,
    first_sums,
    second_sums,
    inner_sums,
    kept,
    sent,
    sums,
    grads,
):
    tokens = context_grad.shape[0]
    low = lax.broadcasted_iota(jnp.int32, (SPAN, 128), 1) < HEAD_DIM
    scale = HEAD_DIM ** (-0.5)
    left_rows, right_rows, attention_in = [ref.ready() for ref in (left_rows, right_rows, attention_in)]

    def attend(span, carry):
        rows = pl.ds(pl.multiple_of(span * SPAN, SPAN), SPAN)
        for at in range(0, D, 128):
            query = left_rows[rows, at : at + 128]
            keys = head_pair(key_columns(left_rows, right_rows, rows, at), low)
            values = head_pair(right_rows[rows, 512 + at : 640 + at], low)
            upstream = context_grad[rows, at : at + 128]
            attention16 = attention_in[rows, 2 * at : 2 * at + 256]
            attention_grad = dot_nt(upstream, values)
            parts = []
            for head in range(2):
                columns = slice(head * SPAN, (head + 1) * SPAN)
                attention = attention16[:, columns].astype(jnp.float32)
                part = attention_grad[:, columns]
                weighted = jnp.sum(attention * part, axis=-1, keepdims=True)
                parts.append((attention * (part - weighted)).astype(jnp.bfloat16))
            scores_grad = jnp.concatenate(parts, axis=1)
            grads[0, rows, at : at + 128] = (dot(scores_grad, keys) * scale).astype(jnp.bfloat16)
            both = dot_tn(scores_grad, query)
            both = jnp.where(low, both[:SPAN], both[SPAN:])
            grads[1, rows, at : at + 128] = (both * scale).astype(jnp.bfloat16)
            both = dot_tn(attention16, upstream)
            both = jnp.where(low, both[:SPAN], both[SPAN:])
            grads[2, rows, at : at + 128] = both.astype(jnp.bfloat16)
        return carry

    lax.fori_loop(0, tokens // SPAN, attend, 0)
    query_grad, key_grad, value_grad = grads[0], grads[1], grads[2]
    half = D // 2
    for at, grad in enumerate((query_grad, key_grad, value_grad)):
        columns = slice(at * half, (at + 1) * half)
        kept[:, columns] = pick(place[0], grad[:, :half], grad[:, half:])
        sent[:, columns] = pick(place[0], grad[:, half:], grad[:, :half])
    sums[0:1, :] = jnp.sum(query_grad.astype(jnp.float32), axis=0, keepdims=True)
    sums[1:2, :] = jnp.sum(value_grad.astype(jnp.float32), axis=0, keepdims=True)
    sums[2:5, :] = first_sums[...]
    sums[5:8, :] = second_sums[...]
    for at, column in vector_places():
        sums[at[0] : at[0] + 1, at[1] : at[1] + ROW] = inner_sums[:, column : column + ROW]
    sums[12:16, :] = jnp.zeros((4, D), jnp.float32)


def attend_back(place, context_grad, left_rows, right_rows, attention, first_sums, second_sums, inner_sums):
    tokens = context_grad.shape[0]
    part = ((tokens, 3 * D // 2), bf16, "V")
    return run(
        attend_kernel,
        "attend_back",
        placed_at("S", place)
        + placed_at("V", context_grad)
        + placed_at("H", left_rows, right_rows, attention)
        + placed_at("V", first_sums, second_sums, inner_sums),
        [part, part, ((16, D), f32, "V")],
        4e9,
        [pltpu.VMEM((3, tokens, D), bf16)],
    )


def attention_gradient_kernel(
    arrange,
    sums,
    other_sums,
    hidden_t,
    other_hidden_t,
    context_t,
    other_context_t,
    grads,
    other_grads,
    residual,
    other_residual,
    left_kept,
    left_sent,
    right_kept,
    right_sent,
):
    half = D // 2
    grad = dot(hidden_t[...], grads[:, :D]) + dot(other_hidden_t[...], other_grads[:, :D])
    grad = grad.astype(jnp.bfloat16)
    left_kept[:, :D] = grad[:half]
    left_sent[:, :D] = grad[half:]
    total = (sums[...] + other_sums[...]).astype(jnp.bfloat16)
    total = jnp.concatenate([total, jnp.zeros((112, D), jnp.bfloat16)])
    small = dot_nt(arrange[...], total).astype(jnp.bfloat16)
    left_kept[:, D:] = small[:half]
    left_sent[:, D:] = small[half:]
    value = dot(hidden_t[...], grads[:, D:]) + dot(other_hidden_t[...], other_grads[:, D:])
    output = dot(context_t[...], residual[...]) + dot(other_context_t[...], other_residual[...])
    grad = jnp.concatenate([value, output], axis=1).astype(jnp.bfloat16)
    part_rows(grad, left_kept, left_sent, right_kept, right_sent, False)


def attention_gradient(*operands):
    left, right = ((D // 2, D + 128), bf16, "V"), ((D // 2, D), bf16, "V")
    places = ["H"] + ["V"] * 2 + ["H"] * 4 + ["V"] * 4
    return run(
        attention_gradient_kernel,
        "attention_gradient",
        list(zip(operands, places)),
        [left, left, right, right],
        2.5e9,
    )


def input_kernel(place, residual_grad, kept, sent, restore, l0, l1, l2, l3, r0, r1, r2, r3, input_grad):
    left, right = (l0, l1, l2, l3), (r0, r1, r2, r3)
    half = D // 2
    parts = []
    for at in range(3):
        columns = slice(at * half, (at + 1) * half)
        parts.append(both_halves(place[0], kept[:, columns], sent[:, columns]))
    query_grad, key_grad, value_grad = parts
    total = dot_nt(query_grad, left_tile(left, slice(0, D)))
    total += dot_nt(key_grad[:, :512], left_tile(left, slice(D, FIRST_HALF)))
    total += dot_nt(key_grad[:, 512:], right_tile(right, slice(256, 512)))
    total += dot_nt(value_grad, right_tile(right, slice(512, FIRST_HALF)))
    total = residual_grad[...] + whole_precision(total, restore[...])
    input_grad[...] = total.astype(jnp.bfloat16)


def input_back(place, residual_grad, kept, sent, restore, pieces):
    return run(
        input_kernel,
        "input_back",
        [(place, "S"), (residual_grad, "H")]
        + placed_at("V", kept, sent)
        + placed_at("H", restore, *in_order(pieces)),
        [(residual_grad.shape, bf16, "H")],
        3e9,
    )[0]


def add_kernel(left, left_in, right, right_in, left_kept, left_sent, right_kept, right_sent):
    for own, received, kept, sent in (
        (left, left_in, left_kept, left_sent),
        (right, right_in, right_kept, right_sent),
    ):
        total = (own[...].astype(jnp.float32) + received[...].astype(jnp.float32)).astype(jnp.bfloat16)
        half = total.shape[0] // 2
        kept[...] = total[:half]
        sent[...] = total[half:]


def add_parts(left, left_in, right, right_in):
    shapes = [(part.shape[0] // 2,) + part.shape[1:] for part in (left, left, right, right)]
    return pl.pallas_call(
        add_kernel,
        in_specs=[VMEM] * 4,
        out_specs=[VMEM] * 4,
        out_shape=[jax.ShapeDtypeStruct(shape, jnp.bfloat16) for shape in shapes],
        compiler_params=params(),
        cost_estimate=cost(1, 1),
        name="add_parts",
    )(left, left_in, right, right_in)


def add_z_kernel(left, left_in, right, right_in, own, first, second, third):
    width = left.shape[-1]
    for part, received, columns in (
        (left, left_in, slice(0, width)),
        (right, right_in, slice(width, width + right.shape[-1])),
    ):
        rows = part.shape[0] // 4
        total = part[...].astype(jnp.float32) + received[...].astype(jnp.float32)
        own[..., columns] = total[:rows]
        for at, sent in enumerate((first, second, third)):
            sent[..., columns] = total[(at + 1) * rows : (at + 2) * rows].astype(jnp.bfloat16)


def add_z(left, left_in, right, right_in):
    shape = (left.shape[0] // 4,) + left.shape[1:-1] + (left.shape[-1] + right.shape[-1],)
    return pl.pallas_call(
        add_z_kernel,
        in_specs=[VMEM] * 4,
        out_specs=[VMEM] * 4,
        out_shape=[jax.ShapeDtypeStruct(shape, jnp.float32)]
        + [jax.ShapeDtypeStruct(shape, jnp.bfloat16)] * 3,
        compiler_params=params(),
        cost_estimate=cost(1, 1),
        name="add_z",
    )(left, left_in, right, right_in)


def finish_kernel(place, own, first, second, third, mine, other):
    total = own[...]
    for received in (first, second, third):
        total = total + received[...].astype(jnp.float32)
    if len(total.shape) == 3:
        low, high = total[0], total[1]
    else:
        low, high = total[:ROW], total[ROW:]
    mine[...] = pick(place[0], low, high)
    other[...] = pick(place[0], high, low)


def finish(place, own, received):
    rows = own.shape[1] if own.ndim == 3 else ROW
    return pl.pallas_call(
        finish_kernel,
        in_specs=[SMEM] + [VMEM] * 4,
        out_specs=[VMEM] * 2,
        out_shape=[jax.ShapeDtypeStruct((rows, own.shape[-1]), jnp.float32)] * 2,
        compiler_params=params(),
        cost_estimate=cost(1, 1),
        name="finish",
    )(place, own, *received)


def put(place, out, mine, received):
    half = mine.shape[1]
    out[:, :half] = pick(place[0], mine, received)
    out[:, half:] = pick(place[0], received, mine)


def outer_out_kernel(place, mine, received, out):
    rows, half = mine.shape[0], mine.shape[1] // 2
    for at in range(2):
        columns = slice(at * half, (at + 1) * half)
        put(place, out.at[at * rows : (at + 1) * rows], mine[:, columns], received[:, columns])


def inner_out_kernel(place, mine, received, out):
    put(place, out, mine[...], received[...])


def rest_out_kernel(place, mine, received, query, key, value, output, inner_bias, *vectors):
    half = D // 2
    for out, at in ((query, 0), (key, half), (value, D + 128), (output, D + 128 + half)):
        columns = slice(at, at + half)
        put(place, out, mine[:, columns], received[:, columns])
    turned = jnp.transpose(mine[:, D : D + 128])
    for at, out in enumerate(vectors):
        out[...] = turned[at : at + 1]
    for at in range(4):
        inner_bias[:, at * ROW : (at + 1) * ROW] = turned[8 + at : 9 + at]


def placed(kernel, name, place, mine, received, shapes):
    return pl.pallas_call(
        kernel,
        in_specs=[SMEM, VMEM, VMEM],
        out_specs=[VMEM] * len(shapes),
        out_shape=[jax.ShapeDtypeStruct(shape, jnp.float32) for shape in shapes],
        compiler_params=params(),
        cost_estimate=cost(1, 1),
        name=name,
    )(place, mine, received)


def first_transfers(pieces):
    return [mate(pieces[1]), across(pieces[3], 2)]


def add_first(pieces, received):
    return add_parts(pieces[0], received[0], pieces[2], received[1])


def second_transfers(pieces):
    return [across(pieces[1], 2), mate(pieces[3])]


def add_second(pieces, received):
    return add_z(pieces[0], received[0], pieces[2], received[1])


def third_transfers(parts):
    return [across(sent, mask) for sent, mask in zip(parts[1:], (4, 8, 12))]


def fast_device(
    hidden_in,
    cotangent,
    span_lengths,
    partner_span,
    query_weight,
    query_bias,
    key_weight,
    value_weight,
    value_bias,
    output_weight,
    output_bias,
    first_gain,
    first_shift,
    inner_weight,
    inner_bias,
    outer_weight,
    outer_bias,
    second_gain,
    second_shift,
):
    core, x_at, z_at, y_at = coordinates()
    place = jnp.stack([core, y_at, x_at, z_at]).astype(jnp.int32)
    restore, arrange = permutations()
    first_block, second_block = pack(
        query_weight,
        key_weight,
        value_weight,
        output_weight,
        inner_weight,
        inner_bias,
        (
            query_bias,
            value_bias,
            output_bias,
            first_gain,
            first_shift,
            outer_bias,
            second_gain,
            second_shift,
        ),
    )
    ff = inner_weight.shape[1]
    first_z = z_exchange(first_block)
    first = stack_z(first_block, first_z, FIRST_HALF)
    first_in = near_exchange(first)
    second_z = z_exchange(after(second_block, *first))
    first = stack_near(first, first_in)
    first_far = far_exchange(first)
    first_core = core_exchange(first)
    second = stack_z(after(second_block, *first_far), second_z, SECOND_HALF)
    second_in = near_exchange(second)
    third_z = z_exchange(after(outer_weight, *second))
    first_far_core = core_exchange(tied(first_far, *second))
    second = stack_near(second, second_in)
    second_far = far_exchange(second)
    second_core = core_exchange(second)
    first_pieces = pieces_of(first, first_far, first_core, tied(first_far_core, *second))
    left_rows, right_rows, vectors, attention, context_arrived, hidden_t, context_t = front(
        span_lengths, hidden_in, restore, arrange, first_pieces
    )
    third = stack_z(after(outer_weight, vectors, *second_far), third_z, D // 2)
    third_in = near_exchange(third)
    second_far_core = core_exchange(tied(second_far, *third))
    third = stack_near(third, third_in)
    third_far = far_exchange(third)
    third_core = core_exchange(third)
    second_pieces = pieces_of(second, second_far, second_core, tied(second_far_core, *third))
    active, active_t, slope, first_normed, first_factor, first_t = middle(
        hidden_in, context_arrived, restore, arrange, vectors, ff, second_pieces
    )
    third_far_core = core_exchange(tied(third_far, first_factor))
    third_pieces = pieces_of(third, third_far, third_core, third_far_core)
    layer_out, second_normed, second_factor, cls_rows, outer_mat = last(
        place, active, first_normed, vectors, third_pieces
    )
    other_rows = mate(cls_rows)
    hidden_t, context_t, first_t, active_t = tied((hidden_t, context_t, first_t, active_t), cls_rows)
    other_hidden_t, other_context_t = across(hidden_t, 1), across(context_t, 1)
    other_first_t, other_active_t = across(first_t, 1), across(active_t, 1)
    second_grad, second_kept, second_sent, second_sums, span_loss = turn(
        place, partner_span, cotangent, second_normed, second_factor, vectors, cls_rows, other_rows
    )
    second_received = across(second_sent, 1)
    preact_kept, preact_sent, inner_sums = slope_back(
        place, second_kept, second_sent, outer_mat, slope
    )
    preact_received = across(preact_sent, 1)
    outer_parts = outer_gradient(
        place, active_t, other_active_t, after(second_kept, preact_kept), second_received
    )
    outer_in = first_transfers(outer_parts)
    residual_grad, residual_kept, residual_sent, context_grad, first_sums = first_back(
        place,
        after(preact_kept, outer_parts[0]),
        preact_sent,
        second_grad,
        first_normed,
        first_factor,
        vectors,
        restore,
        second_pieces,
    )
    outer_parts = add_first(outer_parts, tied(outer_in, context_grad))
    outer_in = second_transfers(outer_parts)
    residual_received = across(after(residual_sent, outer_parts[0]), 1)
    inner_parts = inner_gradient(
        first_t, other_first_t, after(preact_kept, outer_parts[0]), preact_received
    )
    outer_parts = add_second(outer_parts, tied(outer_in, inner_parts[0]))
    outer_in = third_transfers(outer_parts)
    inner_in = first_transfers(tied(inner_parts, outer_parts[0]))
    grads_kept, grads_sent, sums = attend_back(
        place,
        after(context_grad, inner_parts[0], outer_parts[0]),
        left_rows,
        right_rows,
        attention,
        first_sums,
        second_sums,
        inner_sums,
    )
    inner_parts = add_first(inner_parts, tied(inner_in, sums))
    inner_in = second_transfers(inner_parts)
    grads_received = across(after(grads_sent, inner_parts[0]), 1)
    other_sums = across(after(sums, inner_parts[0]), 1)
    outer_mine, outer_other = finish(place, outer_parts[0], tied(outer_in, inner_parts[0]))
    outer_other = across(outer_other, 1)
    rest_parts = attention_gradient(
        arrange,
        sums,
        other_sums,
        hidden_t,
        other_hidden_t,
        context_t,
        other_context_t,
        after(grads_kept, outer_mine),
        grads_received,
        residual_kept,
        residual_received,
    )
    inner_parts = add_second(inner_parts, tied(inner_in, rest_parts[0]))
    rest_in = first_transfers(tied(rest_parts, inner_parts[0]))
    inner_in = third_transfers(inner_parts)
    input_grad = input_back(
        place,
        residual_grad,
        after(grads_kept, rest_parts[0], inner_parts[0]),
        grads_sent,
        restore,
        first_pieces,
    )
    rest_parts = add_first(rest_parts, tied(rest_in, input_grad))
    rest_in = second_transfers(rest_parts)
    inner_mine, inner_other = finish(place, inner_parts[0], tied(inner_in, rest_parts[0]))
    inner_other = across(inner_other, 1)
    (outer_grad,) = placed(
        outer_out_kernel, "outer_out", place, outer_mine, after(outer_other, inner_mine), [(4 * ROW, D)]
    )
    rest_parts = add_second(rest_parts, tied(rest_in, outer_grad))
    rest_in = third_transfers(rest_parts)
    (inner_grad,) = placed(
        inner_out_kernel, "inner_out", place, inner_mine, after(inner_other, rest_parts[0]), [(ROW, ff)]
    )
    rest_mine, rest_other = finish(place, rest_parts[0], tied(rest_in, inner_grad))
    rest_other = across(rest_other, 1)
    query_grad, key_grad, value_grad, output_grad, inner_bias_grad, *vector_grads = placed(
        rest_out_kernel,
        "rest_out",
        place,
        rest_mine,
        rest_other,
        [(ROW, D)] * 4 + [(1, 4 * ROW)] + [(1, ROW)] * 8,
    )
    vector_grads = [grad.reshape(-1) for grad in vector_grads]
    return (
        layer_out,
        input_grad,
        span_loss.reshape(-1),
        query_grad,
        vector_grads[0],
        key_grad,
        value_grad,
        vector_grads[1],
        output_grad,
        vector_grads[2],
        vector_grads[3],
        vector_grads[4],
        inner_grad,
        inner_bias_grad.reshape(-1),
        outer_grad,
        vector_grads[5],
        vector_grads[6],
        vector_grads[7],
    )


def solution(mesh):
    is_block = mesh.shape["doc"] == 2 * PLACES and mesh.shape["pair"] == 2
    return jax.shard_map(
        fast_device if is_block else per_device,
        mesh=mesh,
        in_specs=(
            P(("doc", "pair"), None),
            P(("doc", "pair"), None),
            P(("doc", "pair")),
            P("doc", None),
            P(("doc", "pair"), None),
            P(("doc", "pair")),
            P(("doc", "pair"), None),
            P(("doc", "pair"), None),
            P(("doc", "pair")),
            P(("doc", "pair"), None),
            P(("doc", "pair")),
            P(("doc", "pair")),
            P(("doc", "pair")),
            P(("doc", "pair"), None),
            P(("doc", "pair")),
            P(("doc", "pair"), None),
            P(("doc", "pair")),
            P(("doc", "pair")),
            P(("doc", "pair")),
        ),
        out_specs=(
            P(("doc", "pair"), None),
            P(("doc", "pair"), None),
            P(("doc", "pair")),
            P(("doc", "pair"), None),
            P(("doc", "pair")),
            P(("doc", "pair"), None),
            P(("doc", "pair"), None),
            P(("doc", "pair")),
            P(("doc", "pair"), None),
            P(("doc", "pair")),
            P(("doc", "pair")),
            P(("doc", "pair")),
            P(("doc", "pair"), None),
            P(("doc", "pair")),
            P(("doc", "pair"), None),
            P(("doc", "pair")),
            P(("doc", "pair")),
            P(("doc", "pair")),
        ),
        check_vma=False,
    )
```

```python
from functools import partial
import math

import jax
import jax.numpy as jnp
from jax import lax
from jax.experimental import pallas as pl
from jax.experimental.pallas import tpu as pltpu
from jax.sharding import PartitionSpec as P

D = 768
HEAD_DIM = 64
SPAN = 128
SPANS_ROW = 4


epsilon = 1e-06
masked_out = -1000000000.0
highest = lax.Precision.HIGHEST


def across(block, mask):
    count = lax.axis_size("doc")
    return lax.ppermute(block, "doc", [(at, at ^ mask) for at in range(count)])


def mate(block):
    return lax.ppermute(block, "pair", [(0, 1), (1, 0)])


def far_groups():
    bits = lax.axis_size("doc").bit_length() - 1
    far = [1 << at for at in range(2, bits)]
    return [far[at : at + 2] for at in range(0, len(far), 2)]


def is_upper(mask):
    return (lax.axis_index("doc") & mask) != 0


def joined(own, other, upper):
    return jnp.where(upper, jnp.stack([other, own]), jnp.stack([own, other]))


def gather_rows(block):
    rows, columns = block.shape
    total = block[None]
    for masks in far_groups():
        low = masks[0]
        near = joined(total, across(total, low), is_upper(low))
        if len(masks) == 2:
            high = masks[1]
            straight, crossed = across(total, high), across(total, high | low)
            far = joined(straight, crossed, is_upper(low))
            near = joined(near, far, is_upper(high)).reshape((4,) + total.shape)
        total = near.reshape((-1, rows, columns))
    half = columns // 2
    left, right = total[..., :half], total[..., half:]
    on_pair = lax.axis_index("pair") == 1
    left_x, right_y = across(left, 2), mate(right)
    left, right = joined(left, left_x, is_upper(2)), joined(right, right_y, on_pair)
    left_y, right_x = mate(left), across(right, 2)
    left, right = joined(left, left_y, on_pair), joined(right, right_x, is_upper(2))
    left = joined(left, across(left, 1), is_upper(1))
    right = joined(right, across(right, 1), is_upper(1))
    left = jnp.transpose(left, (3, 2, 0, 1, 4, 5))
    right = jnp.transpose(right, (3, 1, 0, 2, 4, 5))
    return jnp.concatenate([left, right], axis=-1).reshape(-1, rows, columns)


def halves(blocks, axis, upper):
    lower = lax.index_in_dim(blocks, 0, axis, keepdims=False)
    higher = lax.index_in_dim(blocks, 1, axis, keepdims=False)
    return (jnp.where(upper, higher, lower), jnp.where(upper, lower, higher))


def plus(kept, received):
    return kept.astype(jnp.float32) + received.astype(jnp.float32)


def scatter_rows(blocks):
    rows, columns = blocks.shape[1:]
    on_pair = lax.axis_index("pair") == 1
    blocks = blocks.astype(jnp.bfloat16).reshape(-1, 2, 2, 2, rows, columns)
    kept, sent = halves(blocks, 2, is_upper(1))
    total = plus(kept, across(sent, 1)).astype(jnp.bfloat16)
    half = columns // 2
    left, right = total[..., :half], total[..., half:]
    left_kept, left_sent = halves(left, 2, on_pair)
    right_kept, right_sent = halves(right, 1, is_upper(2))
    left = plus(left_kept, mate(left_sent)).astype(jnp.bfloat16)
    right = plus(right_kept, across(right_sent, 2)).astype(jnp.bfloat16)
    left_kept, left_sent = halves(left, 1, is_upper(2))
    right_kept, right_sent = halves(right, 1, on_pair)
    left = plus(left_kept, across(left_sent, 2))
    right = plus(right_kept, mate(right_sent))
    total = jnp.concatenate([left, right], axis=-1)
    for masks in far_groups()[::-1]:
        total = total.astype(jnp.bfloat16).reshape(2 ** len(masks), -1, rows, columns)
        place = (lax.axis_index("doc") // masks[0]) % 2 ** len(masks)
        summed = lax.dynamic_index_in_dim(total, place, 0, keepdims=False).astype(jnp.float32)
        for step in range(1, 2 ** len(masks)):
            sent = lax.dynamic_index_in_dim(total, place ^ step, 0, keepdims=False)
            summed = plus(summed, across(sent, masks[0] * step))
        total = summed
    return total.reshape(rows, columns)


VECTORS = (1, 4, 6, 7, 8, 10, 12, 13, 14)


def pack_vectors(pieces):
    flat = jnp.concatenate(pieces, axis=-1)
    width = -(-flat.shape[-1] // D) * D
    flat = jnp.pad(flat, [(0, 0)] * (flat.ndim - 1) + [(0, width - flat.shape[-1])])
    return flat.reshape(flat.shape[:-1] + (-1, D))


def fold(matrix):
    return jnp.concatenate([matrix[:, at : at + D] for at in range(0, matrix.shape[1], D)])


def collect(shards):
    rows = shards[0].shape[0]
    devices = lax.axis_size("doc") * lax.axis_size("pair")
    small = pack_vectors([shards[at] for at in VECTORS])
    first = gather_rows(jnp.concatenate([shards[0], shards[2], shards[3], small]))
    second = gather_rows(jnp.concatenate([shards[5], fold(shards[9])]))
    outer = lax.all_gather(shards[11], ("doc", "pair"), axis=0, tiled=True)
    whole = {
        0: first[:, :rows].reshape(-1, D),
        2: first[:, rows : 2 * rows].reshape(-1, D),
        3: first[:, 2 * rows : 3 * rows].reshape(-1, D),
        5: second[:, :rows].reshape(-1, D),
        9: jnp.concatenate(
            [
                second[:, at : at + rows].reshape(-1, D)
                for at in range(rows, second.shape[1], rows)
            ],
            axis=1,
        ),
        11: outer,
    }
    vectors, start = first[:, 3 * rows :].reshape(devices, -1), 0
    for at in VECTORS:
        size = shards[at].shape[0]
        whole[at] = vectors[:, start : start + size].reshape(-1).astype(jnp.float32)
        start += size
    return tuple(whole[at] for at in range(15))


def spread(gradients):
    devices = lax.axis_size("doc") * lax.axis_size("pair")
    by_device = [
        piece.reshape((devices, -1) + piece.shape[1:]) for piece in gradients
    ]
    rows = by_device[0].shape[1]
    outer = scatter_rows(by_device[11])
    inner = by_device[9]
    parts = [inner[..., at : at + D] for at in range(0, inner.shape[-1], D)]
    second = scatter_rows(jnp.concatenate([by_device[5]] + parts, axis=1))
    small = pack_vectors([by_device[at] for at in VECTORS])
    first = scatter_rows(
        jnp.concatenate([by_device[0], by_device[2], by_device[3], small], axis=1)
    )
    own = {
        0: first[:rows],
        2: first[rows : 2 * rows],
        3: first[2 * rows : 3 * rows],
        5: second[:rows],
        9: jnp.concatenate(
            [second[at : at + rows] for at in range(rows, second.shape[0], rows)], axis=1
        ),
        11: outer,
    }
    vectors, start = first[3 * rows :].reshape(-1), 0
    for at in VECTORS:
        size = by_device[at].shape[1]
        own[at] = vectors[start : start + size]
        start += size
    return tuple(own[at] for at in range(15))


def normalize(hidden, gain, shift):
    average = jnp.mean(hidden, axis=-1, keepdims=True)
    centred = hidden - average
    factor = lax.rsqrt(jnp.mean(centred * centred, axis=-1, keepdims=True) + epsilon)
    normed = centred * factor
    return (normed * gain + shift, normed, factor)


def normalize_back(upstream, normed, factor, gain):
    scaled = upstream * gain
    hidden_grad = factor * (
        scaled
        - jnp.mean(scaled, axis=-1, keepdims=True)
        - normed * jnp.mean(scaled * normed, axis=-1, keepdims=True)
    )
    return (hidden_grad, jnp.sum(upstream * normed, axis=0), jnp.sum(upstream, axis=0))


def head_scores(query_row, key_row, live_row):
    product = jnp.einsum("sqhd,skhd->shqk", query_row, key_row, preferred_element_type=jnp.float32)
    return jnp.where(live_row[:, None, None, :], product * HEAD_DIM ** (-0.5), masked_out)


def encode(hidden_in, allowed, gathered):
    (
        query_mat,
        query_add,
        key_mat,
        value_mat,
        value_add,
        output_mat,
        output_add,
        gain_one,
        shift_one,
        inner_mat,
        inner_add,
        outer_mat,
        outer_add,
        gain_two,
        shift_two,
    ) = gathered
    row_count = allowed.shape[0]
    shaped = (row_count, SPANS_ROW, SPAN, D // HEAD_DIM, HEAD_DIM)
    queries = (
        jnp.dot(hidden_in, query_mat, preferred_element_type=jnp.float32) + query_add
    ).astype(jnp.bfloat16)
    key_rows = jnp.dot(hidden_in, key_mat, preferred_element_type=jnp.float32).astype(jnp.bfloat16)
    value_rows = (
        jnp.dot(hidden_in, value_mat, preferred_element_type=jnp.float32) + value_add
    ).astype(jnp.bfloat16)

    def attend(element):
        query_row, key_row, value_row, live_row = element
        scores = head_scores(query_row, key_row, live_row)
        highest_score = jnp.max(scores, axis=-1, keepdims=True)
        exponent = jnp.exp(scores - highest_score)
        totals = jnp.sum(exponent, axis=-1, keepdims=True)
        attention = (exponent / totals).astype(jnp.bfloat16)
        context_row = jnp.einsum(
            "shqk,skhd->sqhd", attention, value_row, preferred_element_type=jnp.float32
        )
        return (context_row.astype(jnp.bfloat16), (highest_score + jnp.log(totals))[..., 0])

    context, logsum = lax.map(
        attend,
        (queries.reshape(shaped), key_rows.reshape(shaped), value_rows.reshape(shaped), allowed),
    )
    context = context.reshape(-1, D)
    residual = (
        hidden_in.astype(jnp.float32)
        + jnp.dot(context, output_mat, preferred_element_type=jnp.float32)
        + output_add
    )
    first_out, first_normed, first_factor = normalize(residual, gain_one, shift_one)
    first16 = first_out.astype(jnp.bfloat16)
    preact = jnp.dot(first16, inner_mat, preferred_element_type=jnp.float32) + inner_add
    active = jax.nn.gelu(preact, approximate=False).astype(jnp.bfloat16)
    second = first_out + jnp.dot(active, outer_mat, preferred_element_type=jnp.float32) + outer_add
    encoded, second_normed, second_factor = normalize(second, gain_two, shift_two)
    stored = (
        queries,
        key_rows,
        value_rows,
        logsum,
        context,
        first_normed,
        first_factor,
        first16,
        preact,
        active,
        second_normed,
        second_factor,
    )
    return (encoded, stored)


def backward(hidden_in, allowed, gathered, stored, out_gradient):
    (
        query_mat,
        query_add,
        key_mat,
        value_mat,
        value_add,
        output_mat,
        output_add,
        gain_one,
        shift_one,
        inner_mat,
        inner_add,
        outer_mat,
        outer_add,
        gain_two,
        shift_two,
    ) = gathered
    (
        queries,
        key_rows,
        value_rows,
        logsum,
        context,
        first_normed,
        first_factor,
        first16,
        preact,
        active,
        second_normed,
        second_factor,
    ) = stored
    row_count = allowed.shape[0]
    shaped = (row_count, SPANS_ROW, SPAN, D // HEAD_DIM, HEAD_DIM)
    second_grad, gain_two_grad, shift_two_grad = normalize_back(
        out_gradient, second_normed, second_factor, gain_two
    )
    outer_add_grad = jnp.sum(second_grad, axis=0)
    second16 = second_grad.astype(jnp.bfloat16)
    outer_mat_grad = jnp.dot(active.T, second16, preferred_element_type=jnp.float32)
    active_grad = jnp.dot(second16, outer_mat.T, preferred_element_type=jnp.float32)
    unused, gelu_back = jax.vjp(partial(jax.nn.gelu, approximate=False), preact)
    preact_grad = gelu_back(active_grad)[0]
    inner_add_grad = jnp.sum(preact_grad, axis=0)
    preact16 = preact_grad.astype(jnp.bfloat16)
    inner_mat_grad = jnp.dot(first16.T, preact16, preferred_element_type=jnp.float32)
    first_grad = second_grad + jnp.dot(preact16, inner_mat.T, preferred_element_type=jnp.float32)
    residual_grad, gain_one_grad, shift_one_grad = normalize_back(
        first_grad, first_normed, first_factor, gain_one
    )
    output_add_grad = jnp.sum(residual_grad, axis=0)
    residual16 = residual_grad.astype(jnp.bfloat16)
    output_mat_grad = jnp.dot(context.T, residual16, preferred_element_type=jnp.float32)
    context_grad = jnp.dot(residual16, output_mat.T, preferred_element_type=jnp.float32).astype(
        jnp.bfloat16
    )

    def attend_back(element):
        query_row, key_row, value_row, live_row, logsum_row, context_row = element
        scores = head_scores(query_row, key_row, live_row)
        attention = jnp.exp(scores - logsum_row[..., None])
        attention16 = attention.astype(jnp.bfloat16)
        value_grad = jnp.einsum(
            "shqk,sqhd->skhd", attention16, context_row, preferred_element_type=jnp.float32
        )
        attention_grad = jnp.einsum(
            "sqhd,skhd->shqk", context_row, value_row, preferred_element_type=jnp.float32
        )
        weighted = jnp.sum(attention * attention_grad, axis=-1, keepdims=True)
        scores_grad = (attention * (attention_grad - weighted)).astype(jnp.bfloat16)
        query_grad = jnp.einsum(
            "shqk,skhd->sqhd", scores_grad, key_row, preferred_element_type=jnp.float32
        ) * HEAD_DIM ** (-0.5)
        key_grad = jnp.einsum(
            "shqk,sqhd->skhd", scores_grad, query_row, preferred_element_type=jnp.float32
        ) * HEAD_DIM ** (-0.5)
        return (
            query_grad.astype(jnp.bfloat16),
            key_grad.astype(jnp.bfloat16),
            value_grad.astype(jnp.bfloat16),
        )

    query_grad, key_grad, value_grad = lax.map(
        attend_back,
        (
            queries.reshape(shaped),
            key_rows.reshape(shaped),
            value_rows.reshape(shaped),
            allowed,
            logsum,
            context_grad.reshape(shaped),
        ),
    )
    query_grad = query_grad.reshape(-1, D)
    key_grad = key_grad.reshape(-1, D)
    value_grad = value_grad.reshape(-1, D)
    query_add_grad = jnp.sum(query_grad.astype(jnp.float32), axis=0)
    value_add_grad = jnp.sum(value_grad.astype(jnp.float32), axis=0)
    query_mat_grad = jnp.dot(hidden_in.T, query_grad, preferred_element_type=jnp.float32)
    key_mat_grad = jnp.dot(hidden_in.T, key_grad, preferred_element_type=jnp.float32)
    value_mat_grad = jnp.dot(hidden_in.T, value_grad, preferred_element_type=jnp.float32)
    input_grad = (
        residual_grad
        + jnp.dot(query_grad, query_mat.T, preferred_element_type=jnp.float32)
        + jnp.dot(key_grad, key_mat.T, preferred_element_type=jnp.float32)
        + jnp.dot(value_grad, value_mat.T, preferred_element_type=jnp.float32)
    )
    gradients = (
        query_mat_grad,
        query_add_grad,
        key_mat_grad,
        value_mat_grad,
        value_add_grad,
        output_mat_grad,
        output_add_grad,
        gain_one_grad,
        shift_one_grad,
        inner_mat_grad,
        inner_add_grad,
        outer_mat_grad,
        outer_add_grad,
        gain_two_grad,
        shift_two_grad,
    )
    return (input_grad, gradients)


def per_device(
    hidden_in,
    cotangent,
    span_lengths,
    partner_span,
    query_weight,
    query_bias,
    key_weight,
    value_weight,
    value_bias,
    output_weight,
    output_bias,
    first_gain,
    first_shift,
    inner_weight,
    inner_bias,
    outer_weight,
    outer_bias,
    second_gain,
    second_shift,
):
    shards = (
        query_weight,
        query_bias,
        key_weight,
        value_weight,
        value_bias,
        output_weight,
        output_bias,
        first_gain,
        first_shift,
        inner_weight,
        inner_bias,
        outer_weight,
        outer_bias,
        second_gain,
        second_shift,
    )
    length = SPAN * SPANS_ROW
    row_count = hidden_in.shape[0] // length
    allowed = jnp.arange(SPAN)[None, None, :] < span_lengths.reshape(row_count, SPANS_ROW, 1)
    gathered = collect(shards)
    encoded, stored = encode(hidden_in, allowed, gathered)
    cls_rows = (
        encoded.reshape(row_count, SPANS_ROW, SPAN, D)[:, :, 0, :]
        .reshape(-1, D)
        .astype(jnp.bfloat16)
    )
    other_rows = mate(cls_rows)
    logits = jnp.dot(cls_rows, other_rows.T, preferred_element_type=jnp.float32) / math.sqrt(D)
    span_count = cls_rows.shape[0]
    matches = (partner_span.reshape(span_count, 1) == jnp.arange(span_count)[None, :]).astype(
        jnp.float32
    )
    target = jnp.where(lax.axis_index("pair") == 0, matches, matches.T)
    highest_logit = jnp.max(logits, axis=-1, keepdims=True)
    exponent = jnp.exp(logits - highest_logit)
    totals = jnp.sum(exponent, axis=-1, keepdims=True)
    span_loss = highest_logit[:, 0] + jnp.log(totals[:, 0]) - jnp.sum(target * logits, axis=-1)
    softened = exponent / totals - target
    own_grad = jnp.dot(softened, other_rows.astype(jnp.float32), precision=highest)
    other_logits = logits.T
    other_highest = jnp.max(other_logits, axis=-1, keepdims=True)
    other_exponent = jnp.exp(other_logits - other_highest)
    other_softened = (
        other_exponent / jnp.sum(other_exponent, axis=-1, keepdims=True) - target.T
    )
    back_grad = jnp.dot(
        other_softened.T, other_rows.astype(jnp.float32), precision=highest
    ).astype(jnp.bfloat16)
    cls_gradient = (own_grad + back_grad.astype(jnp.float32)).reshape(row_count, SPANS_ROW, 1, D)
    placed = jnp.concatenate(
        [cls_gradient, jnp.zeros((row_count, SPANS_ROW, SPAN - 1, D), jnp.float32)], axis=2
    )
    out_gradient = cotangent.astype(jnp.float32) + placed.reshape(-1, D)
    input_grad, gradients = backward(hidden_in, allowed, gathered, stored, out_gradient)
    reduced = spread(gradients)
    return (encoded.astype(jnp.bfloat16), input_grad.astype(jnp.bfloat16), span_loss) + tuple(
        reduced
    )


ROW = 24
PLACES = 8


def coordinates():
    doc = lax.axis_index("doc")
    return (doc & 1, (doc >> 1) & 1, doc >> 2, lax.axis_index("pair"))


def blocks_of(row):
    block = (row * 2731) >> 16
    return (block >> 1) & 1, block & 1, (block >> 2) & 1, block >> 3, row - block * ROW


def restore_from(place):
    row = lax.broadcasted_iota(jnp.int32, (D, 1), 0)
    core, y_at, x_at, z_at, inside = blocks_of(row)
    offset = ((core ^ place[0]) * 2 + (y_at ^ place[1])) * 2 + (x_at ^ place[2])
    arrived = (offset * 4 + (z_at ^ place[3])) * ROW + inside
    hit = arrived == lax.broadcasted_iota(jnp.int32, (D, D), 1)
    return jnp.where(hit, 1.0, 0.0).astype(jnp.bfloat16)


def arrange_from(place):
    row = lax.broadcasted_iota(jnp.int32, (1, D), 1)
    core, y_at, x_at, z_at, inside = blocks_of(row)
    offset = ((y_at ^ place[1]) * 2 + (x_at ^ place[2])) * 4 + (z_at ^ place[3])
    leaving = offset * 2 * ROW + core * ROW + inside
    hit = leaving == lax.broadcasted_iota(jnp.int32, (D, D), 0)
    return jnp.where(hit, 1.0, 0.0).astype(jnp.bfloat16)


def after(value, *others):
    return lax.optimization_barrier((value,) + others)[0]


def z_exchange(block, masks=(4, 8, 12)):
    return [across(block, mask) for mask in masks]


def tied(values, *others):
    return lax.optimization_barrier(tuple(values) + others)[: len(values)]


def near_exchange(block):
    return across(block[0], 2), mate(block[1])


def stack_near(block, received):
    return stack_pair(block[0], received[0], block[1], received[1])


def far_exchange(block):
    return mate(block[0]), across(block[1], 2)


def core_exchange(block):
    return [across(part, 1) for part in block]


def pieces_of(near, far, core, far_core):
    return [near[0], far[0], near[1], far[1], core, far_core[0], far_core[1]]


VMEM = pl.BlockSpec(memory_space=pltpu.VMEM)
SMEM = pl.BlockSpec(memory_space=pltpu.SMEM)


def full(shape):
    return pl.BlockSpec(shape, lambda *at: (0,) * len(shape))


class Fetched:
    def __init__(self, source, held, semaphore):
        self.copy, self.held, self.waiting = pltpu.make_async_copy(source, held, semaphore), held, True
        self.shape = held.shape
        self.copy.start()

    def ready(self):
        if self.waiting:
            self.copy.wait()
            self.waiting = False
        return self.held

    def __getitem__(self, at):
        return self.ready()[at]


class Stored:
    def __init__(self, target, held, semaphores):
        self.target, self.held, self.semaphores, self.copies = target, held, semaphores, []
        self.shape = held.shape

    def __getitem__(self, at):
        return self.held[at]

    def __setitem__(self, at, value):
        self.held[at] = value

    def done(self, at=None):
        semaphore = self.semaphores.at[len(self.copies)]
        held, target = (self.held, self.target) if at is None else (self.held.at[at], self.target.at[at])
        self.copies.append(pltpu.make_async_copy(held, target, semaphore))
        self.copies[-1].start()


PARTS = 8


def run(kernel, name, operands, results, flops, scratch=(), mib=12, total=None):
    in_hbm = pl.BlockSpec(memory_space=pltpu.HBM)
    spaces = {"S": SMEM, "V": VMEM, "H": in_hbm, "A": in_hbm}
    spaces["K"] = VMEM
    in_places = [place for _, place in operands]
    out_places = [place for _, _, place in results]
    staged = [pltpu.VMEM(array.shape, array.dtype) for array, place in operands if place == "H"]
    made = [pltpu.VMEM(shape, dtype) for shape, dtype, place in results if place == "H"]
    semaphores = [pltpu.SemaphoreType.DMA((max(1, len(staged)),))]
    semaphores += [pltpu.SemaphoreType.DMA((max(1, len(made)), PARTS))]

    def body(*refs):
        ins, refs = refs[: len(operands)], refs[len(operands) :]
        outs, refs = refs[: len(results)], refs[len(results) :]
        held_in, refs = refs[: len(staged)], refs[len(staged) :]
        held_out, refs = refs[: len(made)], refs[len(made) :]
        fetching, storing, own = refs[0], refs[1], refs[2:]
        arguments, at = [], 0
        for ref, place in zip(ins, in_places):
            if place == "H":
                ref, at = Fetched(ref, held_in[at], fetching.at[at]), at + 1
            arguments.append(ref)
        inputs, at = list(arguments), 0
        for ref, place in zip(outs, out_places):
            if place == "H":
                ref, at = Stored(ref, held_out[at], storing.at[at]), at + 1
            arguments.append(ref)
        kernel(*arguments, *own)
        for ref in inputs:
            if isinstance(ref, Fetched):
                ref.ready()
        made_here = [ref for ref in arguments if isinstance(ref, Stored)]
        for ref in made_here:
            if not ref.copies:
                ref.done()
        for ref in made_here:
            for copy in ref.copies:
                copy.wait()

    size = lambda shape, dtype: math.prod(shape) * jnp.dtype(dtype).itemsize
    inside = sum(size(array.shape, array.dtype) for array, place in operands if place == "H")
    inside += sum(size(shape, dtype) for shape, dtype, place in results if place == "H")
    mib = (mib + inside // 2**20) if total is None else total
    return pl.pallas_call(
        body,
        in_specs=[spaces[place] for place in in_places],
        out_specs=[spaces[place] for place in out_places],
        out_shape=[jax.ShapeDtypeStruct(shape, dtype) for shape, dtype, _ in results],
        scratch_shapes=staged + made + semaphores + list(scratch),
        compiler_params=params(mib),
        cost_estimate=cost(1, 1),
        name=name,
    )(*[array for array, _ in operands])


def placed_at(place, *arrays):
    return [(array, place) for array in arrays]


bf16, f32 = jnp.bfloat16, jnp.float32


def params(mib=16):
    return pltpu.CompilerParams(vmem_limit_bytes=mib << 20)


def cost(flops, moved):
    return pl.CostEstimate(flops=int(flops), bytes_accessed=int(moved), transcendentals=0)


def dot(left, right):
    return jnp.dot(left, right, preferred_element_type=jnp.float32)


def dot_nt(left, right):
    return lax.dot_general(
        left, right, (((1,), (1,)), ((), ())), preferred_element_type=jnp.float32
    )


def dot_tn(left, right):
    return lax.dot_general(
        left, right, (((0,), (0,)), ((), ())), preferred_element_type=jnp.float32
    )


def pack_kernel(*refs):
    query, key, value, output, inner, inner_bias = refs[:6]
    vectors, (first, second, turned) = refs[6:-3], refs[-3:]
    turned[...] = jnp.zeros_like(turned)
    for at, vector in enumerate(vectors):
        turned[at : at + 1, :ROW] = vector[...].astype(jnp.float32)
    bias = inner_bias[...].astype(jnp.float32)
    for at in range(4):
        turned[8 + at : 9 + at, :ROW] = bias[:, at * ROW : (at + 1) * ROW]
    small = jnp.transpose(turned[...])[:ROW].astype(jnp.bfloat16)
    first[:, :D] = query[...]
    first[:, D : D + 512] = key[:, :512]
    first[:, D + 512 : D + 640] = small
    first[:, D + 640 : D + 768] = jnp.zeros_like(small)
    first[:, D + 768 : D + 1024] = key[:, 512:]
    first[:, D + 1024 :] = value[...]
    second[:, :D] = output[...]
    second[:, D:] = inner[...]


def pack(query, key, value, output, inner, inner_bias, vectors):
    rows = [vector.reshape(1, -1) for vector in (inner_bias, *vectors)]
    return run(
        pack_kernel,
        "pack",
        placed_at("H", query, key, value, output, inner, *rows),
        [((ROW, 2 * FIRST_HALF), bf16, "V"), ((ROW, D + inner.shape[1]), bf16, "V")],
        1e6,
        [pltpu.VMEM((128, 128), f32)],
        total=58,
    )


def stack_two_kernel(first, second, left, right):
    blocks = [first[...].astype(jnp.float32), second[...].astype(jnp.float32)]
    whole = jnp.concatenate(blocks).astype(jnp.bfloat16)
    left[...] = whole[:, : left.shape[1]]
    right[...] = whole[:, left.shape[1] :]


def stack_two(block, received, split):
    rows, columns = block.shape
    return pl.pallas_call(
        stack_two_kernel,
        in_specs=[VMEM] * 2,
        out_specs=[VMEM] * 2,
        out_shape=[
            jax.ShapeDtypeStruct((2 * rows, split), jnp.bfloat16),
            jax.ShapeDtypeStruct((2 * rows, columns - split), jnp.bfloat16),
        ],
        compiler_params=params(),
        cost_estimate=cost(1, 1),
        name="stack_two",
    )(block, received)


def stack_z_two_kernel(first, second, out):
    blocks = [first[...].astype(jnp.float32), second[...].astype(jnp.float32)]
    out[...] = jnp.concatenate(blocks).astype(jnp.bfloat16)


def stack_z_two(block, received):
    rows, columns = block.shape
    return pl.pallas_call(
        stack_z_two_kernel,
        in_specs=[VMEM] * 2,
        out_specs=VMEM,
        out_shape=jax.ShapeDtypeStruct((2 * rows, columns), jnp.bfloat16),
        compiler_params=params(),
        cost_estimate=cost(1, 1),
        name="stack_z_two",
    )(block, received)


def stack_z_kernel(split, *refs):
    blocks, (left, right) = refs[:-2], refs[-2:]
    whole = jnp.concatenate([ref[...].astype(jnp.float32) for ref in blocks]).astype(jnp.bfloat16)
    left[...] = whole[:, :split]
    right[...] = whole[:, split:]


def stack_z(block, received, split):
    rows, columns = block.shape
    rows = rows * (1 + len(received)) // 4
    return pl.pallas_call(
        partial(stack_z_kernel, split),
        in_specs=[VMEM] * (1 + len(received)),
        out_specs=[VMEM] * 2,
        out_shape=[
            jax.ShapeDtypeStruct((4 * rows, split), jnp.bfloat16),
            jax.ShapeDtypeStruct((4 * rows, columns - split), jnp.bfloat16),
        ],
        compiler_params=params(),
        cost_estimate=cost(1, 1),
        name="stack_z",
    )(block, *received)


def stack_pair_kernel(left, left_in, right, right_in, left_out, right_out, both_out):
    width = left.shape[1]
    for own, received, out, columns in (
        (left, left_in, left_out, slice(0, width)),
        (right, right_in, right_out, slice(width, width + right.shape[1])),
    ):
        rows = own.shape[0]
        out[:rows, :] = own[...]
        out[rows:, :] = received[...]
        both_out[:rows, columns] = own[...]
        both_out[rows:, columns] = received[...]


def stack_pair(left, left_in, right, right_in):
    double = lambda block: jax.ShapeDtypeStruct((2 * block.shape[0], block.shape[1]), block.dtype)
    both = jax.ShapeDtypeStruct((2 * left.shape[0], left.shape[1] + right.shape[1]), left.dtype)
    return pl.pallas_call(
        stack_pair_kernel,
        in_specs=[VMEM] * 4,
        out_specs=[VMEM] * 3,
        out_shape=[double(left), double(right), both],
        compiler_params=params(),
        cost_estimate=cost(1, 1),
        name="stack_pair",
    )(left, left_in, right, right_in)


def left_tile(refs, columns):
    return jnp.concatenate([ref[:, columns] for ref in refs])


def right_tile(refs, columns):
    near, far, other_near, other_far = refs
    rows = near.shape[0] // 2
    order = [(near, 0), (far, 0), (near, 1), (far, 1)]
    order += [(other_near, 0), (other_far, 0), (other_near, 1), (other_far, 1)]
    return jnp.concatenate([ref[at * rows : (at + 1) * rows, columns] for ref, at in order])


def in_order(pieces):
    left, left_far, right, right_far, c_both, c_left_far, c_right_far = pieces
    return (left, left_far, c_left_far, c_both, right, right_far, c_right_far)


class Side:
    def __init__(self, ref, start, width):
        self.ref, self.start, self.shape = ref, start, (ref.shape[0], width)

    def __getitem__(self, at):
        rows, columns = at
        return self.ref[rows, columns.start + self.start : columns.stop + self.start]


def sides(l0, l1, l3, both, r0, r1, r3):
    left, right = l0.shape[1], r0.shape[1]
    return (l0, l1, Side(both, 0, left), l3), (r0, r1, Side(both, left, right), r3)


FIRST_PARTS = ((0, 0, 768), (0, 768, 512), (1, 256, 256), (1, 512, 768))
SECOND_PARTS = ((0, 0, 768), (0, 768, 512), (0, 1280, 512)) + tuple((1, at, 512) for at in range(0, 2048, 512))


def settle(sides_of, parts, mats, semaphore):
    copies = []
    for (side, start, width), mat in zip(parts, mats):
        for at, piece in enumerate(sides_of[side]):
            rows = piece.shape[0]
            source, first = (piece.ref, piece.start) if isinstance(piece, Side) else (piece, 0)
            columns = pl.ds(first + start, width)
            if side == 0:
                copies.append((source.at[:, columns], mat.at[pl.ds(at * rows, rows), :]))
                continue
            half = rows // 2
            core, far = at // 2, at % 2
            for near in range(2):
                to = ((core * 2 + near) * 2 + far) * half
                copies.append((source.at[pl.ds(near * half, half), columns], mat.at[pl.ds(to, half), :]))
    copies = [pltpu.make_async_copy(*ends, semaphore.at[at]) for at, ends in enumerate(copies)]
    for copy in copies:
        copy.start()
    return copies


FIRST_HALF = 1280
SECOND_HALF = 1792
def head_pair(pair, low):
    nothing = jnp.zeros_like(pair)
    return jnp.concatenate([jnp.where(low, pair, nothing), jnp.where(low, nothing, pair)])


def key_columns(left_rows, right_rows, rows, at):
    if at < 512:
        return left_rows[rows, D + at : D + at + 128]
    return right_rows[rows, at - 256 : at - 128]


def project_kernel(
    place,
    hidden,
    both,
    r0,
    r1,
    r3,
    l0,
    l1,
    l3,
    left_rows,
    right_rows,
    vectors,
    hidden_t,
    query_mat,
    low_key_mat,
    high_key_mat,
    value_mat,
    settling,
):
    tokens = hidden.shape[0]
    lefts, rights = sides(l0, l1, l3, both, r0, r1, r3)
    mats = (query_mat, low_key_mat, high_key_mat, value_mat)
    copies = settle((lefts, rights), FIRST_PARTS, mats, settling)
    restore = restore_from(place)
    moved = dot(hidden[...], restore).astype(jnp.bfloat16)
    small = dot(restore, right_tile(rights, slice(0, 128)))
    turned = jnp.transpose(small)[:16]
    vectors[...] = turned
    for at in range(0, FIRST_HALF, 256):
        columns = slice(at, at + 256)
        rows = dot(moved, left_tile(lefts, columns))
        if at < D:
            rows += turned[0:1, columns]
        left_rows[:, columns] = rows.astype(jnp.bfloat16)
        if at == 0:
            right_rows[:, columns] = jnp.zeros((tokens, 256), jnp.bfloat16)
            continue
        rows = dot(moved, right_tile(rights, columns))
        if at >= 512:
            rows += turned[1:2, at - 512 : at - 256]
        right_rows[:, columns] = rows.astype(jnp.bfloat16)
    left_rows.done()
    right_rows.done()
    hidden_t[...] = dot_nt(arrange_from(place), hidden[...]).astype(jnp.bfloat16)
    for copy in copies:
        copy.wait()


def project(place, hidden, pieces):
    tokens, ordered = hidden.shape[0], in_order(pieces)
    return run(
        project_kernel,
        "project",
        [(place, "S"), (hidden, "H")] + placed_at("K", *ordered[3:], *ordered[:3]),
        [
            ((tokens, FIRST_HALF), bf16, "H"),
            ((tokens, FIRST_HALF), bf16, "H"),
            ((16, D), f32, "V"),
            ((D, tokens), bf16, "H"),
        ]
        + [((D, width), bf16, "A") for _, _, width in FIRST_PARTS],
        9e9,
        [pltpu.SemaphoreType.DMA((24,))],
        total=50,
    )


def attention_kernel(
    place, lengths, left_rows, right_rows, attention_out, context_arrived, context_t, context
):
    tokens = context.shape[0]
    left_rows, right_rows = left_rows.ready(), right_rows.ready()
    low = lax.broadcasted_iota(jnp.int32, (SPAN, 128), 1) < HEAD_DIM

    def attend(span, carry):
        rows = pl.ds(pl.multiple_of(span * SPAN, SPAN), SPAN)
        live = lax.broadcasted_iota(jnp.int32, (SPAN, SPAN), 1) < lengths[span]
        for at in range(0, D, 128):
            query = left_rows[rows, at : at + 128]
            keys = head_pair(key_columns(left_rows, right_rows, rows, at), low)
            values = head_pair(right_rows[rows, 512 + at : 640 + at], low)
            scores = dot_nt(query, keys) * HEAD_DIM ** (-0.5)
            parts = []
            for head in range(2):
                part = jnp.where(live, scores[:, head * SPAN : (head + 1) * SPAN], masked_out)
                exponent = jnp.exp(part - jnp.max(part, axis=-1, keepdims=True))
                parts.append(
                    (exponent * (1.0 / jnp.sum(exponent, axis=-1, keepdims=True))).astype(jnp.bfloat16)
                )
            attention = jnp.concatenate(parts, axis=1)
            attention_out[rows, 2 * at : 2 * at + 256] = attention
            context[rows, at : at + 128] = dot(attention, values).astype(jnp.bfloat16)
        return carry

    lax.fori_loop(0, tokens // SPAN, attend, 0)
    attention_out.done()
    context_arrived[...] = dot(context[...], restore_from(place)).astype(jnp.bfloat16)
    context_t[...] = dot_nt(arrange_from(place), context[...]).astype(jnp.bfloat16)


def attention_forward(place, lengths, left_rows, right_rows):
    tokens = left_rows.shape[0]
    return run(
        attention_kernel,
        "attention_forward",
        placed_at("S", place, lengths) + placed_at("H", left_rows, right_rows),
        [((tokens, 2 * D), bf16, "H"), ((tokens, D), bf16, "V"), ((D, tokens), bf16, "H")],
        9e9,
        [pltpu.VMEM((tokens, D), bf16)],
        total=28,
    )


def gelu_parts(preact):
    scaled = jnp.abs(preact) * (0.5**0.5)
    below_one = 1.0 + 0.3275911 * scaled
    near = pl.reciprocal(below_one, approx=True)
    near = near * (2.0 - below_one * near)
    poly = near * (
        0.254829592
        + near * (-0.284496736 + near * (1.421413741 + near * (-1.453152027 + near * 1.061405429)))
    )
    bell = jnp.exp(-0.5 * preact * preact)
    tail = 0.5 * poly * bell
    below = jnp.where(preact < 0.0, tail, 1.0 - tail)
    return (preact * below, below + preact * bell * (0.5 / math.pi) ** 0.5)


FF_TILE = 512


def second_tiles(left, right):
    for at in range(D, SECOND_HALF, FF_TILE):
        yield at - D, left_tile(left, slice(at, at + FF_TILE))
    for at in range(0, right[0].shape[1], FF_TILE):
        yield SECOND_HALF - D + at, right_tile(right, slice(at, at + FF_TILE))


def vector_places():
    for device in range(D // ROW):
        for part in range(4):
            yield (8 + part, device * ROW), (device * 4 + part) * ROW


def residual_kernel(
    place,
    vectors,
    context_arrived,
    l0,
    l1,
    l3,
    both,
    hidden,
    moved,
    normed_out,
    factor_out,
    first_t,
    output_mat,
    settling,
):
    left = (l0, l1, Side(both, 0, l0.shape[1]), l3)
    copies = settle((left, ()), SECOND_PARTS[:1], (output_mat,), settling)
    residual = dot(context_arrived[...], left_tile(left, slice(0, D)))
    residual += hidden[...].astype(jnp.float32) + vectors[2:3, :]
    first_out, normed, factor = normalize(residual, vectors[3:4, :], vectors[4:5, :])
    normed_out[...] = normed
    factor_out[...] = factor
    first16 = first_out.astype(jnp.bfloat16)
    moved[...] = dot(first16, restore_from(place)).astype(jnp.bfloat16)
    first_t[...] = dot_nt(arrange_from(place), first16).astype(jnp.bfloat16)
    for copy in copies:
        copy.wait()


def residual_forward(place, hidden, context_arrived, vectors, pieces):
    tokens, ordered = hidden.shape[0], in_order(pieces)
    return run(
        residual_kernel,
        "residual",
        [(place, "S")]
        + placed_at("V", vectors, context_arrived, *ordered[:4])
        + [(hidden, "H")],
        [
            ((tokens, D), bf16, "V"),
            ((tokens, D), f32, "V"),
            ((tokens, 1), f32, "V"),
            ((D, tokens), bf16, "H"),
            ((D, D), bf16, "A"),
        ],
        1e9,
        [pltpu.SemaphoreType.DMA((4,))],
        total=24,
    )


def feed_kernel(vectors, moved, l0, l1, l3, both, r0, r1, r3, active, active_t, slope, *rest):
    mats, (inner_bias, settling) = rest[:-2], rest[-2:]
    for at, column in vector_places():
        inner_bias[:, column : column + ROW] = vectors[at[0] : at[0] + 1, at[1] : at[1] + ROW]
    left, right = sides(l0, l1, l3, both, r0, r1, r3)
    copies = settle((left, right), SECOND_PARTS[1:], mats, settling)
    for at, tile in second_tiles(left, right):
        columns = slice(at, at + FF_TILE)
        value, derivative = gelu_parts(dot(moved[...], tile) + inner_bias[:, columns])
        value16 = value.astype(jnp.bfloat16)
        active[:, columns] = value16
        active_t[columns, :] = jnp.transpose(value16)
        slope[:, columns] = derivative.astype(jnp.bfloat16)
        active_t.done((columns, slice(None)))
        slope.done((slice(None), columns))
    for copy in copies:
        copy.wait()


def feed_forward(moved, vectors, ff, pieces):
    tokens = moved.shape[0]
    return run(
        feed_kernel,
        "feed_forward",
        placed_at("V", vectors, moved, *in_order(pieces)),
        [((tokens, ff), bf16, "V"), ((ff, tokens), bf16, "H"), ((tokens, ff), bf16, "H")]
        + [((D, width), bf16, "A") for _, _, width in SECOND_PARTS[1:]],
        8e9,
        [pltpu.VMEM((1, ff), f32), pltpu.SemaphoreType.DMA((44,))],
        total=24,
    )


def natural_rows(place, pieces, target, semaphore):
    rows = 4 * ROW
    left, right = pieces[0].shape[1], pieces[4].shape[1]
    near, far, far_core, near_core, right_near, right_far, right_far_core = pieces
    places = [(near, 0, 0, 0, 0), (far, 0, 0, 1, 0), (near_core, 0, 1, 0, 0), (far_core, 0, 1, 1, 0)]
    places += [(right_near, 1, 0, 0, 0), (right_far, 1, 0, 1, 0)]
    places += [(near_core, 1, 1, 0, left), (right_far_core, 1, 1, 1, 0)]
    for piece, is_right, core_off, far_off, start in places:
        half = right if is_right else left
        for near_off in range(2):
            for z_off in range(4):
                x_off, y_off = (far_off, near_off) if is_right else (near_off, far_off)
                block = ((z_off ^ place[3]) * 2 + (x_off ^ place[2])) * 2 + (core_off ^ place[0])
                block = block * 2 + (y_off ^ place[1])
                to = pl.ds(pl.multiple_of(block * rows, rows), rows)
                pltpu.make_async_copy(
                    piece.at[pl.ds((near_off * 4 + z_off) * rows, rows), pl.ds(start, half)],
                    target.at[to, pl.ds(is_right * left, half)],
                    semaphore,
                ).start()
    pltpu.make_async_copy(target, target, semaphore).wait()


def last_kernel(
    place,
    active,
    first_normed,
    vectors,
    l0,
    l1,
    l3,
    both,
    r0,
    r1,
    r3,
    layer_out,
    normed_out,
    factor_out,
    cls_rows,
    outer_mat,
    semaphore,
):
    natural_rows(place, (l0, l1, l3, both, r0, r1, r3), outer_mat, semaphore)
    total = first_normed[...] * vectors[3:4, :] + vectors[4:5, :] + vectors[5:6, :]
    total += dot(active[...], outer_mat[...])
    encoded, normed, factor = normalize(total, vectors[6:7, :], vectors[7:8, :])
    layer_out[...] = encoded.astype(jnp.bfloat16)
    normed_out[...] = normed
    factor_out[...] = factor
    for span in range(encoded.shape[0] // SPAN):
        cls_rows[span : span + 1, :] = encoded[span * SPAN : span * SPAN + 1].astype(jnp.bfloat16)


def last(place, active, first_normed, vectors, pieces):
    tokens, ff = active.shape
    return run(
        last_kernel,
        "last",
        [(place, "S")]
        + placed_at("V", active, first_normed, vectors, *in_order(pieces)),
        [
            ((tokens, D), bf16, "H"),
            ((tokens, D), f32, "V"),
            ((tokens, 1), f32, "V"),
            ((tokens // SPAN, D), bf16, "V"),
            ((ff, D), bf16, "V"),
        ],
        2.5e9,
        [pltpu.SemaphoreType.DMA],
        total=16,
    )


def pick(place, first, second):
    return jnp.where(place == 0, first, second)


def turn_kernel(
    place,
    partner_span,
    cotangent,
    normed,
    factor,
    vectors,
    own_rows,
    other_rows,
    second_grad,
    kept,
    sent,
    sums,
    loss,
):
    spans = own_rows.shape[0]
    own, other = own_rows[...].astype(jnp.float32), other_rows[...].astype(jnp.float32)
    logits = dot_nt(own_rows[...], other_rows[...]) / math.sqrt(D)
    row = lax.broadcasted_iota(jnp.int32, (spans, spans), 0)
    column = lax.broadcasted_iota(jnp.int32, (spans, spans), 1)
    first_place = place[1] == 0
    target = jnp.zeros((spans, spans), jnp.float32)
    for span in range(spans):
        match = partner_span[0, span]
        hit_row = jnp.where(first_place, span, match)
        hit_column = jnp.where(first_place, match, span)
        target += ((row == hit_row) & (column == hit_column)).astype(jnp.float32)
    highest_logit = jnp.max(logits, axis=1, keepdims=True)
    exponent = jnp.exp(logits - highest_logit)
    totals = jnp.sum(exponent, axis=1, keepdims=True)
    losses = highest_logit + jnp.log(totals) - jnp.sum(target * logits, axis=1, keepdims=True)
    loss[...] = jnp.sum(jnp.where(row == column, losses, 0.0), axis=0, keepdims=True)
    soft = exponent / totals - target
    exponent = jnp.exp(logits - jnp.max(logits, axis=0, keepdims=True))
    back = exponent / jnp.sum(exponent, axis=0, keepdims=True) - target
    own_term, back_term = jnp.zeros_like(own), jnp.zeros_like(own)
    for span in range(spans):
        own_term += soft[:, span : span + 1] * other[span : span + 1]
        back_term += back[:, span : span + 1] * other[span : span + 1]
    cls_gradient = own_term + back_term.astype(jnp.bfloat16).astype(jnp.float32)
    start = lax.broadcasted_iota(jnp.int32, (SPAN, 1), 0) == 0
    gain = vectors[6:7, :]
    gain_sum = jnp.zeros((1, D), jnp.float32)
    shift_sum, bias_sum = gain_sum, gain_sum
    for span in range(spans):
        rows = slice(span * SPAN, (span + 1) * SPAN)
        upstream = cotangent[rows, :].astype(jnp.float32)
        upstream += jnp.where(start, cls_gradient[span : span + 1], 0.0)
        grad, gain_part, shift_part = normalize_back(upstream, normed[rows, :], factor[rows, :], gain)
        second_grad[rows, :] = grad
        gain_sum += gain_part[None]
        shift_sum += shift_part[None]
        bias_sum += jnp.sum(grad, axis=0, keepdims=True)
        grad16 = grad.astype(jnp.bfloat16)
        kept[rows, :] = pick(place[0], grad16[:, : D // 2], grad16[:, D // 2 :])
        sent[rows, :] = pick(place[0], grad16[:, D // 2 :], grad16[:, : D // 2])
    sums[0:1, :] = bias_sum
    sums[1:2, :] = gain_sum
    sums[2:3, :] = shift_sum


def turn(place, partner_span, cotangent, normed, factor, vectors, own_rows, other_rows):
    tokens = cotangent.shape[0]
    return run(
        turn_kernel,
        "turn",
        placed_at("S", place, partner_span)
        + [(cotangent, "H")]
        + placed_at("V", normed, factor, vectors, own_rows, other_rows),
        [
            ((tokens, D), f32, "H"),
            ((tokens, D // 2), bf16, "V"),
            ((tokens, D // 2), bf16, "V"),
            ((3, D), f32, "V"),
            ((1, own_rows.shape[0]), f32, "V"),
        ],
        1e8,
    )


def both_halves(place, kept, sent):
    return jnp.concatenate([pick(place, kept, sent), pick(place, sent, kept)], axis=1)


def slope_kernel(place, second_kept, second_sent, outer_mat, slope, kept, sent, sums, second16):
    second16[...] = both_halves(place[0], second_kept[...], second_sent[...])
    slope = slope.ready()
    per_half = kept.shape[1] // D

    def tile(at, carry):
        columns = pl.ds(pl.multiple_of(at * D, D), D)
        inside = pl.ds(pl.multiple_of((at % per_half) * D, D), D)
        grad = dot_nt(second16[...], outer_mat[columns, :]) * slope[:, columns].astype(jnp.float32)
        sums[:, columns] = jnp.sum(grad, axis=0, keepdims=True)
        grad16 = grad.astype(jnp.bfloat16)
        mine = place[0] == at // per_half

        @pl.when(mine)
        def keep():
            kept[:, inside] = grad16

        @pl.when(jnp.logical_not(mine))
        def send():
            sent[:, inside] = grad16

        return carry

    lax.fori_loop(0, 2 * per_half, tile, 0)


def slope_back(place, second_kept, second_sent, outer_mat, slope):
    tokens, ff = slope.shape
    half = ((tokens, ff // 2), bf16, "V")
    return run(
        slope_kernel,
        "slope_back",
        [(place, "S")] + placed_at("V", second_kept, second_sent, outer_mat) + [(slope, "H")],
        [half, half, ((1, ff), f32, "V")],
        2.5e9,
        [pltpu.VMEM((tokens, D), bf16)],
    )


def outer_kernel(place, active_t, other_active_t, kept, received, left_kept, left_sent, right_kept, right_sent):
    rows = 2 * ROW
    active_t, other_active_t = active_t.ready(), other_active_t.ready()

    def chip_rows(chip, carry):
        x_off, z_off = (chip & 1) ^ place[2], (chip >> 1) ^ place[3]
        tile = pl.ds(pl.multiple_of(chip * 8 * rows, 8 * rows), 8 * rows)
        grad = dot(active_t[tile, :], kept[...]) + dot(other_active_t[tile, :], received[...])
        grad = grad.astype(jnp.bfloat16)
        for core in range(2):
            for y_at in range(2):
                start = (core * 2 + y_at) * 2 * rows
                left, right = grad[start : start + rows], grad[start + rows : start + 2 * rows]
                y_off = place[1] ^ y_at
                left_at = (x_off * 4 + z_off) * 2 + core
                right_at = (y_off * 4 + z_off) * 2 + core

                @pl.when(y_off == 0)
                def left_here():
                    left_kept[left_at] = left

                @pl.when(y_off == 1)
                def left_there():
                    left_sent[left_at] = left

                @pl.when(x_off == 0)
                def right_here():
                    right_kept[right_at] = right

                @pl.when(x_off == 1)
                def right_there():
                    right_sent[right_at] = right

        return carry

    lax.fori_loop(0, PLACES, chip_rows, 0)


def outer_gradient(place, active_t, other_active_t, kept, received):
    piece = ((2 * PLACES, 2 * ROW, kept.shape[1]), bf16, "V")
    return run(
        outer_kernel,
        "outer_gradient",
        [(place, "S")] + placed_at("H", active_t, other_active_t) + placed_at("V", kept, received),
        [piece] * 4,
        2.5e9,
    )


def whole_precision(left, right):
    high = left.astype(jnp.bfloat16)
    rest = (left - high.astype(jnp.float32)).astype(jnp.bfloat16)
    return dot_nt(high, right) + dot_nt(rest, right)


def first_kernel(
    place,
    preact_kept,
    preact_sent,
    factor,
    vectors,
    *refs,
):
    output_mat, inner_mats = refs[0], refs[1:7]
    second_grad, normed, residual_grad, kept, sent, context_grad, sums = refs[7:]
    restore = restore_from(place)
    total = jnp.zeros((factor.shape[0], D), jnp.float32)
    half = preact_kept.shape[1]
    for at, tile in zip(range(0, 2 * half, FF_TILE), inner_mats):
        columns = slice(at % half, at % half + FF_TILE)
        kept_part, sent_part = preact_kept[:, columns], preact_sent[:, columns]
        if at >= half:
            kept_part, sent_part = sent_part, kept_part
        total += dot_nt(pick(place[0], kept_part, sent_part), tile[...])
    first_grad = second_grad[...] + whole_precision(total, restore)
    grad, gain_sum, shift_sum = normalize_back(first_grad, normed[...], factor[...], vectors[3:4, :])
    residual_grad[...] = grad
    sums[0:1, :] = jnp.sum(grad, axis=0, keepdims=True)
    sums[1:2, :] = gain_sum[None]
    sums[2:3, :] = shift_sum[None]
    grad16 = grad.astype(jnp.bfloat16)
    kept[...] = pick(place[0], grad16[:, : D // 2], grad16[:, D // 2 :])
    sent[...] = pick(place[0], grad16[:, D // 2 :], grad16[:, : D // 2])
    moved = dot_nt(grad16, output_mat[...]).astype(jnp.bfloat16)
    context_grad[...] = dot_nt(moved, restore).astype(jnp.bfloat16)


def first_back(place, preact_kept, preact_sent, second_grad, normed, factor, vectors, mats):
    tokens = second_grad.shape[0]
    half = ((tokens, D // 2), bf16, "V")
    return run(
        first_kernel,
        "first_back",
        [(place, "S")]
        + placed_at("V", preact_kept, preact_sent, factor, vectors)
        + placed_at("H", *mats, second_grad, normed),
        [((tokens, D), f32, "H"), half, half, ((tokens, D), bf16, "V"), ((3, D), f32, "V")],
        4.9e9,
    )


def part_rows(grad, left_kept, left_sent, right_kept, right_sent, is_left):
    quarter = D // 4
    if is_left:
        left_kept[...] = grad[: 2 * quarter]
        left_sent[...] = grad[2 * quarter :]
    else:
        right_kept[:quarter, :] = grad[:quarter]
        right_sent[:quarter, :] = grad[quarter : 2 * quarter]
        right_kept[quarter:, :] = grad[2 * quarter : 3 * quarter]
        right_sent[quarter:, :] = grad[3 * quarter :]


def inner_kernel(first_t, other_first_t, kept, received, left_kept, left_sent, right_kept, right_sent):
    for is_left in (True, False):
        columns = slice(0, D) if is_left else slice(D, 2 * D)
        grad = dot(first_t[...], kept[:, columns]) + dot(other_first_t[...], received[:, columns])
        part_rows(grad.astype(jnp.bfloat16), left_kept, left_sent, right_kept, right_sent, is_left)


def inner_gradient(first_t, other_first_t, kept, received):
    piece = ((D // 2, kept.shape[1] // 2), bf16, "V")
    return run(
        inner_kernel,
        "inner_gradient",
        placed_at("H", first_t, other_first_t) + placed_at("V", kept, received),
        [piece] * 4,
        2.5e9,
    )


def attend_kernel(
    place,
    context_grad,
    left_rows,
    right_rows,
    attention_in,
    first_sums,
    second_sums,
    inner_sums,
    kept,
    sent,
    sums,
    grads,
):
    tokens = context_grad.shape[0]
    low = lax.broadcasted_iota(jnp.int32, (SPAN, 128), 1) < HEAD_DIM
    scale = HEAD_DIM ** (-0.5)
    left_rows, right_rows, attention_in = [ref.ready() for ref in (left_rows, right_rows, attention_in)]

    def attend(span, carry):
        rows = pl.ds(pl.multiple_of(span * SPAN, SPAN), SPAN)
        for at in range(0, D, 128):
            query = left_rows[rows, at : at + 128]
            keys = head_pair(key_columns(left_rows, right_rows, rows, at), low)
            values = head_pair(right_rows[rows, 512 + at : 640 + at], low)
            upstream = context_grad[rows, at : at + 128]
            attention16 = attention_in[rows, 2 * at : 2 * at + 256]
            attention_grad = dot_nt(upstream, values)
            parts = []
            for head in range(2):
                columns = slice(head * SPAN, (head + 1) * SPAN)
                attention = attention16[:, columns].astype(jnp.float32)
                part = attention_grad[:, columns]
                weighted = jnp.sum(attention * part, axis=-1, keepdims=True)
                parts.append((attention * (part - weighted)).astype(jnp.bfloat16))
            scores_grad = jnp.concatenate(parts, axis=1)
            grads[0, rows, at : at + 128] = (dot(scores_grad, keys) * scale).astype(jnp.bfloat16)
            both = dot_tn(scores_grad, query)
            both = jnp.where(low, both[:SPAN], both[SPAN:])
            grads[1, rows, at : at + 128] = (both * scale).astype(jnp.bfloat16)
            both = dot_tn(attention16, upstream)
            both = jnp.where(low, both[:SPAN], both[SPAN:])
            grads[2, rows, at : at + 128] = both.astype(jnp.bfloat16)
        return carry

    lax.fori_loop(0, tokens // SPAN, attend, 0)
    query_grad, key_grad, value_grad = grads[0], grads[1], grads[2]
    half = D // 2
    for at, grad in enumerate((query_grad, key_grad, value_grad)):
        columns = slice(at * half, (at + 1) * half)
        kept[:, columns] = pick(place[0], grad[:, :half], grad[:, half:])
        sent[:, columns] = pick(place[0], grad[:, half:], grad[:, :half])
    sums[0:1, :] = jnp.sum(query_grad.astype(jnp.float32), axis=0, keepdims=True)
    sums[1:2, :] = jnp.sum(value_grad.astype(jnp.float32), axis=0, keepdims=True)
    sums[2:5, :] = first_sums[...]
    sums[5:8, :] = second_sums[...]
    for at, column in vector_places():
        sums[at[0] : at[0] + 1, at[1] : at[1] + ROW] = inner_sums[:, column : column + ROW]
    sums[12:16, :] = jnp.zeros((4, D), jnp.float32)


def attend_back(place, context_grad, left_rows, right_rows, attention, first_sums, second_sums, inner_sums):
    tokens = context_grad.shape[0]
    part = ((tokens, 3 * D // 2), bf16, "V")
    return run(
        attend_kernel,
        "attend_back",
        placed_at("S", place)
        + placed_at("V", context_grad)
        + placed_at("H", left_rows, right_rows, attention)
        + placed_at("V", first_sums, second_sums, inner_sums),
        [part, part, ((16, D), f32, "V")],
        4e9,
        [pltpu.VMEM((3, tokens, D), bf16)],
    )


def attention_gradient_kernel(
    place,
    sums,
    other_sums,
    hidden_t,
    other_hidden_t,
    context_t,
    other_context_t,
    grads,
    other_grads,
    residual,
    other_residual,
    left_kept,
    left_sent,
    right_kept,
    right_sent,
):
    half = D // 2
    grad = dot(hidden_t[...], grads[:, :D]) + dot(other_hidden_t[...], other_grads[:, :D])
    grad = grad.astype(jnp.bfloat16)
    left_kept[:, :D] = grad[:half]
    left_sent[:, :D] = grad[half:]
    total = (sums[...] + other_sums[...]).astype(jnp.bfloat16)
    total = jnp.concatenate([total, jnp.zeros((112, D), jnp.bfloat16)])
    small = dot_nt(arrange_from(place), total).astype(jnp.bfloat16)
    left_kept[:, D:] = small[:half]
    left_sent[:, D:] = small[half:]
    value = dot(hidden_t[...], grads[:, D:]) + dot(other_hidden_t[...], other_grads[:, D:])
    output = dot(context_t[...], residual[...]) + dot(other_context_t[...], other_residual[...])
    grad = jnp.concatenate([value, output], axis=1).astype(jnp.bfloat16)
    part_rows(grad, left_kept, left_sent, right_kept, right_sent, False)


def attention_gradient(*operands):
    left, right = ((D // 2, D + 128), bf16, "V"), ((D // 2, D), bf16, "V")
    places = ["S"] + ["V"] * 2 + ["H"] * 4 + ["V"] * 4
    return run(
        attention_gradient_kernel,
        "attention_gradient",
        list(zip(operands, places)),
        [left, left, right, right],
        2.5e9,
    )


def input_kernel(
    place, kept, sent, query_mat, low_key_mat, high_key_mat, value_mat, residual_grad, input_grad
):
    restore = restore_from(place)
    half = D // 2
    parts = []
    for at in range(3):
        columns = slice(at * half, (at + 1) * half)
        parts.append(both_halves(place[0], kept[:, columns], sent[:, columns]))
    query_grad, key_grad, value_grad = parts
    total = dot_nt(query_grad, query_mat[...])
    total += dot_nt(key_grad[:, :512], low_key_mat[...])
    total += dot_nt(key_grad[:, 512:], high_key_mat[...])
    total += dot_nt(value_grad, value_mat[...])
    total = residual_grad[...] + whole_precision(total, restore)
    input_grad[...] = total.astype(jnp.bfloat16)


def input_back(place, residual_grad, kept, sent, mats):
    return run(
        input_kernel,
        "input_back",
        [(place, "S")]
        + placed_at("V", kept, sent)
        + placed_at("H", *mats, residual_grad),
        [(residual_grad.shape, bf16, "H")],
        3e9,
    )[0]


def add_kernel(left, left_in, right, right_in, left_kept, left_sent, right_kept, right_sent):
    for own, received, kept, sent in (
        (left, left_in, left_kept, left_sent),
        (right, right_in, right_kept, right_sent),
    ):
        total = (own[...].astype(jnp.float32) + received[...].astype(jnp.float32)).astype(jnp.bfloat16)
        half = total.shape[0] // 2
        kept[...] = total[:half]
        sent[...] = total[half:]


def add_parts(left, left_in, right, right_in):
    shapes = [(part.shape[0] // 2,) + part.shape[1:] for part in (left, left, right, right)]
    return pl.pallas_call(
        add_kernel,
        in_specs=[VMEM] * 4,
        out_specs=[VMEM] * 4,
        out_shape=[jax.ShapeDtypeStruct(shape, jnp.bfloat16) for shape in shapes],
        compiler_params=params(),
        cost_estimate=cost(1, 1),
        name="add_parts",
    )(left, left_in, right, right_in)


def add_z_kernel(left, left_in, right, right_in, own, first, second, third):
    width = left.shape[-1]
    for part, received, columns in (
        (left, left_in, slice(0, width)),
        (right, right_in, slice(width, width + right.shape[-1])),
    ):
        rows = part.shape[0] // 4
        total = part[...].astype(jnp.float32) + received[...].astype(jnp.float32)
        own[..., columns] = total[:rows]
        for at, sent in enumerate((first, second, third)):
            sent[..., columns] = total[(at + 1) * rows : (at + 2) * rows].astype(jnp.bfloat16)


def add_z(left, left_in, right, right_in):
    shape = (left.shape[0] // 4,) + left.shape[1:-1] + (left.shape[-1] + right.shape[-1],)
    return pl.pallas_call(
        add_z_kernel,
        in_specs=[VMEM] * 4,
        out_specs=[VMEM] * 4,
        out_shape=[jax.ShapeDtypeStruct(shape, jnp.float32)]
        + [jax.ShapeDtypeStruct(shape, jnp.bfloat16)] * 3,
        compiler_params=params(),
        cost_estimate=cost(1, 1),
        name="add_z",
    )(left, left_in, right, right_in)


def add_join_kernel(left, left_in, right, right_in, kept, sent):
    width = left.shape[-1]
    for part, received, columns in (
        (left, left_in, slice(0, width)),
        (right, right_in, slice(width, width + right.shape[-1])),
    ):
        rows = part.shape[0] // 2
        total = part[...].astype(jnp.float32) + received[...].astype(jnp.float32)
        kept[..., columns] = total[:rows]
        sent[..., columns] = total[rows:].astype(jnp.bfloat16)


def add_join(left, left_in, right, right_in):
    shape = (left.shape[0] // 2,) + left.shape[1:-1] + (left.shape[-1] + right.shape[-1],)
    return pl.pallas_call(
        add_join_kernel,
        in_specs=[VMEM] * 4,
        out_specs=[VMEM] * 2,
        out_shape=[jax.ShapeDtypeStruct(shape, jnp.float32), jax.ShapeDtypeStruct(shape, jnp.bfloat16)],
        compiler_params=params(),
        cost_estimate=cost(1, 1),
        name="add_join",
    )(left, left_in, right, right_in)


def add_half_kernel(own, received, kept, sent):
    rows = own.shape[0] // 2
    total = own[...] + received[...].astype(jnp.float32)
    kept[...] = total[:rows]
    sent[...] = total[rows:].astype(jnp.bfloat16)


def add_half(own, received):
    shape = (own.shape[0] // 2,) + own.shape[1:]
    return pl.pallas_call(
        add_half_kernel,
        in_specs=[VMEM] * 2,
        out_specs=[VMEM] * 2,
        out_shape=[jax.ShapeDtypeStruct(shape, jnp.float32), jax.ShapeDtypeStruct(shape, jnp.bfloat16)],
        compiler_params=params(),
        cost_estimate=cost(1, 1),
        name="add_half",
    )(own, received)


def finish_kernel(place, own, *refs):
    received_all, (mine, other) = refs[:-2], refs[-2:]
    total = own[...]
    for received in received_all:
        total = total + received[...].astype(jnp.float32)
    if len(total.shape) == 3:
        low, high = total[0], total[1]
    else:
        low, high = total[:ROW], total[ROW:]
    mine[...] = pick(place[0], low, high)
    other[...] = pick(place[0], high, low)


def finish(place, own, received):
    rows = own.shape[1] if own.ndim == 3 else ROW
    return pl.pallas_call(
        finish_kernel,
        in_specs=[SMEM] + [VMEM] * (1 + len(received)),
        out_specs=[VMEM] * 2,
        out_shape=[jax.ShapeDtypeStruct((rows, own.shape[-1]), jnp.float32)] * 2,
        compiler_params=params(),
        cost_estimate=cost(1, 1),
        name="finish",
    )(place, own, *received)


def put(place, out, mine, received):
    half = mine.shape[1]
    out[:, :half] = pick(place[0], mine, received)
    out[:, half:] = pick(place[0], received, mine)


def outer_out_kernel(place, mine, received, out):
    rows, half = mine.shape[0], mine.shape[1] // 2
    for at in range(2):
        columns = slice(at * half, (at + 1) * half)
        put(place, out.at[at * rows : (at + 1) * rows], mine[:, columns], received[:, columns])


def inner_out_kernel(place, mine, received, out):
    put(place, out, mine[...], received[...])


def rest_out_kernel(place, mine, received, query, key, value, output, inner_bias, *vectors):
    half = D // 2
    for out, at in ((query, 0), (key, half), (value, D + 128), (output, D + 128 + half)):
        columns = slice(at, at + half)
        put(place, out, mine[:, columns], received[:, columns])
    turned = jnp.transpose(mine[:, D : D + 128])
    for at, out in enumerate(vectors):
        out[...] = turned[at : at + 1]
    for at in range(4):
        inner_bias[:, at * ROW : (at + 1) * ROW] = turned[8 + at : 9 + at]


def placed(kernel, name, place, mine, received, shapes):
    return pl.pallas_call(
        kernel,
        in_specs=[SMEM, VMEM, VMEM],
        out_specs=[VMEM] * len(shapes),
        out_shape=[jax.ShapeDtypeStruct(shape, jnp.float32) for shape in shapes],
        compiler_params=params(),
        cost_estimate=cost(1, 1),
        name=name,
    )(place, mine, received)


def first_transfers(pieces):
    return [mate(pieces[1]), across(pieces[3], 2)]


def add_first(pieces, received):
    return add_parts(pieces[0], received[0], pieces[2], received[1])


def second_transfers(pieces):
    return [across(pieces[1], 2), mate(pieces[3])]


def add_joined(pieces, received):
    return add_join(pieces[0], received[0], pieces[2], received[1])


def add_second(pieces, received):
    return add_z(pieces[0], received[0], pieces[2], received[1])


def third_transfers(parts):
    return [across(sent, mask) for sent, mask in zip(parts[1:], (4, 8, 12))]


def fast_device(
    hidden_in,
    cotangent,
    span_lengths,
    partner_span,
    query_weight,
    query_bias,
    key_weight,
    value_weight,
    value_bias,
    output_weight,
    output_bias,
    first_gain,
    first_shift,
    inner_weight,
    inner_bias,
    outer_weight,
    outer_bias,
    second_gain,
    second_shift,
):
    core, x_at, z_at, y_at = coordinates()
    place = jnp.stack([core, y_at, x_at, z_at]).astype(jnp.int32)
    first_block, second_block = pack(
        query_weight,
        key_weight,
        value_weight,
        output_weight,
        inner_weight,
        inner_bias,
        (
            query_bias,
            value_bias,
            output_bias,
            first_gain,
            first_shift,
            outer_bias,
            second_gain,
            second_shift,
        ),
    )
    ff = inner_weight.shape[1]
    first_z = z_exchange(first_block)
    second_z = across(second_block, 4)
    first_z = tied(first_z, second_z)
    first = stack_z(first_block, first_z, FIRST_HALF)
    second = stack_two(after(second_block, *first), second_z, SECOND_HALF)
    first, third_block = tied(first, *second), after(outer_weight, *second)
    first_in = near_exchange(first)
    second_left_z = across(second[0], 8)
    *first, first_both = stack_near(first, tied(first_in, second_left_z))
    second_right = after(second[1], *first)
    first_far = far_exchange(first)
    second_right_z = across(second_right, 8)
    first_core = across(first_both, 1)
    second = stack_pair(
        second[0], second_left_z, second_right, after(second_right_z, first_core, *first_far)
    )[:2]
    first_far, third_block = tied(first_far, *second), after(third_block, *second)
    second_in = near_exchange(second)
    first_far_core = core_exchange(first_far)
    third_z = across(after(third_block, *first_far_core), 4)
    third_two = stack_z_two(third_block, third_z)
    left_rows, right_rows, vectors, hidden_t, *first_mats = project(
        place, hidden_in, pieces_of(first, first_far, first_core, first_far_core)
    )
    *second, second_both = stack_near(second, tied(second_in, vectors, third_two))
    third_two, left_rows = tied((third_two, left_rows), *second)
    second_far = far_exchange(second)
    third_z = across(third_two, 8)
    second_core = across(second_both, 1)
    attention, context_arrived, context_t = attention_forward(
        place, span_lengths, left_rows, right_rows
    )
    third = stack_z(third_two, tied([third_z], context_arrived, second_core, *second_far), D // 2)
    second_far = tied(second_far, *third)
    third_in = near_exchange(third)
    second_far_core = core_exchange(second_far)
    second_pieces = pieces_of(second, second_far, second_core, second_far_core)
    moved, first_normed, first_factor, first_t, output_mat = residual_forward(
        place, hidden_in, context_arrived, vectors, second_pieces
    )
    *third, third_both = stack_near(third, tied(third_in, moved, *second_far_core))
    moved = after(moved, *third)
    third_far = far_exchange(third)
    third_core = across(third_both, 1)
    active, active_t, slope, *inner_mats = feed_forward(moved, vectors, ff, second_pieces)
    second_mats = [output_mat, *inner_mats]
    third_far = tied(third_far, active, third_core)
    third_far_core = core_exchange(third_far)
    third_pieces = pieces_of(third, third_far, third_core, third_far_core)
    hidden_t, context_t, first_t, active_t, active = tied(
        (hidden_t, context_t, first_t, active_t, active), *third_far_core
    )
    other_active_t, other_first_t = across(active_t, 1), across(first_t, 1)
    other_hidden_t, other_context_t = across(hidden_t, 1), across(context_t, 1)
    layer_out, second_normed, second_factor, cls_rows, outer_mat = last(
        place, active, first_normed, vectors, third_pieces
    )
    other_rows = mate(cls_rows)
    second_grad, second_kept, second_sent, second_sums, span_loss = turn(
        place, partner_span, cotangent, second_normed, second_factor, vectors, cls_rows, other_rows
    )
    second_received = across(second_sent, 1)
    preact_kept, preact_sent, inner_sums = slope_back(
        place, second_kept, second_sent, outer_mat, slope
    )
    second_received = after(second_received, preact_kept)
    outer_parts = outer_gradient(place, active_t, other_active_t, second_kept, second_received)
    preact_kept, preact_sent = tied((preact_kept, preact_sent), *outer_parts)
    outer_in = first_transfers(outer_parts)
    preact_received = across(preact_sent, 1)
    residual_grad, residual_kept, residual_sent, context_grad, first_sums = first_back(
        place,
        preact_kept,
        preact_sent,
        second_grad,
        first_normed,
        first_factor,
        vectors,
        second_mats,
    )
    outer_parts = add_first(outer_parts, tied(outer_in, context_grad, preact_received))
    residual_sent, preact_kept = tied((residual_sent, preact_kept), *outer_parts)
    outer_in = second_transfers(outer_parts)
    residual_received = across(residual_sent, 1)
    inner_parts = inner_gradient(first_t, other_first_t, preact_kept, preact_received)
    outer_own, outer_sent = add_joined(
        outer_parts, tied(outer_in, residual_received, *inner_parts)
    )
    inner_parts = tied(inner_parts, outer_own)
    context_grad = after(context_grad, *inner_parts)
    inner_in = first_transfers(inner_parts)
    outer_in = across(outer_sent, 8)
    grads_kept, grads_sent, sums = attend_back(
        place,
        context_grad,
        left_rows,
        right_rows,
        attention,
        first_sums,
        second_sums,
        inner_sums,
    )
    inner_parts = add_first(inner_parts, tied(inner_in, sums, outer_in))
    outer_own, outer_in = tied((outer_own, outer_in), *inner_parts)
    grads_sent, sums = tied((grads_sent, sums), *inner_parts)
    inner_in = second_transfers(inner_parts)
    grads_received, other_sums = across(grads_sent, 1), across(sums, 1)
    outer_own, outer_sent = add_half(outer_own, outer_in)
    grads_received = after(grads_received, outer_own)
    rest_parts = attention_gradient(
        place,
        sums,
        other_sums,
        hidden_t,
        other_hidden_t,
        context_t,
        other_context_t,
        grads_kept,
        grads_received,
        residual_kept,
        residual_received,
    )
    inner_own, inner_sent = add_joined(inner_parts, tied(inner_in, *rest_parts))
    rest_parts = tied(rest_parts, inner_own)
    outer_sent, grads_kept = tied((outer_sent, grads_kept), inner_own)
    rest_in = first_transfers(rest_parts)
    inner_in = across(inner_sent, 8)
    outer_in = across(outer_sent, 4)
    input_grad = input_back(place, residual_grad, grads_kept, grads_sent, first_mats)
    rest_parts = add_first(rest_parts, tied(rest_in, input_grad, outer_in, inner_in))
    inner_own, inner_in, outer_own, outer_in = tied(
        (inner_own, inner_in, outer_own, outer_in), *rest_parts
    )
    rest_in = second_transfers(rest_parts)
    inner_own, inner_sent = add_half(inner_own, inner_in)
    inner_in = across(inner_sent, 4)
    outer_mine, outer_other = finish(place, outer_own, [outer_in])
    outer_other = across(outer_other, 1)
    rest_parts = add_second(rest_parts, tied(rest_in, inner_in, outer_other))
    inner_in, outer_other = tied((inner_in, outer_other), *rest_parts)
    rest_in = third_transfers(rest_parts)
    inner_mine, inner_other = finish(place, inner_own, [inner_in])
    inner_other = across(inner_other, 1)
    (outer_grad,) = placed(
        outer_out_kernel, "outer_out", place, outer_mine, outer_other, [(4 * ROW, D)]
    )
    (inner_grad,) = placed(
        inner_out_kernel, "inner_out", place, inner_mine, after(inner_other, outer_grad), [(ROW, ff)]
    )
    rest_mine, rest_other = finish(place, rest_parts[0], tied(rest_in, inner_grad))
    rest_other = across(rest_other, 1)
    query_grad, key_grad, value_grad, output_grad, inner_bias_grad, *vector_grads = placed(
        rest_out_kernel,
        "rest_out",
        place,
        rest_mine,
        rest_other,
        [(ROW, D)] * 4 + [(1, 4 * ROW)] + [(1, ROW)] * 8,
    )
    vector_grads = [grad.reshape(-1) for grad in vector_grads]
    return (
        layer_out,
        input_grad,
        span_loss.reshape(-1),
        query_grad,
        vector_grads[0],
        key_grad,
        value_grad,
        vector_grads[1],
        output_grad,
        vector_grads[2],
        vector_grads[3],
        vector_grads[4],
        inner_grad,
        inner_bias_grad.reshape(-1),
        outer_grad,
        vector_grads[5],
        vector_grads[6],
        vector_grads[7],
    )


def solution(mesh):
    is_block = mesh.shape["doc"] == 2 * PLACES and mesh.shape["pair"] == 2
    return jax.shard_map(
        fast_device if is_block else per_device,
        mesh=mesh,
        in_specs=(
            P(("doc", "pair"), None),
            P(("doc", "pair"), None),
            P(("doc", "pair")),
            P("doc", None),
            P(("doc", "pair"), None),
            P(("doc", "pair")),
            P(("doc", "pair"), None),
            P(("doc", "pair"), None),
            P(("doc", "pair")),
            P(("doc", "pair"), None),
            P(("doc", "pair")),
            P(("doc", "pair")),
            P(("doc", "pair")),
            P(("doc", "pair"), None),
            P(("doc", "pair")),
            P(("doc", "pair"), None),
            P(("doc", "pair")),
            P(("doc", "pair")),
            P(("doc", "pair")),
        ),
        out_specs=(
            P(("doc", "pair"), None),
            P(("doc", "pair"), None),
            P(("doc", "pair")),
            P(("doc", "pair"), None),
            P(("doc", "pair")),
            P(("doc", "pair"), None),
            P(("doc", "pair"), None),
            P(("doc", "pair")),
            P(("doc", "pair"), None),
            P(("doc", "pair")),
            P(("doc", "pair")),
            P(("doc", "pair")),
            P(("doc", "pair"), None),
            P(("doc", "pair")),
            P(("doc", "pair"), None),
            P(("doc", "pair")),
            P(("doc", "pair")),
            P(("doc", "pair")),
        ),
        check_vma=False,
    )
```

```python
from functools import partial
import math

import jax
import jax.numpy as jnp
from jax import lax
from jax.experimental import pallas as pl
from jax.experimental.pallas import tpu as pltpu
from jax.sharding import PartitionSpec as P

D = 768
HEAD_DIM = 64
SPAN = 128
SPANS_ROW = 4


epsilon = 1e-06
masked_out = -1000000000.0
highest = lax.Precision.HIGHEST


def across(block, mask):
    count = lax.axis_size("doc")
    return lax.ppermute(block, "doc", [(at, at ^ mask) for at in range(count)])


def mate(block):
    return lax.ppermute(block, "pair", [(0, 1), (1, 0)])


def far_groups():
    bits = lax.axis_size("doc").bit_length() - 1
    far = [1 << at for at in range(2, bits)]
    return [far[at : at + 2] for at in range(0, len(far), 2)]


def is_upper(mask):
    return (lax.axis_index("doc") & mask) != 0


def joined(own, other, upper):
    return jnp.where(upper, jnp.stack([other, own]), jnp.stack([own, other]))


def gather_rows(block):
    rows, columns = block.shape
    total = block[None]
    for masks in far_groups():
        low = masks[0]
        near = joined(total, across(total, low), is_upper(low))
        if len(masks) == 2:
            high = masks[1]
            straight, crossed = across(total, high), across(total, high | low)
            far = joined(straight, crossed, is_upper(low))
            near = joined(near, far, is_upper(high)).reshape((4,) + total.shape)
        total = near.reshape((-1, rows, columns))
    half = columns // 2
    left, right = total[..., :half], total[..., half:]
    on_pair = lax.axis_index("pair") == 1
    left_x, right_y = across(left, 2), mate(right)
    left, right = joined(left, left_x, is_upper(2)), joined(right, right_y, on_pair)
    left_y, right_x = mate(left), across(right, 2)
    left, right = joined(left, left_y, on_pair), joined(right, right_x, is_upper(2))
    left = joined(left, across(left, 1), is_upper(1))
    right = joined(right, across(right, 1), is_upper(1))
    left = jnp.transpose(left, (3, 2, 0, 1, 4, 5))
    right = jnp.transpose(right, (3, 1, 0, 2, 4, 5))
    return jnp.concatenate([left, right], axis=-1).reshape(-1, rows, columns)


def halves(blocks, axis, upper):
    lower = lax.index_in_dim(blocks, 0, axis, keepdims=False)
    higher = lax.index_in_dim(blocks, 1, axis, keepdims=False)
    return (jnp.where(upper, higher, lower), jnp.where(upper, lower, higher))


def plus(kept, received):
    return kept.astype(jnp.float32) + received.astype(jnp.float32)


def scatter_rows(blocks):
    rows, columns = blocks.shape[1:]
    on_pair = lax.axis_index("pair") == 1
    blocks = blocks.astype(jnp.bfloat16).reshape(-1, 2, 2, 2, rows, columns)
    kept, sent = halves(blocks, 2, is_upper(1))
    total = plus(kept, across(sent, 1)).astype(jnp.bfloat16)
    half = columns // 2
    left, right = total[..., :half], total[..., half:]
    left_kept, left_sent = halves(left, 2, on_pair)
    right_kept, right_sent = halves(right, 1, is_upper(2))
    left = plus(left_kept, mate(left_sent)).astype(jnp.bfloat16)
    right = plus(right_kept, across(right_sent, 2)).astype(jnp.bfloat16)
    left_kept, left_sent = halves(left, 1, is_upper(2))
    right_kept, right_sent = halves(right, 1, on_pair)
    left = plus(left_kept, across(left_sent, 2))
    right = plus(right_kept, mate(right_sent))
    total = jnp.concatenate([left, right], axis=-1)
    for masks in far_groups()[::-1]:
        total = total.astype(jnp.bfloat16).reshape(2 ** len(masks), -1, rows, columns)
        place = (lax.axis_index("doc") // masks[0]) % 2 ** len(masks)
        summed = lax.dynamic_index_in_dim(total, place, 0, keepdims=False).astype(jnp.float32)
        for step in range(1, 2 ** len(masks)):
            sent = lax.dynamic_index_in_dim(total, place ^ step, 0, keepdims=False)
            summed = plus(summed, across(sent, masks[0] * step))
        total = summed
    return total.reshape(rows, columns)


VECTORS = (1, 4, 6, 7, 8, 10, 12, 13, 14)


def pack_vectors(pieces):
    flat = jnp.concatenate(pieces, axis=-1)
    width = -(-flat.shape[-1] // D) * D
    flat = jnp.pad(flat, [(0, 0)] * (flat.ndim - 1) + [(0, width - flat.shape[-1])])
    return flat.reshape(flat.shape[:-1] + (-1, D))


def fold(matrix):
    return jnp.concatenate([matrix[:, at : at + D] for at in range(0, matrix.shape[1], D)])


def collect(shards):
    rows = shards[0].shape[0]
    devices = lax.axis_size("doc") * lax.axis_size("pair")
    small = pack_vectors([shards[at] for at in VECTORS])
    first = gather_rows(jnp.concatenate([shards[0], shards[2], shards[3], small]))
    second = gather_rows(jnp.concatenate([shards[5], fold(shards[9])]))
    outer = lax.all_gather(shards[11], ("doc", "pair"), axis=0, tiled=True)
    whole = {
        0: first[:, :rows].reshape(-1, D),
        2: first[:, rows : 2 * rows].reshape(-1, D),
        3: first[:, 2 * rows : 3 * rows].reshape(-1, D),
        5: second[:, :rows].reshape(-1, D),
        9: jnp.concatenate(
            [
                second[:, at : at + rows].reshape(-1, D)
                for at in range(rows, second.shape[1], rows)
            ],
            axis=1,
        ),
        11: outer,
    }
    vectors, start = first[:, 3 * rows :].reshape(devices, -1), 0
    for at in VECTORS:
        size = shards[at].shape[0]
        whole[at] = vectors[:, start : start + size].reshape(-1).astype(jnp.float32)
        start += size
    return tuple(whole[at] for at in range(15))


def spread(gradients):
    devices = lax.axis_size("doc") * lax.axis_size("pair")
    by_device = [
        piece.reshape((devices, -1) + piece.shape[1:]) for piece in gradients
    ]
    rows = by_device[0].shape[1]
    outer = scatter_rows(by_device[11])
    inner = by_device[9]
    parts = [inner[..., at : at + D] for at in range(0, inner.shape[-1], D)]
    second = scatter_rows(jnp.concatenate([by_device[5]] + parts, axis=1))
    small = pack_vectors([by_device[at] for at in VECTORS])
    first = scatter_rows(
        jnp.concatenate([by_device[0], by_device[2], by_device[3], small], axis=1)
    )
    own = {
        0: first[:rows],
        2: first[rows : 2 * rows],
        3: first[2 * rows : 3 * rows],
        5: second[:rows],
        9: jnp.concatenate(
            [second[at : at + rows] for at in range(rows, second.shape[0], rows)], axis=1
        ),
        11: outer,
    }
    vectors, start = first[3 * rows :].reshape(-1), 0
    for at in VECTORS:
        size = by_device[at].shape[1]
        own[at] = vectors[start : start + size]
        start += size
    return tuple(own[at] for at in range(15))


def normalize(hidden, gain, shift):
    average = jnp.mean(hidden, axis=-1, keepdims=True)
    centred = hidden - average
    factor = lax.rsqrt(jnp.mean(centred * centred, axis=-1, keepdims=True) + epsilon)
    normed = centred * factor
    return (normed * gain + shift, normed, factor)


def normalize_back(upstream, normed, factor, gain):
    scaled = upstream * gain
    hidden_grad = factor * (
        scaled
        - jnp.mean(scaled, axis=-1, keepdims=True)
        - normed * jnp.mean(scaled * normed, axis=-1, keepdims=True)
    )
    return (hidden_grad, jnp.sum(upstream * normed, axis=0), jnp.sum(upstream, axis=0))


def head_scores(query_row, key_row, live_row):
    product = jnp.einsum("sqhd,skhd->shqk", query_row, key_row, preferred_element_type=jnp.float32)
    return jnp.where(live_row[:, None, None, :], product * HEAD_DIM ** (-0.5), masked_out)


def encode(hidden_in, allowed, gathered):
    (
        query_mat,
        query_add,
        key_mat,
        value_mat,
        value_add,
        output_mat,
        output_add,
        gain_one,
        shift_one,
        inner_mat,
        inner_add,
        outer_mat,
        outer_add,
        gain_two,
        shift_two,
    ) = gathered
    row_count = allowed.shape[0]
    shaped = (row_count, SPANS_ROW, SPAN, D // HEAD_DIM, HEAD_DIM)
    queries = (
        jnp.dot(hidden_in, query_mat, preferred_element_type=jnp.float32) + query_add
    ).astype(jnp.bfloat16)
    key_rows = jnp.dot(hidden_in, key_mat, preferred_element_type=jnp.float32).astype(jnp.bfloat16)
    value_rows = (
        jnp.dot(hidden_in, value_mat, preferred_element_type=jnp.float32) + value_add
    ).astype(jnp.bfloat16)

    def attend(element):
        query_row, key_row, value_row, live_row = element
        scores = head_scores(query_row, key_row, live_row)
        highest_score = jnp.max(scores, axis=-1, keepdims=True)
        exponent = jnp.exp(scores - highest_score)
        totals = jnp.sum(exponent, axis=-1, keepdims=True)
        attention = (exponent / totals).astype(jnp.bfloat16)
        context_row = jnp.einsum(
            "shqk,skhd->sqhd", attention, value_row, preferred_element_type=jnp.float32
        )
        return (context_row.astype(jnp.bfloat16), (highest_score + jnp.log(totals))[..., 0])

    context, logsum = lax.map(
        attend,
        (queries.reshape(shaped), key_rows.reshape(shaped), value_rows.reshape(shaped), allowed),
    )
    context = context.reshape(-1, D)
    residual = (
        hidden_in.astype(jnp.float32)
        + jnp.dot(context, output_mat, preferred_element_type=jnp.float32)
        + output_add
    )
    first_out, first_normed, first_factor = normalize(residual, gain_one, shift_one)
    first16 = first_out.astype(jnp.bfloat16)
    preact = jnp.dot(first16, inner_mat, preferred_element_type=jnp.float32) + inner_add
    active = jax.nn.gelu(preact, approximate=False).astype(jnp.bfloat16)
    second = first_out + jnp.dot(active, outer_mat, preferred_element_type=jnp.float32) + outer_add
    encoded, second_normed, second_factor = normalize(second, gain_two, shift_two)
    stored = (
        queries,
        key_rows,
        value_rows,
        logsum,
        context,
        first_normed,
        first_factor,
        first16,
        preact,
        active,
        second_normed,
        second_factor,
    )
    return (encoded, stored)


def backward(hidden_in, allowed, gathered, stored, out_gradient):
    (
        query_mat,
        query_add,
        key_mat,
        value_mat,
        value_add,
        output_mat,
        output_add,
        gain_one,
        shift_one,
        inner_mat,
        inner_add,
        outer_mat,
        outer_add,
        gain_two,
        shift_two,
    ) = gathered
    (
        queries,
        key_rows,
        value_rows,
        logsum,
        context,
        first_normed,
        first_factor,
        first16,
        preact,
        active,
        second_normed,
        second_factor,
    ) = stored
    row_count = allowed.shape[0]
    shaped = (row_count, SPANS_ROW, SPAN, D // HEAD_DIM, HEAD_DIM)
    second_grad, gain_two_grad, shift_two_grad = normalize_back(
        out_gradient, second_normed, second_factor, gain_two
    )
    outer_add_grad = jnp.sum(second_grad, axis=0)
    second16 = second_grad.astype(jnp.bfloat16)
    outer_mat_grad = jnp.dot(active.T, second16, preferred_element_type=jnp.float32)
    active_grad = jnp.dot(second16, outer_mat.T, preferred_element_type=jnp.float32)
    unused, gelu_back = jax.vjp(partial(jax.nn.gelu, approximate=False), preact)
    preact_grad = gelu_back(active_grad)[0]
    inner_add_grad = jnp.sum(preact_grad, axis=0)
    preact16 = preact_grad.astype(jnp.bfloat16)
    inner_mat_grad = jnp.dot(first16.T, preact16, preferred_element_type=jnp.float32)
    first_grad = second_grad + jnp.dot(preact16, inner_mat.T, preferred_element_type=jnp.float32)
    residual_grad, gain_one_grad, shift_one_grad = normalize_back(
        first_grad, first_normed, first_factor, gain_one
    )
    output_add_grad = jnp.sum(residual_grad, axis=0)
    residual16 = residual_grad.astype(jnp.bfloat16)
    output_mat_grad = jnp.dot(context.T, residual16, preferred_element_type=jnp.float32)
    context_grad = jnp.dot(residual16, output_mat.T, preferred_element_type=jnp.float32).astype(
        jnp.bfloat16
    )

    def attend_back(element):
        query_row, key_row, value_row, live_row, logsum_row, context_row = element
        scores = head_scores(query_row, key_row, live_row)
        attention = jnp.exp(scores - logsum_row[..., None])
        attention16 = attention.astype(jnp.bfloat16)
        value_grad = jnp.einsum(
            "shqk,sqhd->skhd", attention16, context_row, preferred_element_type=jnp.float32
        )
        attention_grad = jnp.einsum(
            "sqhd,skhd->shqk", context_row, value_row, preferred_element_type=jnp.float32
        )
        weighted = jnp.sum(attention * attention_grad, axis=-1, keepdims=True)
        scores_grad = (attention * (attention_grad - weighted)).astype(jnp.bfloat16)
        query_grad = jnp.einsum(
            "shqk,skhd->sqhd", scores_grad, key_row, preferred_element_type=jnp.float32
        ) * HEAD_DIM ** (-0.5)
        key_grad = jnp.einsum(
            "shqk,sqhd->skhd", scores_grad, query_row, preferred_element_type=jnp.float32
        ) * HEAD_DIM ** (-0.5)
        return (
            query_grad.astype(jnp.bfloat16),
            key_grad.astype(jnp.bfloat16),
            value_grad.astype(jnp.bfloat16),
        )

    query_grad, key_grad, value_grad = lax.map(
        attend_back,
        (
            queries.reshape(shaped),
            key_rows.reshape(shaped),
            value_rows.reshape(shaped),
            allowed,
            logsum,
            context_grad.reshape(shaped),
        ),
    )
    query_grad = query_grad.reshape(-1, D)
    key_grad = key_grad.reshape(-1, D)
    value_grad = value_grad.reshape(-1, D)
    query_add_grad = jnp.sum(query_grad.astype(jnp.float32), axis=0)
    value_add_grad = jnp.sum(value_grad.astype(jnp.float32), axis=0)
    query_mat_grad = jnp.dot(hidden_in.T, query_grad, preferred_element_type=jnp.float32)
    key_mat_grad = jnp.dot(hidden_in.T, key_grad, preferred_element_type=jnp.float32)
    value_mat_grad = jnp.dot(hidden_in.T, value_grad, preferred_element_type=jnp.float32)
    input_grad = (
        residual_grad
        + jnp.dot(query_grad, query_mat.T, preferred_element_type=jnp.float32)
        + jnp.dot(key_grad, key_mat.T, preferred_element_type=jnp.float32)
        + jnp.dot(value_grad, value_mat.T, preferred_element_type=jnp.float32)
    )
    gradients = (
        query_mat_grad,
        query_add_grad,
        key_mat_grad,
        value_mat_grad,
        value_add_grad,
        output_mat_grad,
        output_add_grad,
        gain_one_grad,
        shift_one_grad,
        inner_mat_grad,
        inner_add_grad,
        outer_mat_grad,
        outer_add_grad,
        gain_two_grad,
        shift_two_grad,
    )
    return (input_grad, gradients)


def per_device(
    hidden_in,
    cotangent,
    span_lengths,
    partner_span,
    query_weight,
    query_bias,
    key_weight,
    value_weight,
    value_bias,
    output_weight,
    output_bias,
    first_gain,
    first_shift,
    inner_weight,
    inner_bias,
    outer_weight,
    outer_bias,
    second_gain,
    second_shift,
):
    shards = (
        query_weight,
        query_bias,
        key_weight,
        value_weight,
        value_bias,
        output_weight,
        output_bias,
        first_gain,
        first_shift,
        inner_weight,
        inner_bias,
        outer_weight,
        outer_bias,
        second_gain,
        second_shift,
    )
    length = SPAN * SPANS_ROW
    row_count = hidden_in.shape[0] // length
    allowed = jnp.arange(SPAN)[None, None, :] < span_lengths.reshape(row_count, SPANS_ROW, 1)
    gathered = collect(shards)
    encoded, stored = encode(hidden_in, allowed, gathered)
    cls_rows = (
        encoded.reshape(row_count, SPANS_ROW, SPAN, D)[:, :, 0, :]
        .reshape(-1, D)
        .astype(jnp.bfloat16)
    )
    other_rows = mate(cls_rows)
    logits = jnp.dot(cls_rows, other_rows.T, preferred_element_type=jnp.float32) / math.sqrt(D)
    span_count = cls_rows.shape[0]
    matches = (partner_span.reshape(span_count, 1) == jnp.arange(span_count)[None, :]).astype(
        jnp.float32
    )
    target = jnp.where(lax.axis_index("pair") == 0, matches, matches.T)
    highest_logit = jnp.max(logits, axis=-1, keepdims=True)
    exponent = jnp.exp(logits - highest_logit)
    totals = jnp.sum(exponent, axis=-1, keepdims=True)
    span_loss = highest_logit[:, 0] + jnp.log(totals[:, 0]) - jnp.sum(target * logits, axis=-1)
    softened = exponent / totals - target
    own_grad = jnp.dot(softened, other_rows.astype(jnp.float32), precision=highest)
    other_logits = logits.T
    other_highest = jnp.max(other_logits, axis=-1, keepdims=True)
    other_exponent = jnp.exp(other_logits - other_highest)
    other_softened = (
        other_exponent / jnp.sum(other_exponent, axis=-1, keepdims=True) - target.T
    )
    back_grad = jnp.dot(
        other_softened.T, other_rows.astype(jnp.float32), precision=highest
    ).astype(jnp.bfloat16)
    cls_gradient = (own_grad + back_grad.astype(jnp.float32)).reshape(row_count, SPANS_ROW, 1, D)
    placed = jnp.concatenate(
        [cls_gradient, jnp.zeros((row_count, SPANS_ROW, SPAN - 1, D), jnp.float32)], axis=2
    )
    out_gradient = cotangent.astype(jnp.float32) + placed.reshape(-1, D)
    input_grad, gradients = backward(hidden_in, allowed, gathered, stored, out_gradient)
    reduced = spread(gradients)
    return (encoded.astype(jnp.bfloat16), input_grad.astype(jnp.bfloat16), span_loss) + tuple(
        reduced
    )


ROW = 24
PLACES = 8


def coordinates():
    doc = lax.axis_index("doc")
    return (doc & 1, (doc >> 1) & 1, doc >> 2, lax.axis_index("pair"))


def blocks_of(row):
    block = (row * 2731) >> 16
    return (block >> 1) & 1, block & 1, (block >> 2) & 1, block >> 3, row - block * ROW


def restore_from(place):
    row = lax.broadcasted_iota(jnp.int32, (D, 1), 0)
    core, y_at, x_at, z_at, inside = blocks_of(row)
    offset = ((core ^ place[0]) * 2 + (y_at ^ place[1])) * 2 + (x_at ^ place[2])
    arrived = (offset * 4 + (z_at ^ place[3])) * ROW + inside
    hit = arrived == lax.broadcasted_iota(jnp.int32, (D, D), 1)
    return jnp.where(hit, 1.0, 0.0).astype(jnp.bfloat16)


def arrange_from(place):
    row = lax.broadcasted_iota(jnp.int32, (1, D), 1)
    core, y_at, x_at, z_at, inside = blocks_of(row)
    offset = ((y_at ^ place[1]) * 2 + (x_at ^ place[2])) * 4 + (z_at ^ place[3])
    leaving = offset * 2 * ROW + core * ROW + inside
    hit = leaving == lax.broadcasted_iota(jnp.int32, (D, D), 0)
    return jnp.where(hit, 1.0, 0.0).astype(jnp.bfloat16)


def after(value, *others):
    return lax.optimization_barrier((value,) + others)[0]


def z_exchange(block, masks=(4, 8, 12)):
    return [across(block, mask) for mask in masks]


def tied(values, *others):
    return lax.optimization_barrier(tuple(values) + others)[: len(values)]


def near_exchange(block):
    return across(block[0], 2), mate(block[1])


def stack_near(block, received):
    return stack_pair(block[0], received[0], block[1], received[1])


def far_exchange(block):
    return mate(block[0]), across(block[1], 2)


def core_exchange(block):
    return [across(part, 1) for part in block]


def pieces_of(near, far, core, far_core):
    return [near[0], far[0], near[1], far[1], core, far_core[0], far_core[1]]


VMEM = pl.BlockSpec(memory_space=pltpu.VMEM)
SMEM = pl.BlockSpec(memory_space=pltpu.SMEM)


def full(shape):
    return pl.BlockSpec(shape, lambda *at: (0,) * len(shape))


class Fetched:
    def __init__(self, source, held, semaphore):
        self.copy, self.held, self.waiting = pltpu.make_async_copy(source, held, semaphore), held, True
        self.shape = held.shape
        self.copy.start()

    def ready(self):
        if self.waiting:
            self.copy.wait()
            self.waiting = False
        return self.held

    def __getitem__(self, at):
        return self.ready()[at]


class Stored:
    def __init__(self, target, held, semaphores):
        self.target, self.held, self.semaphores, self.copies = target, held, semaphores, []
        self.shape = held.shape

    def __getitem__(self, at):
        return self.held[at]

    def __setitem__(self, at, value):
        self.held[at] = value

    def done(self, at=None):
        semaphore = self.semaphores.at[len(self.copies)]
        held, target = (self.held, self.target) if at is None else (self.held.at[at], self.target.at[at])
        self.copies.append(pltpu.make_async_copy(held, target, semaphore))
        self.copies[-1].start()


PARTS = 8


def ready(ref):
    return ref.ready() if isinstance(ref, Fetched) else ref


def run(kernel, name, operands, results, flops, scratch=(), mib=12, total=None):
    in_hbm = pl.BlockSpec(memory_space=pltpu.HBM)
    spaces = {"S": SMEM, "V": VMEM, "H": in_hbm, "A": in_hbm}
    spaces["K"] = VMEM
    in_places = [place for _, place in operands]
    out_places = [place for _, _, place in results]
    staged = [pltpu.VMEM(array.shape, array.dtype) for array, place in operands if place == "H"]
    made = [pltpu.VMEM(shape, dtype) for shape, dtype, place in results if place == "H"]
    semaphores = [pltpu.SemaphoreType.DMA((max(1, len(staged)),))]
    semaphores += [pltpu.SemaphoreType.DMA((max(1, len(made)), PARTS))]

    def body(*refs):
        ins, refs = refs[: len(operands)], refs[len(operands) :]
        outs, refs = refs[: len(results)], refs[len(results) :]
        held_in, refs = refs[: len(staged)], refs[len(staged) :]
        held_out, refs = refs[: len(made)], refs[len(made) :]
        fetching, storing, own = refs[0], refs[1], refs[2:]
        arguments, at = [], 0
        for ref, place in zip(ins, in_places):
            if place == "H":
                ref, at = Fetched(ref, held_in[at], fetching.at[at]), at + 1
            arguments.append(ref)
        inputs, at = list(arguments), 0
        for ref, place in zip(outs, out_places):
            if place == "H":
                ref, at = Stored(ref, held_out[at], storing.at[at]), at + 1
            arguments.append(ref)
        kernel(*arguments, *own)
        for ref in inputs:
            if isinstance(ref, Fetched):
                ref.ready()
        made_here = [ref for ref in arguments if isinstance(ref, Stored)]
        for ref in made_here:
            if not ref.copies:
                ref.done()
        for ref in made_here:
            for copy in ref.copies:
                copy.wait()

    size = lambda shape, dtype: math.prod(shape) * jnp.dtype(dtype).itemsize
    inside = sum(size(array.shape, array.dtype) for array, place in operands if place == "H")
    inside += sum(size(shape, dtype) for shape, dtype, place in results if place == "H")
    mib = (mib + inside // 2**20) if total is None else total
    return pl.pallas_call(
        body,
        in_specs=[spaces[place] for place in in_places],
        out_specs=[spaces[place] for place in out_places],
        out_shape=[jax.ShapeDtypeStruct(shape, dtype) for shape, dtype, _ in results],
        scratch_shapes=staged + made + semaphores + list(scratch),
        compiler_params=params(mib),
        cost_estimate=cost(1, 1),
        name=name,
    )(*[array for array, _ in operands])


def placed_at(place, *arrays):
    return [(array, place) for array in arrays]


bf16, f32 = jnp.bfloat16, jnp.float32


def params(mib=16):
    return pltpu.CompilerParams(vmem_limit_bytes=mib << 20)


def cost(flops, moved):
    return pl.CostEstimate(flops=int(flops), bytes_accessed=int(moved), transcendentals=0)


def dot(left, right):
    return jnp.dot(left, right, preferred_element_type=jnp.float32)


def dot_nt(left, right):
    return lax.dot_general(
        left, right, (((1,), (1,)), ((), ())), preferred_element_type=jnp.float32
    )


def dot_tn(left, right):
    return lax.dot_general(
        left, right, (((0,), (0,)), ((), ())), preferred_element_type=jnp.float32
    )


def pack_kernel(*refs):
    query, key, value, output, inner, inner_bias = refs[:6]
    vectors, (first, second, turned) = refs[6:-3], refs[-3:]
    turned[...] = jnp.zeros_like(turned)
    for at, vector in enumerate(vectors):
        turned[at : at + 1, :ROW] = vector[...].astype(jnp.float32)
    bias = inner_bias[...].astype(jnp.float32)
    for at in range(4):
        turned[8 + at : 9 + at, :ROW] = bias[:, at * ROW : (at + 1) * ROW]
    small = jnp.transpose(turned[...])[:ROW].astype(jnp.bfloat16)
    first[:, :D] = query[...]
    first[:, D : D + 512] = key[:, :512]
    first[:, D + 512 : D + 640] = small
    first[:, D + 640 : D + 768] = jnp.zeros_like(small)
    first[:, D + 768 : D + 1024] = key[:, 512:]
    first[:, D + 1024 :] = value[...]
    second[:, :D] = output[...]
    second[:, D:] = inner[...]


def pack(query, key, value, output, inner, inner_bias, vectors):
    rows = [vector.reshape(1, -1) for vector in (inner_bias, *vectors)]
    return run(
        pack_kernel,
        "pack",
        placed_at("H", query, key, value, output, inner, *rows),
        [((ROW, 2 * FIRST_HALF), bf16, "V"), ((ROW, D + inner.shape[1]), bf16, "V")],
        1e6,
        [pltpu.VMEM((128, 128), f32)],
        total=58,
    )


def stack_two_kernel(first, second, left, right):
    blocks = [first[...].astype(jnp.float32), second[...].astype(jnp.float32)]
    whole = jnp.concatenate(blocks).astype(jnp.bfloat16)
    left[...] = whole[:, : left.shape[1]]
    right[...] = whole[:, left.shape[1] :]


def stack_two(block, received, split):
    rows, columns = block.shape
    return pl.pallas_call(
        stack_two_kernel,
        in_specs=[VMEM] * 2,
        out_specs=[VMEM] * 2,
        out_shape=[
            jax.ShapeDtypeStruct((2 * rows, split), jnp.bfloat16),
            jax.ShapeDtypeStruct((2 * rows, columns - split), jnp.bfloat16),
        ],
        compiler_params=params(),
        cost_estimate=cost(1, 1),
        name="stack_two",
    )(block, received)


def stack_z_two_kernel(first, second, out):
    blocks = [first[...].astype(jnp.float32), second[...].astype(jnp.float32)]
    out[...] = jnp.concatenate(blocks).astype(jnp.bfloat16)


def stack_z_two(block, received):
    rows, columns = block.shape
    return pl.pallas_call(
        stack_z_two_kernel,
        in_specs=[VMEM] * 2,
        out_specs=VMEM,
        out_shape=jax.ShapeDtypeStruct((2 * rows, columns), jnp.bfloat16),
        compiler_params=params(),
        cost_estimate=cost(1, 1),
        name="stack_z_two",
    )(block, received)


def stack_mixed_kernel(split, two, received, left, right):
    rows = two.shape[0] // 2
    own, other = two[...].astype(jnp.float32), received[...].astype(jnp.float32)
    whole = jnp.concatenate([own[:rows], other[:rows], own[rows:], other[rows:]]).astype(jnp.bfloat16)
    left[...] = whole[:, :split]
    right[...] = whole[:, split:]


def stack_mixed(two, received, split):
    rows, columns = two.shape
    return pl.pallas_call(
        partial(stack_mixed_kernel, split),
        in_specs=[VMEM] * 2,
        out_specs=[VMEM] * 2,
        out_shape=[
            jax.ShapeDtypeStruct((2 * rows, split), jnp.bfloat16),
            jax.ShapeDtypeStruct((2 * rows, columns - split), jnp.bfloat16),
        ],
        compiler_params=params(),
        cost_estimate=cost(1, 1),
        name="stack_mixed",
    )(two, received)


def stack_z_kernel(split, *refs):
    blocks, (left, right) = refs[:-2], refs[-2:]
    whole = jnp.concatenate([ref[...].astype(jnp.float32) for ref in blocks]).astype(jnp.bfloat16)
    left[...] = whole[:, :split]
    right[...] = whole[:, split:]


def stack_z(block, received, split):
    rows, columns = block.shape
    rows = rows * (1 + len(received)) // 4
    return pl.pallas_call(
        partial(stack_z_kernel, split),
        in_specs=[VMEM] * (1 + len(received)),
        out_specs=[VMEM] * 2,
        out_shape=[
            jax.ShapeDtypeStruct((4 * rows, split), jnp.bfloat16),
            jax.ShapeDtypeStruct((4 * rows, columns - split), jnp.bfloat16),
        ],
        compiler_params=params(),
        cost_estimate=cost(1, 1),
        name="stack_z",
    )(block, *received)


def stack_pair_kernel(left, left_in, right, right_in, left_out, right_out, both_out):
    width = left.shape[1]
    for own, received, out, columns in (
        (left, left_in, left_out, slice(0, width)),
        (right, right_in, right_out, slice(width, width + right.shape[1])),
    ):
        rows = own.shape[0]
        out[:rows, :] = own[...]
        out[rows:, :] = received[...]
        both_out[:rows, columns] = own[...]
        both_out[rows:, columns] = received[...]


def stack_pair(left, left_in, right, right_in):
    double = lambda block: jax.ShapeDtypeStruct((2 * block.shape[0], block.shape[1]), block.dtype)
    both = jax.ShapeDtypeStruct((2 * left.shape[0], left.shape[1] + right.shape[1]), left.dtype)
    return pl.pallas_call(
        stack_pair_kernel,
        in_specs=[VMEM] * 4,
        out_specs=[VMEM] * 3,
        out_shape=[double(left), double(right), both],
        compiler_params=params(),
        cost_estimate=cost(1, 1),
        name="stack_pair",
    )(left, left_in, right, right_in)


def left_tile(refs, columns):
    return jnp.concatenate([ref[:, columns] for ref in refs])


def right_tile(refs, columns):
    near, far, other_near, other_far = refs
    rows = near.shape[0] // 2
    order = [(near, 0), (far, 0), (near, 1), (far, 1)]
    order += [(other_near, 0), (other_far, 0), (other_near, 1), (other_far, 1)]
    return jnp.concatenate([ref[at * rows : (at + 1) * rows, columns] for ref, at in order])


def in_order(pieces):
    left, left_far, right, right_far, c_both, c_left_far, c_right_far = pieces
    return (left, left_far, c_left_far, c_both, right, right_far, c_right_far)


class Side:
    def __init__(self, ref, start, width):
        self.ref, self.start, self.shape = ref, start, (ref.shape[0], width)

    def __getitem__(self, at):
        rows, columns = at
        return self.ref[rows, columns.start + self.start : columns.stop + self.start]


def sides(l0, l1, l3, both, r0, r1, r3):
    left, right = l0.shape[1], r0.shape[1]
    return (l0, l1, Side(both, 0, left), l3), (r0, r1, Side(both, left, right), r3)


FIRST_PARTS = ((0, 0, 768), (0, 768, 512), (1, 256, 256), (1, 512, 768))
SECOND_PARTS = ((0, 0, 768), (0, 768, 512), (0, 1280, 512)) + tuple((1, at, 512) for at in range(0, 2048, 512))


def settle(sides_of, parts, mats, semaphore):
    copies = []
    for (side, start, width), mat in zip(parts, mats):
        for at, piece in enumerate(sides_of[side]):
            rows = piece.shape[0]
            source, first = (piece.ref, piece.start) if isinstance(piece, Side) else (piece, 0)
            columns = pl.ds(first + start, width)
            if side == 0:
                copies.append((source.at[:, columns], mat.at[pl.ds(at * rows, rows), :]))
                continue
            half = rows // 2
            core, far = at // 2, at % 2
            for near in range(2):
                to = ((core * 2 + near) * 2 + far) * half
                copies.append((source.at[pl.ds(near * half, half), columns], mat.at[pl.ds(to, half), :]))
    copies = [pltpu.make_async_copy(*ends, semaphore.at[at]) for at, ends in enumerate(copies)]
    for copy in copies:
        copy.start()
    return copies


FIRST_HALF = 1280
SECOND_HALF = 1792
def head_pair(pair, low):
    nothing = jnp.zeros_like(pair)
    return jnp.concatenate([jnp.where(low, pair, nothing), jnp.where(low, nothing, pair)])


def key_columns(left_rows, right_rows, rows, at):
    if at < 512:
        return left_rows[rows, D + at : D + at + 128]
    return right_rows[rows, at - 256 : at - 128]


def project_kernel(
    place,
    hidden,
    both,
    r0,
    r1,
    r3,
    l0,
    l1,
    l3,
    left_rows,
    right_rows,
    vectors,
    hidden_t,
    query_mat,
    low_key_mat,
    high_key_mat,
    value_mat,
    settling,
):
    tokens = hidden.shape[0]
    lefts, rights = sides(l0, l1, l3, both, r0, r1, r3)
    mats = (query_mat, low_key_mat, high_key_mat, value_mat)
    copies = settle((lefts, rights), FIRST_PARTS, mats, settling)
    restore = restore_from(place)
    moved = dot(hidden[...], restore).astype(jnp.bfloat16)
    small = dot(restore, right_tile(rights, slice(0, 128)))
    turned = jnp.transpose(small)[:16]
    vectors[...] = turned
    for at in range(0, FIRST_HALF, 256):
        columns = slice(at, at + 256)
        rows = dot(moved, left_tile(lefts, columns))
        if at < D:
            rows += turned[0:1, columns]
        left_rows[:, columns] = rows.astype(jnp.bfloat16)
        if at == 0:
            right_rows[:, columns] = jnp.zeros((tokens, 256), jnp.bfloat16)
            continue
        rows = dot(moved, right_tile(rights, columns))
        if at >= 512:
            rows += turned[1:2, at - 512 : at - 256]
        right_rows[:, columns] = rows.astype(jnp.bfloat16)
    left_rows.done()
    right_rows.done()
    hidden_t[...] = dot_nt(arrange_from(place), hidden[...]).astype(jnp.bfloat16)
    for copy in copies:
        copy.wait()


def project(place, hidden, pieces):
    tokens, ordered = hidden.shape[0], in_order(pieces)
    return run(
        project_kernel,
        "project",
        [(place, "S"), (hidden, "H")] + placed_at("K", *ordered[3:], *ordered[:3]),
        [
            ((tokens, FIRST_HALF), bf16, "H"),
            ((tokens, FIRST_HALF), bf16, "H"),
            ((16, D), f32, "V"),
            ((D, tokens), bf16, "H"),
        ]
        + [((D, width), bf16, "A") for _, _, width in FIRST_PARTS],
        9e9,
        [pltpu.SemaphoreType.DMA((24,))],
        total=50,
    )


def attention_kernel(
    place, lengths, left_rows, right_rows, attention_out, context_arrived, context_t, context
):
    tokens = context.shape[0]
    left_rows, right_rows = ready(left_rows), ready(right_rows)
    low = lax.broadcasted_iota(jnp.int32, (SPAN, 128), 1) < HEAD_DIM

    def attend(span, carry):
        rows = pl.ds(pl.multiple_of(span * SPAN, SPAN), SPAN)
        live = lax.broadcasted_iota(jnp.int32, (SPAN, SPAN), 1) < lengths[span]
        for at in range(0, D, 128):
            query = left_rows[rows, at : at + 128]
            keys = head_pair(key_columns(left_rows, right_rows, rows, at), low)
            values = head_pair(right_rows[rows, 512 + at : 640 + at], low)
            scores = dot_nt(query, keys) * HEAD_DIM ** (-0.5)
            parts = []
            for head in range(2):
                part = jnp.where(live, scores[:, head * SPAN : (head + 1) * SPAN], masked_out)
                exponent = jnp.exp(part - jnp.max(part, axis=-1, keepdims=True))
                parts.append(
                    (exponent * (1.0 / jnp.sum(exponent, axis=-1, keepdims=True))).astype(jnp.bfloat16)
                )
            attention = jnp.concatenate(parts, axis=1)
            attention_out[rows, 2 * at : 2 * at + 256] = attention
            context[rows, at : at + 128] = dot(attention, values).astype(jnp.bfloat16)
        return carry

    lax.fori_loop(0, tokens // SPAN, attend, 0)
    attention_out.done()
    context_arrived[...] = dot(context[...], restore_from(place)).astype(jnp.bfloat16)
    context_t[...] = dot_nt(arrange_from(place), context[...]).astype(jnp.bfloat16)


def attention_forward(place, lengths, left_rows, right_rows):
    tokens = left_rows.shape[0]
    return run(
        attention_kernel,
        "attention_forward",
        placed_at("S", place, lengths) + placed_at("H", left_rows, right_rows),
        [((tokens, 2 * D), bf16, "H"), ((tokens, D), bf16, "V"), ((D, tokens), bf16, "H")],
        9e9,
        [pltpu.VMEM((tokens, D), bf16)],
        total=28,
    )


def gelu_parts(preact):
    scaled = jnp.abs(preact) * (0.5**0.5)
    below_one = 1.0 + 0.3275911 * scaled
    near = pl.reciprocal(below_one, approx=True)
    near = near * (2.0 - below_one * near)
    poly = near * (
        0.254829592
        + near * (-0.284496736 + near * (1.421413741 + near * (-1.453152027 + near * 1.061405429)))
    )
    bell = jnp.exp(-0.5 * preact * preact)
    tail = 0.5 * poly * bell
    below = jnp.where(preact < 0.0, tail, 1.0 - tail)
    return (preact * below, below + preact * bell * (0.5 / math.pi) ** 0.5)


FF_TILE = 512


def second_tiles(left, right):
    for at in range(D, SECOND_HALF, FF_TILE):
        yield at - D, left_tile(left, slice(at, at + FF_TILE))
    for at in range(0, right[0].shape[1], FF_TILE):
        yield SECOND_HALF - D + at, right_tile(right, slice(at, at + FF_TILE))


def vector_places():
    for device in range(D // ROW):
        for part in range(4):
            yield (8 + part, device * ROW), (device * 4 + part) * ROW


def residual_kernel(
    place,
    vectors,
    context_arrived,
    l0,
    l1,
    l3,
    both,
    hidden,
    moved,
    normed_out,
    factor_out,
    first_t,
    output_mat,
    settling,
):
    left = (l0, l1, Side(both, 0, l0.shape[1]), l3)
    copies = settle((left, ()), SECOND_PARTS[:1], (output_mat,), settling)
    residual = dot(context_arrived[...], left_tile(left, slice(0, D)))
    residual += hidden[...].astype(jnp.float32) + vectors[2:3, :]
    first_out, normed, factor = normalize(residual, vectors[3:4, :], vectors[4:5, :])
    normed_out[...] = normed
    factor_out[...] = factor
    first16 = first_out.astype(jnp.bfloat16)
    moved[...] = dot(first16, restore_from(place)).astype(jnp.bfloat16)
    first_t[...] = dot_nt(arrange_from(place), first16).astype(jnp.bfloat16)
    for copy in copies:
        copy.wait()


def residual_forward(place, hidden, context_arrived, vectors, pieces):
    tokens, ordered = hidden.shape[0], in_order(pieces)
    return run(
        residual_kernel,
        "residual",
        [(place, "S")]
        + placed_at("V", vectors, context_arrived, *ordered[:4])
        + [(hidden, "H")],
        [
            ((tokens, D), bf16, "V"),
            ((tokens, D), f32, "V"),
            ((tokens, 1), f32, "V"),
            ((D, tokens), bf16, "H"),
            ((D, D), bf16, "A"),
        ],
        1e9,
        [pltpu.SemaphoreType.DMA((4,))],
        total=24,
    )


def feed_kernel(vectors, moved, l0, l1, l3, both, r0, r1, r3, active, active_t, slope, *rest):
    mats, (inner_bias, settling) = rest[:-2], rest[-2:]
    for at, column in vector_places():
        inner_bias[:, column : column + ROW] = vectors[at[0] : at[0] + 1, at[1] : at[1] + ROW]
    left, right = sides(l0, l1, l3, both, r0, r1, r3)
    copies = settle((left, right), SECOND_PARTS[1:], mats, settling)
    for at, tile in second_tiles(left, right):
        columns = slice(at, at + FF_TILE)
        value, derivative = gelu_parts(dot(moved[...], tile) + inner_bias[:, columns])
        value16 = value.astype(jnp.bfloat16)
        active[:, columns] = value16
        active_t[columns, :] = jnp.transpose(value16)
        slope[:, columns] = derivative.astype(jnp.bfloat16)
    for copy in copies:
        copy.wait()


def feed_forward(moved, vectors, ff, pieces):
    tokens = moved.shape[0]
    return run(
        feed_kernel,
        "feed_forward",
        placed_at("V", vectors, moved, *in_order(pieces)),
        [((tokens, ff), bf16, "V"), ((ff, tokens), bf16, "V"), ((tokens, ff), bf16, "V")]
        + [((D, width), bf16, "A") for _, _, width in SECOND_PARTS[1:]],
        8e9,
        [pltpu.VMEM((1, ff), f32), pltpu.SemaphoreType.DMA((44,))],
        total=20,
    )


def natural_rows(place, pieces, target, semaphore):
    rows = 4 * ROW
    left, right = pieces[0].shape[1], pieces[4].shape[1]
    near, far, far_core, near_core, right_near, right_far, right_far_core = pieces
    places = [(near, 0, 0, 0, 0), (far, 0, 0, 1, 0), (near_core, 0, 1, 0, 0), (far_core, 0, 1, 1, 0)]
    places += [(right_near, 1, 0, 0, 0), (right_far, 1, 0, 1, 0)]
    places += [(near_core, 1, 1, 0, left), (right_far_core, 1, 1, 1, 0)]
    for piece, is_right, core_off, far_off, start in places:
        half = right if is_right else left
        for near_off in range(2):
            for z_off in range(4):
                x_off, y_off = (far_off, near_off) if is_right else (near_off, far_off)
                block = ((z_off ^ place[3]) * 2 + (x_off ^ place[2])) * 2 + (core_off ^ place[0])
                block = block * 2 + (y_off ^ place[1])
                to = pl.ds(pl.multiple_of(block * rows, rows), rows)
                pltpu.make_async_copy(
                    piece.at[pl.ds((near_off * 4 + z_off) * rows, rows), pl.ds(start, half)],
                    target.at[to, pl.ds(is_right * left, half)],
                    semaphore,
                ).start()
    pltpu.make_async_copy(target, target, semaphore).wait()


def last_kernel(
    place,
    active,
    first_normed,
    vectors,
    l0,
    l1,
    l3,
    both,
    r0,
    r1,
    r3,
    layer_out,
    normed_out,
    factor_out,
    cls_rows,
    outer_mat,
    semaphore,
):
    natural_rows(place, (l0, l1, l3, both, r0, r1, r3), outer_mat, semaphore)
    total = first_normed[...] * vectors[3:4, :] + vectors[4:5, :] + vectors[5:6, :]
    total += dot(active[...], outer_mat[...])
    encoded, normed, factor = normalize(total, vectors[6:7, :], vectors[7:8, :])
    layer_out[...] = encoded.astype(jnp.bfloat16)
    normed_out[...] = normed
    factor_out[...] = factor
    for span in range(encoded.shape[0] // SPAN):
        cls_rows[span : span + 1, :] = encoded[span * SPAN : span * SPAN + 1].astype(jnp.bfloat16)


def last(place, active, first_normed, vectors, pieces):
    tokens, ff = active.shape
    return run(
        last_kernel,
        "last",
        [(place, "S")]
        + placed_at("V", active, first_normed, vectors, *in_order(pieces)),
        [
            ((tokens, D), bf16, "H"),
            ((tokens, D), f32, "V"),
            ((tokens, 1), f32, "V"),
            ((tokens // SPAN, D), bf16, "V"),
            ((ff, D), bf16, "V"),
        ],
        2.5e9,
        [pltpu.SemaphoreType.DMA],
        total=16,
    )


def pick(place, first, second):
    return jnp.where(place == 0, first, second)


def turn_kernel(
    place,
    partner_span,
    cotangent,
    normed,
    factor,
    vectors,
    own_rows,
    other_rows,
    second_grad,
    kept,
    sent,
    sums,
    loss,
):
    spans = own_rows.shape[0]
    own, other = own_rows[...].astype(jnp.float32), other_rows[...].astype(jnp.float32)
    logits = dot_nt(own_rows[...], other_rows[...]) / math.sqrt(D)
    row = lax.broadcasted_iota(jnp.int32, (spans, spans), 0)
    column = lax.broadcasted_iota(jnp.int32, (spans, spans), 1)
    first_place = place[1] == 0
    target = jnp.zeros((spans, spans), jnp.float32)
    for span in range(spans):
        match = partner_span[0, span]
        hit_row = jnp.where(first_place, span, match)
        hit_column = jnp.where(first_place, match, span)
        target += ((row == hit_row) & (column == hit_column)).astype(jnp.float32)
    highest_logit = jnp.max(logits, axis=1, keepdims=True)
    exponent = jnp.exp(logits - highest_logit)
    totals = jnp.sum(exponent, axis=1, keepdims=True)
    losses = highest_logit + jnp.log(totals) - jnp.sum(target * logits, axis=1, keepdims=True)
    loss[...] = jnp.sum(jnp.where(row == column, losses, 0.0), axis=0, keepdims=True)
    soft = exponent / totals - target
    exponent = jnp.exp(logits - jnp.max(logits, axis=0, keepdims=True))
    back = exponent / jnp.sum(exponent, axis=0, keepdims=True) - target
    own_term, back_term = jnp.zeros_like(own), jnp.zeros_like(own)
    for span in range(spans):
        own_term += soft[:, span : span + 1] * other[span : span + 1]
        back_term += back[:, span : span + 1] * other[span : span + 1]
    cls_gradient = own_term + back_term.astype(jnp.bfloat16).astype(jnp.float32)
    start = lax.broadcasted_iota(jnp.int32, (SPAN, 1), 0) == 0
    gain = vectors[6:7, :]
    gain_sum = jnp.zeros((1, D), jnp.float32)
    shift_sum, bias_sum = gain_sum, gain_sum
    for span in range(spans):
        rows = slice(span * SPAN, (span + 1) * SPAN)
        upstream = cotangent[rows, :].astype(jnp.float32)
        upstream += jnp.where(start, cls_gradient[span : span + 1], 0.0)
        grad, gain_part, shift_part = normalize_back(upstream, normed[rows, :], factor[rows, :], gain)
        second_grad[rows, :] = grad
        gain_sum += gain_part[None]
        shift_sum += shift_part[None]
        bias_sum += jnp.sum(grad, axis=0, keepdims=True)
        grad16 = grad.astype(jnp.bfloat16)
        kept[rows, :] = pick(place[0], grad16[:, : D // 2], grad16[:, D // 2 :])
        sent[rows, :] = pick(place[0], grad16[:, D // 2 :], grad16[:, : D // 2])
    sums[0:1, :] = bias_sum
    sums[1:2, :] = gain_sum
    sums[2:3, :] = shift_sum


def turn(place, partner_span, cotangent, normed, factor, vectors, own_rows, other_rows):
    tokens = cotangent.shape[0]
    return run(
        turn_kernel,
        "turn",
        placed_at("S", place, partner_span)
        + [(cotangent, "H")]
        + placed_at("V", normed, factor, vectors, own_rows, other_rows),
        [
            ((tokens, D), f32, "V"),
            ((tokens, D // 2), bf16, "V"),
            ((tokens, D // 2), bf16, "V"),
            ((3, D), f32, "V"),
            ((1, own_rows.shape[0]), f32, "V"),
        ],
        1e8,
    )


def both_halves(place, kept, sent):
    return jnp.concatenate([pick(place, kept, sent), pick(place, sent, kept)], axis=1)


def slope_kernel(place, second_kept, second_sent, outer_mat, slope, kept, sent, sums, second16):
    second16[...] = both_halves(place[0], second_kept[...], second_sent[...])
    per_half = kept.shape[1] // D

    def tile(at, carry):
        columns = pl.ds(pl.multiple_of(at * D, D), D)
        inside = pl.ds(pl.multiple_of((at % per_half) * D, D), D)
        grad = dot_nt(second16[...], outer_mat[columns, :]) * slope[:, columns].astype(jnp.float32)
        sums[:, columns] = jnp.sum(grad, axis=0, keepdims=True)
        grad16 = grad.astype(jnp.bfloat16)
        mine = place[0] == at // per_half

        @pl.when(mine)
        def keep():
            kept[:, inside] = grad16

        @pl.when(jnp.logical_not(mine))
        def send():
            sent[:, inside] = grad16

        return carry

    lax.fori_loop(0, 2 * per_half, tile, 0)


def slope_back(place, second_kept, second_sent, outer_mat, slope):
    tokens, ff = slope.shape
    half = ((tokens, ff // 2), bf16, "V")
    return run(
        slope_kernel,
        "slope_back",
        [(place, "S")] + placed_at("V", second_kept, second_sent, outer_mat, slope),
        [half, half, ((1, ff), f32, "V")],
        2.5e9,
        [pltpu.VMEM((tokens, D), bf16)],
    )


def outer_kernel(place, active_t, other_active_t, kept, received, left_kept, left_sent, right_kept, right_sent):
    rows = 2 * ROW

    def chip_rows(chip, carry):
        x_off, z_off = (chip & 1) ^ place[2], (chip >> 1) ^ place[3]
        tile = pl.ds(pl.multiple_of(chip * 8 * rows, 8 * rows), 8 * rows)
        grad = dot(active_t[tile, :], kept[...]) + dot(other_active_t[tile, :], received[...])
        grad = grad.astype(jnp.bfloat16)
        for core in range(2):
            for y_at in range(2):
                start = (core * 2 + y_at) * 2 * rows
                left, right = grad[start : start + rows], grad[start + rows : start + 2 * rows]
                y_off = place[1] ^ y_at
                left_at = (x_off * 4 + z_off) * 2 + core
                right_at = (y_off * 4 + z_off) * 2 + core

                @pl.when(y_off == 0)
                def left_here():
                    left_kept[left_at] = left

                @pl.when(y_off == 1)
                def left_there():
                    left_sent[left_at] = left

                @pl.when(x_off == 0)
                def right_here():
                    right_kept[right_at] = right

                @pl.when(x_off == 1)
                def right_there():
                    right_sent[right_at] = right

        return carry

    lax.fori_loop(0, PLACES, chip_rows, 0)


def outer_gradient(place, active_t, other_active_t, kept, received):
    piece = ((2 * PLACES, 2 * ROW, kept.shape[1]), bf16, "V")
    return run(
        outer_kernel,
        "outer_gradient",
        [(place, "S")] + placed_at("V", active_t, other_active_t, kept, received),
        [piece] * 4,
        2.5e9,
    )


def whole_precision(left, right):
    high = left.astype(jnp.bfloat16)
    rest = (left - high.astype(jnp.float32)).astype(jnp.bfloat16)
    return dot_nt(high, right) + dot_nt(rest, right)


def first_kernel(
    place,
    preact_kept,
    preact_sent,
    factor,
    vectors,
    *refs,
):
    output_mat, inner_mats = refs[0], refs[1:7]
    second_grad, normed, residual_grad, kept, sent, context_grad, sums = refs[7:]
    restore = restore_from(place)
    total = jnp.zeros((factor.shape[0], D), jnp.float32)
    half = preact_kept.shape[1]
    for at, tile in zip(range(0, 2 * half, FF_TILE), inner_mats):
        columns = slice(at % half, at % half + FF_TILE)
        kept_part, sent_part = preact_kept[:, columns], preact_sent[:, columns]
        if at >= half:
            kept_part, sent_part = sent_part, kept_part
        total += dot_nt(pick(place[0], kept_part, sent_part), tile[...])
    first_grad = second_grad[...] + whole_precision(total, restore)
    grad, gain_sum, shift_sum = normalize_back(first_grad, normed[...], factor[...], vectors[3:4, :])
    residual_grad[...] = grad
    sums[0:1, :] = jnp.sum(grad, axis=0, keepdims=True)
    sums[1:2, :] = gain_sum[None]
    sums[2:3, :] = shift_sum[None]
    grad16 = grad.astype(jnp.bfloat16)
    kept[...] = pick(place[0], grad16[:, : D // 2], grad16[:, D // 2 :])
    sent[...] = pick(place[0], grad16[:, D // 2 :], grad16[:, : D // 2])
    moved = dot_nt(grad16, output_mat[...]).astype(jnp.bfloat16)
    context_grad[...] = dot_nt(moved, restore).astype(jnp.bfloat16)


def first_back(place, preact_kept, preact_sent, second_grad, normed, factor, vectors, mats):
    tokens = second_grad.shape[0]
    half = ((tokens, D // 2), bf16, "V")
    return run(
        first_kernel,
        "first_back",
        [(place, "S")]
        + placed_at("V", preact_kept, preact_sent, factor, vectors)
        + placed_at("V", *mats, second_grad, normed),
        [((tokens, D), f32, "V"), half, half, ((tokens, D), bf16, "V"), ((3, D), f32, "V")],
        4.9e9,
    )


def part_rows(grad, left_kept, left_sent, right_kept, right_sent, is_left):
    quarter = D // 4
    if is_left:
        left_kept[...] = grad[: 2 * quarter]
        left_sent[...] = grad[2 * quarter :]
    else:
        right_kept[:quarter, :] = grad[:quarter]
        right_sent[:quarter, :] = grad[quarter : 2 * quarter]
        right_kept[quarter:, :] = grad[2 * quarter : 3 * quarter]
        right_sent[quarter:, :] = grad[3 * quarter :]


def inner_kernel(first_t, other_first_t, kept, received, left_kept, left_sent, right_kept, right_sent):
    for is_left in (True, False):
        columns = slice(0, D) if is_left else slice(D, 2 * D)
        grad = dot(first_t[...], kept[:, columns]) + dot(other_first_t[...], received[:, columns])
        part_rows(grad.astype(jnp.bfloat16), left_kept, left_sent, right_kept, right_sent, is_left)


def inner_gradient(first_t, other_first_t, kept, received):
    piece = ((D // 2, kept.shape[1] // 2), bf16, "V")
    return run(
        inner_kernel,
        "inner_gradient",
        placed_at("V", first_t, other_first_t) + placed_at("V", kept, received),
        [piece] * 4,
        2.5e9,
    )


def attend_kernel(
    place,
    context_grad,
    left_rows,
    right_rows,
    attention_in,
    first_sums,
    second_sums,
    inner_sums,
    kept,
    sent,
    sums,
    grads,
):
    tokens = context_grad.shape[0]
    low = lax.broadcasted_iota(jnp.int32, (SPAN, 128), 1) < HEAD_DIM
    scale = HEAD_DIM ** (-0.5)
    left_rows, right_rows, attention_in = [ready(ref) for ref in (left_rows, right_rows, attention_in)]

    def attend(span, carry):
        rows = pl.ds(pl.multiple_of(span * SPAN, SPAN), SPAN)
        for at in range(0, D, 128):
            query = left_rows[rows, at : at + 128]
            keys = head_pair(key_columns(left_rows, right_rows, rows, at), low)
            values = head_pair(right_rows[rows, 512 + at : 640 + at], low)
            upstream = context_grad[rows, at : at + 128]
            attention16 = attention_in[rows, 2 * at : 2 * at + 256]
            attention_grad = dot_nt(upstream, values)
            parts = []
            for head in range(2):
                columns = slice(head * SPAN, (head + 1) * SPAN)
                attention = attention16[:, columns].astype(jnp.float32)
                part = attention_grad[:, columns]
                weighted = jnp.sum(attention * part, axis=-1, keepdims=True)
                parts.append((attention * (part - weighted)).astype(jnp.bfloat16))
            scores_grad = jnp.concatenate(parts, axis=1)
            grads[0, rows, at : at + 128] = (dot(scores_grad, keys) * scale).astype(jnp.bfloat16)
            both = dot_tn(scores_grad, query)
            both = jnp.where(low, both[:SPAN], both[SPAN:])
            grads[1, rows, at : at + 128] = (both * scale).astype(jnp.bfloat16)
            both = dot_tn(attention16, upstream)
            both = jnp.where(low, both[:SPAN], both[SPAN:])
            grads[2, rows, at : at + 128] = both.astype(jnp.bfloat16)
        return carry

    lax.fori_loop(0, tokens // SPAN, attend, 0)
    query_grad, key_grad, value_grad = grads[0], grads[1], grads[2]
    half = D // 2
    for at, grad in enumerate((query_grad, key_grad, value_grad)):
        columns = slice(at * half, (at + 1) * half)
        kept[:, columns] = pick(place[0], grad[:, :half], grad[:, half:])
        sent[:, columns] = pick(place[0], grad[:, half:], grad[:, :half])
    sums[0:1, :] = jnp.sum(query_grad.astype(jnp.float32), axis=0, keepdims=True)
    sums[1:2, :] = jnp.sum(value_grad.astype(jnp.float32), axis=0, keepdims=True)
    sums[2:5, :] = first_sums[...]
    sums[5:8, :] = second_sums[...]
    for at, column in vector_places():
        sums[at[0] : at[0] + 1, at[1] : at[1] + ROW] = inner_sums[:, column : column + ROW]
    sums[12:16, :] = jnp.zeros((4, D), jnp.float32)


def attend_back(place, context_grad, left_rows, right_rows, attention, first_sums, second_sums, inner_sums):
    tokens = context_grad.shape[0]
    part = ((tokens, 3 * D // 2), bf16, "V")
    return run(
        attend_kernel,
        "attend_back",
        placed_at("S", place)
        + placed_at("V", context_grad)
        + placed_at("V", left_rows, right_rows, attention)
        + placed_at("V", first_sums, second_sums, inner_sums),
        [part, part, ((16, D), f32, "V")],
        4e9,
        [pltpu.VMEM((3, tokens, D), bf16)],
    )


def attention_gradient_kernel(
    place,
    sums,
    hidden_t,
    other_hidden_t,
    context_t,
    other_context_t,
    grads,
    other_grads,
    residual,
    other_residual,
    left_kept,
    left_sent,
    right_kept,
    right_sent,
):
    half = D // 2
    grad = dot(hidden_t[...], grads[:, :D]) + dot(other_hidden_t[...], other_grads[:, :D])
    grad = grad.astype(jnp.bfloat16)
    left_kept[:, :D] = grad[:half]
    left_sent[:, :D] = grad[half:]
    total = sums[...].astype(jnp.bfloat16)
    total = jnp.concatenate([total, jnp.zeros((112, D), jnp.bfloat16)])
    small = dot_nt(arrange_from(place), total).astype(jnp.bfloat16)
    left_kept[:, D:] = small[:half]
    left_sent[:, D:] = small[half:]
    value = dot(hidden_t[...], grads[:, D:]) + dot(other_hidden_t[...], other_grads[:, D:])
    output = dot(context_t[...], residual[...]) + dot(other_context_t[...], other_residual[...])
    grad = jnp.concatenate([value, output], axis=1).astype(jnp.bfloat16)
    part_rows(grad, left_kept, left_sent, right_kept, right_sent, False)


def attention_gradient(*operands):
    left, right = ((D // 2, D + 128), bf16, "V"), ((D // 2, D), bf16, "V")
    places = ["S"] + ["V"] * 9
    return run(
        attention_gradient_kernel,
        "attention_gradient",
        list(zip(operands, places)),
        [left, left, right, right],
        2.5e9,
    )


def input_kernel(
    place, kept, sent, query_mat, low_key_mat, high_key_mat, value_mat, residual_grad, input_grad
):
    restore = restore_from(place)
    half = D // 2
    parts = []
    for at in range(3):
        columns = slice(at * half, (at + 1) * half)
        parts.append(both_halves(place[0], kept[:, columns], sent[:, columns]))
    query_grad, key_grad, value_grad = parts
    total = dot_nt(query_grad, query_mat[...])
    total += dot_nt(key_grad[:, :512], low_key_mat[...])
    total += dot_nt(key_grad[:, 512:], high_key_mat[...])
    total += dot_nt(value_grad, value_mat[...])
    total = residual_grad[...] + whole_precision(total, restore)
    input_grad[...] = total.astype(jnp.bfloat16)


def input_back(place, residual_grad, kept, sent, mats):
    return run(
        input_kernel,
        "input_back",
        [(place, "S")]
        + placed_at("V", kept, sent)
        + placed_at("V", *mats, residual_grad),
        [(residual_grad.shape, bf16, "H")],
        3e9,
    )[0]


def add_kernel(left, left_in, right, right_in, left_kept, left_sent, right_kept, right_sent):
    for own, received, kept, sent in (
        (left, left_in, left_kept, left_sent),
        (right, right_in, right_kept, right_sent),
    ):
        total = (own[...].astype(jnp.float32) + received[...].astype(jnp.float32)).astype(jnp.bfloat16)
        half = total.shape[0] // 2
        kept[...] = total[:half]
        sent[...] = total[half:]


def add_parts(left, left_in, right, right_in):
    shapes = [(part.shape[0] // 2,) + part.shape[1:] for part in (left, left, right, right)]
    return pl.pallas_call(
        add_kernel,
        in_specs=[VMEM] * 4,
        out_specs=[VMEM] * 4,
        out_shape=[jax.ShapeDtypeStruct(shape, jnp.bfloat16) for shape in shapes],
        compiler_params=params(),
        cost_estimate=cost(1, 1),
        name="add_parts",
    )(left, left_in, right, right_in)


def add_z_kernel(left, left_in, right, right_in, own, first, second, third):
    width = left.shape[-1]
    for part, received, columns in (
        (left, left_in, slice(0, width)),
        (right, right_in, slice(width, width + right.shape[-1])),
    ):
        rows = part.shape[0] // 4
        total = part[...].astype(jnp.float32) + received[...].astype(jnp.float32)
        own[..., columns] = total[:rows]
        for at, sent in enumerate((first, second, third)):
            sent[..., columns] = total[(at + 1) * rows : (at + 2) * rows].astype(jnp.bfloat16)


def add_z(left, left_in, right, right_in):
    shape = (left.shape[0] // 4,) + left.shape[1:-1] + (left.shape[-1] + right.shape[-1],)
    return pl.pallas_call(
        add_z_kernel,
        in_specs=[VMEM] * 4,
        out_specs=[VMEM] * 4,
        out_shape=[jax.ShapeDtypeStruct(shape, jnp.float32)]
        + [jax.ShapeDtypeStruct(shape, jnp.bfloat16)] * 3,
        compiler_params=params(),
        cost_estimate=cost(1, 1),
        name="add_z",
    )(left, left_in, right, right_in)


def add_join_kernel(left, left_in, right, right_in, kept, sent):
    width = left.shape[-1]
    for part, received, columns in (
        (left, left_in, slice(0, width)),
        (right, right_in, slice(width, width + right.shape[-1])),
    ):
        rows = part.shape[0] // 4
        total = part[...].astype(jnp.float32) + received[...].astype(jnp.float32)
        for at in range(2):
            to, start = slice(at * rows, (at + 1) * rows), 2 * at * rows
            kept[to, ..., columns] = total[start : start + rows]
            sent[to, ..., columns] = total[start + rows : start + 2 * rows].astype(jnp.bfloat16)


def add_join(left, left_in, right, right_in):
    shape = (left.shape[0] // 2,) + left.shape[1:-1] + (left.shape[-1] + right.shape[-1],)
    return pl.pallas_call(
        add_join_kernel,
        in_specs=[VMEM] * 4,
        out_specs=[VMEM] * 2,
        out_shape=[jax.ShapeDtypeStruct(shape, jnp.float32), jax.ShapeDtypeStruct(shape, jnp.bfloat16)],
        compiler_params=params(),
        cost_estimate=cost(1, 1),
        name="add_join",
    )(left, left_in, right, right_in)


def add_half_kernel(own, received, kept, sent):
    rows = own.shape[0] // 2
    total = own[...] + received[...].astype(jnp.float32)
    kept[...] = total[:rows]
    sent[...] = total[rows:].astype(jnp.bfloat16)


def add_half(own, received):
    shape = (own.shape[0] // 2,) + own.shape[1:]
    return pl.pallas_call(
        add_half_kernel,
        in_specs=[VMEM] * 2,
        out_specs=[VMEM] * 2,
        out_shape=[jax.ShapeDtypeStruct(shape, jnp.float32), jax.ShapeDtypeStruct(shape, jnp.bfloat16)],
        compiler_params=params(),
        cost_estimate=cost(1, 1),
        name="add_half",
    )(own, received)


def finish_kernel(place, own, *refs):
    received_all, (mine, other) = refs[:-2], refs[-2:]
    total = own[...]
    for received in received_all:
        total = total + received[...].astype(jnp.float32)
    if len(total.shape) == 3:
        low, high = total[0], total[1]
    else:
        low, high = total[:ROW], total[ROW:]
    mine[...] = pick(place[0], low, high)
    other[...] = pick(place[0], high, low)


def finish(place, own, received):
    rows = own.shape[1] if own.ndim == 3 else ROW
    return pl.pallas_call(
        finish_kernel,
        in_specs=[SMEM] + [VMEM] * (1 + len(received)),
        out_specs=[VMEM] * 2,
        out_shape=[jax.ShapeDtypeStruct((rows, own.shape[-1]), jnp.float32)] * 2,
        compiler_params=params(),
        cost_estimate=cost(1, 1),
        name="finish",
    )(place, own, *received)


def put(place, out, mine, received):
    half = mine.shape[1]
    out[:, :half] = pick(place[0], mine, received)
    out[:, half:] = pick(place[0], received, mine)


def outer_out_kernel(place, mine, received, out):
    rows, half = mine.shape[0], mine.shape[1] // 2
    for at in range(2):
        columns = slice(at * half, (at + 1) * half)
        put(place, out.at[at * rows : (at + 1) * rows], mine[:, columns], received[:, columns])


def inner_out_kernel(place, mine, received, out):
    put(place, out, mine[...], received[...])


def rest_out_kernel(place, mine, received, query, key, value, output, inner_bias, *vectors):
    half = D // 2
    for out, at in ((query, 0), (key, half), (value, D + 128), (output, D + 128 + half)):
        columns = slice(at, at + half)
        put(place, out, mine[:, columns], received[:, columns])
    turned = jnp.transpose(mine[:, D : D + 128] + received[:, D : D + 128])
    for at, out in enumerate(vectors):
        out[...] = turned[at : at + 1]
    for at in range(4):
        inner_bias[:, at * ROW : (at + 1) * ROW] = turned[8 + at : 9 + at]


def placed(kernel, name, place, mine, received, shapes):
    return pl.pallas_call(
        kernel,
        in_specs=[SMEM, VMEM, VMEM],
        out_specs=[VMEM] * len(shapes),
        out_shape=[jax.ShapeDtypeStruct(shape, jnp.float32) for shape in shapes],
        compiler_params=params(),
        cost_estimate=cost(1, 1),
        name=name,
    )(place, mine, received)


def first_transfers(pieces):
    return [mate(pieces[1]), across(pieces[3], 2)]


def add_first(pieces, received):
    return add_parts(pieces[0], received[0], pieces[2], received[1])


def second_transfers(pieces):
    return [across(pieces[1], 2), mate(pieces[3])]


def add_joined(pieces, received):
    return add_join(pieces[0], received[0], pieces[2], received[1])


def add_second(pieces, received):
    return add_z(pieces[0], received[0], pieces[2], received[1])


def third_transfers(parts):
    return [across(sent, mask) for sent, mask in zip(parts[1:], (4, 8, 12))]


def fast_device(
    hidden_in,
    cotangent,
    span_lengths,
    partner_span,
    query_weight,
    query_bias,
    key_weight,
    value_weight,
    value_bias,
    output_weight,
    output_bias,
    first_gain,
    first_shift,
    inner_weight,
    inner_bias,
    outer_weight,
    outer_bias,
    second_gain,
    second_shift,
):
    core, x_at, z_at, y_at = coordinates()
    place = jnp.stack([core, y_at, x_at, z_at]).astype(jnp.int32)
    first_block, second_block = pack(
        query_weight,
        key_weight,
        value_weight,
        output_weight,
        inner_weight,
        inner_bias,
        (
            query_bias,
            value_bias,
            output_bias,
            first_gain,
            first_shift,
            outer_bias,
            second_gain,
            second_shift,
        ),
    )
    ff = inner_weight.shape[1]
    first_z = z_exchange(first_block)
    first = stack_z(first_block, first_z, FIRST_HALF)
    second_block, third_block = tied((second_block, outer_weight), *first)
    first_in = near_exchange(first)
    second_z = across(second_block, 8)
    *first, first_both = stack_near(first, tied(first_in, second_z))
    second_two = stack_z_two(after(second_block, *first), second_z)
    first = tied(first, second_two)
    first_far = far_exchange(first)
    second_z = across(second_two, 4)
    first_core = across(first_both, 1)
    second = stack_mixed(second_two, after(second_z, first_core, *first_far), SECOND_HALF)
    first_far, third_block = tied(first_far, *second), after(third_block, *second)
    second_in = near_exchange(second)
    first_far_core = core_exchange(first_far)
    third_z = across(after(third_block, *first_far_core), 8)
    third_two = stack_z_two(third_block, third_z)
    left_rows, right_rows, vectors, hidden_t, *first_mats = project(
        place, hidden_in, pieces_of(first, first_far, first_core, first_far_core)
    )
    *second, second_both = stack_near(second, tied(second_in, vectors, third_two))
    third_two, left_rows = tied((third_two, left_rows), *second)
    second_far = far_exchange(second)
    third_z = across(third_two, 4)
    second_core = across(second_both, 1)
    attention, context_arrived, context_t = attention_forward(
        place, span_lengths, left_rows, right_rows
    )
    third = stack_mixed(
        third_two, after(third_z, context_arrived, second_core, *second_far), D // 2
    )
    second_far = tied(second_far, *third)
    third_in = near_exchange(third)
    second_far_core = core_exchange(second_far)
    second_pieces = pieces_of(second, second_far, second_core, second_far_core)
    moved, first_normed, first_factor, first_t, output_mat = residual_forward(
        place, hidden_in, context_arrived, vectors, second_pieces
    )
    *third, third_both = stack_near(third, tied(third_in, moved, *second_far_core))
    moved = after(moved, *third)
    third_far = far_exchange(third)
    third_core = across(third_both, 1)
    active, active_t, slope, *inner_mats = feed_forward(moved, vectors, ff, second_pieces)
    second_mats = [output_mat, *inner_mats]
    third_far = tied(third_far, active, third_core)
    third_far_core = core_exchange(third_far)
    third_pieces = pieces_of(third, third_far, third_core, third_far_core)
    hidden_t, context_t, first_t, active_t, active = tied(
        (hidden_t, context_t, first_t, active_t, active), *third_far_core
    )
    other_active_t, other_first_t = across(active_t, 1), across(first_t, 1)
    other_hidden_t, other_context_t = across(hidden_t, 1), across(context_t, 1)
    layer_out, second_normed, second_factor, cls_rows, outer_mat = last(
        place, active, first_normed, vectors, third_pieces
    )
    other_rows = mate(cls_rows)
    second_grad, second_kept, second_sent, second_sums, span_loss = turn(
        place, partner_span, cotangent, second_normed, second_factor, vectors, cls_rows, other_rows
    )
    second_received = across(second_sent, 1)
    preact_kept, preact_sent, inner_sums = slope_back(
        place, second_kept, second_sent, outer_mat, slope
    )
    second_received = after(second_received, preact_kept)
    outer_parts = outer_gradient(place, active_t, other_active_t, second_kept, second_received)
    preact_kept, preact_sent = tied((preact_kept, preact_sent), *outer_parts)
    outer_in = first_transfers(outer_parts)
    preact_received = across(preact_sent, 1)
    residual_grad, residual_kept, residual_sent, context_grad, first_sums = first_back(
        place,
        preact_kept,
        preact_sent,
        second_grad,
        first_normed,
        first_factor,
        vectors,
        second_mats,
    )
    residual_received = across(residual_sent, 1)
    preact_kept = after(preact_kept, context_grad)
    inner_parts = inner_gradient(first_t, other_first_t, preact_kept, preact_received)
    outer_parts = add_first(outer_parts, tied(outer_in, residual_received, *inner_parts))
    inner_parts, context_grad = tied(inner_parts, *outer_parts), after(context_grad, *outer_parts)
    outer_in = second_transfers(outer_parts)
    inner_in = first_transfers(inner_parts)
    grads_kept, grads_sent, sums = attend_back(
        place,
        context_grad,
        left_rows,
        right_rows,
        attention,
        first_sums,
        second_sums,
        inner_sums,
    )
    outer_own, outer_sent = add_joined(outer_parts, tied(outer_in, sums))
    inner_parts = add_first(inner_parts, tied(inner_in, outer_own))
    outer_sent, grads_sent = tied((outer_sent, grads_sent), *inner_parts)
    inner_in = second_transfers(inner_parts)
    outer_in = across(outer_sent, 4)
    grads_received = across(grads_sent, 1)
    rest_parts = attention_gradient(
        place,
        sums,
        hidden_t,
        other_hidden_t,
        context_t,
        other_context_t,
        grads_kept,
        grads_received,
        residual_kept,
        residual_received,
    )
    inner_own, inner_sent = add_joined(inner_parts, tied(inner_in, outer_in, *rest_parts))
    outer_own, outer_sent = add_half(outer_own, after(outer_in, inner_own))
    rest_parts = tied(rest_parts, outer_own)
    inner_sent, grads_kept = tied((inner_sent, grads_kept), outer_own)
    rest_in = first_transfers(rest_parts)
    inner_in = across(inner_sent, 4)
    outer_in = across(outer_sent, 8)
    input_grad = input_back(place, residual_grad, grads_kept, grads_sent, first_mats)
    rest_parts = add_first(rest_parts, tied(rest_in, input_grad, outer_in, inner_in))
    inner_own, inner_in, outer_own, outer_in = tied(
        (inner_own, inner_in, outer_own, outer_in), *rest_parts
    )
    rest_in = second_transfers(rest_parts)
    inner_own, inner_sent = add_half(inner_own, inner_in)
    inner_in = across(inner_sent, 8)
    outer_mine, outer_other = finish(place, outer_own, [outer_in])
    outer_other = across(outer_other, 1)
    rest_parts = add_second(rest_parts, tied(rest_in, inner_in, outer_other))
    inner_in, outer_other = tied((inner_in, outer_other), *rest_parts)
    rest_in = third_transfers(rest_parts)
    inner_mine, inner_other = finish(place, inner_own, [inner_in])
    inner_other = across(inner_other, 1)
    (outer_grad,) = placed(
        outer_out_kernel, "outer_out", place, outer_mine, outer_other, [(4 * ROW, D)]
    )
    (inner_grad,) = placed(
        inner_out_kernel, "inner_out", place, inner_mine, after(inner_other, outer_grad), [(ROW, ff)]
    )
    rest_mine, rest_other = finish(place, rest_parts[0], tied(rest_in, inner_grad))
    rest_other = across(rest_other, 1)
    query_grad, key_grad, value_grad, output_grad, inner_bias_grad, *vector_grads = placed(
        rest_out_kernel,
        "rest_out",
        place,
        rest_mine,
        rest_other,
        [(ROW, D)] * 4 + [(1, 4 * ROW)] + [(1, ROW)] * 8,
    )
    vector_grads = [grad.reshape(-1) for grad in vector_grads]
    return (
        layer_out,
        input_grad,
        span_loss.reshape(-1),
        query_grad,
        vector_grads[0],
        key_grad,
        value_grad,
        vector_grads[1],
        output_grad,
        vector_grads[2],
        vector_grads[3],
        vector_grads[4],
        inner_grad,
        inner_bias_grad.reshape(-1),
        outer_grad,
        vector_grads[5],
        vector_grads[6],
        vector_grads[7],
    )


def solution(mesh):
    is_block = mesh.shape["doc"] == 2 * PLACES and mesh.shape["pair"] == 2
    return jax.shard_map(
        fast_device if is_block else per_device,
        mesh=mesh,
        in_specs=(
            P(("doc", "pair"), None),
            P(("doc", "pair"), None),
            P(("doc", "pair")),
            P("doc", None),
            P(("doc", "pair"), None),
            P(("doc", "pair")),
            P(("doc", "pair"), None),
            P(("doc", "pair"), None),
            P(("doc", "pair")),
            P(("doc", "pair"), None),
            P(("doc", "pair")),
            P(("doc", "pair")),
            P(("doc", "pair")),
            P(("doc", "pair"), None),
            P(("doc", "pair")),
            P(("doc", "pair"), None),
            P(("doc", "pair")),
            P(("doc", "pair")),
            P(("doc", "pair")),
        ),
        out_specs=(
            P(("doc", "pair"), None),
            P(("doc", "pair"), None),
            P(("doc", "pair")),
            P(("doc", "pair"), None),
            P(("doc", "pair")),
            P(("doc", "pair"), None),
            P(("doc", "pair"), None),
            P(("doc", "pair")),
            P(("doc", "pair"), None),
            P(("doc", "pair")),
            P(("doc", "pair")),
            P(("doc", "pair")),
            P(("doc", "pair"), None),
            P(("doc", "pair")),
            P(("doc", "pair"), None),
            P(("doc", "pair")),
            P(("doc", "pair")),
            P(("doc", "pair")),
        ),
        check_vma=False,
    )
```

```python
from functools import partial
import math

import jax
import jax.numpy as jnp
from jax import lax
from jax.experimental import pallas as pl
from jax.experimental.pallas import tpu as pltpu
from jax.sharding import PartitionSpec as P

D = 768
HEAD_DIM = 64
SPAN = 128
SPANS_ROW = 4


epsilon = 1e-06
masked_out = -1000000000.0
highest = lax.Precision.HIGHEST


def across(block, mask):
    count = lax.axis_size("doc")
    return lax.ppermute(block, "doc", [(at, at ^ mask) for at in range(count)])


def mate(block):
    return lax.ppermute(block, "pair", [(0, 1), (1, 0)])


def far_groups():
    bits = lax.axis_size("doc").bit_length() - 1
    far = [1 << at for at in range(2, bits)]
    return [far[at : at + 2] for at in range(0, len(far), 2)]


def is_upper(mask):
    return (lax.axis_index("doc") & mask) != 0


def joined(own, other, upper):
    return jnp.where(upper, jnp.stack([other, own]), jnp.stack([own, other]))


def gather_rows(block):
    rows, columns = block.shape
    total = block[None]
    for masks in far_groups():
        low = masks[0]
        near = joined(total, across(total, low), is_upper(low))
        if len(masks) == 2:
            high = masks[1]
            straight, crossed = across(total, high), across(total, high | low)
            far = joined(straight, crossed, is_upper(low))
            near = joined(near, far, is_upper(high)).reshape((4,) + total.shape)
        total = near.reshape((-1, rows, columns))
    half = columns // 2
    left, right = total[..., :half], total[..., half:]
    on_pair = lax.axis_index("pair") == 1
    left_x, right_y = across(left, 2), mate(right)
    left, right = joined(left, left_x, is_upper(2)), joined(right, right_y, on_pair)
    left_y, right_x = mate(left), across(right, 2)
    left, right = joined(left, left_y, on_pair), joined(right, right_x, is_upper(2))
    left = joined(left, across(left, 1), is_upper(1))
    right = joined(right, across(right, 1), is_upper(1))
    left = jnp.transpose(left, (3, 2, 0, 1, 4, 5))
    right = jnp.transpose(right, (3, 1, 0, 2, 4, 5))
    return jnp.concatenate([left, right], axis=-1).reshape(-1, rows, columns)


def halves(blocks, axis, upper):
    lower = lax.index_in_dim(blocks, 0, axis, keepdims=False)
    higher = lax.index_in_dim(blocks, 1, axis, keepdims=False)
    return (jnp.where(upper, higher, lower), jnp.where(upper, lower, higher))


def plus(kept, received):
    return kept.astype(jnp.float32) + received.astype(jnp.float32)


def scatter_rows(blocks):
    rows, columns = blocks.shape[1:]
    on_pair = lax.axis_index("pair") == 1
    blocks = blocks.astype(jnp.bfloat16).reshape(-1, 2, 2, 2, rows, columns)
    kept, sent = halves(blocks, 2, is_upper(1))
    total = plus(kept, across(sent, 1)).astype(jnp.bfloat16)
    half = columns // 2
    left, right = total[..., :half], total[..., half:]
    left_kept, left_sent = halves(left, 2, on_pair)
    right_kept, right_sent = halves(right, 1, is_upper(2))
    left = plus(left_kept, mate(left_sent)).astype(jnp.bfloat16)
    right = plus(right_kept, across(right_sent, 2)).astype(jnp.bfloat16)
    left_kept, left_sent = halves(left, 1, is_upper(2))
    right_kept, right_sent = halves(right, 1, on_pair)
    left = plus(left_kept, across(left_sent, 2))
    right = plus(right_kept, mate(right_sent))
    total = jnp.concatenate([left, right], axis=-1)
    for masks in far_groups()[::-1]:
        total = total.astype(jnp.bfloat16).reshape(2 ** len(masks), -1, rows, columns)
        place = (lax.axis_index("doc") // masks[0]) % 2 ** len(masks)
        summed = lax.dynamic_index_in_dim(total, place, 0, keepdims=False).astype(jnp.float32)
        for step in range(1, 2 ** len(masks)):
            sent = lax.dynamic_index_in_dim(total, place ^ step, 0, keepdims=False)
            summed = plus(summed, across(sent, masks[0] * step))
        total = summed
    return total.reshape(rows, columns)


VECTORS = (1, 4, 6, 7, 8, 10, 12, 13, 14)


def pack_vectors(pieces):
    flat = jnp.concatenate(pieces, axis=-1)
    width = -(-flat.shape[-1] // D) * D
    flat = jnp.pad(flat, [(0, 0)] * (flat.ndim - 1) + [(0, width - flat.shape[-1])])
    return flat.reshape(flat.shape[:-1] + (-1, D))


def fold(matrix):
    return jnp.concatenate([matrix[:, at : at + D] for at in range(0, matrix.shape[1], D)])


def collect(shards):
    rows = shards[0].shape[0]
    devices = lax.axis_size("doc") * lax.axis_size("pair")
    small = pack_vectors([shards[at] for at in VECTORS])
    first = gather_rows(jnp.concatenate([shards[0], shards[2], shards[3], small]))
    second = gather_rows(jnp.concatenate([shards[5], fold(shards[9])]))
    outer = lax.all_gather(shards[11], ("doc", "pair"), axis=0, tiled=True)
    whole = {
        0: first[:, :rows].reshape(-1, D),
        2: first[:, rows : 2 * rows].reshape(-1, D),
        3: first[:, 2 * rows : 3 * rows].reshape(-1, D),
        5: second[:, :rows].reshape(-1, D),
        9: jnp.concatenate(
            [
                second[:, at : at + rows].reshape(-1, D)
                for at in range(rows, second.shape[1], rows)
            ],
            axis=1,
        ),
        11: outer,
    }
    vectors, start = first[:, 3 * rows :].reshape(devices, -1), 0
    for at in VECTORS:
        size = shards[at].shape[0]
        whole[at] = vectors[:, start : start + size].reshape(-1).astype(jnp.float32)
        start += size
    return tuple(whole[at] for at in range(15))


def spread(gradients):
    devices = lax.axis_size("doc") * lax.axis_size("pair")
    by_device = [
        piece.reshape((devices, -1) + piece.shape[1:]) for piece in gradients
    ]
    rows = by_device[0].shape[1]
    outer = scatter_rows(by_device[11])
    inner = by_device[9]
    parts = [inner[..., at : at + D] for at in range(0, inner.shape[-1], D)]
    second = scatter_rows(jnp.concatenate([by_device[5]] + parts, axis=1))
    small = pack_vectors([by_device[at] for at in VECTORS])
    first = scatter_rows(
        jnp.concatenate([by_device[0], by_device[2], by_device[3], small], axis=1)
    )
    own = {
        0: first[:rows],
        2: first[rows : 2 * rows],
        3: first[2 * rows : 3 * rows],
        5: second[:rows],
        9: jnp.concatenate(
            [second[at : at + rows] for at in range(rows, second.shape[0], rows)], axis=1
        ),
        11: outer,
    }
    vectors, start = first[3 * rows :].reshape(-1), 0
    for at in VECTORS:
        size = by_device[at].shape[1]
        own[at] = vectors[start : start + size]
        start += size
    return tuple(own[at] for at in range(15))


def normalize(hidden, gain, shift):
    average = jnp.mean(hidden, axis=-1, keepdims=True)
    centred = hidden - average
    factor = lax.rsqrt(jnp.mean(centred * centred, axis=-1, keepdims=True) + epsilon)
    normed = centred * factor
    return (normed * gain + shift, normed, factor)


def normalize_back(upstream, normed, factor, gain):
    scaled = upstream * gain
    hidden_grad = factor * (
        scaled
        - jnp.mean(scaled, axis=-1, keepdims=True)
        - normed * jnp.mean(scaled * normed, axis=-1, keepdims=True)
    )
    return (hidden_grad, jnp.sum(upstream * normed, axis=0), jnp.sum(upstream, axis=0))


def head_scores(query_row, key_row, live_row):
    product = jnp.einsum("sqhd,skhd->shqk", query_row, key_row, preferred_element_type=jnp.float32)
    return jnp.where(live_row[:, None, None, :], product * HEAD_DIM ** (-0.5), masked_out)


def encode(hidden_in, allowed, gathered):
    (
        query_mat,
        query_add,
        key_mat,
        value_mat,
        value_add,
        output_mat,
        output_add,
        gain_one,
        shift_one,
        inner_mat,
        inner_add,
        outer_mat,
        outer_add,
        gain_two,
        shift_two,
    ) = gathered
    row_count = allowed.shape[0]
    shaped = (row_count, SPANS_ROW, SPAN, D // HEAD_DIM, HEAD_DIM)
    queries = (
        jnp.dot(hidden_in, query_mat, preferred_element_type=jnp.float32) + query_add
    ).astype(jnp.bfloat16)
    key_rows = jnp.dot(hidden_in, key_mat, preferred_element_type=jnp.float32).astype(jnp.bfloat16)
    value_rows = (
        jnp.dot(hidden_in, value_mat, preferred_element_type=jnp.float32) + value_add
    ).astype(jnp.bfloat16)

    def attend(element):
        query_row, key_row, value_row, live_row = element
        scores = head_scores(query_row, key_row, live_row)
        highest_score = jnp.max(scores, axis=-1, keepdims=True)
        exponent = jnp.exp(scores - highest_score)
        totals = jnp.sum(exponent, axis=-1, keepdims=True)
        attention = (exponent / totals).astype(jnp.bfloat16)
        context_row = jnp.einsum(
            "shqk,skhd->sqhd", attention, value_row, preferred_element_type=jnp.float32
        )
        return (context_row.astype(jnp.bfloat16), (highest_score + jnp.log(totals))[..., 0])

    context, logsum = lax.map(
        attend,
        (queries.reshape(shaped), key_rows.reshape(shaped), value_rows.reshape(shaped), allowed),
    )
    context = context.reshape(-1, D)
    residual = (
        hidden_in.astype(jnp.float32)
        + jnp.dot(context, output_mat, preferred_element_type=jnp.float32)
        + output_add
    )
    first_out, first_normed, first_factor = normalize(residual, gain_one, shift_one)
    first16 = first_out.astype(jnp.bfloat16)
    preact = jnp.dot(first16, inner_mat, preferred_element_type=jnp.float32) + inner_add
    active = jax.nn.gelu(preact, approximate=False).astype(jnp.bfloat16)
    second = first_out + jnp.dot(active, outer_mat, preferred_element_type=jnp.float32) + outer_add
    encoded, second_normed, second_factor = normalize(second, gain_two, shift_two)
    stored = (
        queries,
        key_rows,
        value_rows,
        logsum,
        context,
        first_normed,
        first_factor,
        first16,
        preact,
        active,
        second_normed,
        second_factor,
    )
    return (encoded, stored)


def backward(hidden_in, allowed, gathered, stored, out_gradient):
    (
        query_mat,
        query_add,
        key_mat,
        value_mat,
        value_add,
        output_mat,
        output_add,
        gain_one,
        shift_one,
        inner_mat,
        inner_add,
        outer_mat,
        outer_add,
        gain_two,
        shift_two,
    ) = gathered
    (
        queries,
        key_rows,
        value_rows,
        logsum,
        context,
        first_normed,
        first_factor,
        first16,
        preact,
        active,
        second_normed,
        second_factor,
    ) = stored
    row_count = allowed.shape[0]
    shaped = (row_count, SPANS_ROW, SPAN, D // HEAD_DIM, HEAD_DIM)
    second_grad, gain_two_grad, shift_two_grad = normalize_back(
        out_gradient, second_normed, second_factor, gain_two
    )
    outer_add_grad = jnp.sum(second_grad, axis=0)
    second16 = second_grad.astype(jnp.bfloat16)
    outer_mat_grad = jnp.dot(active.T, second16, preferred_element_type=jnp.float32)
    active_grad = jnp.dot(second16, outer_mat.T, preferred_element_type=jnp.float32)
    unused, gelu_back = jax.vjp(partial(jax.nn.gelu, approximate=False), preact)
    preact_grad = gelu_back(active_grad)[0]
    inner_add_grad = jnp.sum(preact_grad, axis=0)
    preact16 = preact_grad.astype(jnp.bfloat16)
    inner_mat_grad = jnp.dot(first16.T, preact16, preferred_element_type=jnp.float32)
    first_grad = second_grad + jnp.dot(preact16, inner_mat.T, preferred_element_type=jnp.float32)
    residual_grad, gain_one_grad, shift_one_grad = normalize_back(
        first_grad, first_normed, first_factor, gain_one
    )
    output_add_grad = jnp.sum(residual_grad, axis=0)
    residual16 = residual_grad.astype(jnp.bfloat16)
    output_mat_grad = jnp.dot(context.T, residual16, preferred_element_type=jnp.float32)
    context_grad = jnp.dot(residual16, output_mat.T, preferred_element_type=jnp.float32).astype(
        jnp.bfloat16
    )

    def attend_back(element):
        query_row, key_row, value_row, live_row, logsum_row, context_row = element
        scores = head_scores(query_row, key_row, live_row)
        attention = jnp.exp(scores - logsum_row[..., None])
        attention16 = attention.astype(jnp.bfloat16)
        value_grad = jnp.einsum(
            "shqk,sqhd->skhd", attention16, context_row, preferred_element_type=jnp.float32
        )
        attention_grad = jnp.einsum(
            "sqhd,skhd->shqk", context_row, value_row, preferred_element_type=jnp.float32
        )
        weighted = jnp.sum(attention * attention_grad, axis=-1, keepdims=True)
        scores_grad = (attention * (attention_grad - weighted)).astype(jnp.bfloat16)
        query_grad = jnp.einsum(
            "shqk,skhd->sqhd", scores_grad, key_row, preferred_element_type=jnp.float32
        ) * HEAD_DIM ** (-0.5)
        key_grad = jnp.einsum(
            "shqk,sqhd->skhd", scores_grad, query_row, preferred_element_type=jnp.float32
        ) * HEAD_DIM ** (-0.5)
        return (
            query_grad.astype(jnp.bfloat16),
            key_grad.astype(jnp.bfloat16),
            value_grad.astype(jnp.bfloat16),
        )

    query_grad, key_grad, value_grad = lax.map(
        attend_back,
        (
            queries.reshape(shaped),
            key_rows.reshape(shaped),
            value_rows.reshape(shaped),
            allowed,
            logsum,
            context_grad.reshape(shaped),
        ),
    )
    query_grad = query_grad.reshape(-1, D)
    key_grad = key_grad.reshape(-1, D)
    value_grad = value_grad.reshape(-1, D)
    query_add_grad = jnp.sum(query_grad.astype(jnp.float32), axis=0)
    value_add_grad = jnp.sum(value_grad.astype(jnp.float32), axis=0)
    query_mat_grad = jnp.dot(hidden_in.T, query_grad, preferred_element_type=jnp.float32)
    key_mat_grad = jnp.dot(hidden_in.T, key_grad, preferred_element_type=jnp.float32)
    value_mat_grad = jnp.dot(hidden_in.T, value_grad, preferred_element_type=jnp.float32)
    input_grad = (
        residual_grad
        + jnp.dot(query_grad, query_mat.T, preferred_element_type=jnp.float32)
        + jnp.dot(key_grad, key_mat.T, preferred_element_type=jnp.float32)
        + jnp.dot(value_grad, value_mat.T, preferred_element_type=jnp.float32)
    )
    gradients = (
        query_mat_grad,
        query_add_grad,
        key_mat_grad,
        value_mat_grad,
        value_add_grad,
        output_mat_grad,
        output_add_grad,
        gain_one_grad,
        shift_one_grad,
        inner_mat_grad,
        inner_add_grad,
        outer_mat_grad,
        outer_add_grad,
        gain_two_grad,
        shift_two_grad,
    )
    return (input_grad, gradients)


def per_device(
    hidden_in,
    cotangent,
    span_lengths,
    partner_span,
    query_weight,
    query_bias,
    key_weight,
    value_weight,
    value_bias,
    output_weight,
    output_bias,
    first_gain,
    first_shift,
    inner_weight,
    inner_bias,
    outer_weight,
    outer_bias,
    second_gain,
    second_shift,
):
    shards = (
        query_weight,
        query_bias,
        key_weight,
        value_weight,
        value_bias,
        output_weight,
        output_bias,
        first_gain,
        first_shift,
        inner_weight,
        inner_bias,
        outer_weight,
        outer_bias,
        second_gain,
        second_shift,
    )
    length = SPAN * SPANS_ROW
    row_count = hidden_in.shape[0] // length
    allowed = jnp.arange(SPAN)[None, None, :] < span_lengths.reshape(row_count, SPANS_ROW, 1)
    gathered = collect(shards)
    encoded, stored = encode(hidden_in, allowed, gathered)
    cls_rows = (
        encoded.reshape(row_count, SPANS_ROW, SPAN, D)[:, :, 0, :]
        .reshape(-1, D)
        .astype(jnp.bfloat16)
    )
    other_rows = mate(cls_rows)
    logits = jnp.dot(cls_rows, other_rows.T, preferred_element_type=jnp.float32) / math.sqrt(D)
    span_count = cls_rows.shape[0]
    matches = (partner_span.reshape(span_count, 1) == jnp.arange(span_count)[None, :]).astype(
        jnp.float32
    )
    target = jnp.where(lax.axis_index("pair") == 0, matches, matches.T)
    highest_logit = jnp.max(logits, axis=-1, keepdims=True)
    exponent = jnp.exp(logits - highest_logit)
    totals = jnp.sum(exponent, axis=-1, keepdims=True)
    span_loss = highest_logit[:, 0] + jnp.log(totals[:, 0]) - jnp.sum(target * logits, axis=-1)
    softened = exponent / totals - target
    own_grad = jnp.dot(softened, other_rows.astype(jnp.float32), precision=highest)
    other_logits = logits.T
    other_highest = jnp.max(other_logits, axis=-1, keepdims=True)
    other_exponent = jnp.exp(other_logits - other_highest)
    other_softened = (
        other_exponent / jnp.sum(other_exponent, axis=-1, keepdims=True) - target.T
    )
    back_grad = jnp.dot(
        other_softened.T, other_rows.astype(jnp.float32), precision=highest
    ).astype(jnp.bfloat16)
    cls_gradient = (own_grad + back_grad.astype(jnp.float32)).reshape(row_count, SPANS_ROW, 1, D)
    placed = jnp.concatenate(
        [cls_gradient, jnp.zeros((row_count, SPANS_ROW, SPAN - 1, D), jnp.float32)], axis=2
    )
    out_gradient = cotangent.astype(jnp.float32) + placed.reshape(-1, D)
    input_grad, gradients = backward(hidden_in, allowed, gathered, stored, out_gradient)
    reduced = spread(gradients)
    return (encoded.astype(jnp.bfloat16), input_grad.astype(jnp.bfloat16), span_loss) + tuple(
        reduced
    )


ROW = 24
PLACES = 8


def coordinates():
    doc = lax.axis_index("doc")
    return (doc & 1, (doc >> 1) & 1, doc >> 2, lax.axis_index("pair"))


def blocks_of(row):
    block = (row * 2731) >> 16
    return (block >> 1) & 1, block & 1, (block >> 2) & 1, block >> 3, row - block * ROW


def restore_from(place):
    row = lax.broadcasted_iota(jnp.int32, (D, 1), 0)
    core, y_at, x_at, z_at, inside = blocks_of(row)
    offset = ((core ^ place[0]) * 2 + (y_at ^ place[1])) * 2 + (x_at ^ place[2])
    arrived = (offset * 4 + (z_at ^ place[3])) * ROW + inside
    hit = arrived == lax.broadcasted_iota(jnp.int32, (D, D), 1)
    return jnp.where(hit, 1.0, 0.0).astype(jnp.bfloat16)


def arrange_from(place):
    row = lax.broadcasted_iota(jnp.int32, (1, D), 1)
    core, y_at, x_at, z_at, inside = blocks_of(row)
    offset = ((y_at ^ place[1]) * 2 + (x_at ^ place[2])) * 4 + (z_at ^ place[3])
    leaving = offset * 2 * ROW + core * ROW + inside
    hit = leaving == lax.broadcasted_iota(jnp.int32, (D, D), 0)
    return jnp.where(hit, 1.0, 0.0).astype(jnp.bfloat16)


def after(value, *others):
    return lax.optimization_barrier((value,) + others)[0]


def z_exchange(block, masks=(4, 8, 12)):
    return [across(block, mask) for mask in masks]


def tied(values, *others):
    return lax.optimization_barrier(tuple(values) + others)[: len(values)]


def near_exchange(block):
    return across(block[0], 2), mate(block[1])


def stack_near(block, received):
    return stack_pair(block[0], received[0], block[1], received[1])


def far_exchange(block):
    return mate(block[0]), across(block[1], 2)


def core_exchange(block):
    return [across(part, 1) for part in block]


def pieces_of(near, far, core, far_core):
    return [near[0], far[0], near[1], far[1], core, far_core[0], far_core[1]]


VMEM = pl.BlockSpec(memory_space=pltpu.VMEM)
SMEM = pl.BlockSpec(memory_space=pltpu.SMEM)


def full(shape):
    return pl.BlockSpec(shape, lambda *at: (0,) * len(shape))


class Fetched:
    def __init__(self, source, held, semaphore):
        self.copy, self.held, self.waiting = pltpu.make_async_copy(source, held, semaphore), held, True
        self.shape = held.shape
        self.copy.start()

    def ready(self):
        if self.waiting:
            self.copy.wait()
            self.waiting = False
        return self.held

    def __getitem__(self, at):
        return self.ready()[at]


class Stored:
    def __init__(self, target, held, semaphores):
        self.target, self.held, self.semaphores, self.copies = target, held, semaphores, []
        self.shape = held.shape

    def __getitem__(self, at):
        return self.held[at]

    def __setitem__(self, at, value):
        self.held[at] = value

    def done(self, at=None):
        semaphore = self.semaphores.at[len(self.copies)]
        held, target = (self.held, self.target) if at is None else (self.held.at[at], self.target.at[at])
        self.copies.append(pltpu.make_async_copy(held, target, semaphore))
        self.copies[-1].start()


PARTS = 8


def ready(ref):
    return ref.ready() if isinstance(ref, Fetched) else ref


def run(kernel, name, operands, results, flops, scratch=(), mib=12, total=None):
    in_hbm = pl.BlockSpec(memory_space=pltpu.HBM)
    spaces = {"S": SMEM, "V": VMEM, "H": in_hbm, "A": in_hbm}
    spaces["K"] = VMEM
    in_places = [place for _, place in operands]
    out_places = [place for _, _, place in results]
    staged = [pltpu.VMEM(array.shape, array.dtype) for array, place in operands if place == "H"]
    made = [pltpu.VMEM(shape, dtype) for shape, dtype, place in results if place == "H"]
    semaphores = [pltpu.SemaphoreType.DMA((max(1, len(staged)),))]
    semaphores += [pltpu.SemaphoreType.DMA((max(1, len(made)), PARTS))]

    def body(*refs):
        ins, refs = refs[: len(operands)], refs[len(operands) :]
        outs, refs = refs[: len(results)], refs[len(results) :]
        held_in, refs = refs[: len(staged)], refs[len(staged) :]
        held_out, refs = refs[: len(made)], refs[len(made) :]
        fetching, storing, own = refs[0], refs[1], refs[2:]
        arguments, at = [], 0
        for ref, place in zip(ins, in_places):
            if place == "H":
                ref, at = Fetched(ref, held_in[at], fetching.at[at]), at + 1
            arguments.append(ref)
        inputs, at = list(arguments), 0
        for ref, place in zip(outs, out_places):
            if place == "H":
                ref, at = Stored(ref, held_out[at], storing.at[at]), at + 1
            arguments.append(ref)
        kernel(*arguments, *own)
        for ref in inputs:
            if isinstance(ref, Fetched):
                ref.ready()
        made_here = [ref for ref in arguments if isinstance(ref, Stored)]
        for ref in made_here:
            if not ref.copies:
                ref.done()
        for ref in made_here:
            for copy in ref.copies:
                copy.wait()

    size = lambda shape, dtype: math.prod(shape) * jnp.dtype(dtype).itemsize
    inside = sum(size(array.shape, array.dtype) for array, place in operands if place == "H")
    inside += sum(size(shape, dtype) for shape, dtype, place in results if place == "H")
    mib = (mib + inside // 2**20) if total is None else total
    return pl.pallas_call(
        body,
        in_specs=[spaces[place] for place in in_places],
        out_specs=[spaces[place] for place in out_places],
        out_shape=[jax.ShapeDtypeStruct(shape, dtype) for shape, dtype, _ in results],
        scratch_shapes=staged + made + semaphores + list(scratch),
        compiler_params=params(mib),
        cost_estimate=cost(1, 1),
        name=name,
    )(*[array for array, _ in operands])


def placed_at(place, *arrays):
    return [(array, place) for array in arrays]


bf16, f32 = jnp.bfloat16, jnp.float32


def params(mib=16):
    return pltpu.CompilerParams(vmem_limit_bytes=mib << 20)


def cost(flops, moved):
    return pl.CostEstimate(flops=int(flops), bytes_accessed=int(moved), transcendentals=0)


def dot(left, right):
    return jnp.dot(left, right, preferred_element_type=jnp.float32)


def dot_nt(left, right):
    return lax.dot_general(
        left, right, (((1,), (1,)), ((), ())), preferred_element_type=jnp.float32
    )


def dot_tn(left, right):
    return lax.dot_general(
        left, right, (((0,), (0,)), ((), ())), preferred_element_type=jnp.float32
    )


def pack_kernel(*refs):
    query, key, value, output, inner, inner_bias = refs[:6]
    vectors, (first, second, turned) = refs[6:-3], refs[-3:]
    turned[...] = jnp.zeros_like(turned)
    for at, vector in enumerate(vectors):
        turned[at : at + 1, :ROW] = vector[...].astype(jnp.float32)
    bias = inner_bias[...].astype(jnp.float32)
    for at in range(4):
        turned[8 + at : 9 + at, :ROW] = bias[:, at * ROW : (at + 1) * ROW]
    small = jnp.transpose(turned[...])[:ROW].astype(jnp.bfloat16)
    first[:, :D] = query[...]
    first[:, D : D + 512] = key[:, :512]
    first[:, D + 512 : D + 640] = small
    first[:, D + 640 : D + 768] = jnp.zeros_like(small)
    first[:, D + 768 : D + 1024] = key[:, 512:]
    first[:, D + 1024 :] = value[...]
    second[:, :D] = output[...]
    second[:, D:] = inner[...]


def pack(query, key, value, output, inner, inner_bias, vectors):
    rows = [vector.reshape(1, -1) for vector in (inner_bias, *vectors)]
    return run(
        pack_kernel,
        "pack",
        placed_at("H", query, key, value, output, inner, *rows),
        [((ROW, 2 * FIRST_HALF), bf16, "V"), ((ROW, D + inner.shape[1]), bf16, "V")],
        1e6,
        [pltpu.VMEM((128, 128), f32)],
        total=58,
    )


def stack_two_kernel(first, second, left, right):
    blocks = [first[...].astype(jnp.float32), second[...].astype(jnp.float32)]
    whole = jnp.concatenate(blocks).astype(jnp.bfloat16)
    left[...] = whole[:, : left.shape[1]]
    right[...] = whole[:, left.shape[1] :]


def stack_two(block, received, split):
    rows, columns = block.shape
    return pl.pallas_call(
        stack_two_kernel,
        in_specs=[VMEM] * 2,
        out_specs=[VMEM] * 2,
        out_shape=[
            jax.ShapeDtypeStruct((2 * rows, split), jnp.bfloat16),
            jax.ShapeDtypeStruct((2 * rows, columns - split), jnp.bfloat16),
        ],
        compiler_params=params(),
        cost_estimate=cost(1, 1),
        name="stack_two",
    )(block, received)


def stack_z_two_kernel(first, second, out):
    blocks = [first[...].astype(jnp.float32), second[...].astype(jnp.float32)]
    out[...] = jnp.concatenate(blocks).astype(jnp.bfloat16)


def stack_z_two(block, received):
    rows, columns = block.shape
    return pl.pallas_call(
        stack_z_two_kernel,
        in_specs=[VMEM] * 2,
        out_specs=VMEM,
        out_shape=jax.ShapeDtypeStruct((2 * rows, columns), jnp.bfloat16),
        compiler_params=params(),
        cost_estimate=cost(1, 1),
        name="stack_z_two",
    )(block, received)


def stack_mixed_kernel(split, two, received, left, right):
    rows = two.shape[0] // 2
    own, other = two[...].astype(jnp.float32), received[...].astype(jnp.float32)
    whole = jnp.concatenate([own[:rows], other[:rows], own[rows:], other[rows:]]).astype(jnp.bfloat16)
    left[...] = whole[:, :split]
    right[...] = whole[:, split:]


def stack_mixed(two, received, split):
    rows, columns = two.shape
    return pl.pallas_call(
        partial(stack_mixed_kernel, split),
        in_specs=[VMEM] * 2,
        out_specs=[VMEM] * 2,
        out_shape=[
            jax.ShapeDtypeStruct((2 * rows, split), jnp.bfloat16),
            jax.ShapeDtypeStruct((2 * rows, columns - split), jnp.bfloat16),
        ],
        compiler_params=params(),
        cost_estimate=cost(1, 1),
        name="stack_mixed",
    )(two, received)


def stack_z_kernel(split, *refs):
    blocks, (left, right) = refs[:-2], refs[-2:]
    whole = jnp.concatenate([ref[...].astype(jnp.float32) for ref in blocks]).astype(jnp.bfloat16)
    left[...] = whole[:, :split]
    right[...] = whole[:, split:]


def stack_z(block, received, split):
    rows, columns = block.shape
    rows = rows * (1 + len(received)) // 4
    return pl.pallas_call(
        partial(stack_z_kernel, split),
        in_specs=[VMEM] * (1 + len(received)),
        out_specs=[VMEM] * 2,
        out_shape=[
            jax.ShapeDtypeStruct((4 * rows, split), jnp.bfloat16),
            jax.ShapeDtypeStruct((4 * rows, columns - split), jnp.bfloat16),
        ],
        compiler_params=params(),
        cost_estimate=cost(1, 1),
        name="stack_z",
    )(block, *received)


def stack_pair_kernel(left, left_in, right, right_in, left_out, right_out, both_out):
    width = left.shape[1]
    for own, received, out, columns in (
        (left, left_in, left_out, slice(0, width)),
        (right, right_in, right_out, slice(width, width + right.shape[1])),
    ):
        rows = own.shape[0]
        out[:rows, :] = own[...]
        out[rows:, :] = received[...]
        both_out[:rows, columns] = own[...]
        both_out[rows:, columns] = received[...]


def stack_pair(left, left_in, right, right_in):
    double = lambda block: jax.ShapeDtypeStruct((2 * block.shape[0], block.shape[1]), block.dtype)
    both = jax.ShapeDtypeStruct((2 * left.shape[0], left.shape[1] + right.shape[1]), left.dtype)
    return pl.pallas_call(
        stack_pair_kernel,
        in_specs=[VMEM] * 4,
        out_specs=[VMEM] * 3,
        out_shape=[double(left), double(right), both],
        compiler_params=params(),
        cost_estimate=cost(1, 1),
        name="stack_pair",
    )(left, left_in, right, right_in)


def left_tile(refs, columns):
    return jnp.concatenate([ref[:, columns] for ref in refs])


def right_tile(refs, columns):
    near, far, other_near, other_far = refs
    rows = near.shape[0] // 2
    order = [(near, 0), (far, 0), (near, 1), (far, 1)]
    order += [(other_near, 0), (other_far, 0), (other_near, 1), (other_far, 1)]
    return jnp.concatenate([ref[at * rows : (at + 1) * rows, columns] for ref, at in order])


def in_order(pieces):
    left, left_far, right, right_far, c_both, c_left_far, c_right_far = pieces
    return (left, left_far, c_left_far, c_both, right, right_far, c_right_far)


class Side:
    def __init__(self, ref, start, width):
        self.ref, self.start, self.shape = ref, start, (ref.shape[0], width)

    def __getitem__(self, at):
        rows, columns = at
        return self.ref[rows, columns.start + self.start : columns.stop + self.start]


def sides(l0, l1, l3, both, r0, r1, r3):
    left, right = l0.shape[1], r0.shape[1]
    return (l0, l1, Side(both, 0, left), l3), (r0, r1, Side(both, left, right), r3)


FIRST_PARTS = ((0, 0, 768), (0, 768, 512), (1, 256, 256), (1, 512, 768))
SECOND_PARTS = ((0, 0, 768), (0, 768, 512), (0, 1280, 512)) + tuple((1, at, 512) for at in range(0, 2048, 512))


def settle(sides_of, parts, mats, semaphore):
    copies = []
    for (side, start, width), mat in zip(parts, mats):
        for at, piece in enumerate(sides_of[side]):
            rows = piece.shape[0]
            source, first = (piece.ref, piece.start) if isinstance(piece, Side) else (piece, 0)
            columns = pl.ds(first + start, width)
            if side == 0:
                copies.append((source.at[:, columns], mat.at[pl.ds(at * rows, rows), :]))
                continue
            half = rows // 2
            core, far = at // 2, at % 2
            for near in range(2):
                to = ((core * 2 + near) * 2 + far) * half
                copies.append((source.at[pl.ds(near * half, half), columns], mat.at[pl.ds(to, half), :]))
    copies = [pltpu.make_async_copy(*ends, semaphore.at[at]) for at, ends in enumerate(copies)]
    for copy in copies:
        copy.start()
    return copies


FIRST_HALF = 1280
SECOND_HALF = 1792
def head_pair(pair, low):
    nothing = jnp.zeros_like(pair)
    return jnp.concatenate([jnp.where(low, pair, nothing), jnp.where(low, nothing, pair)])


def key_columns(left_rows, right_rows, rows, at):
    if at < 512:
        return left_rows[rows, D + at : D + at + 128]
    return right_rows[rows, at - 256 : at - 128]


def project_kernel(
    place,
    hidden,
    both,
    r0,
    r1,
    r3,
    l0,
    l1,
    l3,
    left_rows,
    right_rows,
    vectors,
    hidden_t,
    query_mat,
    low_key_mat,
    high_key_mat,
    value_mat,
    settling,
):
    tokens = hidden.shape[0]
    lefts, rights = sides(l0, l1, l3, both, r0, r1, r3)
    mats = (query_mat, low_key_mat, high_key_mat, value_mat)
    copies = settle((lefts, rights), FIRST_PARTS, mats, settling)
    restore = restore_from(place)
    moved = dot(hidden[...], restore).astype(jnp.bfloat16)
    small = dot(restore, right_tile(rights, slice(0, 128)))
    turned = jnp.transpose(small)[:16]
    vectors[...] = turned
    for at in range(0, FIRST_HALF, 256):
        columns = slice(at, at + 256)
        rows = dot(moved, left_tile(lefts, columns))
        if at < D:
            rows += turned[0:1, columns]
        left_rows[:, columns] = rows.astype(jnp.bfloat16)
        if at == 0:
            right_rows[:, columns] = jnp.zeros((tokens, 256), jnp.bfloat16)
            continue
        rows = dot(moved, right_tile(rights, columns))
        if at >= 512:
            rows += turned[1:2, at - 512 : at - 256]
        right_rows[:, columns] = rows.astype(jnp.bfloat16)
    left_rows.done()
    right_rows.done()
    hidden_t[...] = dot_nt(arrange_from(place), hidden[...]).astype(jnp.bfloat16)
    for copy in copies:
        copy.wait()


def project(place, hidden, pieces):
    tokens, ordered = hidden.shape[0], in_order(pieces)
    return run(
        project_kernel,
        "project",
        [(place, "S"), (hidden, "H")] + placed_at("K", *ordered[3:], *ordered[:3]),
        [
            ((tokens, FIRST_HALF), bf16, "H"),
            ((tokens, FIRST_HALF), bf16, "H"),
            ((16, D), f32, "V"),
            ((D, tokens), bf16, "H"),
        ]
        + [((D, width), bf16, "A") for _, _, width in FIRST_PARTS],
        9e9,
        [pltpu.SemaphoreType.DMA((24,))],
        total=50,
    )


def attention_kernel(
    place, lengths, left_rows, right_rows, attention_out, context_arrived, context_t, context
):
    tokens = context.shape[0]
    left_rows, right_rows = ready(left_rows), ready(right_rows)
    low = lax.broadcasted_iota(jnp.int32, (SPAN, 128), 1) < HEAD_DIM

    def attend(span, carry):
        rows = pl.ds(pl.multiple_of(span * SPAN, SPAN), SPAN)
        live = lax.broadcasted_iota(jnp.int32, (SPAN, SPAN), 1) < lengths[span]
        for at in range(0, D, 128):
            query = left_rows[rows, at : at + 128]
            keys = head_pair(key_columns(left_rows, right_rows, rows, at), low)
            values = head_pair(right_rows[rows, 512 + at : 640 + at], low)
            scores = dot_nt(query, keys) * HEAD_DIM ** (-0.5)
            parts = []
            for head in range(2):
                part = jnp.where(live, scores[:, head * SPAN : (head + 1) * SPAN], masked_out)
                exponent = jnp.exp(part - jnp.max(part, axis=-1, keepdims=True))
                parts.append(
                    (exponent * (1.0 / jnp.sum(exponent, axis=-1, keepdims=True))).astype(jnp.bfloat16)
                )
            attention = jnp.concatenate(parts, axis=1)
            attention_out[rows, 2 * at : 2 * at + 256] = attention
            context[rows, at : at + 128] = dot(attention, values).astype(jnp.bfloat16)
        return carry

    lax.fori_loop(0, tokens // SPAN, attend, 0)
    attention_out.done()
    context_arrived[...] = dot(context[...], restore_from(place)).astype(jnp.bfloat16)
    context_t[...] = dot_nt(arrange_from(place), context[...]).astype(jnp.bfloat16)


def attention_forward(place, lengths, left_rows, right_rows):
    tokens = left_rows.shape[0]
    return run(
        attention_kernel,
        "attention_forward",
        placed_at("S", place, lengths) + placed_at("H", left_rows, right_rows),
        [((tokens, 2 * D), bf16, "H"), ((tokens, D), bf16, "V"), ((D, tokens), bf16, "H")],
        9e9,
        [pltpu.VMEM((tokens, D), bf16)],
        total=28,
    )


def gelu_parts(preact):
    scaled = jnp.abs(preact) * (0.5**0.5)
    below_one = 1.0 + 0.3275911 * scaled
    near = pl.reciprocal(below_one, approx=True)
    near = near * (2.0 - below_one * near)
    poly = near * (
        0.254829592
        + near * (-0.284496736 + near * (1.421413741 + near * (-1.453152027 + near * 1.061405429)))
    )
    bell = jnp.exp(-0.5 * preact * preact)
    tail = 0.5 * poly * bell
    below = jnp.where(preact < 0.0, tail, 1.0 - tail)
    return (preact * below, below + preact * bell * (0.5 / math.pi) ** 0.5)


FF_TILE = 512


def second_tiles(left, right):
    for at in range(D, SECOND_HALF, FF_TILE):
        yield at - D, left_tile(left, slice(at, at + FF_TILE))
    for at in range(0, right[0].shape[1], FF_TILE):
        yield SECOND_HALF - D + at, right_tile(right, slice(at, at + FF_TILE))


def vector_places():
    for device in range(D // ROW):
        for part in range(4):
            yield (8 + part, device * ROW), (device * 4 + part) * ROW


def residual_kernel(
    place,
    vectors,
    context_arrived,
    l0,
    l1,
    l3,
    both,
    hidden,
    moved,
    normed_out,
    factor_out,
    first_t,
    output_mat,
    settling,
):
    left = (l0, l1, Side(both, 0, l0.shape[1]), l3)
    copies = settle((left, ()), SECOND_PARTS[:1], (output_mat,), settling)
    residual = dot(context_arrived[...], left_tile(left, slice(0, D)))
    residual += hidden[...].astype(jnp.float32) + vectors[2:3, :]
    first_out, normed, factor = normalize(residual, vectors[3:4, :], vectors[4:5, :])
    normed_out[...] = normed
    factor_out[...] = factor
    first16 = first_out.astype(jnp.bfloat16)
    moved[...] = dot(first16, restore_from(place)).astype(jnp.bfloat16)
    first_t[...] = dot_nt(arrange_from(place), first16).astype(jnp.bfloat16)
    for copy in copies:
        copy.wait()


def residual_forward(place, hidden, context_arrived, vectors, pieces):
    tokens, ordered = hidden.shape[0], in_order(pieces)
    return run(
        residual_kernel,
        "residual",
        [(place, "S")]
        + placed_at("V", vectors, context_arrived, *ordered[:4])
        + [(hidden, "H")],
        [
            ((tokens, D), bf16, "V"),
            ((tokens, D), f32, "V"),
            ((tokens, 1), f32, "V"),
            ((D, tokens), bf16, "H"),
            ((D, D), bf16, "A"),
        ],
        1e9,
        [pltpu.SemaphoreType.DMA((4,))],
        total=24,
    )


def feed_kernel(vectors, moved, l0, l1, l3, both, r0, r1, r3, active, active_t, slope, *rest):
    mats, (inner_bias, settling) = rest[:-2], rest[-2:]
    for at, column in vector_places():
        inner_bias[:, column : column + ROW] = vectors[at[0] : at[0] + 1, at[1] : at[1] + ROW]
    left, right = sides(l0, l1, l3, both, r0, r1, r3)
    copies = settle((left, right), SECOND_PARTS[1:], mats, settling)
    for at, tile in second_tiles(left, right):
        columns = slice(at, at + FF_TILE)
        value, derivative = gelu_parts(dot(moved[...], tile) + inner_bias[:, columns])
        value16 = value.astype(jnp.bfloat16)
        active[:, columns] = value16
        active_t[columns, :] = jnp.transpose(value16)
        slope[:, columns] = derivative.astype(jnp.bfloat16)
    for copy in copies:
        copy.wait()


def feed_forward(moved, vectors, ff, pieces):
    tokens = moved.shape[0]
    return run(
        feed_kernel,
        "feed_forward",
        placed_at("V", vectors, moved, *in_order(pieces)),
        [((tokens, ff), bf16, "V"), ((ff, tokens), bf16, "V"), ((tokens, ff), bf16, "V")]
        + [((D, width), bf16, "A") for _, _, width in SECOND_PARTS[1:]],
        8e9,
        [pltpu.VMEM((1, ff), f32), pltpu.SemaphoreType.DMA((44,))],
        total=20,
    )


def natural_rows(place, pieces, target, semaphore):
    rows = 4 * ROW
    left, right = pieces[0].shape[1], pieces[4].shape[1]
    near, far, far_core, near_core, right_near, right_far, right_far_core = pieces
    places = [(near, 0, 0, 0, 0), (far, 0, 0, 1, 0), (near_core, 0, 1, 0, 0), (far_core, 0, 1, 1, 0)]
    places += [(right_near, 1, 0, 0, 0), (right_far, 1, 0, 1, 0)]
    places += [(near_core, 1, 1, 0, left), (right_far_core, 1, 1, 1, 0)]
    for piece, is_right, core_off, far_off, start in places:
        half = right if is_right else left
        for near_off in range(2):
            for z_off in range(4):
                x_off, y_off = (far_off, near_off) if is_right else (near_off, far_off)
                block = ((z_off ^ place[3]) * 2 + (x_off ^ place[2])) * 2 + (core_off ^ place[0])
                block = block * 2 + (y_off ^ place[1])
                to = pl.ds(pl.multiple_of(block * rows, rows), rows)
                pltpu.make_async_copy(
                    piece.at[pl.ds((near_off * 4 + z_off) * rows, rows), pl.ds(start, half)],
                    target.at[to, pl.ds(is_right * left, half)],
                    semaphore,
                ).start()
    pltpu.make_async_copy(target, target, semaphore).wait()


def last_kernel(
    place,
    active,
    first_normed,
    vectors,
    l0,
    l1,
    l3,
    both,
    r0,
    r1,
    r3,
    layer_out,
    normed_out,
    factor_out,
    cls_rows,
    outer_mat,
    semaphore,
):
    natural_rows(place, (l0, l1, l3, both, r0, r1, r3), outer_mat, semaphore)
    total = first_normed[...] * vectors[3:4, :] + vectors[4:5, :] + vectors[5:6, :]
    total += dot(active[...], outer_mat[...])
    encoded, normed, factor = normalize(total, vectors[6:7, :], vectors[7:8, :])
    layer_out[...] = encoded.astype(jnp.bfloat16)
    normed_out[...] = normed
    factor_out[...] = factor
    for span in range(encoded.shape[0] // SPAN):
        cls_rows[span : span + 1, :] = encoded[span * SPAN : span * SPAN + 1].astype(jnp.bfloat16)


def last(place, active, first_normed, vectors, pieces):
    tokens, ff = active.shape
    return run(
        last_kernel,
        "last",
        [(place, "S")]
        + placed_at("V", active, first_normed, vectors, *in_order(pieces)),
        [
            ((tokens, D), bf16, "H"),
            ((tokens, D), f32, "V"),
            ((tokens, 1), f32, "V"),
            ((tokens // SPAN, D), bf16, "V"),
            ((ff, D), bf16, "V"),
        ],
        2.5e9,
        [pltpu.SemaphoreType.DMA],
        total=16,
    )


def pick(place, first, second):
    return jnp.where(place == 0, first, second)


def turn_kernel(
    place,
    partner_span,
    cotangent,
    normed,
    factor,
    vectors,
    own_rows,
    other_rows,
    second_grad,
    kept,
    sent,
    sums,
    loss,
):
    spans = own_rows.shape[0]
    own, other = own_rows[...].astype(jnp.float32), other_rows[...].astype(jnp.float32)
    logits = dot_nt(own_rows[...], other_rows[...]) / math.sqrt(D)
    row = lax.broadcasted_iota(jnp.int32, (spans, spans), 0)
    column = lax.broadcasted_iota(jnp.int32, (spans, spans), 1)
    first_place = place[1] == 0
    target = jnp.zeros((spans, spans), jnp.float32)
    for span in range(spans):
        match = partner_span[0, span]
        hit_row = jnp.where(first_place, span, match)
        hit_column = jnp.where(first_place, match, span)
        target += ((row == hit_row) & (column == hit_column)).astype(jnp.float32)
    highest_logit = jnp.max(logits, axis=1, keepdims=True)
    exponent = jnp.exp(logits - highest_logit)
    totals = jnp.sum(exponent, axis=1, keepdims=True)
    losses = highest_logit + jnp.log(totals) - jnp.sum(target * logits, axis=1, keepdims=True)
    loss[...] = jnp.sum(jnp.where(row == column, losses, 0.0), axis=0, keepdims=True)
    soft = exponent / totals - target
    exponent = jnp.exp(logits - jnp.max(logits, axis=0, keepdims=True))
    back = exponent / jnp.sum(exponent, axis=0, keepdims=True) - target
    own_term, back_term = jnp.zeros_like(own), jnp.zeros_like(own)
    for span in range(spans):
        own_term += soft[:, span : span + 1] * other[span : span + 1]
        back_term += back[:, span : span + 1] * other[span : span + 1]
    cls_gradient = own_term + back_term.astype(jnp.bfloat16).astype(jnp.float32)
    start = lax.broadcasted_iota(jnp.int32, (SPAN, 1), 0) == 0
    gain = vectors[6:7, :]
    gain_sum = jnp.zeros((1, D), jnp.float32)
    shift_sum, bias_sum = gain_sum, gain_sum
    for span in range(spans):
        rows = slice(span * SPAN, (span + 1) * SPAN)
        upstream = cotangent[rows, :].astype(jnp.float32)
        upstream += jnp.where(start, cls_gradient[span : span + 1], 0.0)
        grad, gain_part, shift_part = normalize_back(upstream, normed[rows, :], factor[rows, :], gain)
        second_grad[rows, :] = grad
        gain_sum += gain_part[None]
        shift_sum += shift_part[None]
        bias_sum += jnp.sum(grad, axis=0, keepdims=True)
        grad16 = grad.astype(jnp.bfloat16)
        kept[rows, :] = pick(place[0], grad16[:, : D // 2], grad16[:, D // 2 :])
        sent[rows, :] = pick(place[0], grad16[:, D // 2 :], grad16[:, : D // 2])
    sums[0:1, :] = bias_sum
    sums[1:2, :] = gain_sum
    sums[2:3, :] = shift_sum


def turn(place, partner_span, cotangent, normed, factor, vectors, own_rows, other_rows):
    tokens = cotangent.shape[0]
    return run(
        turn_kernel,
        "turn",
        placed_at("S", place, partner_span)
        + [(cotangent, "H")]
        + placed_at("V", normed, factor, vectors, own_rows, other_rows),
        [
            ((tokens, D), f32, "V"),
            ((tokens, D // 2), bf16, "V"),
            ((tokens, D // 2), bf16, "V"),
            ((3, D), f32, "V"),
            ((1, own_rows.shape[0]), f32, "V"),
        ],
        1e8,
    )


def both_halves(place, kept, sent):
    return jnp.concatenate([pick(place, kept, sent), pick(place, sent, kept)], axis=1)


def slope_kernel(place, second_kept, second_sent, outer_mat, slope, kept, sent, sums, second16):
    second16[...] = both_halves(place[0], second_kept[...], second_sent[...])
    per_half = kept.shape[1] // D

    def tile(at, carry):
        columns = pl.ds(pl.multiple_of(at * D, D), D)
        inside = pl.ds(pl.multiple_of((at % per_half) * D, D), D)
        grad = dot_nt(second16[...], outer_mat[columns, :]) * slope[:, columns].astype(jnp.float32)
        sums[:, columns] = jnp.sum(grad, axis=0, keepdims=True)
        grad16 = grad.astype(jnp.bfloat16)
        mine = place[0] == at // per_half

        @pl.when(mine)
        def keep():
            kept[:, inside] = grad16

        @pl.when(jnp.logical_not(mine))
        def send():
            sent[:, inside] = grad16

        return carry

    lax.fori_loop(0, 2 * per_half, tile, 0)


def slope_back(place, second_kept, second_sent, outer_mat, slope):
    tokens, ff = slope.shape
    half = ((tokens, ff // 2), bf16, "V")
    return run(
        slope_kernel,
        "slope_back",
        [(place, "S")] + placed_at("V", second_kept, second_sent, outer_mat, slope),
        [half, half, ((1, ff), f32, "V")],
        2.5e9,
        [pltpu.VMEM((tokens, D), bf16)],
    )


CHIPS_TILE = 2


def outer_kernel(place, active_t, other_active_t, kept, received, left_kept, left_sent, right_kept, right_sent):
    rows = 2 * ROW
    height = 8 * CHIPS_TILE * rows

    def chips(at, carry):
        tile = pl.ds(pl.multiple_of(at * height, height), height)
        grad = dot(active_t[tile, :], kept[...]) + dot(other_active_t[tile, :], received[...])
        grad = grad.astype(jnp.bfloat16)
        z_off = (at * CHIPS_TILE // 2) ^ place[3]
        for block in range(4 * CHIPS_TILE):
            x_at, core, y_at = block // 4, block // 2 % 2, block % 2
            start = block * 2 * rows
            left, right = grad[start : start + rows], grad[start + rows : start + 2 * rows]
            x_off, y_off = x_at ^ place[2], y_at ^ place[1]
            left_at = (x_off * 4 + z_off) * 2 + core
            right_at = (y_off * 4 + z_off) * 2 + core

            @pl.when(y_off == 0)
            def left_here():
                left_kept[left_at] = left

            @pl.when(y_off == 1)
            def left_there():
                left_sent[left_at] = left

            @pl.when(x_off == 0)
            def right_here():
                right_kept[right_at] = right

            @pl.when(x_off == 1)
            def right_there():
                right_sent[right_at] = right

        return carry

    lax.fori_loop(0, PLACES // CHIPS_TILE, chips, 0)


def outer_gradient(place, active_t, other_active_t, kept, received):
    piece = ((2 * PLACES, 2 * ROW, kept.shape[1]), bf16, "V")
    return run(
        outer_kernel,
        "outer_gradient",
        [(place, "S")] + placed_at("V", active_t, other_active_t, kept, received),
        [piece] * 4,
        2.5e9,
    )


def whole_precision(left, right):
    high = left.astype(jnp.bfloat16)
    rest = (left - high.astype(jnp.float32)).astype(jnp.bfloat16)
    return dot_nt(high, right) + dot_nt(rest, right)


def first_kernel(
    place,
    preact_kept,
    preact_sent,
    factor,
    vectors,
    *refs,
):
    output_mat, inner_mats = refs[0], refs[1:7]
    second_grad, normed, residual_grad, kept, sent, context_grad, sums = refs[7:]
    restore = restore_from(place)
    total = jnp.zeros((factor.shape[0], D), jnp.float32)
    half = preact_kept.shape[1]
    for at, tile in zip(range(0, 2 * half, FF_TILE), inner_mats):
        columns = slice(at % half, at % half + FF_TILE)
        kept_part, sent_part = preact_kept[:, columns], preact_sent[:, columns]
        if at >= half:
            kept_part, sent_part = sent_part, kept_part
        total += dot_nt(pick(place[0], kept_part, sent_part), tile[...])
    first_grad = second_grad[...] + whole_precision(total, restore)
    grad, gain_sum, shift_sum = normalize_back(first_grad, normed[...], factor[...], vectors[3:4, :])
    residual_grad[...] = grad
    sums[0:1, :] = jnp.sum(grad, axis=0, keepdims=True)
    sums[1:2, :] = gain_sum[None]
    sums[2:3, :] = shift_sum[None]
    grad16 = grad.astype(jnp.bfloat16)
    kept[...] = pick(place[0], grad16[:, : D // 2], grad16[:, D // 2 :])
    sent[...] = pick(place[0], grad16[:, D // 2 :], grad16[:, : D // 2])
    moved = dot_nt(grad16, output_mat[...]).astype(jnp.bfloat16)
    context_grad[...] = dot_nt(moved, restore).astype(jnp.bfloat16)


def first_back(place, preact_kept, preact_sent, second_grad, normed, factor, vectors, mats):
    tokens = second_grad.shape[0]
    half = ((tokens, D // 2), bf16, "V")
    return run(
        first_kernel,
        "first_back",
        [(place, "S")]
        + placed_at("V", preact_kept, preact_sent, factor, vectors)
        + placed_at("V", *mats, second_grad, normed),
        [((tokens, D), f32, "V"), half, half, ((tokens, D), bf16, "V"), ((3, D), f32, "V")],
        4.9e9,
    )


def part_rows(grad, left_kept, left_sent, right_kept, right_sent, is_left):
    quarter = D // 4
    if is_left:
        left_kept[...] = grad[: 2 * quarter]
        left_sent[...] = grad[2 * quarter :]
    else:
        right_kept[:quarter, :] = grad[:quarter]
        right_sent[:quarter, :] = grad[quarter : 2 * quarter]
        right_kept[quarter:, :] = grad[2 * quarter : 3 * quarter]
        right_sent[quarter:, :] = grad[3 * quarter :]


def inner_kernel(first_t, other_first_t, kept, received, left_kept, left_sent, right_kept, right_sent):
    for is_left in (True, False):
        columns = slice(0, D) if is_left else slice(D, 2 * D)
        grad = dot(first_t[...], kept[:, columns]) + dot(other_first_t[...], received[:, columns])
        part_rows(grad.astype(jnp.bfloat16), left_kept, left_sent, right_kept, right_sent, is_left)


def inner_gradient(first_t, other_first_t, kept, received):
    piece = ((D // 2, kept.shape[1] // 2), bf16, "V")
    return run(
        inner_kernel,
        "inner_gradient",
        placed_at("V", first_t, other_first_t) + placed_at("V", kept, received),
        [piece] * 4,
        2.5e9,
    )


def attend_kernel(
    place,
    context_grad,
    left_rows,
    right_rows,
    attention_in,
    first_sums,
    second_sums,
    inner_sums,
    kept,
    sent,
    sums,
    grads,
):
    tokens = context_grad.shape[0]
    low = lax.broadcasted_iota(jnp.int32, (SPAN, 128), 1) < HEAD_DIM
    scale = HEAD_DIM ** (-0.5)
    left_rows, right_rows, attention_in = [ready(ref) for ref in (left_rows, right_rows, attention_in)]

    def attend(span, carry):
        rows = pl.ds(pl.multiple_of(span * SPAN, SPAN), SPAN)
        for at in range(0, D, 128):
            query = left_rows[rows, at : at + 128]
            keys = head_pair(key_columns(left_rows, right_rows, rows, at), low)
            values = head_pair(right_rows[rows, 512 + at : 640 + at], low)
            upstream = context_grad[rows, at : at + 128]
            attention16 = attention_in[rows, 2 * at : 2 * at + 256]
            attention_grad = dot_nt(upstream, values)
            parts = []
            for head in range(2):
                columns = slice(head * SPAN, (head + 1) * SPAN)
                attention = attention16[:, columns].astype(jnp.float32)
                part = attention_grad[:, columns]
                weighted = jnp.sum(attention * part, axis=-1, keepdims=True)
                parts.append((attention * (part - weighted)).astype(jnp.bfloat16))
            scores_grad = jnp.concatenate(parts, axis=1)
            grads[0, rows, at : at + 128] = (dot(scores_grad, keys) * scale).astype(jnp.bfloat16)
            both = dot_tn(scores_grad, query)
            both = jnp.where(low, both[:SPAN], both[SPAN:])
            grads[1, rows, at : at + 128] = (both * scale).astype(jnp.bfloat16)
            both = dot_tn(attention16, upstream)
            both = jnp.where(low, both[:SPAN], both[SPAN:])
            grads[2, rows, at : at + 128] = both.astype(jnp.bfloat16)
        return carry

    lax.fori_loop(0, tokens // SPAN, attend, 0)
    query_grad, key_grad, value_grad = grads[0], grads[1], grads[2]
    half = D // 2
    for at, grad in enumerate((query_grad, key_grad, value_grad)):
        columns = slice(at * half, (at + 1) * half)
        kept[:, columns] = pick(place[0], grad[:, :half], grad[:, half:])
        sent[:, columns] = pick(place[0], grad[:, half:], grad[:, :half])
    sums[0:1, :] = jnp.sum(query_grad.astype(jnp.float32), axis=0, keepdims=True)
    sums[1:2, :] = jnp.sum(value_grad.astype(jnp.float32), axis=0, keepdims=True)
    sums[2:5, :] = first_sums[...]
    sums[5:8, :] = second_sums[...]
    for at, column in vector_places():
        sums[at[0] : at[0] + 1, at[1] : at[1] + ROW] = inner_sums[:, column : column + ROW]
    sums[12:16, :] = jnp.zeros((4, D), jnp.float32)


def attend_back(place, context_grad, left_rows, right_rows, attention, first_sums, second_sums, inner_sums):
    tokens = context_grad.shape[0]
    part = ((tokens, 3 * D // 2), bf16, "V")
    return run(
        attend_kernel,
        "attend_back",
        placed_at("S", place)
        + placed_at("V", context_grad)
        + placed_at("V", left_rows, right_rows, attention)
        + placed_at("V", first_sums, second_sums, inner_sums),
        [part, part, ((16, D), f32, "V")],
        4e9,
        [pltpu.VMEM((3, tokens, D), bf16)],
    )


def attention_gradient_kernel(
    place,
    sums,
    hidden_t,
    other_hidden_t,
    context_t,
    other_context_t,
    grads,
    other_grads,
    residual,
    other_residual,
    left_kept,
    left_sent,
    right_kept,
    right_sent,
):
    half = D // 2
    grad = dot(hidden_t[...], grads[:, :D]) + dot(other_hidden_t[...], other_grads[:, :D])
    grad = grad.astype(jnp.bfloat16)
    left_kept[:, :D] = grad[:half]
    left_sent[:, :D] = grad[half:]
    total = sums[...].astype(jnp.bfloat16)
    total = jnp.concatenate([total, jnp.zeros((112, D), jnp.bfloat16)])
    small = dot_nt(arrange_from(place), total).astype(jnp.bfloat16)
    left_kept[:, D:] = small[:half]
    left_sent[:, D:] = small[half:]
    value = dot(hidden_t[...], grads[:, D:]) + dot(other_hidden_t[...], other_grads[:, D:])
    output = dot(context_t[...], residual[...]) + dot(other_context_t[...], other_residual[...])
    grad = jnp.concatenate([value, output], axis=1).astype(jnp.bfloat16)
    part_rows(grad, left_kept, left_sent, right_kept, right_sent, False)


def attention_gradient(*operands):
    left, right = ((D // 2, D + 128), bf16, "V"), ((D // 2, D), bf16, "V")
    places = ["S"] + ["V"] * 9
    return run(
        attention_gradient_kernel,
        "attention_gradient",
        list(zip(operands, places)),
        [left, left, right, right],
        2.5e9,
    )


def input_kernel(
    place, kept, sent, query_mat, low_key_mat, high_key_mat, value_mat, residual_grad, input_grad
):
    restore = restore_from(place)
    half = D // 2
    parts = []
    for at in range(3):
        columns = slice(at * half, (at + 1) * half)
        parts.append(both_halves(place[0], kept[:, columns], sent[:, columns]))
    query_grad, key_grad, value_grad = parts
    total = dot_nt(query_grad, query_mat[...])
    total += dot_nt(key_grad[:, :512], low_key_mat[...])
    total += dot_nt(key_grad[:, 512:], high_key_mat[...])
    total += dot_nt(value_grad, value_mat[...])
    total = residual_grad[...] + whole_precision(total, restore)
    input_grad[...] = total.astype(jnp.bfloat16)


def input_back(place, residual_grad, kept, sent, mats):
    return run(
        input_kernel,
        "input_back",
        [(place, "S")]
        + placed_at("V", kept, sent)
        + placed_at("V", *mats, residual_grad),
        [(residual_grad.shape, bf16, "H")],
        3e9,
    )[0]


def add_kernel(left, left_in, right, right_in, left_kept, left_sent, right_kept, right_sent):
    for own, received, kept, sent in (
        (left, left_in, left_kept, left_sent),
        (right, right_in, right_kept, right_sent),
    ):
        total = (own[...].astype(jnp.float32) + received[...].astype(jnp.float32)).astype(jnp.bfloat16)
        half = total.shape[0] // 2
        kept[...] = total[:half]
        sent[...] = total[half:]


def add_parts(left, left_in, right, right_in):
    shapes = [(part.shape[0] // 2,) + part.shape[1:] for part in (left, left, right, right)]
    return pl.pallas_call(
        add_kernel,
        in_specs=[VMEM] * 4,
        out_specs=[VMEM] * 4,
        out_shape=[jax.ShapeDtypeStruct(shape, jnp.bfloat16) for shape in shapes],
        compiler_params=params(),
        cost_estimate=cost(1, 1),
        name="add_parts",
    )(left, left_in, right, right_in)


def add_z_kernel(left, left_in, right, right_in, own, first, second, third):
    width = left.shape[-1]
    for part, received, columns in (
        (left, left_in, slice(0, width)),
        (right, right_in, slice(width, width + right.shape[-1])),
    ):
        rows = part.shape[0] // 4
        total = part[...].astype(jnp.float32) + received[...].astype(jnp.float32)
        own[..., columns] = total[:rows]
        for at, sent in enumerate((first, second, third)):
            sent[..., columns] = total[(at + 1) * rows : (at + 2) * rows].astype(jnp.bfloat16)


def add_z(left, left_in, right, right_in):
    shape = (left.shape[0] // 4,) + left.shape[1:-1] + (left.shape[-1] + right.shape[-1],)
    return pl.pallas_call(
        add_z_kernel,
        in_specs=[VMEM] * 4,
        out_specs=[VMEM] * 4,
        out_shape=[jax.ShapeDtypeStruct(shape, jnp.float32)]
        + [jax.ShapeDtypeStruct(shape, jnp.bfloat16)] * 3,
        compiler_params=params(),
        cost_estimate=cost(1, 1),
        name="add_z",
    )(left, left_in, right, right_in)


def add_join_kernel(left, left_in, right, right_in, kept, sent):
    width = left.shape[-1]
    for part, received, columns in (
        (left, left_in, slice(0, width)),
        (right, right_in, slice(width, width + right.shape[-1])),
    ):
        rows = part.shape[0] // 4
        total = part[...].astype(jnp.float32) + received[...].astype(jnp.float32)
        for at in range(2):
            to, start = slice(at * rows, (at + 1) * rows), 2 * at * rows
            kept[to, ..., columns] = total[start : start + rows]
            sent[to, ..., columns] = total[start + rows : start + 2 * rows].astype(jnp.bfloat16)


def add_join(left, left_in, right, right_in):
    shape = (left.shape[0] // 2,) + left.shape[1:-1] + (left.shape[-1] + right.shape[-1],)
    return pl.pallas_call(
        add_join_kernel,
        in_specs=[VMEM] * 4,
        out_specs=[VMEM] * 2,
        out_shape=[jax.ShapeDtypeStruct(shape, jnp.float32), jax.ShapeDtypeStruct(shape, jnp.bfloat16)],
        compiler_params=params(),
        cost_estimate=cost(1, 1),
        name="add_join",
    )(left, left_in, right, right_in)


def add_half_kernel(own, received, kept, sent):
    rows = own.shape[0] // 2
    total = own[...] + received[...].astype(jnp.float32)
    kept[...] = total[:rows]
    sent[...] = total[rows:].astype(jnp.bfloat16)


def add_half(own, received):
    shape = (own.shape[0] // 2,) + own.shape[1:]
    return pl.pallas_call(
        add_half_kernel,
        in_specs=[VMEM] * 2,
        out_specs=[VMEM] * 2,
        out_shape=[jax.ShapeDtypeStruct(shape, jnp.float32), jax.ShapeDtypeStruct(shape, jnp.bfloat16)],
        compiler_params=params(),
        cost_estimate=cost(1, 1),
        name="add_half",
    )(own, received)


def finish_kernel(place, own, *refs):
    received_all, (mine, other) = refs[:-2], refs[-2:]
    total = own[...]
    for received in received_all:
        total = total + received[...].astype(jnp.float32)
    if len(total.shape) == 3:
        low, high = total[0], total[1]
    else:
        low, high = total[:ROW], total[ROW:]
    mine[...] = pick(place[0], low, high)
    other[...] = pick(place[0], high, low)


def finish(place, own, received):
    rows = own.shape[1] if own.ndim == 3 else ROW
    return pl.pallas_call(
        finish_kernel,
        in_specs=[SMEM] + [VMEM] * (1 + len(received)),
        out_specs=[VMEM] * 2,
        out_shape=[jax.ShapeDtypeStruct((rows, own.shape[-1]), jnp.float32)] * 2,
        compiler_params=params(),
        cost_estimate=cost(1, 1),
        name="finish",
    )(place, own, *received)


def put(place, out, mine, received):
    half = mine.shape[1]
    out[:, :half] = pick(place[0], mine, received)
    out[:, half:] = pick(place[0], received, mine)


def outer_out_kernel(place, mine, received, out):
    rows, half = mine.shape[0], mine.shape[1] // 2
    for at in range(2):
        columns = slice(at * half, (at + 1) * half)
        put(place, out.at[at * rows : (at + 1) * rows], mine[:, columns], received[:, columns])


def inner_out_kernel(place, mine, received, out):
    put(place, out, mine[...], received[...])


def rest_out_kernel(place, mine, received, query, key, value, output, inner_bias, *vectors):
    half = D // 2
    for out, at in ((query, 0), (key, half), (value, D + 128), (output, D + 128 + half)):
        columns = slice(at, at + half)
        put(place, out, mine[:, columns], received[:, columns])
    turned = jnp.transpose(mine[:, D : D + 128] + received[:, D : D + 128])
    for at, out in enumerate(vectors):
        out[...] = turned[at : at + 1]
    for at in range(4):
        inner_bias[:, at * ROW : (at + 1) * ROW] = turned[8 + at : 9 + at]


def placed(kernel, name, place, mine, received, shapes):
    return pl.pallas_call(
        kernel,
        in_specs=[SMEM, VMEM, VMEM],
        out_specs=[VMEM] * len(shapes),
        out_shape=[jax.ShapeDtypeStruct(shape, jnp.float32) for shape in shapes],
        compiler_params=params(),
        cost_estimate=cost(1, 1),
        name=name,
    )(place, mine, received)


def first_transfers(pieces):
    return [mate(pieces[1]), across(pieces[3], 2)]


def add_first(pieces, received):
    return add_parts(pieces[0], received[0], pieces[2], received[1])


def second_transfers(pieces):
    return [across(pieces[1], 2), mate(pieces[3])]


def add_joined(pieces, received):
    return add_join(pieces[0], received[0], pieces[2], received[1])


def add_second(pieces, received):
    return add_z(pieces[0], received[0], pieces[2], received[1])


def third_transfers(parts):
    return [across(sent, mask) for sent, mask in zip(parts[1:], (4, 8, 12))]


def fast_device(
    hidden_in,
    cotangent,
    span_lengths,
    partner_span,
    query_weight,
    query_bias,
    key_weight,
    value_weight,
    value_bias,
    output_weight,
    output_bias,
    first_gain,
    first_shift,
    inner_weight,
    inner_bias,
    outer_weight,
    outer_bias,
    second_gain,
    second_shift,
):
    core, x_at, z_at, y_at = coordinates()
    place = jnp.stack([core, y_at, x_at, z_at]).astype(jnp.int32)
    first_block, second_block = pack(
        query_weight,
        key_weight,
        value_weight,
        output_weight,
        inner_weight,
        inner_bias,
        (
            query_bias,
            value_bias,
            output_bias,
            first_gain,
            first_shift,
            outer_bias,
            second_gain,
            second_shift,
        ),
    )
    ff = inner_weight.shape[1]
    first_z = z_exchange(first_block)
    first = stack_z(first_block, first_z, FIRST_HALF)
    second_block, third_block = tied((second_block, outer_weight), *first)
    first_in = near_exchange(first)
    second_z = across(second_block, 8)
    *first, first_both = stack_near(first, tied(first_in, second_z))
    second_two = stack_z_two(after(second_block, *first), second_z)
    first = tied(first, second_two)
    first_far = far_exchange(first)
    second_z = across(second_two, 4)
    first_core = across(first_both, 1)
    second = stack_mixed(second_two, after(second_z, first_core, *first_far), SECOND_HALF)
    first_far, third_block = tied(first_far, *second), after(third_block, *second)
    second_in = near_exchange(second)
    first_far_core = core_exchange(first_far)
    third_z = across(after(third_block, *first_far_core), 8)
    third_two = stack_z_two(third_block, third_z)
    left_rows, right_rows, vectors, hidden_t, *first_mats = project(
        place, hidden_in, pieces_of(first, first_far, first_core, first_far_core)
    )
    *second, second_both = stack_near(second, tied(second_in, vectors, third_z))
    third_two, left_rows = tied((third_two, left_rows), *second)
    second_far = far_exchange(second)
    third_z = across(third_two, 4)
    second_core = across(second_both, 1)
    attention, context_arrived, context_t = attention_forward(
        place, span_lengths, left_rows, right_rows
    )
    third = stack_mixed(
        third_two, after(third_z, context_arrived, second_core, *second_far), D // 2
    )
    second_far = tied(second_far, *third)
    third_in = near_exchange(third)
    second_far_core = core_exchange(second_far)
    second_pieces = pieces_of(second, second_far, second_core, second_far_core)
    moved, first_normed, first_factor, first_t, output_mat = residual_forward(
        place, hidden_in, context_arrived, vectors, second_pieces
    )
    *third, third_both = stack_near(third, tied(third_in, moved, *second_far_core))
    moved = after(moved, *third)
    third_far = far_exchange(third)
    third_core = across(third_both, 1)
    active, active_t, slope, *inner_mats = feed_forward(moved, vectors, ff, second_pieces)
    second_mats = [output_mat, *inner_mats]
    third_far = tied(third_far, active, third_core)
    third_far_core = core_exchange(third_far)
    third_pieces = pieces_of(third, third_far, third_core, third_far_core)
    hidden_t, context_t, first_t, active_t, active = tied(
        (hidden_t, context_t, first_t, active_t, active), *third_far_core
    )
    other_active_t, other_first_t = across(active_t, 1), across(first_t, 1)
    other_hidden_t, other_context_t = across(hidden_t, 1), across(context_t, 1)
    layer_out, second_normed, second_factor, cls_rows, outer_mat = last(
        place, active, first_normed, vectors, third_pieces
    )
    other_rows = mate(cls_rows)
    second_grad, second_kept, second_sent, second_sums, span_loss = turn(
        place, partner_span, cotangent, second_normed, second_factor, vectors, cls_rows, other_rows
    )
    second_received = across(second_sent, 1)
    preact_kept, preact_sent, inner_sums = slope_back(
        place, second_kept, second_sent, outer_mat, slope
    )
    second_received = after(second_received, preact_kept)
    outer_parts = outer_gradient(place, active_t, other_active_t, second_kept, second_received)
    preact_kept, preact_sent = tied((preact_kept, preact_sent), *outer_parts)
    outer_in = first_transfers(outer_parts)
    preact_received = across(preact_sent, 1)
    residual_grad, residual_kept, residual_sent, context_grad, first_sums = first_back(
        place,
        preact_kept,
        preact_sent,
        second_grad,
        first_normed,
        first_factor,
        vectors,
        second_mats,
    )
    residual_received = across(residual_sent, 1)
    preact_kept = after(preact_kept, context_grad)
    inner_parts = inner_gradient(first_t, other_first_t, preact_kept, preact_received)
    outer_parts = add_first(outer_parts, tied(outer_in, residual_received, *inner_parts))
    inner_parts, context_grad = tied(inner_parts, *outer_parts), after(context_grad, *outer_parts)
    outer_in = second_transfers(outer_parts)
    inner_in = first_transfers(inner_parts)
    grads_kept, grads_sent, sums = attend_back(
        place,
        context_grad,
        left_rows,
        right_rows,
        attention,
        first_sums,
        second_sums,
        inner_sums,
    )
    received = tied(outer_in + inner_in, sums)
    inner_parts = add_first(inner_parts, received[2:])
    outer_parts, grads_sent = tied(outer_parts, *inner_parts), after(grads_sent, *inner_parts)
    outer_own, outer_sent = add_joined(outer_parts, received[:2])
    inner_in = second_transfers(inner_parts)
    outer_in = across(outer_sent, 4)
    grads_received = after(across(grads_sent, 1), outer_own)
    rest_parts = attention_gradient(
        place,
        sums,
        hidden_t,
        other_hidden_t,
        context_t,
        other_context_t,
        grads_kept,
        grads_received,
        residual_kept,
        residual_received,
    )
    *inner_in, outer_in = tied(inner_in + [outer_in], *rest_parts)
    rest_parts = tied(rest_parts, outer_in, *inner_in)
    inner_own, inner_sent = add_joined(inner_parts, inner_in)
    outer_own, outer_sent = add_half(outer_own, after(outer_in, inner_own))
    grads_kept = after(grads_kept, outer_own)
    rest_in = first_transfers(rest_parts)
    inner_in = across(inner_sent, 4)
    outer_in = across(outer_sent, 8)
    input_grad = input_back(place, residual_grad, grads_kept, grads_sent, first_mats)
    rest_parts = add_first(rest_parts, tied(rest_in, input_grad, outer_in, inner_in))
    inner_own, inner_in, outer_own, outer_in = tied(
        (inner_own, inner_in, outer_own, outer_in), *rest_parts
    )
    rest_in = second_transfers(rest_parts)
    inner_own, inner_sent = add_half(inner_own, inner_in)
    inner_in = across(inner_sent, 8)
    outer_mine, outer_other = finish(place, outer_own, [outer_in])
    outer_other = across(outer_other, 1)
    rest_parts = add_second(rest_parts, tied(rest_in, inner_in, outer_other))
    inner_in, outer_other = tied((inner_in, outer_other), *rest_parts)
    rest_in = third_transfers(rest_parts)
    inner_mine, inner_other = finish(place, inner_own, [inner_in])
    inner_other = across(inner_other, 1)
    (outer_grad,) = placed(
        outer_out_kernel, "outer_out", place, outer_mine, outer_other, [(4 * ROW, D)]
    )
    (inner_grad,) = placed(
        inner_out_kernel, "inner_out", place, inner_mine, after(inner_other, outer_grad), [(ROW, ff)]
    )
    rest_mine, rest_other = finish(place, rest_parts[0], tied(rest_in, inner_grad))
    rest_other = across(rest_other, 1)
    query_grad, key_grad, value_grad, output_grad, inner_bias_grad, *vector_grads = placed(
        rest_out_kernel,
        "rest_out",
        place,
        rest_mine,
        rest_other,
        [(ROW, D)] * 4 + [(1, 4 * ROW)] + [(1, ROW)] * 8,
    )
    vector_grads = [grad.reshape(-1) for grad in vector_grads]
    return (
        layer_out,
        input_grad,
        span_loss.reshape(-1),
        query_grad,
        vector_grads[0],
        key_grad,
        value_grad,
        vector_grads[1],
        output_grad,
        vector_grads[2],
        vector_grads[3],
        vector_grads[4],
        inner_grad,
        inner_bias_grad.reshape(-1),
        outer_grad,
        vector_grads[5],
        vector_grads[6],
        vector_grads[7],
    )


def solution(mesh):
    is_block = mesh.shape["doc"] == 2 * PLACES and mesh.shape["pair"] == 2
    return jax.shard_map(
        fast_device if is_block else per_device,
        mesh=mesh,
        in_specs=(
            P(("doc", "pair"), None),
            P(("doc", "pair"), None),
            P(("doc", "pair")),
            P("doc", None),
            P(("doc", "pair"), None),
            P(("doc", "pair")),
            P(("doc", "pair"), None),
            P(("doc", "pair"), None),
            P(("doc", "pair")),
            P(("doc", "pair"), None),
            P(("doc", "pair")),
            P(("doc", "pair")),
            P(("doc", "pair")),
            P(("doc", "pair"), None),
            P(("doc", "pair")),
            P(("doc", "pair"), None),
            P(("doc", "pair")),
            P(("doc", "pair")),
            P(("doc", "pair")),
        ),
        out_specs=(
            P(("doc", "pair"), None),
            P(("doc", "pair"), None),
            P(("doc", "pair")),
            P(("doc", "pair"), None),
            P(("doc", "pair")),
            P(("doc", "pair"), None),
            P(("doc", "pair"), None),
            P(("doc", "pair")),
            P(("doc", "pair"), None),
            P(("doc", "pair")),
            P(("doc", "pair")),
            P(("doc", "pair")),
            P(("doc", "pair"), None),
            P(("doc", "pair")),
            P(("doc", "pair"), None),
            P(("doc", "pair")),
            P(("doc", "pair")),
            P(("doc", "pair")),
        ),
        check_vma=False,
    )
```

```python
from functools import partial
import math

import jax
import jax.numpy as jnp
from jax import lax
from jax.experimental import pallas as pl
from jax.experimental.pallas import tpu as pltpu
from jax.sharding import PartitionSpec as P

D = 768
HEAD_DIM = 64
SPAN = 128
SPANS_ROW = 4


epsilon = 1e-06
masked_out = -1000000000.0
highest = lax.Precision.HIGHEST


def across(block, mask):
    count = lax.axis_size("doc")
    return lax.ppermute(block, "doc", [(at, at ^ mask) for at in range(count)])


def mate(block):
    return lax.ppermute(block, "pair", [(0, 1), (1, 0)])


def far_groups():
    bits = lax.axis_size("doc").bit_length() - 1
    far = [1 << at for at in range(2, bits)]
    return [far[at : at + 2] for at in range(0, len(far), 2)]


def is_upper(mask):
    return (lax.axis_index("doc") & mask) != 0


def joined(own, other, upper):
    return jnp.where(upper, jnp.stack([other, own]), jnp.stack([own, other]))


def gather_rows(block):
    rows, columns = block.shape
    total = block[None]
    for masks in far_groups():
        low = masks[0]
        near = joined(total, across(total, low), is_upper(low))
        if len(masks) == 2:
            high = masks[1]
            straight, crossed = across(total, high), across(total, high | low)
            far = joined(straight, crossed, is_upper(low))
            near = joined(near, far, is_upper(high)).reshape((4,) + total.shape)
        total = near.reshape((-1, rows, columns))
    half = columns // 2
    left, right = total[..., :half], total[..., half:]
    on_pair = lax.axis_index("pair") == 1
    left_x, right_y = across(left, 2), mate(right)
    left, right = joined(left, left_x, is_upper(2)), joined(right, right_y, on_pair)
    left_y, right_x = mate(left), across(right, 2)
    left, right = joined(left, left_y, on_pair), joined(right, right_x, is_upper(2))
    left = joined(left, across(left, 1), is_upper(1))
    right = joined(right, across(right, 1), is_upper(1))
    left = jnp.transpose(left, (3, 2, 0, 1, 4, 5))
    right = jnp.transpose(right, (3, 1, 0, 2, 4, 5))
    return jnp.concatenate([left, right], axis=-1).reshape(-1, rows, columns)


def halves(blocks, axis, upper):
    lower = lax.index_in_dim(blocks, 0, axis, keepdims=False)
    higher = lax.index_in_dim(blocks, 1, axis, keepdims=False)
    return (jnp.where(upper, higher, lower), jnp.where(upper, lower, higher))


def plus(kept, received):
    return kept.astype(jnp.float32) + received.astype(jnp.float32)


def scatter_rows(blocks):
    rows, columns = blocks.shape[1:]
    on_pair = lax.axis_index("pair") == 1
    blocks = blocks.astype(jnp.bfloat16).reshape(-1, 2, 2, 2, rows, columns)
    kept, sent = halves(blocks, 2, is_upper(1))
    total = plus(kept, across(sent, 1)).astype(jnp.bfloat16)
    half = columns // 2
    left, right = total[..., :half], total[..., half:]
    left_kept, left_sent = halves(left, 2, on_pair)
    right_kept, right_sent = halves(right, 1, is_upper(2))
    left = plus(left_kept, mate(left_sent)).astype(jnp.bfloat16)
    right = plus(right_kept, across(right_sent, 2)).astype(jnp.bfloat16)
    left_kept, left_sent = halves(left, 1, is_upper(2))
    right_kept, right_sent = halves(right, 1, on_pair)
    left = plus(left_kept, across(left_sent, 2))
    right = plus(right_kept, mate(right_sent))
    total = jnp.concatenate([left, right], axis=-1)
    for masks in far_groups()[::-1]:
        total = total.astype(jnp.bfloat16).reshape(2 ** len(masks), -1, rows, columns)
        place = (lax.axis_index("doc") // masks[0]) % 2 ** len(masks)
        summed = lax.dynamic_index_in_dim(total, place, 0, keepdims=False).astype(jnp.float32)
        for step in range(1, 2 ** len(masks)):
            sent = lax.dynamic_index_in_dim(total, place ^ step, 0, keepdims=False)
            summed = plus(summed, across(sent, masks[0] * step))
        total = summed
    return total.reshape(rows, columns)


VECTORS = (1, 4, 6, 7, 8, 10, 12, 13, 14)


def pack_vectors(pieces):
    flat = jnp.concatenate(pieces, axis=-1)
    width = -(-flat.shape[-1] // D) * D
    flat = jnp.pad(flat, [(0, 0)] * (flat.ndim - 1) + [(0, width - flat.shape[-1])])
    return flat.reshape(flat.shape[:-1] + (-1, D))


def fold(matrix):
    return jnp.concatenate([matrix[:, at : at + D] for at in range(0, matrix.shape[1], D)])


def collect(shards):
    rows = shards[0].shape[0]
    devices = lax.axis_size("doc") * lax.axis_size("pair")
    small = pack_vectors([shards[at] for at in VECTORS])
    first = gather_rows(jnp.concatenate([shards[0], shards[2], shards[3], small]))
    second = gather_rows(jnp.concatenate([shards[5], fold(shards[9])]))
    outer = lax.all_gather(shards[11], ("doc", "pair"), axis=0, tiled=True)
    whole = {
        0: first[:, :rows].reshape(-1, D),
        2: first[:, rows : 2 * rows].reshape(-1, D),
        3: first[:, 2 * rows : 3 * rows].reshape(-1, D),
        5: second[:, :rows].reshape(-1, D),
        9: jnp.concatenate(
            [
                second[:, at : at + rows].reshape(-1, D)
                for at in range(rows, second.shape[1], rows)
            ],
            axis=1,
        ),
        11: outer,
    }
    vectors, start = first[:, 3 * rows :].reshape(devices, -1), 0
    for at in VECTORS:
        size = shards[at].shape[0]
        whole[at] = vectors[:, start : start + size].reshape(-1).astype(jnp.float32)
        start += size
    return tuple(whole[at] for at in range(15))


def spread(gradients):
    devices = lax.axis_size("doc") * lax.axis_size("pair")
    by_device = [
        piece.reshape((devices, -1) + piece.shape[1:]) for piece in gradients
    ]
    rows = by_device[0].shape[1]
    outer = scatter_rows(by_device[11])
    inner = by_device[9]
    parts = [inner[..., at : at + D] for at in range(0, inner.shape[-1], D)]
    second = scatter_rows(jnp.concatenate([by_device[5]] + parts, axis=1))
    small = pack_vectors([by_device[at] for at in VECTORS])
    first = scatter_rows(
        jnp.concatenate([by_device[0], by_device[2], by_device[3], small], axis=1)
    )
    own = {
        0: first[:rows],
        2: first[rows : 2 * rows],
        3: first[2 * rows : 3 * rows],
        5: second[:rows],
        9: jnp.concatenate(
            [second[at : at + rows] for at in range(rows, second.shape[0], rows)], axis=1
        ),
        11: outer,
    }
    vectors, start = first[3 * rows :].reshape(-1), 0
    for at in VECTORS:
        size = by_device[at].shape[1]
        own[at] = vectors[start : start + size]
        start += size
    return tuple(own[at] for at in range(15))


def normalize(hidden, gain, shift):
    average = jnp.mean(hidden, axis=-1, keepdims=True)
    centred = hidden - average
    factor = lax.rsqrt(jnp.mean(centred * centred, axis=-1, keepdims=True) + epsilon)
    normed = centred * factor
    return (normed * gain + shift, normed, factor)


def normalize_back(upstream, normed, factor, gain):
    scaled = upstream * gain
    hidden_grad = factor * (
        scaled
        - jnp.mean(scaled, axis=-1, keepdims=True)
        - normed * jnp.mean(scaled * normed, axis=-1, keepdims=True)
    )
    return (hidden_grad, jnp.sum(upstream * normed, axis=0), jnp.sum(upstream, axis=0))


def head_scores(query_row, key_row, live_row):
    product = jnp.einsum("sqhd,skhd->shqk", query_row, key_row, preferred_element_type=jnp.float32)
    return jnp.where(live_row[:, None, None, :], product * HEAD_DIM ** (-0.5), masked_out)


def encode(hidden_in, allowed, gathered):
    (
        query_mat,
        query_add,
        key_mat,
        value_mat,
        value_add,
        output_mat,
        output_add,
        gain_one,
        shift_one,
        inner_mat,
        inner_add,
        outer_mat,
        outer_add,
        gain_two,
        shift_two,
    ) = gathered
    row_count = allowed.shape[0]
    shaped = (row_count, SPANS_ROW, SPAN, D // HEAD_DIM, HEAD_DIM)
    queries = (
        jnp.dot(hidden_in, query_mat, preferred_element_type=jnp.float32) + query_add
    ).astype(jnp.bfloat16)
    key_rows = jnp.dot(hidden_in, key_mat, preferred_element_type=jnp.float32).astype(jnp.bfloat16)
    value_rows = (
        jnp.dot(hidden_in, value_mat, preferred_element_type=jnp.float32) + value_add
    ).astype(jnp.bfloat16)

    def attend(element):
        query_row, key_row, value_row, live_row = element
        scores = head_scores(query_row, key_row, live_row)
        highest_score = jnp.max(scores, axis=-1, keepdims=True)
        exponent = jnp.exp(scores - highest_score)
        totals = jnp.sum(exponent, axis=-1, keepdims=True)
        attention = (exponent / totals).astype(jnp.bfloat16)
        context_row = jnp.einsum(
            "shqk,skhd->sqhd", attention, value_row, preferred_element_type=jnp.float32
        )
        return (context_row.astype(jnp.bfloat16), (highest_score + jnp.log(totals))[..., 0])

    context, logsum = lax.map(
        attend,
        (queries.reshape(shaped), key_rows.reshape(shaped), value_rows.reshape(shaped), allowed),
    )
    context = context.reshape(-1, D)
    residual = (
        hidden_in.astype(jnp.float32)
        + jnp.dot(context, output_mat, preferred_element_type=jnp.float32)
        + output_add
    )
    first_out, first_normed, first_factor = normalize(residual, gain_one, shift_one)
    first16 = first_out.astype(jnp.bfloat16)
    preact = jnp.dot(first16, inner_mat, preferred_element_type=jnp.float32) + inner_add
    active = jax.nn.gelu(preact, approximate=False).astype(jnp.bfloat16)
    second = first_out + jnp.dot(active, outer_mat, preferred_element_type=jnp.float32) + outer_add
    encoded, second_normed, second_factor = normalize(second, gain_two, shift_two)
    stored = (
        queries,
        key_rows,
        value_rows,
        logsum,
        context,
        first_normed,
        first_factor,
        first16,
        preact,
        active,
        second_normed,
        second_factor,
    )
    return (encoded, stored)


def backward(hidden_in, allowed, gathered, stored, out_gradient):
    (
        query_mat,
        query_add,
        key_mat,
        value_mat,
        value_add,
        output_mat,
        output_add,
        gain_one,
        shift_one,
        inner_mat,
        inner_add,
        outer_mat,
        outer_add,
        gain_two,
        shift_two,
    ) = gathered
    (
        queries,
        key_rows,
        value_rows,
        logsum,
        context,
        first_normed,
        first_factor,
        first16,
        preact,
        active,
        second_normed,
        second_factor,
    ) = stored
    row_count = allowed.shape[0]
    shaped = (row_count, SPANS_ROW, SPAN, D // HEAD_DIM, HEAD_DIM)
    second_grad, gain_two_grad, shift_two_grad = normalize_back(
        out_gradient, second_normed, second_factor, gain_two
    )
    outer_add_grad = jnp.sum(second_grad, axis=0)
    second16 = second_grad.astype(jnp.bfloat16)
    outer_mat_grad = jnp.dot(active.T, second16, preferred_element_type=jnp.float32)
    active_grad = jnp.dot(second16, outer_mat.T, preferred_element_type=jnp.float32)
    unused, gelu_back = jax.vjp(partial(jax.nn.gelu, approximate=False), preact)
    preact_grad = gelu_back(active_grad)[0]
    inner_add_grad = jnp.sum(preact_grad, axis=0)
    preact16 = preact_grad.astype(jnp.bfloat16)
    inner_mat_grad = jnp.dot(first16.T, preact16, preferred_element_type=jnp.float32)
    first_grad = second_grad + jnp.dot(preact16, inner_mat.T, preferred_element_type=jnp.float32)
    residual_grad, gain_one_grad, shift_one_grad = normalize_back(
        first_grad, first_normed, first_factor, gain_one
    )
    output_add_grad = jnp.sum(residual_grad, axis=0)
    residual16 = residual_grad.astype(jnp.bfloat16)
    output_mat_grad = jnp.dot(context.T, residual16, preferred_element_type=jnp.float32)
    context_grad = jnp.dot(residual16, output_mat.T, preferred_element_type=jnp.float32).astype(
        jnp.bfloat16
    )

    def attend_back(element):
        query_row, key_row, value_row, live_row, logsum_row, context_row = element
        scores = head_scores(query_row, key_row, live_row)
        attention = jnp.exp(scores - logsum_row[..., None])
        attention16 = attention.astype(jnp.bfloat16)
        value_grad = jnp.einsum(
            "shqk,sqhd->skhd", attention16, context_row, preferred_element_type=jnp.float32
        )
        attention_grad = jnp.einsum(
            "sqhd,skhd->shqk", context_row, value_row, preferred_element_type=jnp.float32
        )
        weighted = jnp.sum(attention * attention_grad, axis=-1, keepdims=True)
        scores_grad = (attention * (attention_grad - weighted)).astype(jnp.bfloat16)
        query_grad = jnp.einsum(
            "shqk,skhd->sqhd", scores_grad, key_row, preferred_element_type=jnp.float32
        ) * HEAD_DIM ** (-0.5)
        key_grad = jnp.einsum(
            "shqk,sqhd->skhd", scores_grad, query_row, preferred_element_type=jnp.float32
        ) * HEAD_DIM ** (-0.5)
        return (
            query_grad.astype(jnp.bfloat16),
            key_grad.astype(jnp.bfloat16),
            value_grad.astype(jnp.bfloat16),
        )

    query_grad, key_grad, value_grad = lax.map(
        attend_back,
        (
            queries.reshape(shaped),
            key_rows.reshape(shaped),
            value_rows.reshape(shaped),
            allowed,
            logsum,
            context_grad.reshape(shaped),
        ),
    )
    query_grad = query_grad.reshape(-1, D)
    key_grad = key_grad.reshape(-1, D)
    value_grad = value_grad.reshape(-1, D)
    query_add_grad = jnp.sum(query_grad.astype(jnp.float32), axis=0)
    value_add_grad = jnp.sum(value_grad.astype(jnp.float32), axis=0)
    query_mat_grad = jnp.dot(hidden_in.T, query_grad, preferred_element_type=jnp.float32)
    key_mat_grad = jnp.dot(hidden_in.T, key_grad, preferred_element_type=jnp.float32)
    value_mat_grad = jnp.dot(hidden_in.T, value_grad, preferred_element_type=jnp.float32)
    input_grad = (
        residual_grad
        + jnp.dot(query_grad, query_mat.T, preferred_element_type=jnp.float32)
        + jnp.dot(key_grad, key_mat.T, preferred_element_type=jnp.float32)
        + jnp.dot(value_grad, value_mat.T, preferred_element_type=jnp.float32)
    )
    gradients = (
        query_mat_grad,
        query_add_grad,
        key_mat_grad,
        value_mat_grad,
        value_add_grad,
        output_mat_grad,
        output_add_grad,
        gain_one_grad,
        shift_one_grad,
        inner_mat_grad,
        inner_add_grad,
        outer_mat_grad,
        outer_add_grad,
        gain_two_grad,
        shift_two_grad,
    )
    return (input_grad, gradients)


def per_device(
    hidden_in,
    cotangent,
    span_lengths,
    partner_span,
    query_weight,
    query_bias,
    key_weight,
    value_weight,
    value_bias,
    output_weight,
    output_bias,
    first_gain,
    first_shift,
    inner_weight,
    inner_bias,
    outer_weight,
    outer_bias,
    second_gain,
    second_shift,
):
    shards = (
        query_weight,
        query_bias,
        key_weight,
        value_weight,
        value_bias,
        output_weight,
        output_bias,
        first_gain,
        first_shift,
        inner_weight,
        inner_bias,
        outer_weight,
        outer_bias,
        second_gain,
        second_shift,
    )
    length = SPAN * SPANS_ROW
    row_count = hidden_in.shape[0] // length
    allowed = jnp.arange(SPAN)[None, None, :] < span_lengths.reshape(row_count, SPANS_ROW, 1)
    gathered = collect(shards)
    encoded, stored = encode(hidden_in, allowed, gathered)
    cls_rows = (
        encoded.reshape(row_count, SPANS_ROW, SPAN, D)[:, :, 0, :]
        .reshape(-1, D)
        .astype(jnp.bfloat16)
    )
    other_rows = mate(cls_rows)
    logits = jnp.dot(cls_rows, other_rows.T, preferred_element_type=jnp.float32) / math.sqrt(D)
    span_count = cls_rows.shape[0]
    matches = (partner_span.reshape(span_count, 1) == jnp.arange(span_count)[None, :]).astype(
        jnp.float32
    )
    target = jnp.where(lax.axis_index("pair") == 0, matches, matches.T)
    highest_logit = jnp.max(logits, axis=-1, keepdims=True)
    exponent = jnp.exp(logits - highest_logit)
    totals = jnp.sum(exponent, axis=-1, keepdims=True)
    span_loss = highest_logit[:, 0] + jnp.log(totals[:, 0]) - jnp.sum(target * logits, axis=-1)
    softened = exponent / totals - target
    own_grad = jnp.dot(softened, other_rows.astype(jnp.float32), precision=highest)
    other_logits = logits.T
    other_highest = jnp.max(other_logits, axis=-1, keepdims=True)
    other_exponent = jnp.exp(other_logits - other_highest)
    other_softened = (
        other_exponent / jnp.sum(other_exponent, axis=-1, keepdims=True) - target.T
    )
    back_grad = jnp.dot(
        other_softened.T, other_rows.astype(jnp.float32), precision=highest
    ).astype(jnp.bfloat16)
    cls_gradient = (own_grad + back_grad.astype(jnp.float32)).reshape(row_count, SPANS_ROW, 1, D)
    placed = jnp.concatenate(
        [cls_gradient, jnp.zeros((row_count, SPANS_ROW, SPAN - 1, D), jnp.float32)], axis=2
    )
    out_gradient = cotangent.astype(jnp.float32) + placed.reshape(-1, D)
    input_grad, gradients = backward(hidden_in, allowed, gathered, stored, out_gradient)
    reduced = spread(gradients)
    return (encoded.astype(jnp.bfloat16), input_grad.astype(jnp.bfloat16), span_loss) + tuple(
        reduced
    )


ROW = 24
PLACES = 8


def coordinates():
    doc = lax.axis_index("doc")
    return (doc & 1, (doc >> 1) & 1, doc >> 2, lax.axis_index("pair"))


def blocks_of(row):
    block = (row * 2731) >> 16
    return (block >> 1) & 1, block & 1, (block >> 2) & 1, block >> 3, row - block * ROW


def restore_from(place):
    row = lax.broadcasted_iota(jnp.int32, (D, 1), 0)
    core, y_at, x_at, z_at, inside = blocks_of(row)
    offset = ((core ^ place[0]) * 2 + (y_at ^ place[1])) * 2 + (x_at ^ place[2])
    arrived = (offset * 4 + (z_at ^ place[3])) * ROW + inside
    hit = arrived == lax.broadcasted_iota(jnp.int32, (D, D), 1)
    return jnp.where(hit, 1.0, 0.0).astype(jnp.bfloat16)


def arrange_from(place):
    row = lax.broadcasted_iota(jnp.int32, (1, D), 1)
    core, y_at, x_at, z_at, inside = blocks_of(row)
    offset = ((y_at ^ place[1]) * 2 + (x_at ^ place[2])) * 4 + (z_at ^ place[3])
    leaving = offset * 2 * ROW + core * ROW + inside
    hit = leaving == lax.broadcasted_iota(jnp.int32, (D, D), 0)
    return jnp.where(hit, 1.0, 0.0).astype(jnp.bfloat16)


def after(value, *others):
    return lax.optimization_barrier((value,) + others)[0]


def z_exchange(block, masks=(4, 8, 12)):
    return [across(block, mask) for mask in masks]


def tied(values, *others):
    return lax.optimization_barrier(tuple(values) + others)[: len(values)]


def near_exchange(block):
    return across(block[0], 2), mate(block[1])


def stack_near(block, received):
    return stack_pair(block[0], received[0], block[1], received[1])


def far_exchange(block):
    return mate(block[0]), across(block[1], 2)


def core_exchange(block):
    return [across(part, 1) for part in block]


def pieces_of(near, far, core, far_core):
    return [near[0], far[0], near[1], far[1], core, far_core[0], far_core[1]]


VMEM = pl.BlockSpec(memory_space=pltpu.VMEM)
SMEM = pl.BlockSpec(memory_space=pltpu.SMEM)


def full(shape):
    return pl.BlockSpec(shape, lambda *at: (0,) * len(shape))


class Fetched:
    def __init__(self, source, held, semaphore):
        self.copy, self.held, self.waiting = pltpu.make_async_copy(source, held, semaphore), held, True
        self.shape = held.shape
        self.copy.start()

    def ready(self):
        if self.waiting:
            self.copy.wait()
            self.waiting = False
        return self.held

    def __getitem__(self, at):
        return self.ready()[at]


class Stored:
    def __init__(self, target, held, semaphores):
        self.target, self.held, self.semaphores, self.copies = target, held, semaphores, []
        self.shape = held.shape

    def __getitem__(self, at):
        return self.held[at]

    def __setitem__(self, at, value):
        self.held[at] = value

    def done(self, at=None):
        semaphore = self.semaphores.at[len(self.copies)]
        held, target = (self.held, self.target) if at is None else (self.held.at[at], self.target.at[at])
        self.copies.append(pltpu.make_async_copy(held, target, semaphore))
        self.copies[-1].start()


PARTS = 8


def ready(ref):
    return ref.ready() if isinstance(ref, Fetched) else ref


def run(kernel, name, operands, results, flops, scratch=(), mib=12, total=None):
    in_hbm = pl.BlockSpec(memory_space=pltpu.HBM)
    spaces = {"S": SMEM, "V": VMEM, "H": in_hbm, "A": in_hbm}
    spaces["K"] = VMEM
    in_places = [place for _, place in operands]
    out_places = [place for _, _, place in results]
    staged = [pltpu.VMEM(array.shape, array.dtype) for array, place in operands if place == "H"]
    made = [pltpu.VMEM(shape, dtype) for shape, dtype, place in results if place == "H"]
    semaphores = [pltpu.SemaphoreType.DMA((max(1, len(staged)),))]
    semaphores += [pltpu.SemaphoreType.DMA((max(1, len(made)), PARTS))]

    def body(*refs):
        ins, refs = refs[: len(operands)], refs[len(operands) :]
        outs, refs = refs[: len(results)], refs[len(results) :]
        held_in, refs = refs[: len(staged)], refs[len(staged) :]
        held_out, refs = refs[: len(made)], refs[len(made) :]
        fetching, storing, own = refs[0], refs[1], refs[2:]
        arguments, at = [], 0
        for ref, place in zip(ins, in_places):
            if place == "H":
                ref, at = Fetched(ref, held_in[at], fetching.at[at]), at + 1
            arguments.append(ref)
        inputs, at = list(arguments), 0
        for ref, place in zip(outs, out_places):
            if place == "H":
                ref, at = Stored(ref, held_out[at], storing.at[at]), at + 1
            arguments.append(ref)
        kernel(*arguments, *own)
        for ref in inputs:
            if isinstance(ref, Fetched):
                ref.ready()
        made_here = [ref for ref in arguments if isinstance(ref, Stored)]
        for ref in made_here:
            if not ref.copies:
                ref.done()
        for ref in made_here:
            for copy in ref.copies:
                copy.wait()

    size = lambda shape, dtype: math.prod(shape) * jnp.dtype(dtype).itemsize
    inside = sum(size(array.shape, array.dtype) for array, place in operands if place == "H")
    inside += sum(size(shape, dtype) for shape, dtype, place in results if place == "H")
    mib = (mib + inside // 2**20) if total is None else total
    return pl.pallas_call(
        body,
        in_specs=[spaces[place] for place in in_places],
        out_specs=[spaces[place] for place in out_places],
        out_shape=[jax.ShapeDtypeStruct(shape, dtype) for shape, dtype, _ in results],
        scratch_shapes=staged + made + semaphores + list(scratch),
        compiler_params=params(mib),
        cost_estimate=cost(1, 1),
        name=name,
    )(*[array for array, _ in operands])


def placed_at(place, *arrays):
    return [(array, place) for array in arrays]


bf16, f32 = jnp.bfloat16, jnp.float32


def params(mib=16):
    return pltpu.CompilerParams(vmem_limit_bytes=mib << 20)


def cost(flops, moved):
    return pl.CostEstimate(flops=int(flops), bytes_accessed=int(moved), transcendentals=0)


def dot(left, right):
    return jnp.dot(left, right, preferred_element_type=jnp.float32)


def dot_nt(left, right):
    return lax.dot_general(
        left, right, (((1,), (1,)), ((), ())), preferred_element_type=jnp.float32
    )


def dot_tn(left, right):
    return lax.dot_general(
        left, right, (((0,), (0,)), ((), ())), preferred_element_type=jnp.float32
    )


def pack_kernel(*refs):
    query, key, value, output, inner, inner_bias = refs[:6]
    vectors, (first, second, turned) = refs[6:-3], refs[-3:]
    turned[...] = jnp.zeros_like(turned)
    for at, vector in enumerate(vectors):
        turned[at : at + 1, :ROW] = vector[...].astype(jnp.float32)
    bias = inner_bias[...].astype(jnp.float32)
    for at in range(4):
        turned[8 + at : 9 + at, :ROW] = bias[:, at * ROW : (at + 1) * ROW]
    small = jnp.transpose(turned[...])[:ROW].astype(jnp.bfloat16)
    first[:, :D] = query[...]
    first[:, D : D + 512] = key[:, :512]
    first[:, D + 512 : D + 640] = small
    first[:, D + 640 : D + 768] = jnp.zeros_like(small)
    first[:, D + 768 : D + 1024] = key[:, 512:]
    first[:, D + 1024 :] = value[...]
    second[:, :D] = output[...]
    second[:, D:] = inner[...]


def pack(query, key, value, output, inner, inner_bias, vectors):
    rows = [vector.reshape(1, -1) for vector in (inner_bias, *vectors)]
    return run(
        pack_kernel,
        "pack",
        placed_at("H", query, key, value, output, inner, *rows),
        [((ROW, 2 * FIRST_HALF), bf16, "V"), ((ROW, D + inner.shape[1]), bf16, "V")],
        1e6,
        [pltpu.VMEM((128, 128), f32)],
        total=58,
    )


def stack_two_kernel(first, second, left, right):
    blocks = [first[...].astype(jnp.float32), second[...].astype(jnp.float32)]
    whole = jnp.concatenate(blocks).astype(jnp.bfloat16)
    left[...] = whole[:, : left.shape[1]]
    right[...] = whole[:, left.shape[1] :]


def stack_two(block, received, split):
    rows, columns = block.shape
    return pl.pallas_call(
        stack_two_kernel,
        in_specs=[VMEM] * 2,
        out_specs=[VMEM] * 2,
        out_shape=[
            jax.ShapeDtypeStruct((2 * rows, split), jnp.bfloat16),
            jax.ShapeDtypeStruct((2 * rows, columns - split), jnp.bfloat16),
        ],
        compiler_params=params(),
        cost_estimate=cost(1, 1),
        name="stack_two",
    )(block, received)


def stack_z_two_kernel(first, second, out):
    blocks = [first[...].astype(jnp.float32), second[...].astype(jnp.float32)]
    out[...] = jnp.concatenate(blocks).astype(jnp.bfloat16)


def stack_z_two(block, received):
    rows, columns = block.shape
    return pl.pallas_call(
        stack_z_two_kernel,
        in_specs=[VMEM] * 2,
        out_specs=VMEM,
        out_shape=jax.ShapeDtypeStruct((2 * rows, columns), jnp.bfloat16),
        compiler_params=params(),
        cost_estimate=cost(1, 1),
        name="stack_z_two",
    )(block, received)


def stack_mixed_kernel(split, two, received, left, right):
    rows = two.shape[0] // 2
    own, other = two[...].astype(jnp.float32), received[...].astype(jnp.float32)
    whole = jnp.concatenate([own[:rows], other[:rows], own[rows:], other[rows:]]).astype(jnp.bfloat16)
    left[...] = whole[:, :split]
    right[...] = whole[:, split:]


def stack_mixed(two, received, split):
    rows, columns = two.shape
    return pl.pallas_call(
        partial(stack_mixed_kernel, split),
        in_specs=[VMEM] * 2,
        out_specs=[VMEM] * 2,
        out_shape=[
            jax.ShapeDtypeStruct((2 * rows, split), jnp.bfloat16),
            jax.ShapeDtypeStruct((2 * rows, columns - split), jnp.bfloat16),
        ],
        compiler_params=params(),
        cost_estimate=cost(1, 1),
        name="stack_mixed",
    )(two, received)


def stack_z_kernel(split, *refs):
    blocks, (left, right) = refs[:-2], refs[-2:]
    whole = jnp.concatenate([ref[...].astype(jnp.float32) for ref in blocks]).astype(jnp.bfloat16)
    left[...] = whole[:, :split]
    right[...] = whole[:, split:]


def stack_z(block, received, split):
    rows, columns = block.shape
    rows = rows * (1 + len(received)) // 4
    return pl.pallas_call(
        partial(stack_z_kernel, split),
        in_specs=[VMEM] * (1 + len(received)),
        out_specs=[VMEM] * 2,
        out_shape=[
            jax.ShapeDtypeStruct((4 * rows, split), jnp.bfloat16),
            jax.ShapeDtypeStruct((4 * rows, columns - split), jnp.bfloat16),
        ],
        compiler_params=params(),
        cost_estimate=cost(1, 1),
        name="stack_z",
    )(block, *received)


def stack_pair_kernel(left, left_in, right, right_in, left_out, right_out, both_out):
    width = left.shape[1]
    for own, received, out, columns in (
        (left, left_in, left_out, slice(0, width)),
        (right, right_in, right_out, slice(width, width + right.shape[1])),
    ):
        rows = own.shape[0]
        out[:rows, :] = own[...]
        out[rows:, :] = received[...]
        both_out[:rows, columns] = own[...]
        both_out[rows:, columns] = received[...]


def stack_pair(left, left_in, right, right_in):
    double = lambda block: jax.ShapeDtypeStruct((2 * block.shape[0], block.shape[1]), block.dtype)
    both = jax.ShapeDtypeStruct((2 * left.shape[0], left.shape[1] + right.shape[1]), left.dtype)
    return pl.pallas_call(
        stack_pair_kernel,
        in_specs=[VMEM] * 4,
        out_specs=[VMEM] * 3,
        out_shape=[double(left), double(right), both],
        compiler_params=params(),
        cost_estimate=cost(1, 1),
        name="stack_pair",
    )(left, left_in, right, right_in)


def left_tile(refs, columns):
    return jnp.concatenate([ref[:, columns] for ref in refs])


def right_tile(refs, columns):
    near, far, other_near, other_far = refs
    rows = near.shape[0] // 2
    order = [(near, 0), (far, 0), (near, 1), (far, 1)]
    order += [(other_near, 0), (other_far, 0), (other_near, 1), (other_far, 1)]
    return jnp.concatenate([ref[at * rows : (at + 1) * rows, columns] for ref, at in order])


def in_order(pieces):
    left, left_far, right, right_far, c_both, c_left_far, c_right_far = pieces
    return (left, left_far, c_left_far, c_both, right, right_far, c_right_far)


class Side:
    def __init__(self, ref, start, width):
        self.ref, self.start, self.shape = ref, start, (ref.shape[0], width)

    def __getitem__(self, at):
        rows, columns = at
        return self.ref[rows, columns.start + self.start : columns.stop + self.start]


def sides(l0, l1, l3, both, r0, r1, r3):
    left, right = l0.shape[1], r0.shape[1]
    return (l0, l1, Side(both, 0, left), l3), (r0, r1, Side(both, left, right), r3)


FIRST_PARTS = ((0, 0, 768), (0, 768, 512), (1, 256, 256), (1, 512, 768))
SECOND_PARTS = ((0, 0, 768), (0, 768, 512), (0, 1280, 640))
SECOND_PARTS += ((1, 0, 384), (1, 384, 512), (1, 896, 512), (1, 1408, 512))


def settle(sides_of, parts, mats, semaphore):
    copies = []
    for (side, start, width), mat in zip(parts, mats):
        for at, piece in enumerate(sides_of[side]):
            rows = piece.shape[0]
            source, first = (piece.ref, piece.start) if isinstance(piece, Side) else (piece, 0)
            columns = pl.ds(first + start, width)
            if side == 0:
                copies.append((source.at[:, columns], mat.at[pl.ds(at * rows, rows), :]))
                continue
            half = rows // 2
            core, far = at // 2, at % 2
            for near in range(2):
                to = ((core * 2 + near) * 2 + far) * half
                copies.append((source.at[pl.ds(near * half, half), columns], mat.at[pl.ds(to, half), :]))
    copies = [pltpu.make_async_copy(*ends, semaphore.at[at]) for at, ends in enumerate(copies)]
    for copy in copies:
        copy.start()
    return copies


FIRST_HALF = 1280
SECOND_HALF = 1920
def head_pair(pair, low):
    nothing = jnp.zeros_like(pair)
    return jnp.concatenate([jnp.where(low, pair, nothing), jnp.where(low, nothing, pair)])


def key_columns(left_rows, right_rows, rows, at):
    if at < 512:
        return left_rows[rows, D + at : D + at + 128]
    return right_rows[rows, at - 256 : at - 128]


def project_kernel(
    place,
    hidden,
    both,
    r0,
    r1,
    r3,
    l0,
    l1,
    l3,
    left_rows,
    right_rows,
    vectors,
    hidden_t,
    query_mat,
    low_key_mat,
    high_key_mat,
    value_mat,
    settling,
):
    tokens = hidden.shape[0]
    lefts, rights = sides(l0, l1, l3, both, r0, r1, r3)
    mats = (query_mat, low_key_mat, high_key_mat, value_mat)
    copies = settle((lefts, rights), FIRST_PARTS, mats, settling)
    restore = restore_from(place)
    moved = dot(hidden[...], restore).astype(jnp.bfloat16)
    small = dot(restore, right_tile(rights, slice(0, 128)))
    turned = jnp.transpose(small)[:16]
    vectors[...] = turned
    for at in range(0, FIRST_HALF, 256):
        columns = slice(at, at + 256)
        rows = dot(moved, left_tile(lefts, columns))
        if at < D:
            rows += turned[0:1, columns]
        left_rows[:, columns] = rows.astype(jnp.bfloat16)
        if at == 0:
            right_rows[:, columns] = jnp.zeros((tokens, 256), jnp.bfloat16)
            continue
        rows = dot(moved, right_tile(rights, columns))
        if at >= 512:
            rows += turned[1:2, at - 512 : at - 256]
        right_rows[:, columns] = rows.astype(jnp.bfloat16)
    left_rows.done()
    right_rows.done()
    hidden_t[...] = dot_nt(arrange_from(place), hidden[...]).astype(jnp.bfloat16)
    for copy in copies:
        copy.wait()


def project(place, hidden, pieces):
    tokens, ordered = hidden.shape[0], in_order(pieces)
    return run(
        project_kernel,
        "project",
        [(place, "S"), (hidden, "H")] + placed_at("K", *ordered[3:], *ordered[:3]),
        [
            ((tokens, FIRST_HALF), bf16, "H"),
            ((tokens, FIRST_HALF), bf16, "H"),
            ((16, D), f32, "V"),
            ((D, tokens), bf16, "H"),
        ]
        + [((D, width), bf16, "A") for _, _, width in FIRST_PARTS],
        9e9,
        [pltpu.SemaphoreType.DMA((24,))],
        total=50,
    )


def attention_kernel(
    place, lengths, left_rows, right_rows, attention_out, context_arrived, context_t, context
):
    tokens = context.shape[0]
    left_rows, right_rows = ready(left_rows), ready(right_rows)
    low = lax.broadcasted_iota(jnp.int32, (SPAN, 128), 1) < HEAD_DIM

    def attend(span, carry):
        rows = pl.ds(pl.multiple_of(span * SPAN, SPAN), SPAN)
        live = lax.broadcasted_iota(jnp.int32, (SPAN, SPAN), 1) < lengths[span]
        for at in range(0, D, 128):
            query = left_rows[rows, at : at + 128]
            keys = head_pair(key_columns(left_rows, right_rows, rows, at), low)
            values = head_pair(right_rows[rows, 512 + at : 640 + at], low)
            scores = dot_nt(query, keys) * HEAD_DIM ** (-0.5)
            parts = []
            for head in range(2):
                part = jnp.where(live, scores[:, head * SPAN : (head + 1) * SPAN], masked_out)
                exponent = jnp.exp(part - jnp.max(part, axis=-1, keepdims=True))
                parts.append(
                    (exponent * (1.0 / jnp.sum(exponent, axis=-1, keepdims=True))).astype(jnp.bfloat16)
                )
            attention = jnp.concatenate(parts, axis=1)
            attention_out[rows, 2 * at : 2 * at + 256] = attention
            context[rows, at : at + 128] = dot(attention, values).astype(jnp.bfloat16)
        return carry

    lax.fori_loop(0, tokens // SPAN, attend, 0)
    attention_out.done()
    context_arrived[...] = dot(context[...], restore_from(place)).astype(jnp.bfloat16)
    context_t[...] = dot_nt(arrange_from(place), context[...]).astype(jnp.bfloat16)


def attention_forward(place, lengths, left_rows, right_rows):
    tokens = left_rows.shape[0]
    return run(
        attention_kernel,
        "attention_forward",
        placed_at("S", place, lengths) + placed_at("H", left_rows, right_rows),
        [((tokens, 2 * D), bf16, "H"), ((tokens, D), bf16, "V"), ((D, tokens), bf16, "H")],
        9e9,
        [pltpu.VMEM((tokens, D), bf16)],
        total=28,
    )


def gelu_parts(preact):
    scaled = jnp.abs(preact) * (0.5**0.5)
    below_one = 1.0 + 0.3275911 * scaled
    near = pl.reciprocal(below_one, approx=True)
    near = near * (2.0 - below_one * near)
    poly = near * (
        0.254829592
        + near * (-0.284496736 + near * (1.421413741 + near * (-1.453152027 + near * 1.061405429)))
    )
    bell = jnp.exp(-0.5 * preact * preact)
    tail = 0.5 * poly * bell
    below = jnp.where(preact < 0.0, tail, 1.0 - tail)
    return (preact * below, below + preact * bell * (0.5 / math.pi) ** 0.5)


def feed_columns():
    for side, start, width in SECOND_PARTS[1:]:
        at = start - D if side == 0 else SECOND_HALF - D + start
        yield side, slice(start, start + width), slice(at, at + width)


def vector_places():
    for device in range(D // ROW):
        for part in range(4):
            yield (8 + part, device * ROW), (device * 4 + part) * ROW


def residual_kernel(
    place,
    vectors,
    context_arrived,
    l0,
    l1,
    l3,
    both,
    hidden,
    moved,
    normed_out,
    factor_out,
    first_t,
    output_mat,
    settling,
):
    left = (l0, l1, Side(both, 0, l0.shape[1]), l3)
    copies = settle((left, ()), SECOND_PARTS[:1], (output_mat,), settling)
    residual = dot(context_arrived[...], left_tile(left, slice(0, D)))
    residual += hidden[...].astype(jnp.float32) + vectors[2:3, :]
    first_out, normed, factor = normalize(residual, vectors[3:4, :], vectors[4:5, :])
    normed_out[...] = normed
    factor_out[...] = factor
    first16 = first_out.astype(jnp.bfloat16)
    moved[...] = dot(first16, restore_from(place)).astype(jnp.bfloat16)
    first_t[...] = dot_nt(arrange_from(place), first16).astype(jnp.bfloat16)
    for copy in copies:
        copy.wait()


def residual_forward(place, hidden, context_arrived, vectors, pieces):
    tokens, ordered = hidden.shape[0], in_order(pieces)
    return run(
        residual_kernel,
        "residual",
        [(place, "S")]
        + placed_at("V", vectors, context_arrived, *ordered[:4])
        + [(hidden, "H")],
        [
            ((tokens, D), bf16, "V"),
            ((tokens, D), f32, "V"),
            ((tokens, 1), f32, "V"),
            ((D, tokens), bf16, "H"),
            ((D, D), bf16, "A"),
        ],
        1e9,
        [pltpu.SemaphoreType.DMA((4,))],
        total=24,
    )


def feed_kernel(vectors, moved, l0, l1, l3, both, r0, r1, r3, active, active_t, slope, *rest):
    mats, (inner_bias, settling) = rest[:-2], rest[-2:]
    for at, column in vector_places():
        inner_bias[:, column : column + ROW] = vectors[at[0] : at[0] + 1, at[1] : at[1] + ROW]
    left, right = sides(l0, l1, l3, both, r0, r1, r3)
    copies = settle((left, right), SECOND_PARTS[1:], mats, settling)
    for side, part, columns in feed_columns():
        tile = right_tile(right, part) if side else left_tile(left, part)
        value, derivative = gelu_parts(dot(moved[...], tile) + inner_bias[:, columns])
        value16 = value.astype(jnp.bfloat16)
        active[:, columns] = value16
        active_t[columns, :] = jnp.transpose(value16)
        slope[:, columns] = derivative.astype(jnp.bfloat16)
    for copy in copies:
        copy.wait()


def feed_forward(moved, vectors, ff, pieces):
    tokens = moved.shape[0]
    return run(
        feed_kernel,
        "feed_forward",
        placed_at("V", vectors, moved, *in_order(pieces)),
        [((tokens, ff), bf16, "V"), ((ff, tokens), bf16, "V"), ((tokens, ff), bf16, "V")]
        + [((D, width), bf16, "A") for _, _, width in SECOND_PARTS[1:]],
        8e9,
        [pltpu.VMEM((1, ff), f32), pltpu.SemaphoreType.DMA((44,))],
        total=20,
    )


def natural_rows(place, pieces, target, semaphore):
    rows = 4 * ROW
    left, right = pieces[0].shape[1], pieces[4].shape[1]
    near, far, far_core, near_core, right_near, right_far, right_far_core = pieces
    places = [(near, 0, 0, 0, 0), (far, 0, 0, 1, 0), (near_core, 0, 1, 0, 0), (far_core, 0, 1, 1, 0)]
    places += [(right_near, 1, 0, 0, 0), (right_far, 1, 0, 1, 0)]
    places += [(near_core, 1, 1, 0, left), (right_far_core, 1, 1, 1, 0)]
    for piece, is_right, core_off, far_off, start in places:
        half = right if is_right else left
        for near_off in range(2):
            for z_off in range(4):
                x_off, y_off = (far_off, near_off) if is_right else (near_off, far_off)
                block = ((z_off ^ place[3]) * 2 + (x_off ^ place[2])) * 2 + (core_off ^ place[0])
                block = block * 2 + (y_off ^ place[1])
                to = pl.ds(pl.multiple_of(block * rows, rows), rows)
                pltpu.make_async_copy(
                    piece.at[pl.ds((near_off * 4 + z_off) * rows, rows), pl.ds(start, half)],
                    target.at[to, pl.ds(is_right * left, half)],
                    semaphore,
                ).start()
    pltpu.make_async_copy(target, target, semaphore).wait()


def last_kernel(
    place,
    active,
    first_normed,
    vectors,
    l0,
    l1,
    l3,
    both,
    r0,
    r1,
    r3,
    layer_out,
    normed_out,
    factor_out,
    cls_rows,
    outer_mat,
    semaphore,
):
    natural_rows(place, (l0, l1, l3, both, r0, r1, r3), outer_mat, semaphore)
    total = first_normed[...] * vectors[3:4, :] + vectors[4:5, :] + vectors[5:6, :]
    total += dot(active[...], outer_mat[...])
    encoded, normed, factor = normalize(total, vectors[6:7, :], vectors[7:8, :])
    layer_out[...] = encoded.astype(jnp.bfloat16)
    normed_out[...] = normed
    factor_out[...] = factor
    for span in range(encoded.shape[0] // SPAN):
        cls_rows[span : span + 1, :] = encoded[span * SPAN : span * SPAN + 1].astype(jnp.bfloat16)


def last(place, active, first_normed, vectors, pieces):
    tokens, ff = active.shape
    return run(
        last_kernel,
        "last",
        [(place, "S")]
        + placed_at("V", active, first_normed, vectors, *in_order(pieces)),
        [
            ((tokens, D), bf16, "H"),
            ((tokens, D), f32, "V"),
            ((tokens, 1), f32, "V"),
            ((tokens // SPAN, D), bf16, "V"),
            ((ff, D), bf16, "V"),
        ],
        2.5e9,
        [pltpu.SemaphoreType.DMA],
        total=16,
    )


def pick(place, first, second):
    return jnp.where(place == 0, first, second)


def turn_kernel(
    place,
    partner_span,
    cotangent,
    normed,
    factor,
    vectors,
    own_rows,
    other_rows,
    second_grad,
    kept,
    sent,
    sums,
    loss,
):
    spans = own_rows.shape[0]
    own, other = own_rows[...].astype(jnp.float32), other_rows[...].astype(jnp.float32)
    logits = dot_nt(own_rows[...], other_rows[...]) / math.sqrt(D)
    row = lax.broadcasted_iota(jnp.int32, (spans, spans), 0)
    column = lax.broadcasted_iota(jnp.int32, (spans, spans), 1)
    first_place = place[1] == 0
    target = jnp.zeros((spans, spans), jnp.float32)
    for span in range(spans):
        match = partner_span[0, span]
        hit_row = jnp.where(first_place, span, match)
        hit_column = jnp.where(first_place, match, span)
        target += ((row == hit_row) & (column == hit_column)).astype(jnp.float32)
    highest_logit = jnp.max(logits, axis=1, keepdims=True)
    exponent = jnp.exp(logits - highest_logit)
    totals = jnp.sum(exponent, axis=1, keepdims=True)
    losses = highest_logit + jnp.log(totals) - jnp.sum(target * logits, axis=1, keepdims=True)
    loss[...] = jnp.sum(jnp.where(row == column, losses, 0.0), axis=0, keepdims=True)
    soft = exponent / totals - target
    exponent = jnp.exp(logits - jnp.max(logits, axis=0, keepdims=True))
    back = exponent / jnp.sum(exponent, axis=0, keepdims=True) - target
    own_term, back_term = jnp.zeros_like(own), jnp.zeros_like(own)
    for span in range(spans):
        own_term += soft[:, span : span + 1] * other[span : span + 1]
        back_term += back[:, span : span + 1] * other[span : span + 1]
    cls_gradient = own_term + back_term.astype(jnp.bfloat16).astype(jnp.float32)
    start = lax.broadcasted_iota(jnp.int32, (SPAN, 1), 0) == 0
    gain = vectors[6:7, :]
    gain_sum = jnp.zeros((1, D), jnp.float32)
    shift_sum, bias_sum = gain_sum, gain_sum
    for span in range(spans):
        rows = slice(span * SPAN, (span + 1) * SPAN)
        upstream = cotangent[rows, :].astype(jnp.float32)
        upstream += jnp.where(start, cls_gradient[span : span + 1], 0.0)
        grad, gain_part, shift_part = normalize_back(upstream, normed[rows, :], factor[rows, :], gain)
        second_grad[rows, :] = grad
        gain_sum += gain_part[None]
        shift_sum += shift_part[None]
        bias_sum += jnp.sum(grad, axis=0, keepdims=True)
        grad16 = grad.astype(jnp.bfloat16)
        kept[rows, :] = pick(place[0], grad16[:, : D // 2], grad16[:, D // 2 :])
        sent[rows, :] = pick(place[0], grad16[:, D // 2 :], grad16[:, : D // 2])
    sums[0:1, :] = bias_sum
    sums[1:2, :] = gain_sum
    sums[2:3, :] = shift_sum


def turn(place, partner_span, cotangent, normed, factor, vectors, own_rows, other_rows):
    tokens = cotangent.shape[0]
    return run(
        turn_kernel,
        "turn",
        placed_at("S", place, partner_span)
        + [(cotangent, "H")]
        + placed_at("V", normed, factor, vectors, own_rows, other_rows),
        [
            ((tokens, D), f32, "V"),
            ((tokens, D // 2), bf16, "V"),
            ((tokens, D // 2), bf16, "V"),
            ((3, D), f32, "V"),
            ((1, own_rows.shape[0]), f32, "V"),
        ],
        1e8,
    )


def both_halves(place, kept, sent):
    return jnp.concatenate([pick(place, kept, sent), pick(place, sent, kept)], axis=1)


def slope_kernel(place, second_kept, second_sent, outer_mat, slope, kept, sent, sums, second16):
    second16[...] = both_halves(place[0], second_kept[...], second_sent[...])
    per_half = kept.shape[1] // D

    def tile(at, carry):
        columns = pl.ds(pl.multiple_of(at * D, D), D)
        inside = pl.ds(pl.multiple_of((at % per_half) * D, D), D)
        grad = dot_nt(second16[...], outer_mat[columns, :]) * slope[:, columns].astype(jnp.float32)
        sums[:, columns] = jnp.sum(grad, axis=0, keepdims=True)
        grad16 = grad.astype(jnp.bfloat16)
        mine = place[0] == at // per_half

        @pl.when(mine)
        def keep():
            kept[:, inside] = grad16

        @pl.when(jnp.logical_not(mine))
        def send():
            sent[:, inside] = grad16

        return carry

    lax.fori_loop(0, 2 * per_half, tile, 0)


def slope_back(place, second_kept, second_sent, outer_mat, slope):
    tokens, ff = slope.shape
    half = ((tokens, ff // 2), bf16, "V")
    return run(
        slope_kernel,
        "slope_back",
        [(place, "S")] + placed_at("V", second_kept, second_sent, outer_mat, slope),
        [half, half, ((1, ff), f32, "V")],
        2.5e9,
        [pltpu.VMEM((tokens, D), bf16)],
    )


CHIPS_TILE = 2


def outer_kernel(place, active_t, other_active_t, kept, received, left_kept, left_sent, right_kept, right_sent):
    rows = 2 * ROW
    height = 8 * CHIPS_TILE * rows

    def chips(at, carry):
        tile = pl.ds(pl.multiple_of(at * height, height), height)
        grad = dot(active_t[tile, :], kept[...]) + dot(other_active_t[tile, :], received[...])
        grad = grad.astype(jnp.bfloat16)
        z_off = (at * CHIPS_TILE // 2) ^ place[3]
        for block in range(4 * CHIPS_TILE):
            x_at, core, y_at = block // 4, block // 2 % 2, block % 2
            start = block * 2 * rows
            left, right = grad[start : start + rows], grad[start + rows : start + 2 * rows]
            x_off, y_off = x_at ^ place[2], y_at ^ place[1]
            left_at = (x_off * 4 + z_off) * 2 + core
            right_at = (y_off * 4 + z_off) * 2 + core

            @pl.when(y_off == 0)
            def left_here():
                left_kept[left_at] = left

            @pl.when(y_off == 1)
            def left_there():
                left_sent[left_at] = left

            @pl.when(x_off == 0)
            def right_here():
                right_kept[right_at] = right

            @pl.when(x_off == 1)
            def right_there():
                right_sent[right_at] = right

        return carry

    lax.fori_loop(0, PLACES // CHIPS_TILE, chips, 0)


def outer_gradient(place, active_t, other_active_t, kept, received):
    piece = ((2 * PLACES, 2 * ROW, kept.shape[1]), bf16, "V")
    return run(
        outer_kernel,
        "outer_gradient",
        [(place, "S")] + placed_at("V", active_t, other_active_t, kept, received),
        [piece] * 4,
        2.5e9,
    )


def whole_precision(left, right):
    high = left.astype(jnp.bfloat16)
    rest = (left - high.astype(jnp.float32)).astype(jnp.bfloat16)
    return dot_nt(high, right) + dot_nt(rest, right)


def first_kernel(
    place,
    preact_kept,
    preact_sent,
    factor,
    vectors,
    *refs,
):
    output_mat, inner_mats = refs[0], refs[1:7]
    second_grad, normed, residual_grad, kept, sent, context_grad, sums = refs[7:]
    restore = restore_from(place)
    total = jnp.zeros((factor.shape[0], D), jnp.float32)
    half = preact_kept.shape[1]
    for (_, _, whole), tile in zip(feed_columns(), inner_mats):
        at, width = whole.start, whole.stop - whole.start
        columns = slice(at % half, at % half + width)
        kept_part, sent_part = preact_kept[:, columns], preact_sent[:, columns]
        if at >= half:
            kept_part, sent_part = sent_part, kept_part
        total += dot_nt(pick(place[0], kept_part, sent_part), tile[...])
    first_grad = second_grad[...] + whole_precision(total, restore)
    grad, gain_sum, shift_sum = normalize_back(first_grad, normed[...], factor[...], vectors[3:4, :])
    residual_grad[...] = grad
    sums[0:1, :] = jnp.sum(grad, axis=0, keepdims=True)
    sums[1:2, :] = gain_sum[None]
    sums[2:3, :] = shift_sum[None]
    grad16 = grad.astype(jnp.bfloat16)
    kept[...] = pick(place[0], grad16[:, : D // 2], grad16[:, D // 2 :])
    sent[...] = pick(place[0], grad16[:, D // 2 :], grad16[:, : D // 2])
    moved = dot_nt(grad16, output_mat[...]).astype(jnp.bfloat16)
    context_grad[...] = dot_nt(moved, restore).astype(jnp.bfloat16)


def first_back(place, preact_kept, preact_sent, second_grad, normed, factor, vectors, mats):
    tokens = second_grad.shape[0]
    half = ((tokens, D // 2), bf16, "V")
    return run(
        first_kernel,
        "first_back",
        [(place, "S")]
        + placed_at("V", preact_kept, preact_sent, factor, vectors)
        + placed_at("V", *mats, second_grad, normed),
        [((tokens, D), f32, "V"), half, half, ((tokens, D), bf16, "V"), ((3, D), f32, "V")],
        4.9e9,
    )


def part_rows(grad, left_kept, left_sent, right_kept, right_sent, is_left):
    quarter = D // 4
    if is_left:
        left_kept[...] = grad[: 2 * quarter]
        left_sent[...] = grad[2 * quarter :]
    else:
        right_kept[:quarter, :] = grad[:quarter]
        right_sent[:quarter, :] = grad[quarter : 2 * quarter]
        right_kept[quarter:, :] = grad[2 * quarter : 3 * quarter]
        right_sent[quarter:, :] = grad[3 * quarter :]


def inner_kernel(first_t, other_first_t, kept, received, left_kept, left_sent, right_kept, right_sent):
    for is_left in (True, False):
        columns = slice(0, D) if is_left else slice(D, 2 * D)
        grad = dot(first_t[...], kept[:, columns]) + dot(other_first_t[...], received[:, columns])
        part_rows(grad.astype(jnp.bfloat16), left_kept, left_sent, right_kept, right_sent, is_left)


def inner_gradient(first_t, other_first_t, kept, received):
    piece = ((D // 2, kept.shape[1] // 2), bf16, "V")
    return run(
        inner_kernel,
        "inner_gradient",
        placed_at("V", first_t, other_first_t) + placed_at("V", kept, received),
        [piece] * 4,
        2.5e9,
    )


def attend_kernel(
    place,
    context_grad,
    left_rows,
    right_rows,
    attention_in,
    first_sums,
    second_sums,
    inner_sums,
    kept,
    sent,
    sums,
    grads,
):
    tokens = context_grad.shape[0]
    low = lax.broadcasted_iota(jnp.int32, (SPAN, 128), 1) < HEAD_DIM
    scale = HEAD_DIM ** (-0.5)
    left_rows, right_rows, attention_in = [ready(ref) for ref in (left_rows, right_rows, attention_in)]

    def attend(span, carry):
        rows = pl.ds(pl.multiple_of(span * SPAN, SPAN), SPAN)
        for at in range(0, D, 128):
            query = left_rows[rows, at : at + 128]
            keys = head_pair(key_columns(left_rows, right_rows, rows, at), low)
            values = head_pair(right_rows[rows, 512 + at : 640 + at], low)
            upstream = context_grad[rows, at : at + 128]
            attention16 = attention_in[rows, 2 * at : 2 * at + 256]
            attention_grad = dot_nt(upstream, values)
            parts = []
            for head in range(2):
                columns = slice(head * SPAN, (head + 1) * SPAN)
                attention = attention16[:, columns].astype(jnp.float32)
                part = attention_grad[:, columns]
                weighted = jnp.sum(attention * part, axis=-1, keepdims=True)
                parts.append((attention * (part - weighted)).astype(jnp.bfloat16))
            scores_grad = jnp.concatenate(parts, axis=1)
            grads[0, rows, at : at + 128] = (dot(scores_grad, keys) * scale).astype(jnp.bfloat16)
            both = dot_tn(scores_grad, query)
            both = jnp.where(low, both[:SPAN], both[SPAN:])
            grads[1, rows, at : at + 128] = (both * scale).astype(jnp.bfloat16)
            both = dot_tn(attention16, upstream)
            both = jnp.where(low, both[:SPAN], both[SPAN:])
            grads[2, rows, at : at + 128] = both.astype(jnp.bfloat16)
        return carry

    lax.fori_loop(0, tokens // SPAN, attend, 0)
    query_grad, key_grad, value_grad = grads[0], grads[1], grads[2]
    half = D // 2
    for at, grad in enumerate((query_grad, key_grad, value_grad)):
        columns = slice(at * half, (at + 1) * half)
        kept[:, columns] = pick(place[0], grad[:, :half], grad[:, half:])
        sent[:, columns] = pick(place[0], grad[:, half:], grad[:, :half])
    sums[0:1, :] = jnp.sum(query_grad.astype(jnp.float32), axis=0, keepdims=True)
    sums[1:2, :] = jnp.sum(value_grad.astype(jnp.float32), axis=0, keepdims=True)
    sums[2:5, :] = first_sums[...]
    sums[5:8, :] = second_sums[...]
    for at, column in vector_places():
        sums[at[0] : at[0] + 1, at[1] : at[1] + ROW] = inner_sums[:, column : column + ROW]
    sums[12:16, :] = jnp.zeros((4, D), jnp.float32)


def attend_back(place, context_grad, left_rows, right_rows, attention, first_sums, second_sums, inner_sums):
    tokens = context_grad.shape[0]
    part = ((tokens, 3 * D // 2), bf16, "V")
    return run(
        attend_kernel,
        "attend_back",
        placed_at("S", place)
        + placed_at("V", context_grad)
        + placed_at("V", left_rows, right_rows, attention)
        + placed_at("V", first_sums, second_sums, inner_sums),
        [part, part, ((16, D), f32, "V")],
        4e9,
        [pltpu.VMEM((3, tokens, D), bf16)],
    )


def attention_gradient_kernel(
    place,
    sums,
    hidden_t,
    other_hidden_t,
    context_t,
    other_context_t,
    grads,
    other_grads,
    residual,
    other_residual,
    left_kept,
    left_sent,
    right_kept,
    right_sent,
):
    half = D // 2
    grad = dot(hidden_t[...], grads[:, :D]) + dot(other_hidden_t[...], other_grads[:, :D])
    grad = grad.astype(jnp.bfloat16)
    left_kept[:, :D] = grad[:half]
    left_sent[:, :D] = grad[half:]
    total = sums[...].astype(jnp.bfloat16)
    total = jnp.concatenate([total, jnp.zeros((112, D), jnp.bfloat16)])
    small = dot_nt(arrange_from(place), total).astype(jnp.bfloat16)
    left_kept[:, D:] = small[:half]
    left_sent[:, D:] = small[half:]
    value = dot(hidden_t[...], grads[:, D:]) + dot(other_hidden_t[...], other_grads[:, D:])
    output = dot(context_t[...], residual[...]) + dot(other_context_t[...], other_residual[...])
    grad = jnp.concatenate([value, output], axis=1).astype(jnp.bfloat16)
    part_rows(grad, left_kept, left_sent, right_kept, right_sent, False)


def attention_gradient(*operands):
    left, right = ((D // 2, D + 128), bf16, "V"), ((D // 2, D), bf16, "V")
    places = ["S"] + ["V"] * 9
    return run(
        attention_gradient_kernel,
        "attention_gradient",
        list(zip(operands, places)),
        [left, left, right, right],
        2.5e9,
    )


def input_kernel(
    place, kept, sent, query_mat, low_key_mat, high_key_mat, value_mat, residual_grad, input_grad
):
    restore = restore_from(place)
    half = D // 2
    parts = []
    for at in range(3):
        columns = slice(at * half, (at + 1) * half)
        parts.append(both_halves(place[0], kept[:, columns], sent[:, columns]))
    query_grad, key_grad, value_grad = parts
    total = dot_nt(query_grad, query_mat[...])
    total += dot_nt(key_grad[:, :512], low_key_mat[...])
    total += dot_nt(key_grad[:, 512:], high_key_mat[...])
    total += dot_nt(value_grad, value_mat[...])
    total = residual_grad[...] + whole_precision(total, restore)
    input_grad[...] = total.astype(jnp.bfloat16)


def input_back(place, residual_grad, kept, sent, mats):
    return run(
        input_kernel,
        "input_back",
        [(place, "S")]
        + placed_at("V", kept, sent)
        + placed_at("V", *mats, residual_grad),
        [(residual_grad.shape, bf16, "H")],
        3e9,
    )[0]


def add_kernel(left, left_in, right, right_in, left_kept, left_sent, right_kept, right_sent):
    for own, received, kept, sent in (
        (left, left_in, left_kept, left_sent),
        (right, right_in, right_kept, right_sent),
    ):
        total = (own[...].astype(jnp.float32) + received[...].astype(jnp.float32)).astype(jnp.bfloat16)
        half = total.shape[0] // 2
        kept[...] = total[:half]
        sent[...] = total[half:]


def add_parts(left, left_in, right, right_in):
    shapes = [(part.shape[0] // 2,) + part.shape[1:] for part in (left, left, right, right)]
    return pl.pallas_call(
        add_kernel,
        in_specs=[VMEM] * 4,
        out_specs=[VMEM] * 4,
        out_shape=[jax.ShapeDtypeStruct(shape, jnp.bfloat16) for shape in shapes],
        compiler_params=params(),
        cost_estimate=cost(1, 1),
        name="add_parts",
    )(left, left_in, right, right_in)


def add_z_kernel(left, left_in, right, right_in, own, first, second, third):
    width = left.shape[-1]
    for part, received, columns in (
        (left, left_in, slice(0, width)),
        (right, right_in, slice(width, width + right.shape[-1])),
    ):
        rows = part.shape[0] // 4
        total = part[...].astype(jnp.float32) + received[...].astype(jnp.float32)
        own[..., columns] = total[:rows]
        for at, sent in enumerate((first, second, third)):
            sent[..., columns] = total[(at + 1) * rows : (at + 2) * rows].astype(jnp.bfloat16)


def add_z(left, left_in, right, right_in):
    shape = (left.shape[0] // 4,) + left.shape[1:-1] + (left.shape[-1] + right.shape[-1],)
    return pl.pallas_call(
        add_z_kernel,
        in_specs=[VMEM] * 4,
        out_specs=[VMEM] * 4,
        out_shape=[jax.ShapeDtypeStruct(shape, jnp.float32)]
        + [jax.ShapeDtypeStruct(shape, jnp.bfloat16)] * 3,
        compiler_params=params(),
        cost_estimate=cost(1, 1),
        name="add_z",
    )(left, left_in, right, right_in)


def add_join_kernel(left, left_in, right, right_in, kept, sent):
    width = left.shape[-1]
    for part, received, columns in (
        (left, left_in, slice(0, width)),
        (right, right_in, slice(width, width + right.shape[-1])),
    ):
        rows = part.shape[0] // 4
        total = part[...].astype(jnp.float32) + received[...].astype(jnp.float32)
        for at in range(2):
            to, start = slice(at * rows, (at + 1) * rows), 2 * at * rows
            kept[to, ..., columns] = total[start : start + rows]
            sent[to, ..., columns] = total[start + rows : start + 2 * rows].astype(jnp.bfloat16)


def add_join(left, left_in, right, right_in):
    shape = (left.shape[0] // 2,) + left.shape[1:-1] + (left.shape[-1] + right.shape[-1],)
    return pl.pallas_call(
        add_join_kernel,
        in_specs=[VMEM] * 4,
        out_specs=[VMEM] * 2,
        out_shape=[jax.ShapeDtypeStruct(shape, jnp.float32), jax.ShapeDtypeStruct(shape, jnp.bfloat16)],
        compiler_params=params(),
        cost_estimate=cost(1, 1),
        name="add_join",
    )(left, left_in, right, right_in)


def add_half_kernel(own, received, kept, sent):
    rows = own.shape[0] // 2
    total = own[...] + received[...].astype(jnp.float32)
    kept[...] = total[:rows]
    sent[...] = total[rows:].astype(jnp.bfloat16)


def add_half(own, received):
    shape = (own.shape[0] // 2,) + own.shape[1:]
    return pl.pallas_call(
        add_half_kernel,
        in_specs=[VMEM] * 2,
        out_specs=[VMEM] * 2,
        out_shape=[jax.ShapeDtypeStruct(shape, jnp.float32), jax.ShapeDtypeStruct(shape, jnp.bfloat16)],
        compiler_params=params(),
        cost_estimate=cost(1, 1),
        name="add_half",
    )(own, received)


def finish_kernel(place, own, *refs):
    received_all, (mine, other) = refs[:-2], refs[-2:]
    total = own[...]
    for received in received_all:
        total = total + received[...].astype(jnp.float32)
    if len(total.shape) == 3:
        low, high = total[0], total[1]
    else:
        low, high = total[:ROW], total[ROW:]
    mine[...] = pick(place[0], low, high)
    other[...] = pick(place[0], high, low)


def finish(place, own, received):
    rows = own.shape[1] if own.ndim == 3 else ROW
    return pl.pallas_call(
        finish_kernel,
        in_specs=[SMEM] + [VMEM] * (1 + len(received)),
        out_specs=[VMEM] * 2,
        out_shape=[jax.ShapeDtypeStruct((rows, own.shape[-1]), jnp.float32)] * 2,
        compiler_params=params(),
        cost_estimate=cost(1, 1),
        name="finish",
    )(place, own, *received)


def put(place, out, mine, received):
    half = mine.shape[1]
    out[:, :half] = pick(place[0], mine, received)
    out[:, half:] = pick(place[0], received, mine)


def outer_out_kernel(place, mine, received, out):
    rows, half = mine.shape[0], mine.shape[1] // 2
    for at in range(2):
        columns = slice(at * half, (at + 1) * half)
        put(place, out.at[at * rows : (at + 1) * rows], mine[:, columns], received[:, columns])


def inner_out_kernel(place, mine, received, out):
    put(place, out, mine[...], received[...])


def rest_out_kernel(place, mine, received, query, key, value, output, inner_bias, *vectors):
    half = D // 2
    for out, at in ((query, 0), (key, half), (value, D + 128), (output, D + 128 + half)):
        columns = slice(at, at + half)
        put(place, out, mine[:, columns], received[:, columns])
    turned = jnp.transpose(mine[:, D : D + 128] + received[:, D : D + 128])
    for at, out in enumerate(vectors):
        out[...] = turned[at : at + 1]
    for at in range(4):
        inner_bias[:, at * ROW : (at + 1) * ROW] = turned[8 + at : 9 + at]


def placed(kernel, name, place, mine, received, shapes):
    return pl.pallas_call(
        kernel,
        in_specs=[SMEM, VMEM, VMEM],
        out_specs=[VMEM] * len(shapes),
        out_shape=[jax.ShapeDtypeStruct(shape, jnp.float32) for shape in shapes],
        compiler_params=params(),
        cost_estimate=cost(1, 1),
        name=name,
    )(place, mine, received)


def first_transfers(pieces):
    return [mate(pieces[1]), across(pieces[3], 2)]


def add_first(pieces, received):
    return add_parts(pieces[0], received[0], pieces[2], received[1])


def second_transfers(pieces):
    return [across(pieces[1], 2), mate(pieces[3])]


def add_joined(pieces, received):
    return add_join(pieces[0], received[0], pieces[2], received[1])


def add_second(pieces, received):
    return add_z(pieces[0], received[0], pieces[2], received[1])


def third_transfers(parts):
    return [across(sent, mask) for sent, mask in zip(parts[1:], (4, 8, 12))]


def fast_device(
    hidden_in,
    cotangent,
    span_lengths,
    partner_span,
    query_weight,
    query_bias,
    key_weight,
    value_weight,
    value_bias,
    output_weight,
    output_bias,
    first_gain,
    first_shift,
    inner_weight,
    inner_bias,
    outer_weight,
    outer_bias,
    second_gain,
    second_shift,
):
    core, x_at, z_at, y_at = coordinates()
    place = jnp.stack([core, y_at, x_at, z_at]).astype(jnp.int32)
    first_block, second_block = pack(
        query_weight,
        key_weight,
        value_weight,
        output_weight,
        inner_weight,
        inner_bias,
        (
            query_bias,
            value_bias,
            output_bias,
            first_gain,
            first_shift,
            outer_bias,
            second_gain,
            second_shift,
        ),
    )
    ff = inner_weight.shape[1]
    first_z = z_exchange(first_block)
    first = stack_z(first_block, first_z, FIRST_HALF)
    second_block, third_block = tied((second_block, outer_weight), *first)
    first_in = near_exchange(first)
    second_z = across(second_block, 8)
    *first, first_both = stack_near(first, tied(first_in, second_z))
    second_two = stack_z_two(after(second_block, *first), second_z)
    first = tied(first, second_two)
    first_far = far_exchange(first)
    second_z = across(second_two, 4)
    first_core = across(first_both, 1)
    second = stack_mixed(second_two, after(second_z, first_core, *first_far), SECOND_HALF)
    first_far, third_block = tied(first_far, *second), after(third_block, *second)
    second_in = near_exchange(second)
    first_far_core = core_exchange(first_far)
    third_z = across(after(third_block, *first_far_core), 8)
    third_two = stack_z_two(third_block, third_z)
    left_rows, right_rows, vectors, hidden_t, *first_mats = project(
        place, hidden_in, pieces_of(first, first_far, first_core, first_far_core)
    )
    *second, second_both = stack_near(second, tied(second_in, vectors, third_z))
    third_two, left_rows = tied((third_two, left_rows), *second)
    second_far = far_exchange(second)
    third_z = across(third_two, 4)
    second_core = across(second_both, 1)
    attention, context_arrived, context_t = attention_forward(
        place, span_lengths, left_rows, right_rows
    )
    third = stack_mixed(
        third_two, after(third_z, context_arrived, second_core, *second_far), D // 2
    )
    second_far = tied(second_far, *third)
    third_in = near_exchange(third)
    second_far_core = core_exchange(second_far)
    second_pieces = pieces_of(second, second_far, second_core, second_far_core)
    moved, first_normed, first_factor, first_t, output_mat = residual_forward(
        place, hidden_in, context_arrived, vectors, second_pieces
    )
    *third, third_both = stack_near(third, tied(third_in, moved, *second_far_core))
    moved = after(moved, *third)
    third_far = far_exchange(third)
    third_core = across(third_both, 1)
    active, active_t, slope, *inner_mats = feed_forward(moved, vectors, ff, second_pieces)
    second_mats = [output_mat, *inner_mats]
    third_far = tied(third_far, active, third_core)
    third_far_core = core_exchange(third_far)
    third_pieces = pieces_of(third, third_far, third_core, third_far_core)
    hidden_t, context_t, first_t, active_t, active = tied(
        (hidden_t, context_t, first_t, active_t, active), *third_far_core
    )
    other_active_t, other_first_t = across(active_t, 1), across(first_t, 1)
    other_hidden_t, other_context_t = across(hidden_t, 1), across(context_t, 1)
    layer_out, second_normed, second_factor, cls_rows, outer_mat = last(
        place, active, first_normed, vectors, third_pieces
    )
    other_rows = mate(cls_rows)
    second_grad, second_kept, second_sent, second_sums, span_loss = turn(
        place, partner_span, cotangent, second_normed, second_factor, vectors, cls_rows, other_rows
    )
    second_received = across(second_sent, 1)
    preact_kept, preact_sent, inner_sums = slope_back(
        place, second_kept, second_sent, outer_mat, slope
    )
    second_received = after(second_received, preact_kept)
    outer_parts = outer_gradient(place, active_t, other_active_t, second_kept, second_received)
    preact_kept, preact_sent = tied((preact_kept, preact_sent), *outer_parts)
    outer_in = first_transfers(outer_parts)
    preact_received = across(preact_sent, 1)
    residual_grad, residual_kept, residual_sent, context_grad, first_sums = first_back(
        place,
        preact_kept,
        preact_sent,
        second_grad,
        first_normed,
        first_factor,
        vectors,
        second_mats,
    )
    residual_received = across(residual_sent, 1)
    preact_kept = after(preact_kept, context_grad)
    inner_parts = inner_gradient(first_t, other_first_t, preact_kept, preact_received)
    outer_parts = add_first(outer_parts, tied(outer_in, residual_received, *inner_parts))
    inner_parts, context_grad = tied(inner_parts, *outer_parts), after(context_grad, *outer_parts)
    outer_in = second_transfers(outer_parts)
    inner_in = first_transfers(inner_parts)
    grads_kept, grads_sent, sums = attend_back(
        place,
        context_grad,
        left_rows,
        right_rows,
        attention,
        first_sums,
        second_sums,
        inner_sums,
    )
    received = tied(outer_in + inner_in, sums)
    inner_parts = add_first(inner_parts, received[2:])
    outer_parts, grads_sent = tied(outer_parts, *inner_parts), after(grads_sent, *inner_parts)
    outer_own, outer_sent = add_joined(outer_parts, received[:2])
    inner_in = second_transfers(inner_parts)
    outer_in = across(outer_sent, 4)
    grads_received = after(across(grads_sent, 1), outer_own)
    rest_parts = attention_gradient(
        place,
        sums,
        hidden_t,
        other_hidden_t,
        context_t,
        other_context_t,
        grads_kept,
        grads_received,
        residual_kept,
        residual_received,
    )
    *inner_in, outer_in = tied(inner_in + [outer_in], *rest_parts)
    rest_parts = tied(rest_parts, outer_in, *inner_in)
    inner_own, inner_sent = add_joined(inner_parts, inner_in)
    outer_own, outer_sent = add_half(outer_own, after(outer_in, inner_own))
    grads_kept = after(grads_kept, outer_own)
    rest_in = first_transfers(rest_parts)
    inner_in = across(inner_sent, 4)
    outer_in = across(outer_sent, 8)
    input_grad = input_back(place, residual_grad, grads_kept, grads_sent, first_mats)
    rest_parts = add_first(rest_parts, tied(rest_in, input_grad, outer_in, inner_in))
    inner_own, inner_in, outer_own, outer_in = tied(
        (inner_own, inner_in, outer_own, outer_in), *rest_parts
    )
    rest_in = second_transfers(rest_parts)
    inner_own, inner_sent = add_half(inner_own, inner_in)
    inner_in = across(inner_sent, 8)
    outer_mine, outer_other = finish(place, outer_own, [outer_in])
    outer_other = across(outer_other, 1)
    rest_parts = add_second(rest_parts, tied(rest_in, inner_in, outer_other))
    inner_in, outer_other = tied((inner_in, outer_other), *rest_parts)
    rest_in = third_transfers(rest_parts)
    inner_mine, inner_other = finish(place, inner_own, [inner_in])
    inner_other = across(inner_other, 1)
    (outer_grad,) = placed(
        outer_out_kernel, "outer_out", place, outer_mine, outer_other, [(4 * ROW, D)]
    )
    (inner_grad,) = placed(
        inner_out_kernel, "inner_out", place, inner_mine, after(inner_other, outer_grad), [(ROW, ff)]
    )
    rest_mine, rest_other = finish(place, rest_parts[0], tied(rest_in, inner_grad))
    rest_other = across(rest_other, 1)
    query_grad, key_grad, value_grad, output_grad, inner_bias_grad, *vector_grads = placed(
        rest_out_kernel,
        "rest_out",
        place,
        rest_mine,
        rest_other,
        [(ROW, D)] * 4 + [(1, 4 * ROW)] + [(1, ROW)] * 8,
    )
    vector_grads = [grad.reshape(-1) for grad in vector_grads]
    return (
        layer_out,
        input_grad,
        span_loss.reshape(-1),
        query_grad,
        vector_grads[0],
        key_grad,
        value_grad,
        vector_grads[1],
        output_grad,
        vector_grads[2],
        vector_grads[3],
        vector_grads[4],
        inner_grad,
        inner_bias_grad.reshape(-1),
        outer_grad,
        vector_grads[5],
        vector_grads[6],
        vector_grads[7],
    )


def solution(mesh):
    is_block = mesh.shape["doc"] == 2 * PLACES and mesh.shape["pair"] == 2
    return jax.shard_map(
        fast_device if is_block else per_device,
        mesh=mesh,
        in_specs=(
            P(("doc", "pair"), None),
            P(("doc", "pair"), None),
            P(("doc", "pair")),
            P("doc", None),
            P(("doc", "pair"), None),
            P(("doc", "pair")),
            P(("doc", "pair"), None),
            P(("doc", "pair"), None),
            P(("doc", "pair")),
            P(("doc", "pair"), None),
            P(("doc", "pair")),
            P(("doc", "pair")),
            P(("doc", "pair")),
            P(("doc", "pair"), None),
            P(("doc", "pair")),
            P(("doc", "pair"), None),
            P(("doc", "pair")),
            P(("doc", "pair")),
            P(("doc", "pair")),
        ),
        out_specs=(
            P(("doc", "pair"), None),
            P(("doc", "pair"), None),
            P(("doc", "pair")),
            P(("doc", "pair"), None),
            P(("doc", "pair")),
            P(("doc", "pair"), None),
            P(("doc", "pair"), None),
            P(("doc", "pair")),
            P(("doc", "pair"), None),
            P(("doc", "pair")),
            P(("doc", "pair")),
            P(("doc", "pair")),
            P(("doc", "pair"), None),
            P(("doc", "pair")),
            P(("doc", "pair"), None),
            P(("doc", "pair")),
            P(("doc", "pair")),
            P(("doc", "pair")),
        ),
        check_vma=False,
    )
```

```python
from functools import partial
import math

import jax
import jax.numpy as jnp
from jax import lax
from jax.experimental import pallas as pl
from jax.experimental.pallas import tpu as pltpu
from jax.sharding import PartitionSpec as P

D = 768
HEAD_DIM = 64
SPAN = 128
SPANS_ROW = 4


epsilon = 1e-06
masked_out = -1000000000.0
highest = lax.Precision.HIGHEST


def across(block, mask):
    count = lax.axis_size("doc")
    return lax.ppermute(block, "doc", [(at, at ^ mask) for at in range(count)])


def mate(block):
    return lax.ppermute(block, "pair", [(0, 1), (1, 0)])


def far_groups():
    bits = lax.axis_size("doc").bit_length() - 1
    far = [1 << at for at in range(2, bits)]
    return [far[at : at + 2] for at in range(0, len(far), 2)]


def is_upper(mask):
    return (lax.axis_index("doc") & mask) != 0


def joined(own, other, upper):
    return jnp.where(upper, jnp.stack([other, own]), jnp.stack([own, other]))


def gather_rows(block):
    rows, columns = block.shape
    total = block[None]
    for masks in far_groups():
        low = masks[0]
        near = joined(total, across(total, low), is_upper(low))
        if len(masks) == 2:
            high = masks[1]
            straight, crossed = across(total, high), across(total, high | low)
            far = joined(straight, crossed, is_upper(low))
            near = joined(near, far, is_upper(high)).reshape((4,) + total.shape)
        total = near.reshape((-1, rows, columns))
    half = columns // 2
    left, right = total[..., :half], total[..., half:]
    on_pair = lax.axis_index("pair") == 1
    left_x, right_y = across(left, 2), mate(right)
    left, right = joined(left, left_x, is_upper(2)), joined(right, right_y, on_pair)
    left_y, right_x = mate(left), across(right, 2)
    left, right = joined(left, left_y, on_pair), joined(right, right_x, is_upper(2))
    left = joined(left, across(left, 1), is_upper(1))
    right = joined(right, across(right, 1), is_upper(1))
    left = jnp.transpose(left, (3, 2, 0, 1, 4, 5))
    right = jnp.transpose(right, (3, 1, 0, 2, 4, 5))
    return jnp.concatenate([left, right], axis=-1).reshape(-1, rows, columns)


def halves(blocks, axis, upper):
    lower = lax.index_in_dim(blocks, 0, axis, keepdims=False)
    higher = lax.index_in_dim(blocks, 1, axis, keepdims=False)
    return (jnp.where(upper, higher, lower), jnp.where(upper, lower, higher))


def plus(kept, received):
    return kept.astype(jnp.float32) + received.astype(jnp.float32)


def scatter_rows(blocks):
    rows, columns = blocks.shape[1:]
    on_pair = lax.axis_index("pair") == 1
    blocks = blocks.astype(jnp.bfloat16).reshape(-1, 2, 2, 2, rows, columns)
    kept, sent = halves(blocks, 2, is_upper(1))
    total = plus(kept, across(sent, 1)).astype(jnp.bfloat16)
    half = columns // 2
    left, right = total[..., :half], total[..., half:]
    left_kept, left_sent = halves(left, 2, on_pair)
    right_kept, right_sent = halves(right, 1, is_upper(2))
    left = plus(left_kept, mate(left_sent)).astype(jnp.bfloat16)
    right = plus(right_kept, across(right_sent, 2)).astype(jnp.bfloat16)
    left_kept, left_sent = halves(left, 1, is_upper(2))
    right_kept, right_sent = halves(right, 1, on_pair)
    left = plus(left_kept, across(left_sent, 2))
    right = plus(right_kept, mate(right_sent))
    total = jnp.concatenate([left, right], axis=-1)
    for masks in far_groups()[::-1]:
        total = total.astype(jnp.bfloat16).reshape(2 ** len(masks), -1, rows, columns)
        place = (lax.axis_index("doc") // masks[0]) % 2 ** len(masks)
        summed = lax.dynamic_index_in_dim(total, place, 0, keepdims=False).astype(jnp.float32)
        for step in range(1, 2 ** len(masks)):
            sent = lax.dynamic_index_in_dim(total, place ^ step, 0, keepdims=False)
            summed = plus(summed, across(sent, masks[0] * step))
        total = summed
    return total.reshape(rows, columns)


VECTORS = (1, 4, 6, 7, 8, 10, 12, 13, 14)


def pack_vectors(pieces):
    flat = jnp.concatenate(pieces, axis=-1)
    width = -(-flat.shape[-1] // D) * D
    flat = jnp.pad(flat, [(0, 0)] * (flat.ndim - 1) + [(0, width - flat.shape[-1])])
    return flat.reshape(flat.shape[:-1] + (-1, D))


def fold(matrix):
    return jnp.concatenate([matrix[:, at : at + D] for at in range(0, matrix.shape[1], D)])


def collect(shards):
    rows = shards[0].shape[0]
    devices = lax.axis_size("doc") * lax.axis_size("pair")
    small = pack_vectors([shards[at] for at in VECTORS])
    first = gather_rows(jnp.concatenate([shards[0], shards[2], shards[3], small]))
    second = gather_rows(jnp.concatenate([shards[5], fold(shards[9])]))
    outer = lax.all_gather(shards[11], ("doc", "pair"), axis=0, tiled=True)
    whole = {
        0: first[:, :rows].reshape(-1, D),
        2: first[:, rows : 2 * rows].reshape(-1, D),
        3: first[:, 2 * rows : 3 * rows].reshape(-1, D),
        5: second[:, :rows].reshape(-1, D),
        9: jnp.concatenate(
            [
                second[:, at : at + rows].reshape(-1, D)
                for at in range(rows, second.shape[1], rows)
            ],
            axis=1,
        ),
        11: outer,
    }
    vectors, start = first[:, 3 * rows :].reshape(devices, -1), 0
    for at in VECTORS:
        size = shards[at].shape[0]
        whole[at] = vectors[:, start : start + size].reshape(-1).astype(jnp.float32)
        start += size
    return tuple(whole[at] for at in range(15))


def spread(gradients):
    devices = lax.axis_size("doc") * lax.axis_size("pair")
    by_device = [
        piece.reshape((devices, -1) + piece.shape[1:]) for piece in gradients
    ]
    rows = by_device[0].shape[1]
    outer = scatter_rows(by_device[11])
    inner = by_device[9]
    parts = [inner[..., at : at + D] for at in range(0, inner.shape[-1], D)]
    second = scatter_rows(jnp.concatenate([by_device[5]] + parts, axis=1))
    small = pack_vectors([by_device[at] for at in VECTORS])
    first = scatter_rows(
        jnp.concatenate([by_device[0], by_device[2], by_device[3], small], axis=1)
    )
    own = {
        0: first[:rows],
        2: first[rows : 2 * rows],
        3: first[2 * rows : 3 * rows],
        5: second[:rows],
        9: jnp.concatenate(
            [second[at : at + rows] for at in range(rows, second.shape[0], rows)], axis=1
        ),
        11: outer,
    }
    vectors, start = first[3 * rows :].reshape(-1), 0
    for at in VECTORS:
        size = by_device[at].shape[1]
        own[at] = vectors[start : start + size]
        start += size
    return tuple(own[at] for at in range(15))


def normalize(hidden, gain, shift):
    average = jnp.mean(hidden, axis=-1, keepdims=True)
    centred = hidden - average
    factor = lax.rsqrt(jnp.mean(centred * centred, axis=-1, keepdims=True) + epsilon)
    normed = centred * factor
    return (normed * gain + shift, normed, factor)


def normalize_back(upstream, normed, factor, gain):
    scaled = upstream * gain
    hidden_grad = factor * (
        scaled
        - jnp.mean(scaled, axis=-1, keepdims=True)
        - normed * jnp.mean(scaled * normed, axis=-1, keepdims=True)
    )
    return (hidden_grad, jnp.sum(upstream * normed, axis=0), jnp.sum(upstream, axis=0))


def head_scores(query_row, key_row, live_row):
    product = jnp.einsum("sqhd,skhd->shqk", query_row, key_row, preferred_element_type=jnp.float32)
    return jnp.where(live_row[:, None, None, :], product * HEAD_DIM ** (-0.5), masked_out)


def encode(hidden_in, allowed, gathered):
    (
        query_mat,
        query_add,
        key_mat,
        value_mat,
        value_add,
        output_mat,
        output_add,
        gain_one,
        shift_one,
        inner_mat,
        inner_add,
        outer_mat,
        outer_add,
        gain_two,
        shift_two,
    ) = gathered
    row_count = allowed.shape[0]
    shaped = (row_count, SPANS_ROW, SPAN, D // HEAD_DIM, HEAD_DIM)
    queries = (
        jnp.dot(hidden_in, query_mat, preferred_element_type=jnp.float32) + query_add
    ).astype(jnp.bfloat16)
    key_rows = jnp.dot(hidden_in, key_mat, preferred_element_type=jnp.float32).astype(jnp.bfloat16)
    value_rows = (
        jnp.dot(hidden_in, value_mat, preferred_element_type=jnp.float32) + value_add
    ).astype(jnp.bfloat16)

    def attend(element):
        query_row, key_row, value_row, live_row = element
        scores = head_scores(query_row, key_row, live_row)
        highest_score = jnp.max(scores, axis=-1, keepdims=True)
        exponent = jnp.exp(scores - highest_score)
        totals = jnp.sum(exponent, axis=-1, keepdims=True)
        attention = (exponent / totals).astype(jnp.bfloat16)
        context_row = jnp.einsum(
            "shqk,skhd->sqhd", attention, value_row, preferred_element_type=jnp.float32
        )
        return (context_row.astype(jnp.bfloat16), (highest_score + jnp.log(totals))[..., 0])

    context, logsum = lax.map(
        attend,
        (queries.reshape(shaped), key_rows.reshape(shaped), value_rows.reshape(shaped), allowed),
    )
    context = context.reshape(-1, D)
    residual = (
        hidden_in.astype(jnp.float32)
        + jnp.dot(context, output_mat, preferred_element_type=jnp.float32)
        + output_add
    )
    first_out, first_normed, first_factor = normalize(residual, gain_one, shift_one)
    first16 = first_out.astype(jnp.bfloat16)
    preact = jnp.dot(first16, inner_mat, preferred_element_type=jnp.float32) + inner_add
    active = jax.nn.gelu(preact, approximate=False).astype(jnp.bfloat16)
    second = first_out + jnp.dot(active, outer_mat, preferred_element_type=jnp.float32) + outer_add
    encoded, second_normed, second_factor = normalize(second, gain_two, shift_two)
    stored = (
        queries,
        key_rows,
        value_rows,
        logsum,
        context,
        first_normed,
        first_factor,
        first16,
        preact,
        active,
        second_normed,
        second_factor,
    )
    return (encoded, stored)


def backward(hidden_in, allowed, gathered, stored, out_gradient):
    (
        query_mat,
        query_add,
        key_mat,
        value_mat,
        value_add,
        output_mat,
        output_add,
        gain_one,
        shift_one,
        inner_mat,
        inner_add,
        outer_mat,
        outer_add,
        gain_two,
        shift_two,
    ) = gathered
    (
        queries,
        key_rows,
        value_rows,
        logsum,
        context,
        first_normed,
        first_factor,
        first16,
        preact,
        active,
        second_normed,
        second_factor,
    ) = stored
    row_count = allowed.shape[0]
    shaped = (row_count, SPANS_ROW, SPAN, D // HEAD_DIM, HEAD_DIM)
    second_grad, gain_two_grad, shift_two_grad = normalize_back(
        out_gradient, second_normed, second_factor, gain_two
    )
    outer_add_grad = jnp.sum(second_grad, axis=0)
    second16 = second_grad.astype(jnp.bfloat16)
    outer_mat_grad = jnp.dot(active.T, second16, preferred_element_type=jnp.float32)
    active_grad = jnp.dot(second16, outer_mat.T, preferred_element_type=jnp.float32)
    unused, gelu_back = jax.vjp(partial(jax.nn.gelu, approximate=False), preact)
    preact_grad = gelu_back(active_grad)[0]
    inner_add_grad = jnp.sum(preact_grad, axis=0)
    preact16 = preact_grad.astype(jnp.bfloat16)
    inner_mat_grad = jnp.dot(first16.T, preact16, preferred_element_type=jnp.float32)
    first_grad = second_grad + jnp.dot(preact16, inner_mat.T, preferred_element_type=jnp.float32)
    residual_grad, gain_one_grad, shift_one_grad = normalize_back(
        first_grad, first_normed, first_factor, gain_one
    )
    output_add_grad = jnp.sum(residual_grad, axis=0)
    residual16 = residual_grad.astype(jnp.bfloat16)
    output_mat_grad = jnp.dot(context.T, residual16, preferred_element_type=jnp.float32)
    context_grad = jnp.dot(residual16, output_mat.T, preferred_element_type=jnp.float32).astype(
        jnp.bfloat16
    )

    def attend_back(element):
        query_row, key_row, value_row, live_row, logsum_row, context_row = element
        scores = head_scores(query_row, key_row, live_row)
        attention = jnp.exp(scores - logsum_row[..., None])
        attention16 = attention.astype(jnp.bfloat16)
        value_grad = jnp.einsum(
            "shqk,sqhd->skhd", attention16, context_row, preferred_element_type=jnp.float32
        )
        attention_grad = jnp.einsum(
            "sqhd,skhd->shqk", context_row, value_row, preferred_element_type=jnp.float32
        )
        weighted = jnp.sum(attention * attention_grad, axis=-1, keepdims=True)
        scores_grad = (attention * (attention_grad - weighted)).astype(jnp.bfloat16)
        query_grad = jnp.einsum(
            "shqk,skhd->sqhd", scores_grad, key_row, preferred_element_type=jnp.float32
        ) * HEAD_DIM ** (-0.5)
        key_grad = jnp.einsum(
            "shqk,sqhd->skhd", scores_grad, query_row, preferred_element_type=jnp.float32
        ) * HEAD_DIM ** (-0.5)
        return (
            query_grad.astype(jnp.bfloat16),
            key_grad.astype(jnp.bfloat16),
            value_grad.astype(jnp.bfloat16),
        )

    query_grad, key_grad, value_grad = lax.map(
        attend_back,
        (
            queries.reshape(shaped),
            key_rows.reshape(shaped),
            value_rows.reshape(shaped),
            allowed,
            logsum,
            context_grad.reshape(shaped),
        ),
    )
    query_grad = query_grad.reshape(-1, D)
    key_grad = key_grad.reshape(-1, D)
    value_grad = value_grad.reshape(-1, D)
    query_add_grad = jnp.sum(query_grad.astype(jnp.float32), axis=0)
    value_add_grad = jnp.sum(value_grad.astype(jnp.float32), axis=0)
    query_mat_grad = jnp.dot(hidden_in.T, query_grad, preferred_element_type=jnp.float32)
    key_mat_grad = jnp.dot(hidden_in.T, key_grad, preferred_element_type=jnp.float32)
    value_mat_grad = jnp.dot(hidden_in.T, value_grad, preferred_element_type=jnp.float32)
    input_grad = (
        residual_grad
        + jnp.dot(query_grad, query_mat.T, preferred_element_type=jnp.float32)
        + jnp.dot(key_grad, key_mat.T, preferred_element_type=jnp.float32)
        + jnp.dot(value_grad, value_mat.T, preferred_element_type=jnp.float32)
    )
    gradients = (
        query_mat_grad,
        query_add_grad,
        key_mat_grad,
        value_mat_grad,
        value_add_grad,
        output_mat_grad,
        output_add_grad,
        gain_one_grad,
        shift_one_grad,
        inner_mat_grad,
        inner_add_grad,
        outer_mat_grad,
        outer_add_grad,
        gain_two_grad,
        shift_two_grad,
    )
    return (input_grad, gradients)


def per_device(
    hidden_in,
    cotangent,
    span_lengths,
    partner_span,
    query_weight,
    query_bias,
    key_weight,
    value_weight,
    value_bias,
    output_weight,
    output_bias,
    first_gain,
    first_shift,
    inner_weight,
    inner_bias,
    outer_weight,
    outer_bias,
    second_gain,
    second_shift,
):
    shards = (
        query_weight,
        query_bias,
        key_weight,
        value_weight,
        value_bias,
        output_weight,
        output_bias,
        first_gain,
        first_shift,
        inner_weight,
        inner_bias,
        outer_weight,
        outer_bias,
        second_gain,
        second_shift,
    )
    length = SPAN * SPANS_ROW
    row_count = hidden_in.shape[0] // length
    allowed = jnp.arange(SPAN)[None, None, :] < span_lengths.reshape(row_count, SPANS_ROW, 1)
    gathered = collect(shards)
    encoded, stored = encode(hidden_in, allowed, gathered)
    cls_rows = (
        encoded.reshape(row_count, SPANS_ROW, SPAN, D)[:, :, 0, :]
        .reshape(-1, D)
        .astype(jnp.bfloat16)
    )
    other_rows = mate(cls_rows)
    logits = jnp.dot(cls_rows, other_rows.T, preferred_element_type=jnp.float32) / math.sqrt(D)
    span_count = cls_rows.shape[0]
    matches = (partner_span.reshape(span_count, 1) == jnp.arange(span_count)[None, :]).astype(
        jnp.float32
    )
    target = jnp.where(lax.axis_index("pair") == 0, matches, matches.T)
    highest_logit = jnp.max(logits, axis=-1, keepdims=True)
    exponent = jnp.exp(logits - highest_logit)
    totals = jnp.sum(exponent, axis=-1, keepdims=True)
    span_loss = highest_logit[:, 0] + jnp.log(totals[:, 0]) - jnp.sum(target * logits, axis=-1)
    softened = exponent / totals - target
    own_grad = jnp.dot(softened, other_rows.astype(jnp.float32), precision=highest)
    other_logits = logits.T
    other_highest = jnp.max(other_logits, axis=-1, keepdims=True)
    other_exponent = jnp.exp(other_logits - other_highest)
    other_softened = (
        other_exponent / jnp.sum(other_exponent, axis=-1, keepdims=True) - target.T
    )
    back_grad = jnp.dot(
        other_softened.T, other_rows.astype(jnp.float32), precision=highest
    ).astype(jnp.bfloat16)
    cls_gradient = (own_grad + back_grad.astype(jnp.float32)).reshape(row_count, SPANS_ROW, 1, D)
    placed = jnp.concatenate(
        [cls_gradient, jnp.zeros((row_count, SPANS_ROW, SPAN - 1, D), jnp.float32)], axis=2
    )
    out_gradient = cotangent.astype(jnp.float32) + placed.reshape(-1, D)
    input_grad, gradients = backward(hidden_in, allowed, gathered, stored, out_gradient)
    reduced = spread(gradients)
    return (encoded.astype(jnp.bfloat16), input_grad.astype(jnp.bfloat16), span_loss) + tuple(
        reduced
    )


ROW = 24
PLACES = 8


def coordinates():
    doc = lax.axis_index("doc")
    return (doc & 1, (doc >> 1) & 1, doc >> 2, lax.axis_index("pair"))


def blocks_of(row):
    block = (row * 2731) >> 16
    return (block >> 1) & 1, block & 1, (block >> 2) & 1, block >> 3, row - block * ROW


def restore_from(place):
    row = lax.broadcasted_iota(jnp.int32, (D, 1), 0)
    core, y_at, x_at, z_at, inside = blocks_of(row)
    offset = ((core ^ place[0]) * 2 + (y_at ^ place[1])) * 2 + (x_at ^ place[2])
    arrived = (offset * 4 + (z_at ^ place[3])) * ROW + inside
    hit = arrived == lax.broadcasted_iota(jnp.int32, (D, D), 1)
    return jnp.where(hit, 1.0, 0.0).astype(jnp.bfloat16)


def arrange_from(place):
    row = lax.broadcasted_iota(jnp.int32, (1, D), 1)
    core, y_at, x_at, z_at, inside = blocks_of(row)
    offset = ((y_at ^ place[1]) * 2 + (x_at ^ place[2])) * 4 + (z_at ^ place[3])
    leaving = offset * 2 * ROW + core * ROW + inside
    hit = leaving == lax.broadcasted_iota(jnp.int32, (D, D), 0)
    return jnp.where(hit, 1.0, 0.0).astype(jnp.bfloat16)


def after(value, *others):
    return lax.optimization_barrier((value,) + others)[0]


def z_exchange(block, masks=(4, 8, 12)):
    return [across(block, mask) for mask in masks]


def tied(values, *others):
    return lax.optimization_barrier(tuple(values) + others)[: len(values)]


def near_exchange(block):
    return across(block[0], 2), mate(block[1])


def stack_near(block, received):
    return stack_pair(block[0], received[0], block[1], received[1])


def far_exchange(block):
    return mate(block[0]), across(block[1], 2)


def core_exchange(block):
    return [across(part, 1) for part in block]


def pieces_of(near, far, core, far_core):
    return [near[0], far[0], near[1], far[1], core, far_core[0], far_core[1]]


VMEM = pl.BlockSpec(memory_space=pltpu.VMEM)
SMEM = pl.BlockSpec(memory_space=pltpu.SMEM)


def full(shape):
    return pl.BlockSpec(shape, lambda *at: (0,) * len(shape))


class Fetched:
    def __init__(self, source, held, semaphore):
        self.copy, self.held, self.waiting = pltpu.make_async_copy(source, held, semaphore), held, True
        self.shape = held.shape
        self.copy.start()

    def ready(self):
        if self.waiting:
            self.copy.wait()
            self.waiting = False
        return self.held

    def __getitem__(self, at):
        return self.ready()[at]


class Stored:
    def __init__(self, target, held, semaphores):
        self.target, self.held, self.semaphores, self.copies = target, held, semaphores, []
        self.shape = held.shape

    def __getitem__(self, at):
        return self.held[at]

    def __setitem__(self, at, value):
        self.held[at] = value

    def done(self, at=None):
        semaphore = self.semaphores.at[len(self.copies)]
        held, target = (self.held, self.target) if at is None else (self.held.at[at], self.target.at[at])
        self.copies.append(pltpu.make_async_copy(held, target, semaphore))
        self.copies[-1].start()


PARTS = 8


def ready(ref):
    return ref.ready() if isinstance(ref, Fetched) else ref


def run(kernel, name, operands, results, flops, scratch=(), mib=12, total=None):
    in_hbm = pl.BlockSpec(memory_space=pltpu.HBM)
    spaces = {"S": SMEM, "V": VMEM, "H": in_hbm, "A": in_hbm}
    spaces["K"] = VMEM
    in_places = [place for _, place in operands]
    out_places = [place for _, _, place in results]
    staged = [pltpu.VMEM(array.shape, array.dtype) for array, place in operands if place == "H"]
    made = [pltpu.VMEM(shape, dtype) for shape, dtype, place in results if place == "H"]
    semaphores = [pltpu.SemaphoreType.DMA((max(1, len(staged)),))]
    semaphores += [pltpu.SemaphoreType.DMA((max(1, len(made)), PARTS))]

    def body(*refs):
        ins, refs = refs[: len(operands)], refs[len(operands) :]
        outs, refs = refs[: len(results)], refs[len(results) :]
        held_in, refs = refs[: len(staged)], refs[len(staged) :]
        held_out, refs = refs[: len(made)], refs[len(made) :]
        fetching, storing, own = refs[0], refs[1], refs[2:]
        arguments, at = [], 0
        for ref, place in zip(ins, in_places):
            if place == "H":
                ref, at = Fetched(ref, held_in[at], fetching.at[at]), at + 1
            arguments.append(ref)
        inputs, at = list(arguments), 0
        for ref, place in zip(outs, out_places):
            if place == "H":
                ref, at = Stored(ref, held_out[at], storing.at[at]), at + 1
            arguments.append(ref)
        kernel(*arguments, *own)
        for ref in inputs:
            if isinstance(ref, Fetched):
                ref.ready()
        made_here = [ref for ref in arguments if isinstance(ref, Stored)]
        for ref in made_here:
            if not ref.copies:
                ref.done()
        for ref in made_here:
            for copy in ref.copies:
                copy.wait()

    size = lambda shape, dtype: math.prod(shape) * jnp.dtype(dtype).itemsize
    inside = sum(size(array.shape, array.dtype) for array, place in operands if place == "H")
    inside += sum(size(shape, dtype) for shape, dtype, place in results if place == "H")
    mib = (mib + inside // 2**20) if total is None else total
    return pl.pallas_call(
        body,
        in_specs=[spaces[place] for place in in_places],
        out_specs=[spaces[place] for place in out_places],
        out_shape=[jax.ShapeDtypeStruct(shape, dtype) for shape, dtype, _ in results],
        scratch_shapes=staged + made + semaphores + list(scratch),
        compiler_params=params(mib),
        cost_estimate=cost(1, 1),
        name=name,
    )(*[array for array, _ in operands])


def placed_at(place, *arrays):
    return [(array, place) for array in arrays]


bf16, f32 = jnp.bfloat16, jnp.float32


def params(mib=16):
    return pltpu.CompilerParams(vmem_limit_bytes=mib << 20)


def cost(flops, moved):
    return pl.CostEstimate(flops=int(flops), bytes_accessed=int(moved), transcendentals=0)


def dot(left, right):
    return jnp.dot(left, right, preferred_element_type=jnp.float32)


def dot_nt(left, right):
    return lax.dot_general(
        left, right, (((1,), (1,)), ((), ())), preferred_element_type=jnp.float32
    )


def dot_tn(left, right):
    return lax.dot_general(
        left, right, (((0,), (0,)), ((), ())), preferred_element_type=jnp.float32
    )


def pack_kernel(*refs):
    query, key, value, output, inner, inner_bias = refs[:6]
    vectors, (first, second, turned) = refs[6:-3], refs[-3:]
    turned[...] = jnp.zeros_like(turned)
    for at, vector in enumerate(vectors):
        turned[at : at + 1, :ROW] = vector[...].astype(jnp.float32)
    bias = inner_bias[...].astype(jnp.float32)
    for at in range(4):
        turned[8 + at : 9 + at, :ROW] = bias[:, at * ROW : (at + 1) * ROW]
    small = jnp.transpose(turned[...])[:ROW].astype(jnp.bfloat16)
    first[:, :D] = query[...]
    first[:, D : D + 512] = key[:, :512]
    first[:, D + 512 : D + 640] = small
    first[:, D + 640 : D + 768] = jnp.zeros_like(small)
    first[:, D + 768 : D + 1024] = key[:, 512:]
    first[:, D + 1024 :] = value[...]
    second[:, :D] = output[...]
    second[:, D:] = inner[...]


def pack(query, key, value, output, inner, inner_bias, vectors):
    rows = [vector.reshape(1, -1) for vector in (inner_bias, *vectors)]
    return run(
        pack_kernel,
        "pack",
        placed_at("H", query, key, value, output, inner, *rows),
        [((ROW, 2 * FIRST_HALF), bf16, "V"), ((ROW, D + inner.shape[1]), bf16, "V")],
        1e6,
        [pltpu.VMEM((128, 128), f32)],
        total=58,
    )


def stack_two_kernel(first, second, left, right):
    blocks = [first[...].astype(jnp.float32), second[...].astype(jnp.float32)]
    whole = jnp.concatenate(blocks).astype(jnp.bfloat16)
    left[...] = whole[:, : left.shape[1]]
    right[...] = whole[:, left.shape[1] :]


def stack_two(block, received, split):
    rows, columns = block.shape
    return pl.pallas_call(
        stack_two_kernel,
        in_specs=[VMEM] * 2,
        out_specs=[VMEM] * 2,
        out_shape=[
            jax.ShapeDtypeStruct((2 * rows, split), jnp.bfloat16),
            jax.ShapeDtypeStruct((2 * rows, columns - split), jnp.bfloat16),
        ],
        compiler_params=params(),
        cost_estimate=cost(1, 1),
        name="stack_two",
    )(block, received)


def stack_z_two_kernel(first, second, out):
    blocks = [first[...].astype(jnp.float32), second[...].astype(jnp.float32)]
    out[...] = jnp.concatenate(blocks).astype(jnp.bfloat16)


def stack_z_two(block, received):
    rows, columns = block.shape
    return pl.pallas_call(
        stack_z_two_kernel,
        in_specs=[VMEM] * 2,
        out_specs=VMEM,
        out_shape=jax.ShapeDtypeStruct((2 * rows, columns), jnp.bfloat16),
        compiler_params=params(),
        cost_estimate=cost(1, 1),
        name="stack_z_two",
    )(block, received)


def stack_mixed_kernel(split, two, received, left, right):
    rows = two.shape[0] // 2
    own, other = two[...].astype(jnp.float32), received[...].astype(jnp.float32)
    whole = jnp.concatenate([own[:rows], other[:rows], own[rows:], other[rows:]]).astype(jnp.bfloat16)
    left[...] = whole[:, :split]
    right[...] = whole[:, split:]


def stack_mixed(two, received, split):
    rows, columns = two.shape
    return pl.pallas_call(
        partial(stack_mixed_kernel, split),
        in_specs=[VMEM] * 2,
        out_specs=[VMEM] * 2,
        out_shape=[
            jax.ShapeDtypeStruct((2 * rows, split), jnp.bfloat16),
            jax.ShapeDtypeStruct((2 * rows, columns - split), jnp.bfloat16),
        ],
        compiler_params=params(),
        cost_estimate=cost(1, 1),
        name="stack_mixed",
    )(two, received)


def stack_z_kernel(split, *refs):
    blocks, (left, right) = refs[:-2], refs[-2:]
    whole = jnp.concatenate([ref[...].astype(jnp.float32) for ref in blocks]).astype(jnp.bfloat16)
    left[...] = whole[:, :split]
    right[...] = whole[:, split:]


def stack_z(block, received, split):
    rows, columns = block.shape
    rows = rows * (1 + len(received)) // 4
    return pl.pallas_call(
        partial(stack_z_kernel, split),
        in_specs=[VMEM] * (1 + len(received)),
        out_specs=[VMEM] * 2,
        out_shape=[
            jax.ShapeDtypeStruct((4 * rows, split), jnp.bfloat16),
            jax.ShapeDtypeStruct((4 * rows, columns - split), jnp.bfloat16),
        ],
        compiler_params=params(),
        cost_estimate=cost(1, 1),
        name="stack_z",
    )(block, *received)


def stack_pair_kernel(left, left_in, right, right_in, left_out, right_out, both_out):
    width = left.shape[1]
    for own, received, out, columns in (
        (left, left_in, left_out, slice(0, width)),
        (right, right_in, right_out, slice(width, width + right.shape[1])),
    ):
        rows = own.shape[0]
        out[:rows, :] = own[...]
        out[rows:, :] = received[...]
        both_out[:rows, columns] = own[...]
        both_out[rows:, columns] = received[...]


def stack_pair(left, left_in, right, right_in):
    double = lambda block: jax.ShapeDtypeStruct((2 * block.shape[0], block.shape[1]), block.dtype)
    both = jax.ShapeDtypeStruct((2 * left.shape[0], left.shape[1] + right.shape[1]), left.dtype)
    return pl.pallas_call(
        stack_pair_kernel,
        in_specs=[VMEM] * 4,
        out_specs=[VMEM] * 3,
        out_shape=[double(left), double(right), both],
        compiler_params=params(),
        cost_estimate=cost(1, 1),
        name="stack_pair",
    )(left, left_in, right, right_in)


def left_tile(refs, columns):
    return jnp.concatenate([ref[:, columns] for ref in refs])


def right_tile(refs, columns):
    near, far, other_near, other_far = refs
    rows = near.shape[0] // 2
    order = [(near, 0), (far, 0), (near, 1), (far, 1)]
    order += [(other_near, 0), (other_far, 0), (other_near, 1), (other_far, 1)]
    return jnp.concatenate([ref[at * rows : (at + 1) * rows, columns] for ref, at in order])


def in_order(pieces):
    left, left_far, right, right_far, c_both, c_left_far, c_right_far = pieces
    return (left, left_far, c_left_far, c_both, right, right_far, c_right_far)


class Side:
    def __init__(self, ref, start, width):
        self.ref, self.start, self.shape = ref, start, (ref.shape[0], width)

    def __getitem__(self, at):
        rows, columns = at
        return self.ref[rows, columns.start + self.start : columns.stop + self.start]


def sides(l0, l1, l3, both, r0, r1, r3):
    left, right = l0.shape[1], r0.shape[1]
    return (l0, l1, Side(both, 0, left), l3), (r0, r1, Side(both, left, right), r3)


FIRST_PARTS = ((0, 0, 768), (0, 768, 512), (1, 256, 256), (1, 512, 768))
SECOND_PARTS = ((0, 0, 768), (0, 768, 512), (0, 1280, 512)) + tuple((1, at, 512) for at in range(0, 2048, 512))


def settle(sides_of, parts, mats, semaphore):
    copies = []
    for (side, start, width), mat in zip(parts, mats):
        for at, piece in enumerate(sides_of[side]):
            rows = piece.shape[0]
            source, first = (piece.ref, piece.start) if isinstance(piece, Side) else (piece, 0)
            columns = pl.ds(first + start, width)
            if side == 0:
                copies.append((source.at[:, columns], mat.at[pl.ds(at * rows, rows), :]))
                continue
            half = rows // 2
            core, far = at // 2, at % 2
            for near in range(2):
                to = ((core * 2 + near) * 2 + far) * half
                copies.append((source.at[pl.ds(near * half, half), columns], mat.at[pl.ds(to, half), :]))
    copies = [pltpu.make_async_copy(*ends, semaphore.at[at]) for at, ends in enumerate(copies)]
    for copy in copies:
        copy.start()
    return copies


FIRST_HALF = 1280
SECOND_HALF = 1792
def head_pair(pair, low):
    nothing = jnp.zeros_like(pair)
    return jnp.concatenate([jnp.where(low, pair, nothing), jnp.where(low, nothing, pair)])


def key_columns(left_rows, right_rows, rows, at):
    if at < 512:
        return left_rows[rows, D + at : D + at + 128]
    return right_rows[rows, at - 256 : at - 128]


def project_kernel(
    place,
    hidden,
    both,
    r0,
    r1,
    r3,
    l0,
    l1,
    l3,
    left_rows,
    right_rows,
    vectors,
    hidden_t,
    query_mat,
    low_key_mat,
    high_key_mat,
    value_mat,
    settling,
):
    tokens = hidden.shape[0]
    lefts, rights = sides(l0, l1, l3, both, r0, r1, r3)
    mats = (query_mat, low_key_mat, high_key_mat, value_mat)
    copies = settle((lefts, rights), FIRST_PARTS, mats, settling)
    restore = restore_from(place)
    moved = dot(hidden[...], restore).astype(jnp.bfloat16)
    small = dot(restore, right_tile(rights, slice(0, 128)))
    turned = jnp.transpose(small)[:16]
    vectors[...] = turned
    for at in range(0, FIRST_HALF, 256):
        columns = slice(at, at + 256)
        rows = dot(moved, left_tile(lefts, columns))
        if at < D:
            rows += turned[0:1, columns]
        left_rows[:, columns] = rows.astype(jnp.bfloat16)
        if at == 0:
            right_rows[:, columns] = jnp.zeros((tokens, 256), jnp.bfloat16)
            continue
        rows = dot(moved, right_tile(rights, columns))
        if at >= 512:
            rows += turned[1:2, at - 512 : at - 256]
        right_rows[:, columns] = rows.astype(jnp.bfloat16)
    left_rows.done()
    right_rows.done()
    hidden_t[...] = dot_nt(arrange_from(place), hidden[...]).astype(jnp.bfloat16)
    for copy in copies:
        copy.wait()


def project(place, hidden, pieces):
    tokens, ordered = hidden.shape[0], in_order(pieces)
    return run(
        project_kernel,
        "project",
        [(place, "S"), (hidden, "H")] + placed_at("K", *ordered[3:], *ordered[:3]),
        [
            ((tokens, FIRST_HALF), bf16, "H"),
            ((tokens, FIRST_HALF), bf16, "H"),
            ((16, D), f32, "V"),
            ((D, tokens), bf16, "H"),
        ]
        + [((D, width), bf16, "A") for _, _, width in FIRST_PARTS],
        9e9,
        [pltpu.SemaphoreType.DMA((24,))],
        total=50,
    )


def attention_kernel(
    place, lengths, left_rows, right_rows, attention_out, context_arrived, context_t, context
):
    tokens = context.shape[0]
    left_rows, right_rows = ready(left_rows), ready(right_rows)
    low = lax.broadcasted_iota(jnp.int32, (SPAN, 128), 1) < HEAD_DIM

    def attend(span, carry):
        rows = pl.ds(pl.multiple_of(span * SPAN, SPAN), SPAN)
        live = lax.broadcasted_iota(jnp.int32, (SPAN, SPAN), 1) < lengths[span]
        for at in range(0, D, 128):
            query = left_rows[rows, at : at + 128]
            keys = head_pair(key_columns(left_rows, right_rows, rows, at), low)
            values = head_pair(right_rows[rows, 512 + at : 640 + at], low)
            scores = dot_nt(query, keys) * HEAD_DIM ** (-0.5)
            parts = []
            for head in range(2):
                part = jnp.where(live, scores[:, head * SPAN : (head + 1) * SPAN], masked_out)
                exponent = jnp.exp(part - jnp.max(part, axis=-1, keepdims=True))
                parts.append(
                    (exponent * (1.0 / jnp.sum(exponent, axis=-1, keepdims=True))).astype(jnp.bfloat16)
                )
            attention = jnp.concatenate(parts, axis=1)
            attention_out[rows, 2 * at : 2 * at + 256] = attention
            context[rows, at : at + 128] = dot(attention, values).astype(jnp.bfloat16)
        return carry

    lax.fori_loop(0, tokens // SPAN, attend, 0)
    attention_out.done()
    context_arrived[...] = dot(context[...], restore_from(place)).astype(jnp.bfloat16)
    context_t[...] = dot_nt(arrange_from(place), context[...]).astype(jnp.bfloat16)


def attention_forward(place, lengths, left_rows, right_rows):
    tokens = left_rows.shape[0]
    return run(
        attention_kernel,
        "attention_forward",
        placed_at("S", place, lengths) + placed_at("H", left_rows, right_rows),
        [((tokens, 2 * D), bf16, "H"), ((tokens, D), bf16, "V"), ((D, tokens), bf16, "H")],
        9e9,
        [pltpu.VMEM((tokens, D), bf16)],
        total=28,
    )


def gelu_parts(preact):
    scaled = jnp.abs(preact) * (0.5**0.5)
    below_one = 1.0 + 0.3275911 * scaled
    near = pl.reciprocal(below_one, approx=True)
    near = near * (2.0 - below_one * near)
    poly = near * (
        0.254829592
        + near * (-0.284496736 + near * (1.421413741 + near * (-1.453152027 + near * 1.061405429)))
    )
    bell = jnp.exp(-0.5 * preact * preact)
    tail = 0.5 * poly * bell
    below = jnp.where(preact < 0.0, tail, 1.0 - tail)
    return (preact * below, below + preact * bell * (0.5 / math.pi) ** 0.5)


FF_TILE = 512


def second_tiles(left, right):
    for at in range(D, SECOND_HALF, FF_TILE):
        yield at - D, left_tile(left, slice(at, at + FF_TILE))
    for at in range(0, right[0].shape[1], FF_TILE):
        yield SECOND_HALF - D + at, right_tile(right, slice(at, at + FF_TILE))


def vector_places():
    for device in range(D // ROW):
        for part in range(4):
            yield (8 + part, device * ROW), (device * 4 + part) * ROW


def residual_kernel(
    place,
    vectors,
    context_arrived,
    l0,
    l1,
    l3,
    both,
    hidden,
    moved,
    normed_out,
    factor_out,
    first_t,
    output_mat,
    settling,
):
    left = (l0, l1, Side(both, 0, l0.shape[1]), l3)
    copies = settle((left, ()), SECOND_PARTS[:1], (output_mat,), settling)
    residual = dot(context_arrived[...], left_tile(left, slice(0, D)))
    residual += hidden[...].astype(jnp.float32) + vectors[2:3, :]
    first_out, normed, factor = normalize(residual, vectors[3:4, :], vectors[4:5, :])
    normed_out[...] = normed
    factor_out[...] = factor
    first16 = first_out.astype(jnp.bfloat16)
    moved[...] = dot(first16, restore_from(place)).astype(jnp.bfloat16)
    first_t[...] = dot_nt(arrange_from(place), first16).astype(jnp.bfloat16)
    for copy in copies:
        copy.wait()


def residual_forward(place, hidden, context_arrived, vectors, pieces):
    tokens, ordered = hidden.shape[0], in_order(pieces)
    return run(
        residual_kernel,
        "residual",
        [(place, "S")]
        + placed_at("V", vectors, context_arrived, *ordered[:4])
        + [(hidden, "H")],
        [
            ((tokens, D), bf16, "V"),
            ((tokens, D), f32, "V"),
            ((tokens, 1), f32, "V"),
            ((D, tokens), bf16, "H"),
            ((D, D), bf16, "A"),
        ],
        1e9,
        [pltpu.SemaphoreType.DMA((4,))],
        total=24,
    )


def feed_kernel(vectors, moved, l0, l1, l3, both, r0, r1, r3, active, active_t, slope, *rest):
    mats, (inner_bias, settling) = rest[:-2], rest[-2:]
    for at, column in vector_places():
        inner_bias[:, column : column + ROW] = vectors[at[0] : at[0] + 1, at[1] : at[1] + ROW]
    left, right = sides(l0, l1, l3, both, r0, r1, r3)
    copies = settle((left, right), SECOND_PARTS[1:], mats, settling)
    for at, tile in second_tiles(left, right):
        columns = slice(at, at + FF_TILE)
        value, derivative = gelu_parts(dot(moved[...], tile) + inner_bias[:, columns])
        value16 = value.astype(jnp.bfloat16)
        active[:, columns] = value16
        active_t[columns, :] = jnp.transpose(value16)
        slope[:, columns] = derivative.astype(jnp.bfloat16)
    for copy in copies:
        copy.wait()


def feed_forward(moved, vectors, ff, pieces):
    tokens = moved.shape[0]
    return run(
        feed_kernel,
        "feed_forward",
        placed_at("V", vectors, moved, *in_order(pieces)),
        [((tokens, ff), bf16, "V"), ((ff, tokens), bf16, "V"), ((tokens, ff), bf16, "V")]
        + [((D, width), bf16, "A") for _, _, width in SECOND_PARTS[1:]],
        8e9,
        [pltpu.VMEM((1, ff), f32), pltpu.SemaphoreType.DMA((44,))],
        total=20,
    )


def natural_rows(place, pieces, target, semaphore):
    rows = 4 * ROW
    left, right = pieces[0].shape[1], pieces[4].shape[1]
    near, far, far_core, near_core, right_near, right_far, right_far_core = pieces
    places = [(near, 0, 0, 0, 0), (far, 0, 0, 1, 0), (near_core, 0, 1, 0, 0), (far_core, 0, 1, 1, 0)]
    places += [(right_near, 1, 0, 0, 0), (right_far, 1, 0, 1, 0)]
    places += [(near_core, 1, 1, 0, left), (right_far_core, 1, 1, 1, 0)]
    for piece, is_right, core_off, far_off, start in places:
        half = right if is_right else left
        for near_off in range(2):
            for z_off in range(4):
                x_off, y_off = (far_off, near_off) if is_right else (near_off, far_off)
                block = ((z_off ^ place[3]) * 2 + (x_off ^ place[2])) * 2 + (core_off ^ place[0])
                block = block * 2 + (y_off ^ place[1])
                to = pl.ds(pl.multiple_of(block * rows, rows), rows)
                pltpu.make_async_copy(
                    piece.at[pl.ds((near_off * 4 + z_off) * rows, rows), pl.ds(start, half)],
                    target.at[to, pl.ds(is_right * left, half)],
                    semaphore,
                ).start()
    pltpu.make_async_copy(target, target, semaphore).wait()


def last_kernel(
    place,
    active,
    first_normed,
    vectors,
    l0,
    l1,
    l3,
    both,
    r0,
    r1,
    r3,
    layer_out,
    normed_out,
    factor_out,
    cls_rows,
    outer_mat,
    semaphore,
):
    natural_rows(place, (l0, l1, l3, both, r0, r1, r3), outer_mat, semaphore)
    total = first_normed[...] * vectors[3:4, :] + vectors[4:5, :] + vectors[5:6, :]
    total += dot(active[...], outer_mat[...])
    encoded, normed, factor = normalize(total, vectors[6:7, :], vectors[7:8, :])
    layer_out[...] = encoded.astype(jnp.bfloat16)
    normed_out[...] = normed
    factor_out[...] = factor
    for span in range(encoded.shape[0] // SPAN):
        cls_rows[span : span + 1, :] = encoded[span * SPAN : span * SPAN + 1].astype(jnp.bfloat16)


def last(place, active, first_normed, vectors, pieces):
    tokens, ff = active.shape
    return run(
        last_kernel,
        "last",
        [(place, "S")]
        + placed_at("V", active, first_normed, vectors, *in_order(pieces)),
        [
            ((tokens, D), bf16, "H"),
            ((tokens, D), f32, "V"),
            ((tokens, 1), f32, "V"),
            ((tokens // SPAN, D), bf16, "V"),
            ((ff, D), bf16, "V"),
        ],
        2.5e9,
        [pltpu.SemaphoreType.DMA],
        total=16,
    )


def pick(place, first, second):
    return jnp.where(place == 0, first, second)


def turn_kernel(
    place,
    partner_span,
    cotangent,
    normed,
    factor,
    vectors,
    own_rows,
    other_rows,
    second_grad,
    kept,
    sent,
    sums,
    loss,
):
    spans = own_rows.shape[0]
    own, other = own_rows[...].astype(jnp.float32), other_rows[...].astype(jnp.float32)
    logits = dot_nt(own_rows[...], other_rows[...]) / math.sqrt(D)
    row = lax.broadcasted_iota(jnp.int32, (spans, spans), 0)
    column = lax.broadcasted_iota(jnp.int32, (spans, spans), 1)
    first_place = place[1] == 0
    target = jnp.zeros((spans, spans), jnp.float32)
    for span in range(spans):
        match = partner_span[0, span]
        hit_row = jnp.where(first_place, span, match)
        hit_column = jnp.where(first_place, match, span)
        target += ((row == hit_row) & (column == hit_column)).astype(jnp.float32)
    highest_logit = jnp.max(logits, axis=1, keepdims=True)
    exponent = jnp.exp(logits - highest_logit)
    totals = jnp.sum(exponent, axis=1, keepdims=True)
    losses = highest_logit + jnp.log(totals) - jnp.sum(target * logits, axis=1, keepdims=True)
    loss[...] = jnp.sum(jnp.where(row == column, losses, 0.0), axis=0, keepdims=True)
    soft = exponent / totals - target
    exponent = jnp.exp(logits - jnp.max(logits, axis=0, keepdims=True))
    back = exponent / jnp.sum(exponent, axis=0, keepdims=True) - target
    own_term, back_term = jnp.zeros_like(own), jnp.zeros_like(own)
    for span in range(spans):
        own_term += soft[:, span : span + 1] * other[span : span + 1]
        back_term += back[:, span : span + 1] * other[span : span + 1]
    cls_gradient = own_term + back_term.astype(jnp.bfloat16).astype(jnp.float32)
    start = lax.broadcasted_iota(jnp.int32, (SPAN, 1), 0) == 0
    gain = vectors[6:7, :]
    gain_sum = jnp.zeros((1, D), jnp.float32)
    shift_sum, bias_sum = gain_sum, gain_sum
    for span in range(spans):
        rows = slice(span * SPAN, (span + 1) * SPAN)
        upstream = cotangent[rows, :].astype(jnp.float32)
        upstream += jnp.where(start, cls_gradient[span : span + 1], 0.0)
        grad, gain_part, shift_part = normalize_back(upstream, normed[rows, :], factor[rows, :], gain)
        second_grad[rows, :] = grad
        gain_sum += gain_part[None]
        shift_sum += shift_part[None]
        bias_sum += jnp.sum(grad, axis=0, keepdims=True)
        grad16 = grad.astype(jnp.bfloat16)
        kept[rows, :] = pick(place[0], grad16[:, : D // 2], grad16[:, D // 2 :])
        sent[rows, :] = pick(place[0], grad16[:, D // 2 :], grad16[:, : D // 2])
    sums[0:1, :] = bias_sum
    sums[1:2, :] = gain_sum
    sums[2:3, :] = shift_sum


def turn(place, partner_span, cotangent, normed, factor, vectors, own_rows, other_rows):
    tokens = cotangent.shape[0]
    return run(
        turn_kernel,
        "turn",
        placed_at("S", place, partner_span)
        + [(cotangent, "V")]
        + placed_at("V", normed, factor, vectors, own_rows, other_rows),
        [
            ((tokens, D), f32, "V"),
            ((tokens, D // 2), bf16, "V"),
            ((tokens, D // 2), bf16, "V"),
            ((3, D), f32, "V"),
            ((1, own_rows.shape[0]), f32, "V"),
        ],
        1e8,
    )


def both_halves(place, kept, sent):
    return jnp.concatenate([pick(place, kept, sent), pick(place, sent, kept)], axis=1)


def slope_kernel(place, second_kept, second_sent, outer_mat, slope, kept, sent, sums, second16):
    second16[...] = both_halves(place[0], second_kept[...], second_sent[...])
    per_half = kept.shape[1] // D

    def tile(at, carry):
        columns = pl.ds(pl.multiple_of(at * D, D), D)
        inside = pl.ds(pl.multiple_of((at % per_half) * D, D), D)
        grad = dot_nt(second16[...], outer_mat[columns, :]) * slope[:, columns].astype(jnp.float32)
        sums[:, columns] = jnp.sum(grad, axis=0, keepdims=True)
        grad16 = grad.astype(jnp.bfloat16)
        mine = place[0] == at // per_half

        @pl.when(mine)
        def keep():
            kept[:, inside] = grad16

        @pl.when(jnp.logical_not(mine))
        def send():
            sent[:, inside] = grad16

        return carry

    lax.fori_loop(0, 2 * per_half, tile, 0)


def slope_back(place, second_kept, second_sent, outer_mat, slope):
    tokens, ff = slope.shape
    half = ((tokens, ff // 2), bf16, "V")
    return run(
        slope_kernel,
        "slope_back",
        [(place, "S")] + placed_at("V", second_kept, second_sent, outer_mat, slope),
        [half, half, ((1, ff), f32, "V")],
        2.5e9,
        [pltpu.VMEM((tokens, D), bf16)],
    )


CHIPS_TILE = 2


def outer_kernel(place, active_t, other_active_t, kept, received, left_kept, left_sent, right_kept, right_sent):
    rows = 2 * ROW
    height = 8 * CHIPS_TILE * rows

    def chips(at, carry):
        tile = pl.ds(pl.multiple_of(at * height, height), height)
        grad = dot(active_t[tile, :], kept[...]) + dot(other_active_t[tile, :], received[...])
        grad = grad.astype(jnp.bfloat16)
        z_off = (at * CHIPS_TILE // 2) ^ place[3]
        for block in range(4 * CHIPS_TILE):
            x_at, core, y_at = block // 4, block // 2 % 2, block % 2
            start = block * 2 * rows
            left, right = grad[start : start + rows], grad[start + rows : start + 2 * rows]
            x_off, y_off = x_at ^ place[2], y_at ^ place[1]
            left_at = (x_off * 4 + z_off) * 2 + core
            right_at = (y_off * 4 + z_off) * 2 + core

            @pl.when(y_off == 0)
            def left_here():
                left_kept[left_at] = left

            @pl.when(y_off == 1)
            def left_there():
                left_sent[left_at] = left

            @pl.when(x_off == 0)
            def right_here():
                right_kept[right_at] = right

            @pl.when(x_off == 1)
            def right_there():
                right_sent[right_at] = right

        return carry

    lax.fori_loop(0, PLACES // CHIPS_TILE, chips, 0)


def outer_gradient(place, active_t, other_active_t, kept, received):
    piece = ((2 * PLACES, 2 * ROW, kept.shape[1]), bf16, "V")
    return run(
        outer_kernel,
        "outer_gradient",
        [(place, "S")] + placed_at("V", active_t, other_active_t, kept, received),
        [piece] * 4,
        2.5e9,
    )


def whole_precision(left, right):
    high = left.astype(jnp.bfloat16)
    rest = (left - high.astype(jnp.float32)).astype(jnp.bfloat16)
    return dot_nt(high, right) + dot_nt(rest, right)


def first_kernel(
    place,
    preact_kept,
    preact_sent,
    factor,
    vectors,
    *refs,
):
    output_mat, inner_mats = refs[0], refs[1:7]
    second_grad, normed, residual_grad, kept, sent, context_grad, sums = refs[7:]
    restore = restore_from(place)
    total = jnp.zeros((factor.shape[0], D), jnp.float32)
    half = preact_kept.shape[1]
    for at, tile in zip(range(0, 2 * half, FF_TILE), inner_mats):
        columns = slice(at % half, at % half + FF_TILE)
        kept_part, sent_part = preact_kept[:, columns], preact_sent[:, columns]
        if at >= half:
            kept_part, sent_part = sent_part, kept_part
        total += dot_nt(pick(place[0], kept_part, sent_part), tile[...])
    first_grad = second_grad[...] + whole_precision(total, restore)
    grad, gain_sum, shift_sum = normalize_back(first_grad, normed[...], factor[...], vectors[3:4, :])
    residual_grad[...] = grad
    sums[0:1, :] = jnp.sum(grad, axis=0, keepdims=True)
    sums[1:2, :] = gain_sum[None]
    sums[2:3, :] = shift_sum[None]
    grad16 = grad.astype(jnp.bfloat16)
    kept[...] = pick(place[0], grad16[:, : D // 2], grad16[:, D // 2 :])
    sent[...] = pick(place[0], grad16[:, D // 2 :], grad16[:, : D // 2])
    moved = dot_nt(grad16, output_mat[...]).astype(jnp.bfloat16)
    context_grad[...] = dot_nt(moved, restore).astype(jnp.bfloat16)


def first_back(place, preact_kept, preact_sent, second_grad, normed, factor, vectors, mats):
    tokens = second_grad.shape[0]
    half = ((tokens, D // 2), bf16, "V")
    return run(
        first_kernel,
        "first_back",
        [(place, "S")]
        + placed_at("V", preact_kept, preact_sent, factor, vectors)
        + placed_at("V", *mats, second_grad, normed),
        [((tokens, D), f32, "V"), half, half, ((tokens, D), bf16, "V"), ((3, D), f32, "V")],
        4.9e9,
    )


def part_rows(grad, left_kept, left_sent, right_kept, right_sent, is_left):
    quarter = D // 4
    if is_left:
        left_kept[...] = grad[: 2 * quarter]
        left_sent[...] = grad[2 * quarter :]
    else:
        right_kept[:quarter, :] = grad[:quarter]
        right_sent[:quarter, :] = grad[quarter : 2 * quarter]
        right_kept[quarter:, :] = grad[2 * quarter : 3 * quarter]
        right_sent[quarter:, :] = grad[3 * quarter :]


def inner_kernel(first_t, other_first_t, kept, received, left_kept, left_sent, right_kept, right_sent):
    for is_left in (True, False):
        columns = slice(0, D) if is_left else slice(D, 2 * D)
        grad = dot(first_t[...], kept[:, columns]) + dot(other_first_t[...], received[:, columns])
        part_rows(grad.astype(jnp.bfloat16), left_kept, left_sent, right_kept, right_sent, is_left)


def inner_gradient(first_t, other_first_t, kept, received):
    piece = ((D // 2, kept.shape[1] // 2), bf16, "V")
    return run(
        inner_kernel,
        "inner_gradient",
        placed_at("V", first_t, other_first_t) + placed_at("V", kept, received),
        [piece] * 4,
        2.5e9,
    )


def attend_kernel(
    place,
    context_grad,
    left_rows,
    right_rows,
    attention_in,
    first_sums,
    second_sums,
    inner_sums,
    kept,
    sent,
    sums,
    grads,
):
    tokens = context_grad.shape[0]
    low = lax.broadcasted_iota(jnp.int32, (SPAN, 128), 1) < HEAD_DIM
    scale = HEAD_DIM ** (-0.5)
    left_rows, right_rows, attention_in = [ready(ref) for ref in (left_rows, right_rows, attention_in)]

    def attend(span, carry):
        rows = pl.ds(pl.multiple_of(span * SPAN, SPAN), SPAN)
        for at in range(0, D, 128):
            query = left_rows[rows, at : at + 128]
            keys = head_pair(key_columns(left_rows, right_rows, rows, at), low)
            values = head_pair(right_rows[rows, 512 + at : 640 + at], low)
            upstream = context_grad[rows, at : at + 128]
            attention16 = attention_in[rows, 2 * at : 2 * at + 256]
            attention_grad = dot_nt(upstream, values)
            parts = []
            for head in range(2):
                columns = slice(head * SPAN, (head + 1) * SPAN)
                attention = attention16[:, columns].astype(jnp.float32)
                part = attention_grad[:, columns]
                weighted = jnp.sum(attention * part, axis=-1, keepdims=True)
                parts.append((attention * (part - weighted)).astype(jnp.bfloat16))
            scores_grad = jnp.concatenate(parts, axis=1)
            grads[0, rows, at : at + 128] = (dot(scores_grad, keys) * scale).astype(jnp.bfloat16)
            both = dot_tn(scores_grad, query)
            both = jnp.where(low, both[:SPAN], both[SPAN:])
            grads[1, rows, at : at + 128] = (both * scale).astype(jnp.bfloat16)
            both = dot_tn(attention16, upstream)
            both = jnp.where(low, both[:SPAN], both[SPAN:])
            grads[2, rows, at : at + 128] = both.astype(jnp.bfloat16)
        return carry

    lax.fori_loop(0, tokens // SPAN, attend, 0)
    query_grad, key_grad, value_grad = grads[0], grads[1], grads[2]
    half = D // 2
    for at, grad in enumerate((query_grad, key_grad, value_grad)):
        columns = slice(at * half, (at + 1) * half)
        kept[:, columns] = pick(place[0], grad[:, :half], grad[:, half:])
        sent[:, columns] = pick(place[0], grad[:, half:], grad[:, :half])
    sums[0:1, :] = jnp.sum(query_grad.astype(jnp.float32), axis=0, keepdims=True)
    sums[1:2, :] = jnp.sum(value_grad.astype(jnp.float32), axis=0, keepdims=True)
    sums[2:5, :] = first_sums[...]
    sums[5:8, :] = second_sums[...]
    for at, column in vector_places():
        sums[at[0] : at[0] + 1, at[1] : at[1] + ROW] = inner_sums[:, column : column + ROW]
    sums[12:16, :] = jnp.zeros((4, D), jnp.float32)


def attend_back(place, context_grad, left_rows, right_rows, attention, first_sums, second_sums, inner_sums):
    tokens = context_grad.shape[0]
    part = ((tokens, 3 * D // 2), bf16, "V")
    return run(
        attend_kernel,
        "attend_back",
        placed_at("S", place)
        + placed_at("V", context_grad)
        + placed_at("V", left_rows, right_rows, attention)
        + placed_at("V", first_sums, second_sums, inner_sums),
        [part, part, ((16, D), f32, "V")],
        4e9,
        [pltpu.VMEM((3, tokens, D), bf16)],
    )


def attention_gradient_kernel(
    place,
    sums,
    hidden_t,
    other_hidden_t,
    context_t,
    other_context_t,
    grads,
    other_grads,
    residual,
    other_residual,
    left_kept,
    left_sent,
    right_kept,
    right_sent,
):
    half = D // 2
    grad = dot(hidden_t[...], grads[:, :D]) + dot(other_hidden_t[...], other_grads[:, :D])
    grad = grad.astype(jnp.bfloat16)
    left_kept[:, :D] = grad[:half]
    left_sent[:, :D] = grad[half:]
    total = sums[...].astype(jnp.bfloat16)
    total = jnp.concatenate([total, jnp.zeros((112, D), jnp.bfloat16)])
    small = dot_nt(arrange_from(place), total).astype(jnp.bfloat16)
    left_kept[:, D:] = small[:half]
    left_sent[:, D:] = small[half:]
    value = dot(hidden_t[...], grads[:, D:]) + dot(other_hidden_t[...], other_grads[:, D:])
    output = dot(context_t[...], residual[...]) + dot(other_context_t[...], other_residual[...])
    grad = jnp.concatenate([value, output], axis=1).astype(jnp.bfloat16)
    part_rows(grad, left_kept, left_sent, right_kept, right_sent, False)


def attention_gradient(*operands):
    left, right = ((D // 2, D + 128), bf16, "V"), ((D // 2, D), bf16, "V")
    places = ["S"] + ["V"] * 9
    return run(
        attention_gradient_kernel,
        "attention_gradient",
        list(zip(operands, places)),
        [left, left, right, right],
        2.5e9,
    )


def input_kernel(
    place, kept, sent, query_mat, low_key_mat, high_key_mat, value_mat, residual_grad, input_grad
):
    restore = restore_from(place)
    half = D // 2
    parts = []
    for at in range(3):
        columns = slice(at * half, (at + 1) * half)
        parts.append(both_halves(place[0], kept[:, columns], sent[:, columns]))
    query_grad, key_grad, value_grad = parts
    total = dot_nt(query_grad, query_mat[...])
    total += dot_nt(key_grad[:, :512], low_key_mat[...])
    total += dot_nt(key_grad[:, 512:], high_key_mat[...])
    total += dot_nt(value_grad, value_mat[...])
    total = residual_grad[...] + whole_precision(total, restore)
    input_grad[...] = total.astype(jnp.bfloat16)


def input_back(place, residual_grad, kept, sent, mats):
    return run(
        input_kernel,
        "input_back",
        [(place, "S")]
        + placed_at("V", kept, sent)
        + placed_at("V", *mats, residual_grad),
        [(residual_grad.shape, bf16, "H")],
        3e9,
    )[0]


def add_kernel(left, left_in, right, right_in, left_kept, left_sent, right_kept, right_sent):
    for own, received, kept, sent in (
        (left, left_in, left_kept, left_sent),
        (right, right_in, right_kept, right_sent),
    ):
        total = (own[...].astype(jnp.float32) + received[...].astype(jnp.float32)).astype(jnp.bfloat16)
        half = total.shape[0] // 2
        kept[...] = total[:half]
        sent[...] = total[half:]


def add_parts(left, left_in, right, right_in):
    shapes = [(part.shape[0] // 2,) + part.shape[1:] for part in (left, left, right, right)]
    return pl.pallas_call(
        add_kernel,
        in_specs=[VMEM] * 4,
        out_specs=[VMEM] * 4,
        out_shape=[jax.ShapeDtypeStruct(shape, jnp.bfloat16) for shape in shapes],
        compiler_params=params(),
        cost_estimate=cost(1, 1),
        name="add_parts",
    )(left, left_in, right, right_in)


def add_z_kernel(left, left_in, right, right_in, own, first, second, third):
    width = left.shape[-1]
    for part, received, columns in (
        (left, left_in, slice(0, width)),
        (right, right_in, slice(width, width + right.shape[-1])),
    ):
        rows = part.shape[0] // 4
        total = part[...].astype(jnp.float32) + received[...].astype(jnp.float32)
        own[..., columns] = total[:rows]
        for at, sent in enumerate((first, second, third)):
            sent[..., columns] = total[(at + 1) * rows : (at + 2) * rows].astype(jnp.bfloat16)


def add_z(left, left_in, right, right_in):
    shape = (left.shape[0] // 4,) + left.shape[1:-1] + (left.shape[-1] + right.shape[-1],)
    return pl.pallas_call(
        add_z_kernel,
        in_specs=[VMEM] * 4,
        out_specs=[VMEM] * 4,
        out_shape=[jax.ShapeDtypeStruct(shape, jnp.float32)]
        + [jax.ShapeDtypeStruct(shape, jnp.bfloat16)] * 3,
        compiler_params=params(),
        cost_estimate=cost(1, 1),
        name="add_z",
    )(left, left_in, right, right_in)


def add_join_kernel(left, left_in, right, right_in, kept, sent):
    width = left.shape[-1]
    for part, received, columns in (
        (left, left_in, slice(0, width)),
        (right, right_in, slice(width, width + right.shape[-1])),
    ):
        rows = part.shape[0] // 4
        total = part[...].astype(jnp.float32) + received[...].astype(jnp.float32)
        for at in range(2):
            to, start = slice(at * rows, (at + 1) * rows), 2 * at * rows
            kept[to, ..., columns] = total[start : start + rows]
            sent[to, ..., columns] = total[start + rows : start + 2 * rows].astype(jnp.bfloat16)


def add_join(left, left_in, right, right_in):
    shape = (left.shape[0] // 2,) + left.shape[1:-1] + (left.shape[-1] + right.shape[-1],)
    return pl.pallas_call(
        add_join_kernel,
        in_specs=[VMEM] * 4,
        out_specs=[VMEM] * 2,
        out_shape=[jax.ShapeDtypeStruct(shape, jnp.float32), jax.ShapeDtypeStruct(shape, jnp.bfloat16)],
        compiler_params=params(),
        cost_estimate=cost(1, 1),
        name="add_join",
    )(left, left_in, right, right_in)


def add_half_kernel(own, received, kept, sent):
    rows = own.shape[0] // 2
    total = own[...] + received[...].astype(jnp.float32)
    kept[...] = total[:rows]
    sent[...] = total[rows:].astype(jnp.bfloat16)


def add_half(own, received):
    shape = (own.shape[0] // 2,) + own.shape[1:]
    return pl.pallas_call(
        add_half_kernel,
        in_specs=[VMEM] * 2,
        out_specs=[VMEM] * 2,
        out_shape=[jax.ShapeDtypeStruct(shape, jnp.float32), jax.ShapeDtypeStruct(shape, jnp.bfloat16)],
        compiler_params=params(),
        cost_estimate=cost(1, 1),
        name="add_half",
    )(own, received)


def finish_kernel(place, own, *refs):
    received_all, (mine, other) = refs[:-2], refs[-2:]
    total = own[...]
    for received in received_all:
        total = total + received[...].astype(jnp.float32)
    if len(total.shape) == 3:
        low, high = total[0], total[1]
    else:
        low, high = total[:ROW], total[ROW:]
    mine[...] = pick(place[0], low, high)
    other[...] = pick(place[0], high, low)


def finish(place, own, received):
    rows = own.shape[1] if own.ndim == 3 else ROW
    return pl.pallas_call(
        finish_kernel,
        in_specs=[SMEM] + [VMEM] * (1 + len(received)),
        out_specs=[VMEM] * 2,
        out_shape=[jax.ShapeDtypeStruct((rows, own.shape[-1]), jnp.float32)] * 2,
        compiler_params=params(),
        cost_estimate=cost(1, 1),
        name="finish",
    )(place, own, *received)


def put(place, out, mine, received):
    half = mine.shape[1]
    out[:, :half] = pick(place[0], mine, received)
    out[:, half:] = pick(place[0], received, mine)


def outer_out_kernel(place, mine, received, out):
    rows, half = mine.shape[0], mine.shape[1] // 2
    for at in range(2):
        columns = slice(at * half, (at + 1) * half)
        put(place, out.at[at * rows : (at + 1) * rows], mine[:, columns], received[:, columns])


def inner_out_kernel(place, mine, received, out):
    put(place, out, mine[...], received[...])


def rest_out_kernel(place, mine, received, query, key, value, output, inner_bias, *vectors):
    half = D // 2
    for out, at in ((query, 0), (key, half), (value, D + 128), (output, D + 128 + half)):
        columns = slice(at, at + half)
        put(place, out, mine[:, columns], received[:, columns])
    turned = jnp.transpose(mine[:, D : D + 128] + received[:, D : D + 128])
    for at, out in enumerate(vectors):
        out[...] = turned[at : at + 1]
    for at in range(4):
        inner_bias[:, at * ROW : (at + 1) * ROW] = turned[8 + at : 9 + at]


def placed(kernel, name, place, mine, received, shapes):
    return pl.pallas_call(
        kernel,
        in_specs=[SMEM, VMEM, VMEM],
        out_specs=[VMEM] * len(shapes),
        out_shape=[jax.ShapeDtypeStruct(shape, jnp.float32) for shape in shapes],
        compiler_params=params(),
        cost_estimate=cost(1, 1),
        name=name,
    )(place, mine, received)


def first_transfers(pieces):
    return [mate(pieces[1]), across(pieces[3], 2)]


def add_first(pieces, received):
    return add_parts(pieces[0], received[0], pieces[2], received[1])


def second_transfers(pieces):
    return [across(pieces[1], 2), mate(pieces[3])]


def add_joined(pieces, received):
    return add_join(pieces[0], received[0], pieces[2], received[1])


def add_second(pieces, received):
    return add_z(pieces[0], received[0], pieces[2], received[1])


def third_transfers(parts):
    return [across(sent, mask) for sent, mask in zip(parts[1:], (4, 8, 12))]


def fast_device(
    hidden_in,
    cotangent,
    span_lengths,
    partner_span,
    query_weight,
    query_bias,
    key_weight,
    value_weight,
    value_bias,
    output_weight,
    output_bias,
    first_gain,
    first_shift,
    inner_weight,
    inner_bias,
    outer_weight,
    outer_bias,
    second_gain,
    second_shift,
):
    core, x_at, z_at, y_at = coordinates()
    place = jnp.stack([core, y_at, x_at, z_at]).astype(jnp.int32)
    first_block, second_block = pack(
        query_weight,
        key_weight,
        value_weight,
        output_weight,
        inner_weight,
        inner_bias,
        (
            query_bias,
            value_bias,
            output_bias,
            first_gain,
            first_shift,
            outer_bias,
            second_gain,
            second_shift,
        ),
    )
    ff = inner_weight.shape[1]
    first_z = z_exchange(first_block)
    first = stack_z(first_block, first_z, FIRST_HALF)
    second_block, third_block = tied((second_block, outer_weight), *first)
    first_in = near_exchange(first)
    second_z = across(second_block, 8)
    *first, first_both = stack_near(first, tied(first_in, second_z))
    second_two = stack_z_two(after(second_block, *first), second_z)
    first = tied(first, second_two)
    first_far = far_exchange(first)
    second_z = across(second_two, 4)
    first_core = across(first_both, 1)
    second = stack_mixed(second_two, after(second_z, first_core, *first_far), SECOND_HALF)
    first_far, third_block = tied(first_far, *second), after(third_block, *second)
    second_in = near_exchange(second)
    first_far_core = core_exchange(first_far)
    third_z = across(after(third_block, *first_far_core), 8)
    third_two = stack_z_two(third_block, third_z)
    left_rows, right_rows, vectors, hidden_t, *first_mats = project(
        place, hidden_in, pieces_of(first, first_far, first_core, first_far_core)
    )
    *second, second_both = stack_near(second, tied(second_in, vectors, third_z))
    third_two, left_rows = tied((third_two, left_rows), *second)
    second_far = far_exchange(second)
    third_z = across(third_two, 4)
    second_core = across(second_both, 1)
    attention, context_arrived, context_t = attention_forward(
        place, span_lengths, left_rows, right_rows
    )
    third = stack_mixed(
        third_two, after(third_z, context_arrived, second_core, *second_far), D // 2
    )
    second_far = tied(second_far, *third)
    third_in = near_exchange(third)
    second_far_core = core_exchange(second_far)
    second_pieces = pieces_of(second, second_far, second_core, second_far_core)
    moved, first_normed, first_factor, first_t, output_mat = residual_forward(
        place, hidden_in, context_arrived, vectors, second_pieces
    )
    *third, third_both = stack_near(third, tied(third_in, moved, *second_far_core))
    moved = after(moved, *third)
    third_far = far_exchange(third)
    third_core = across(third_both, 1)
    active, active_t, slope, *inner_mats = feed_forward(moved, vectors, ff, second_pieces)
    second_mats = [output_mat, *inner_mats]
    third_far = tied(third_far, active, third_core)
    third_far_core = core_exchange(third_far)
    third_pieces = pieces_of(third, third_far, third_core, third_far_core)
    hidden_t, context_t, first_t, active_t, active = tied(
        (hidden_t, context_t, first_t, active_t, active), *third_far_core
    )
    other_active_t, other_first_t = across(active_t, 1), across(first_t, 1)
    other_hidden_t, other_context_t = across(hidden_t, 1), across(context_t, 1)
    layer_out, second_normed, second_factor, cls_rows, outer_mat = last(
        place, active, first_normed, vectors, third_pieces
    )
    other_rows = mate(cls_rows)
    second_grad, second_kept, second_sent, second_sums, span_loss = turn(
        place, partner_span, cotangent, second_normed, second_factor, vectors, cls_rows, other_rows
    )
    second_received = across(second_sent, 1)
    preact_kept, preact_sent, inner_sums = slope_back(
        place, second_kept, second_sent, outer_mat, slope
    )
    second_received = after(second_received, preact_kept)
    outer_parts = outer_gradient(place, active_t, other_active_t, second_kept, second_received)
    preact_kept, preact_sent = tied((preact_kept, preact_sent), *outer_parts)
    outer_in = first_transfers(outer_parts)
    preact_received = across(preact_sent, 1)
    residual_grad, residual_kept, residual_sent, context_grad, first_sums = first_back(
        place,
        preact_kept,
        preact_sent,
        second_grad,
        first_normed,
        first_factor,
        vectors,
        second_mats,
    )
    residual_received = across(residual_sent, 1)
    preact_kept = after(preact_kept, context_grad)
    inner_parts = inner_gradient(first_t, other_first_t, preact_kept, preact_received)
    outer_parts = add_first(outer_parts, tied(outer_in, residual_received, *inner_parts))
    inner_parts, context_grad = tied(inner_parts, *outer_parts), after(context_grad, *outer_parts)
    outer_in = second_transfers(outer_parts)
    inner_in = first_transfers(inner_parts)
    grads_kept, grads_sent, sums = attend_back(
        place,
        context_grad,
        left_rows,
        right_rows,
        attention,
        first_sums,
        second_sums,
        inner_sums,
    )
    received = tied(outer_in + inner_in, sums)
    inner_parts = add_first(inner_parts, received[2:])
    outer_parts, grads_sent = tied(outer_parts, *inner_parts), after(grads_sent, *inner_parts)
    outer_own, outer_sent = add_joined(outer_parts, received[:2])
    inner_in = second_transfers(inner_parts)
    outer_in = across(outer_sent, 4)
    grads_received = after(across(grads_sent, 1), outer_own)
    rest_parts = attention_gradient(
        place,
        sums,
        hidden_t,
        other_hidden_t,
        context_t,
        other_context_t,
        grads_kept,
        grads_received,
        residual_kept,
        residual_received,
    )
    *inner_in, outer_in = tied(inner_in + [outer_in], *rest_parts)
    rest_parts = tied(rest_parts, outer_in, *inner_in)
    inner_own, inner_sent = add_joined(inner_parts, inner_in)
    outer_own, outer_sent = add_half(outer_own, after(outer_in, inner_own))
    grads_kept = after(grads_kept, outer_own)
    rest_in = first_transfers(rest_parts)
    inner_in = across(inner_sent, 4)
    outer_in = across(outer_sent, 8)
    input_grad = input_back(place, residual_grad, grads_kept, grads_sent, first_mats)
    rest_parts = add_first(rest_parts, tied(rest_in, input_grad, outer_in, inner_in))
    inner_own, inner_in, outer_own, outer_in = tied(
        (inner_own, inner_in, outer_own, outer_in), *rest_parts
    )
    rest_in = second_transfers(rest_parts)
    inner_own, inner_sent = add_half(inner_own, inner_in)
    inner_in = across(inner_sent, 8)
    outer_mine, outer_other = finish(place, outer_own, [outer_in])
    outer_other = across(outer_other, 1)
    rest_parts = add_second(rest_parts, tied(rest_in, inner_in, outer_other))
    inner_in, outer_other = tied((inner_in, outer_other), *rest_parts)
    rest_in = third_transfers(rest_parts)
    inner_mine, inner_other = finish(place, inner_own, [inner_in])
    inner_other = across(inner_other, 1)
    (outer_grad,) = placed(
        outer_out_kernel, "outer_out", place, outer_mine, outer_other, [(4 * ROW, D)]
    )
    (inner_grad,) = placed(
        inner_out_kernel, "inner_out", place, inner_mine, after(inner_other, outer_grad), [(ROW, ff)]
    )
    rest_mine, rest_other = finish(place, rest_parts[0], tied(rest_in, inner_grad))
    rest_other = across(rest_other, 1)
    query_grad, key_grad, value_grad, output_grad, inner_bias_grad, *vector_grads = placed(
        rest_out_kernel,
        "rest_out",
        place,
        rest_mine,
        rest_other,
        [(ROW, D)] * 4 + [(1, 4 * ROW)] + [(1, ROW)] * 8,
    )
    vector_grads = [grad.reshape(-1) for grad in vector_grads]
    return (
        layer_out,
        input_grad,
        span_loss.reshape(-1),
        query_grad,
        vector_grads[0],
        key_grad,
        value_grad,
        vector_grads[1],
        output_grad,
        vector_grads[2],
        vector_grads[3],
        vector_grads[4],
        inner_grad,
        inner_bias_grad.reshape(-1),
        outer_grad,
        vector_grads[5],
        vector_grads[6],
        vector_grads[7],
    )


def solution(mesh):
    is_block = mesh.shape["doc"] == 2 * PLACES and mesh.shape["pair"] == 2
    return jax.shard_map(
        fast_device if is_block else per_device,
        mesh=mesh,
        in_specs=(
            P(("doc", "pair"), None),
            P(("doc", "pair"), None),
            P(("doc", "pair")),
            P("doc", None),
            P(("doc", "pair"), None),
            P(("doc", "pair")),
            P(("doc", "pair"), None),
            P(("doc", "pair"), None),
            P(("doc", "pair")),
            P(("doc", "pair"), None),
            P(("doc", "pair")),
            P(("doc", "pair")),
            P(("doc", "pair")),
            P(("doc", "pair"), None),
            P(("doc", "pair")),
            P(("doc", "pair"), None),
            P(("doc", "pair")),
            P(("doc", "pair")),
            P(("doc", "pair")),
        ),
        out_specs=(
            P(("doc", "pair"), None),
            P(("doc", "pair"), None),
            P(("doc", "pair")),
            P(("doc", "pair"), None),
            P(("doc", "pair")),
            P(("doc", "pair"), None),
            P(("doc", "pair"), None),
            P(("doc", "pair")),
            P(("doc", "pair"), None),
            P(("doc", "pair")),
            P(("doc", "pair")),
            P(("doc", "pair")),
            P(("doc", "pair"), None),
            P(("doc", "pair")),
            P(("doc", "pair"), None),
            P(("doc", "pair")),
            P(("doc", "pair")),
            P(("doc", "pair")),
        ),
        check_vma=False,
    )
```
